32 devices in a mesh: fibre: 2 (over y), blk: 8 (over z, x), src: 2 (over core).
Axes of the slice: x: 2, y: 2, z: 4, core: 2. Of those that a mesh axis runs over, the one named last changes fastest.
Arguments:
- traces: float32 [96, 16, 512], P(('fibre', 'src'), 'blk'), parts along dimension 0, may hold values from -200 to 200
- valid_flags: int32 [96, 16], P(('fibre', 'src'), 'blk'), parts along dimension 0, may hold values 0 or 1
- source_index: int32 [256], replicated, may hold values from 0 to 47, as said below
Outputs:
- stacked: float32 [96, 129, 256], P(('fibre', 'src', 'blk')), parts along dimension 0
The draws below stay inside these ranges and needn't reach their ends.
There are 2 independent parts, one for each index of `fibre`. The reference program is written for one: setup_inputs(seed, part) draws one part's arguments, and reference() takes and returns one part's arrays. A program takes and returns all parts, laid end to end along the dimension named above; an argument that names none is the same for every part. Nothing has to cross between parts.
Inputs may be any that keep to these rules, and one draw needn't show every extreme that they name: `source_index`: no channel appears twice where 256 <= 48; otherwise every channel appears, none more often than 256 / 48 rounded up.
All inputs are finite; a program needn't handle non-finite values. No bound on the sum of `valid_flags` on one device may be relied on, other than what follows from the above.
Results may differ from the reference program's by a relative error of at most 0.0026.
Values may be sent and summed in bfloat16 or wider, within the bound.
No kernel may reach another device: no remote copies, remote signals or barrier semaphores. Data moves between devices by JAX's collectives and lax.ppermute only.
A program may use at most 128 MiB of HBM per device.

```python
import math
import jax
import jax.numpy as jnp
from jax import lax

NSRC = 256
MAXLAG = 64
SEG = 512
NWIN = 16
CH = 48


def draw_traces(key, part):
    key = jax.random.fold_in(key, 11)
    noise_key, scale_key, offset_key = jax.random.split(key, 3)
    shape = (CH, NWIN, SEG)
    noise = jax.random.truncated_normal(noise_key, -4.0, 4.0, shape, jnp.float32)
    spread = jax.random.uniform(scale_key, (CH, NWIN, 1), jnp.float32, 0.0, math.log(10.0))
    amplitude = jnp.exp(spread)
    offset = jax.random.uniform(offset_key, (CH, NWIN, 1), jnp.float32, -2.0, 2.0)
    return (noise + offset) * amplitude


def draw_source_index(key, part):
    key = jax.random.fold_in(key, 23)
    inner_key, order_key = jax.random.split(key, 2)
    inner = jax.random.permutation(inner_key, jnp.arange(1, CH - 1, dtype=jnp.int32))
    ends = jnp.array([0, CH - 1], dtype=jnp.int32)
    every = jnp.concatenate([ends, inner], axis=0)
    copies = -(-NSRC // CH)
    chosen = jnp.tile(every, copies)[:NSRC]
    return jax.random.permutation(order_key, chosen).astype(jnp.int32)


def place_ends(values, rng, smallest, high):
    longest = values.shape.index(max(values.shape))
    spots = []
    for shift in (0, 1):
        where = [jax.random.randint(jax.random.fold_in(rng, axis), (), 0, length) for axis, length in enumerate(values.shape)]
        where[longest] = (where[longest] + shift) % values.shape[longest]
        spots.append(tuple(where))
    return values.at[spots[0]].set(smallest).at[spots[1]].set(high)


def setup_inputs(seed: int = 0, part: int = 0) -> dict:
    arg_keys = jax.random.split(jax.random.key(seed), 4)
    own_keys = jax.random.split(jax.random.fold_in(arg_keys[3], part), 4)
    return {
        "traces": draw_traces(jax.random.fold_in(jax.random.fold_in(arg_keys[3], part), 71), part),
        "valid_flags": place_ends((jax.random.randint(own_keys[1], (CH, NWIN), 0, 4) < 3).astype(jnp.int32), jax.random.fold_in(own_keys[1], 1), 0, 1),
        "source_index": draw_source_index(jax.random.fold_in(arg_keys[3], 71), part),
    }


def reference(traces, valid_flags, source_index):
    centered = traces - lax.optimization_barrier(jnp.mean(traces, axis=2, keepdims=True))
    mean_power = lax.optimization_barrier(jnp.mean(centered * centered, axis=2, keepdims=True))
    flag_values = valid_flags[:, :, None].astype(jnp.float32)
    whitened = (centered * lax.rsqrt(mean_power + 1e-05) * flag_values).astype(jnp.bfloat16)
    sources = jnp.take(whitened, source_index.astype(jnp.int32), axis=0)
    fft_length = 2 * SEG
    receiver_spec = jnp.fft.rfft(whitened.astype(jnp.float32), n=fft_length, axis=2)
    source_spec = jnp.fft.rfft(sources.astype(jnp.float32), n=fft_length, axis=2)
    receiver_real = jnp.transpose(jnp.real(receiver_spec), (2, 0, 1))
    receiver_imag = jnp.transpose(jnp.imag(receiver_spec), (2, 0, 1))
    source_real = jnp.transpose(jnp.real(source_spec), (2, 0, 1))
    source_imag = jnp.transpose(jnp.imag(source_spec), (2, 0, 1))
    highest = lax.Precision.HIGHEST
    real_part = jnp.einsum('fcw,fsw->fcs', receiver_real, source_real, precision=highest)
    real_part = real_part + jnp.einsum('fcw,fsw->fcs', receiver_imag, source_imag, precision=highest)
    imag_part = jnp.einsum('fcw,fsw->fcs', receiver_imag, source_real, precision=highest)
    imag_part = imag_part - jnp.einsum('fcw,fsw->fcs', receiver_real, source_imag, precision=highest)
    cross_spectrum = lax.complex(real_part, imag_part)
    series = jnp.fft.irfft(cross_spectrum, n=fft_length, axis=0)
    lagged = jnp.concatenate([series[fft_length - MAXLAG:], series[:MAXLAG + 1]], axis=0)
    return jnp.transpose(lagged, (1, 0, 2)) * (1.0 / math.sqrt(NWIN * SEG))
```

```python
import functools
import math

import jax
import jax.numpy as jnp
from jax import lax
from jax.experimental import pallas as pl
from jax.experimental.pallas import tpu as pltpu
from jax.sharding import PartitionSpec as P

MAXLAG = 64
LAG_COUNT = 2 * MAXLAG + 1
LANES = 256
GROUP = 8


def broadcast(value, axis, source):
    kept = jnp.where(lax.axis_index(axis) == source, value, 0).astype(value.dtype)
    return lax.psum(kept, axis)


def toeplitz_rows(group, lag_count, segment):
    shifted = jnp.stack(
        [group[:, :, lag_step : lag_step + segment] for lag_step in range(lag_count)], axis=1
    )
    return shifted.reshape(group.shape[0] * lag_count, -1)


def many_channels(traces, valid_flags, source_index):
    segment = traces.shape[2]
    centered = traces - jnp.mean(traces, axis=2, keepdims=True)
    mean_power = jnp.mean(centered * centered, axis=2, keepdims=True)
    flag_values = valid_flags[:, :, None].astype(jnp.float32)
    whitened = (centered * lax.rsqrt(mean_power + 1e-05) * flag_values).astype(jnp.bfloat16)
    pieces = []
    for owner in range(lax.axis_size("src")):
        pieces.append(broadcast(whitened, "src", owner))
    everyone = jnp.concatenate(pieces, axis=0)
    sources = jnp.take(everyone, source_index, axis=0)
    source_count = sources.shape[0]
    norm_factor = 1.0 / math.sqrt(traces.shape[1] * lax.axis_size("blk") * segment)
    own_rows = whitened.shape[0] // lax.axis_size("blk")
    flat_sources = sources.reshape(source_count, -1)
    padded = jnp.pad(whitened, ((0, 0), (0, 0), (MAXLAG, MAXLAG)))
    block_rows = math.gcd(lax.axis_size("blk") * own_rows, 16)
    grouped = padded.reshape(
        (lax.axis_size("blk") * own_rows // block_rows, block_rows) + padded.shape[1:]
    )

    def one_block(group):
        toeplitz = toeplitz_rows(group, LAG_COUNT, segment)
        products = lax.dot_general(
            toeplitz, flat_sources, (((1,), (1,)), ((), ())), preferred_element_type=jnp.float32
        )
        return (products * norm_factor).reshape(block_rows, LAG_COUNT, source_count)

    result = lax.map(one_block, grouped)
    return lax.psum_scatter(
        result.reshape(lax.axis_size("blk") * own_rows, LAG_COUNT, source_count),
        "blk",
        scatter_dimension=0,
        tiled=True,
    )


class Plan:
    def __init__(self, half, windows, segment, blk_size, src_size, source_count):
        self.half = half
        self.windows = windows
        self.segment = segment
        self.blk_size = blk_size
        self.channels = half * src_size
        self.source_count = source_count
        self.coarse = LANES // self.channels if self.channels <= LANES else 0
        if self.coarse == 0:
            return
        self.fine = -(-LAG_COUNT // self.coarse)
        self.fine_padded = -(-self.fine // (2 * GROUP)) * 2 * GROUP
        self.own = half // blk_size
        reach = segment + (self.coarse - 1) * self.fine
        self.span = -(-max(reach, segment + 2 * MAXLAG) // 128) * 128
        self.whole_groups = self.fine // GROUP * GROUP
        self.rest = self.fine - self.whole_groups
        rows = self.own * self.fine
        self.rows = -(-rows // 16) * 16
        self.norm_factor = 1.0 / math.sqrt(windows * blk_size * segment)

    def fits(self, src_size):
        return (
            self.coarse >= 2
            and src_size == 2
            and self.half % self.blk_size == 0
            and self.half % GROUP == 0
            and self.channels % 16 == 0
            and self.blk_size & (self.blk_size - 1) == 0
            and self.blk_size <= 16
        )


def whiten(plan, traces_ref, flags_ref, window):
    values = traces_ref[:, window, :]
    centered = values - jnp.mean(values, axis=1, keepdims=True)
    mean_power = jnp.mean(centered * centered, axis=1, keepdims=True)
    flag_values = flags_ref[:, window : window + 1].astype(jnp.float32)
    whitened = centered * lax.rsqrt(mean_power + 1e-05) * flag_values
    rounded = whitened.astype(jnp.bfloat16).astype(jnp.float32)
    filler = jnp.zeros((plan.half, plan.span - plan.segment), jnp.float32)
    return jnp.concatenate([rounded, filler], axis=1)


def correlate_kernel(plan, traces_ref, flags_ref, peer_traces_ref, peer_flags_ref, *refs):
    out_refs = refs[: plan.blk_size]
    toeplitz_ref, columns_ref = refs[plan.blk_size :]
    me = lax.axis_index("blk")
    span = plan.span
    filled = plan.coarse * plan.channels
    if filled < LANES:
        columns_ref[filled:, :] = jnp.zeros((LANES - filled, columns_ref.shape[1]), jnp.bfloat16)
    for window in range(plan.windows):
        at = slice(window * span, (window + 1) * span)
        mine = whiten(plan, traces_ref, flags_ref, window)
        other = whiten(plan, peer_traces_ref, peer_flags_ref, window)
        both = jnp.concatenate([mine, other], axis=0)
        for step in range(plan.coarse):
            moved = pltpu.roll(both, step * plan.fine, 1) if step else both
            columns_ref[step * plan.channels : (step + 1) * plan.channels, at] = moved.astype(jnp.bfloat16)
        for block in range(plan.blk_size):
            for member in range(plan.own):
                channel = block * plan.own + member
                row = jnp.broadcast_to(mine[channel : channel + 1, :], (GROUP, span))
                pieces = [
                    pltpu.roll(row, (MAXLAG - plan.fine + 1 + start) % span, 1, stride=1, stride_axis=0)
                    for start in range(0, plan.fine_padded, GROUP)
                ]
                rows = slice(member * plan.fine_padded, (member + 1) * plan.fine_padded)
                toeplitz_ref[block ^ me, rows, at] = jnp.concatenate(pieces, axis=0).astype(jnp.bfloat16)
    height = plan.own * plan.fine_padded
    products = lax.dot_general(
        toeplitz_ref[...].reshape(plan.blk_size * height, -1),
        columns_ref[...],
        (((1,), (1,)), ((), ())),
        preferred_element_type=jnp.float32,
    ).reshape(plan.blk_size, plan.own, plan.fine_padded, LANES)
    for hop in range(plan.blk_size):
        part = products[hop]
        pieces = [part[member, : plan.whole_groups] for member in range(plan.own)]
        if plan.rest:
            pieces += [part[member, plan.whole_groups : plan.fine] for member in range(plan.own)]
        if plan.rows > plan.own * plan.fine:
            pieces.append(jnp.zeros((plan.rows - plan.own * plan.fine, LANES), jnp.float32))
        out_refs[hop][...] = jnp.concatenate(pieces, axis=0).astype(jnp.bfloat16)


def expand_kernel(plan, index_ref, *refs):
    part_refs = refs[: plan.blk_size]
    out_ref = refs[plan.blk_size]
    height = plan.own * plan.fine_padded
    at_row = lax.broadcasted_iota(jnp.int32, (height, plan.rows), 0)
    at_part = lax.broadcasted_iota(jnp.int32, (height, plan.rows), 1)
    order = jnp.zeros((height, plan.rows), jnp.bool_)
    for member in range(plan.own):
        reverse = plan.fine - 1 - (at_row - member * plan.fine_padded)
        whole = (reverse >= 0) & (reverse < plan.whole_groups) & (at_part == member * plan.whole_groups + reverse)
        tail = plan.own * plan.whole_groups + member * plan.rest + reverse - plan.whole_groups
        rest = (reverse >= plan.whole_groups) & (reverse < plan.fine) & (at_part == tail)
        order = order | whole | rest
    order = order.astype(jnp.float32).astype(jnp.bfloat16)
    total = jnp.zeros((height, LANES), jnp.float32)
    for part_ref in part_refs:
        total += jnp.dot(order, part_ref[...], preferred_element_type=jnp.float32)
    total = total * plan.norm_factor
    first = lax.axis_index("src") * plan.half
    index = index_ref[...] - first
    index = jnp.where(index < 0, index + plan.channels, index)
    at_column = lax.broadcasted_iota(jnp.int32, (LANES, plan.source_count), 0)
    chosen = jnp.zeros((LANES, plan.source_count), jnp.bool_)
    for step in range(plan.coarse):
        chosen = chosen | (at_column == index + step * plan.channels)
    chosen = chosen.astype(jnp.float32).astype(jnp.bfloat16)
    lane = lax.broadcasted_iota(jnp.int32, (height, LANES), 1)
    high = total.astype(jnp.bfloat16)
    low = (total - high.astype(jnp.float32)).astype(jnp.bfloat16)
    for step in range(plan.coarse):
        inside = (lane >= step * plan.channels) & (lane < (step + 1) * plan.channels)
        kept = jnp.concatenate(
            [jnp.where(inside, total_part.astype(jnp.float32), 0.0).astype(jnp.bfloat16) for total_part in (high, low)],
            axis=1,
        )
        expanded = jnp.dot(kept, jnp.concatenate([chosen, chosen], axis=0), preferred_element_type=jnp.float32)
        count = min(plan.fine, LAG_COUNT - step * plan.fine)
        for member in range(plan.own):
            out_ref[member, step * plan.fine : step * plan.fine + count, :] = expanded[
                member * plan.fine_padded : member * plan.fine_padded + count
            ]


def few_channels(plan, traces, valid_flags, source_index):
    swap = [(0, 1), (1, 0)]
    peer_traces = lax.ppermute(traces, "src", swap)
    peer_flags = lax.ppermute(valid_flags, "src", swap)
    vmem = pl.BlockSpec(memory_space=pltpu.VMEM)
    width = plan.windows * plan.span
    parts = pl.pallas_call(
        functools.partial(correlate_kernel, plan),
        out_shape=[jax.ShapeDtypeStruct((plan.rows, LANES), jnp.bfloat16)] * plan.blk_size,
        in_specs=[vmem] * 4,
        out_specs=[vmem] * plan.blk_size,
        scratch_shapes=[
            pltpu.VMEM((plan.blk_size, plan.own * plan.fine_padded, width), jnp.bfloat16),
            pltpu.VMEM((LANES, width), jnp.bfloat16),
        ],
        compiler_params=pltpu.CompilerParams(vmem_limit_bytes=32 * 1024 * 1024),
        name="correlate",
    )(traces, valid_flags, peer_traces, peer_flags)
    arrived = [parts[0]]
    for hop in range(1, plan.blk_size):
        pairs = [(place, place ^ hop) for place in range(plan.blk_size)]
        arrived.append(lax.ppermute(parts[hop], "blk", pairs))
    return pl.pallas_call(
        functools.partial(expand_kernel, plan),
        out_shape=jax.ShapeDtypeStruct((plan.own, LAG_COUNT, plan.source_count), jnp.float32),
        in_specs=[vmem] * (1 + plan.blk_size),
        out_specs=vmem,
        compiler_params=pltpu.CompilerParams(vmem_limit_bytes=32 * 1024 * 1024),
        name="expand",
    )(source_index.reshape(1, -1), *arrived)


def body(traces, valid_flags, source_index):
    plan = Plan(
        traces.shape[0],
        traces.shape[1],
        traces.shape[2],
        lax.axis_size("blk"),
        lax.axis_size("src"),
        source_index.shape[0],
    )
    if plan.fits(lax.axis_size("src")):
        return few_channels(plan, traces, valid_flags, source_index)
    return many_channels(traces, valid_flags, source_index)


def solution(mesh):
    in_specs = (P(("fibre", "src"), "blk", None), P(("fibre", "src"), "blk"), P())
    out_specs = P(("fibre", "src", "blk"), None, None)
    return jax.shard_map(body, mesh=mesh, in_specs=in_specs, out_specs=out_specs, check_vma=False)
```

```python
import functools
import math

import jax
import jax.numpy as jnp
from jax import lax
from jax.experimental import pallas as pl
from jax.experimental.pallas import tpu as pltpu
from jax.sharding import PartitionSpec as P

MAXLAG = 64
LAG_COUNT = 2 * MAXLAG + 1
LANES = 256
GROUP = 8


def broadcast(value, axis, source):
    kept = jnp.where(lax.axis_index(axis) == source, value, 0).astype(value.dtype)
    return lax.psum(kept, axis)


def toeplitz_rows(group, lag_count, segment):
    shifted = jnp.stack(
        [group[:, :, lag_step : lag_step + segment] for lag_step in range(lag_count)], axis=1
    )
    return shifted.reshape(group.shape[0] * lag_count, -1)


def many_channels(traces, valid_flags, source_index):
    segment = traces.shape[2]
    centered = traces - jnp.mean(traces, axis=2, keepdims=True)
    mean_power = jnp.mean(centered * centered, axis=2, keepdims=True)
    flag_values = valid_flags[:, :, None].astype(jnp.float32)
    whitened = (centered * lax.rsqrt(mean_power + 1e-05) * flag_values).astype(jnp.bfloat16)
    pieces = []
    for owner in range(lax.axis_size("src")):
        pieces.append(broadcast(whitened, "src", owner))
    everyone = jnp.concatenate(pieces, axis=0)
    sources = jnp.take(everyone, source_index, axis=0)
    source_count = sources.shape[0]
    norm_factor = 1.0 / math.sqrt(traces.shape[1] * lax.axis_size("blk") * segment)
    own_rows = whitened.shape[0] // lax.axis_size("blk")
    flat_sources = sources.reshape(source_count, -1)
    padded = jnp.pad(whitened, ((0, 0), (0, 0), (MAXLAG, MAXLAG)))
    block_rows = math.gcd(lax.axis_size("blk") * own_rows, 16)
    grouped = padded.reshape(
        (lax.axis_size("blk") * own_rows // block_rows, block_rows) + padded.shape[1:]
    )

    def one_block(group):
        toeplitz = toeplitz_rows(group, LAG_COUNT, segment)
        products = lax.dot_general(
            toeplitz, flat_sources, (((1,), (1,)), ((), ())), preferred_element_type=jnp.float32
        )
        return (products * norm_factor).reshape(block_rows, LAG_COUNT, source_count)

    result = lax.map(one_block, grouped)
    return lax.psum_scatter(
        result.reshape(lax.axis_size("blk") * own_rows, LAG_COUNT, source_count),
        "blk",
        scatter_dimension=0,
        tiled=True,
    )


class Plan:
    def __init__(self, half, windows, segment, blk_size, src_size, source_count):
        self.half = half
        self.windows = windows
        self.segment = segment
        self.blk_size = blk_size
        self.channels = half * src_size
        self.source_count = source_count
        self.coarse = LANES // self.channels if self.channels <= LANES else 0
        if self.coarse == 0:
            return
        self.fine = -(-LAG_COUNT // self.coarse)
        self.fine_padded = -(-self.fine // (2 * GROUP)) * 2 * GROUP
        self.own = half // blk_size
        reach = segment + (self.coarse - 1) * self.fine
        self.span = -(-max(reach, segment + 2 * MAXLAG) // 128) * 128
        self.whole_groups = self.fine // GROUP * GROUP
        self.rest = self.fine - self.whole_groups
        rows = self.own * self.fine
        self.rows = -(-rows // 16) * 16
        self.norm_factor = 1.0 / math.sqrt(windows * blk_size * segment)

    def fits(self, src_size):
        return (
            self.coarse >= 2
            and src_size == 2
            and self.half % self.blk_size == 0
            and self.half % GROUP == 0
            and self.channels % 16 == 0
            and self.blk_size & (self.blk_size - 1) == 0
            and self.blk_size <= 16
        )


def whiten(plan, traces_ref, flags_ref, window):
    values = traces_ref[:, window, :]
    centered = values - jnp.mean(values, axis=1, keepdims=True)
    mean_power = jnp.mean(centered * centered, axis=1, keepdims=True)
    flag_values = flags_ref[window : window + 1, :].astype(jnp.float32).reshape(plan.half, 1)
    whitened = centered * lax.rsqrt(mean_power + 1e-05) * flag_values
    rounded = whitened.astype(jnp.bfloat16).astype(jnp.float32)
    filler = jnp.zeros((plan.half, plan.span - plan.segment), jnp.float32)
    return jnp.concatenate([rounded, filler], axis=1)


def correlate_kernel(plan, traces_ref, flags_ref, peer_traces_ref, peer_flags_ref, out_ref, toeplitz_ref, columns_ref):
    span = plan.span
    filled = plan.coarse * plan.channels
    if filled < LANES:
        columns_ref[filled:, :] = jnp.zeros((LANES - filled, columns_ref.shape[1]), jnp.bfloat16)
    for window in range(plan.windows):
        at = slice(window * span, (window + 1) * span)
        mine = whiten(plan, traces_ref, flags_ref, window)
        other = whiten(plan, peer_traces_ref, peer_flags_ref, window)
        both = jnp.concatenate([mine, other], axis=0)
        for step in range(plan.coarse):
            moved = pltpu.roll(both, step * plan.fine, 1) if step else both
            columns_ref[step * plan.channels : (step + 1) * plan.channels, at] = moved.astype(jnp.bfloat16)
        for block in range(plan.blk_size):
            for member in range(plan.own):
                channel = block * plan.own + member
                row = jnp.broadcast_to(mine[channel : channel + 1, :], (GROUP, span))
                pieces = [
                    pltpu.roll(row, (MAXLAG - plan.fine + 1 + start) % span, 1, stride=1, stride_axis=0)
                    for start in range(0, plan.fine_padded, GROUP)
                ]
                rows = slice(member * plan.fine_padded, (member + 1) * plan.fine_padded)
                toeplitz_ref[block, rows, at] = jnp.concatenate(pieces, axis=0).astype(jnp.bfloat16)
    height = plan.own * plan.fine_padded
    products = lax.dot_general(
        toeplitz_ref[...].reshape(plan.blk_size * height, -1),
        columns_ref[...],
        (((1,), (1,)), ((), ())),
        preferred_element_type=jnp.float32,
    ).reshape(plan.blk_size, plan.own, plan.fine_padded, LANES)
    for block in range(plan.blk_size):
        part = products[block]
        pieces = [part[member, : plan.whole_groups] for member in range(plan.own)]
        if plan.rest:
            pieces += [part[member, plan.whole_groups : plan.fine] for member in range(plan.own)]
        if plan.rows > plan.own * plan.fine:
            pieces.append(jnp.zeros((plan.rows - plan.own * plan.fine, LANES), jnp.float32))
        out_ref[block] = jnp.concatenate(pieces, axis=0).astype(jnp.bfloat16)


def expand_kernel(plan, index_ref, parts_ref, out_ref):
    height = plan.own * plan.fine_padded
    at_row = lax.broadcasted_iota(jnp.int32, (height, plan.rows), 0)
    at_part = lax.broadcasted_iota(jnp.int32, (height, plan.rows), 1)
    order = jnp.zeros((height, plan.rows), jnp.bool_)
    for member in range(plan.own):
        reverse = plan.fine - 1 - (at_row - member * plan.fine_padded)
        whole = (reverse >= 0) & (reverse < plan.whole_groups) & (at_part == member * plan.whole_groups + reverse)
        tail = plan.own * plan.whole_groups + member * plan.rest + reverse - plan.whole_groups
        rest = (reverse >= plan.whole_groups) & (reverse < plan.fine) & (at_part == tail)
        order = order | whole | rest
    order = order.astype(jnp.float32).astype(jnp.bfloat16)
    total = jnp.zeros((height, LANES), jnp.float32)
    for block in range(plan.blk_size):
        total += jnp.dot(order, parts_ref[block], preferred_element_type=jnp.float32)
    total = total * plan.norm_factor
    first = lax.axis_index("src") * plan.half
    index = index_ref[...] - first
    index = jnp.where(index < 0, index + plan.channels, index)
    at_column = lax.broadcasted_iota(jnp.int32, (LANES, plan.source_count), 0)
    chosen = jnp.zeros((LANES, plan.source_count), jnp.bool_)
    for step in range(plan.coarse):
        chosen = chosen | (at_column == index + step * plan.channels)
    chosen = chosen.astype(jnp.float32).astype(jnp.bfloat16)
    lane = lax.broadcasted_iota(jnp.int32, (height, LANES), 1)
    high = total.astype(jnp.bfloat16)
    low = (total - high.astype(jnp.float32)).astype(jnp.bfloat16)
    for step in range(plan.coarse):
        inside = (lane >= step * plan.channels) & (lane < (step + 1) * plan.channels)
        kept = jnp.concatenate(
            [jnp.where(inside, total_part.astype(jnp.float32), 0.0).astype(jnp.bfloat16) for total_part in (high, low)],
            axis=1,
        )
        expanded = jnp.dot(kept, jnp.concatenate([chosen, chosen], axis=0), preferred_element_type=jnp.float32)
        count = min(plan.fine, LAG_COUNT - step * plan.fine)
        for member in range(plan.own):
            out_ref[member, step * plan.fine : step * plan.fine + count, :] = expanded[
                member * plan.fine_padded : member * plan.fine_padded + count
            ]


def few_channels(plan, traces, valid_flags, source_index):
    swap = [(0, 1), (1, 0)]
    peer_traces = lax.ppermute(traces, "src", swap)
    flags = valid_flags.T
    peer_flags = lax.ppermute(flags, "src", swap)
    vmem = pl.BlockSpec(memory_space=pltpu.VMEM)
    width = plan.windows * plan.span
    parts = pl.pallas_call(
        functools.partial(correlate_kernel, plan),
        out_shape=jax.ShapeDtypeStruct((plan.blk_size, plan.rows, LANES), jnp.bfloat16),
        in_specs=[vmem] * 4,
        out_specs=vmem,
        scratch_shapes=[
            pltpu.VMEM((plan.blk_size, plan.own * plan.fine_padded, width), jnp.bfloat16),
            pltpu.VMEM((LANES, width), jnp.bfloat16),
        ],
        compiler_params=pltpu.CompilerParams(vmem_limit_bytes=32 * 1024 * 1024),
        name="correlate",
    )(traces, flags, peer_traces, peer_flags)
    arrived = lax.all_to_all(parts, "blk", 0, 0, tiled=True)
    return pl.pallas_call(
        functools.partial(expand_kernel, plan),
        out_shape=jax.ShapeDtypeStruct((plan.own, LAG_COUNT, plan.source_count), jnp.float32),
        in_specs=[vmem] * 2,
        out_specs=vmem,
        compiler_params=pltpu.CompilerParams(vmem_limit_bytes=32 * 1024 * 1024),
        name="expand",
    )(source_index.reshape(1, -1), arrived)


def body(traces, valid_flags, source_index):
    plan = Plan(
        traces.shape[0],
        traces.shape[1],
        traces.shape[2],
        lax.axis_size("blk"),
        lax.axis_size("src"),
        source_index.shape[0],
    )
    if plan.fits(lax.axis_size("src")):
        return few_channels(plan, traces, valid_flags, source_index)
    return many_channels(traces, valid_flags, source_index)


def solution(mesh):
    in_specs = (P(("fibre", "src"), "blk", None), P(("fibre", "src"), "blk"), P())
    out_specs = P(("fibre", "src", "blk"), None, None)
    return jax.shard_map(body, mesh=mesh, in_specs=in_specs, out_specs=out_specs, check_vma=False)
```

```python
import functools
import math

import jax
import jax.numpy as jnp
from jax import lax
from jax.experimental import pallas as pl
from jax.experimental.pallas import tpu as pltpu
from jax.sharding import PartitionSpec as P

MAXLAG = 64
LAG_COUNT = 2 * MAXLAG + 1
LANES = 256
GROUP = 8


def broadcast(value, axis, source):
    kept = jnp.where(lax.axis_index(axis) == source, value, 0).astype(value.dtype)
    return lax.psum(kept, axis)


def toeplitz_rows(group, lag_count, segment):
    shifted = jnp.stack(
        [group[:, :, lag_step : lag_step + segment] for lag_step in range(lag_count)], axis=1
    )
    return shifted.reshape(group.shape[0] * lag_count, -1)


def many_channels(traces, valid_flags, source_index):
    segment = traces.shape[2]
    centered = traces - jnp.mean(traces, axis=2, keepdims=True)
    mean_power = jnp.mean(centered * centered, axis=2, keepdims=True)
    flag_values = valid_flags[:, :, None].astype(jnp.float32)
    whitened = (centered * lax.rsqrt(mean_power + 1e-05) * flag_values).astype(jnp.bfloat16)
    pieces = []
    for owner in range(lax.axis_size("src")):
        pieces.append(broadcast(whitened, "src", owner))
    everyone = jnp.concatenate(pieces, axis=0)
    sources = jnp.take(everyone, source_index, axis=0)
    source_count = sources.shape[0]
    norm_factor = 1.0 / math.sqrt(traces.shape[1] * lax.axis_size("blk") * segment)
    own_rows = whitened.shape[0] // lax.axis_size("blk")
    flat_sources = sources.reshape(source_count, -1)
    padded = jnp.pad(whitened, ((0, 0), (0, 0), (MAXLAG, MAXLAG)))
    block_rows = math.gcd(lax.axis_size("blk") * own_rows, 16)
    grouped = padded.reshape(
        (lax.axis_size("blk") * own_rows // block_rows, block_rows) + padded.shape[1:]
    )

    def one_block(group):
        toeplitz = toeplitz_rows(group, LAG_COUNT, segment)
        products = lax.dot_general(
            toeplitz, flat_sources, (((1,), (1,)), ((), ())), preferred_element_type=jnp.float32
        )
        return (products * norm_factor).reshape(block_rows, LAG_COUNT, source_count)

    result = lax.map(one_block, grouped)
    return lax.psum_scatter(
        result.reshape(lax.axis_size("blk") * own_rows, LAG_COUNT, source_count),
        "blk",
        scatter_dimension=0,
        tiled=True,
    )


class Plan:
    def __init__(self, half, windows, segment, blk_size, src_size, source_count):
        self.half = half
        self.windows = windows
        self.segment = segment
        self.blk_size = blk_size
        self.src_size = src_size
        self.channels = half * src_size
        self.source_count = source_count
        self.coarse = LANES // self.channels
        if self.coarse == 0:
            return
        self.fine = -(-LAG_COUNT // self.coarse)
        self.fine_padded = -(-self.fine // (2 * GROUP)) * 2 * GROUP
        self.own = half // blk_size
        reach = segment + (self.coarse - 1) * self.fine
        self.span = -(-max(reach, segment + 2 * MAXLAG) // 128) * 128
        self.whole_groups = self.fine // GROUP * GROUP
        self.rest = self.fine - self.whole_groups
        rows = self.own * self.fine
        self.rows = -(-rows // 16) * 16
        self.height = self.own * self.fine_padded
        self.near = blk_size // 2
        self.norm_factor = 1.0 / math.sqrt(windows * blk_size * segment)

    def fits(self):
        return (
            self.coarse >= 2
            and self.src_size == 2
            and self.half % self.blk_size == 0
            and self.half % GROUP == 0
            and self.channels % 16 == 0
            and self.windows * self.half % 16 == 0
            and self.blk_size & (self.blk_size - 1) == 0
            and 2 <= self.blk_size <= 8
        )


def whiten_kernel(plan, traces_hbm, flags_hbm, out_ref, traces_ref, flags_ref, sems):
    copies = [
        pltpu.make_async_copy(traces_hbm, traces_ref, sems.at[0]),
        pltpu.make_async_copy(flags_hbm, flags_ref, sems.at[1]),
    ]
    for copy in copies:
        copy.start()
    for copy in copies:
        copy.wait()
    pieces = []
    for window in range(plan.windows):
        values = traces_ref[:, window, :]
        centered = values - jnp.mean(values, axis=1, keepdims=True)
        mean_power = jnp.mean(centered * centered, axis=1, keepdims=True)
        flag_values = flags_ref[window : window + 1, :].astype(jnp.float32).reshape(plan.half, 1)
        pieces.append(centered * lax.rsqrt(mean_power + 1e-05) * flag_values)
    out_ref[...] = jnp.concatenate(pieces, axis=0).astype(jnp.bfloat16)


def choose_kernel(plan, index_ref, after_ref, out_ref):
    first = lax.axis_index("src") * plan.half
    index = index_ref[...] - first
    index = jnp.where(index < 0, index + plan.channels, index)
    at_column = lax.broadcasted_iota(jnp.int32, (LANES, plan.source_count), 0)
    chosen = jnp.zeros((LANES, plan.source_count), jnp.bool_)
    for step in range(plan.coarse):
        chosen = chosen | (at_column == index + step * plan.channels)
    out_ref[...] = chosen.astype(jnp.float32).astype(jnp.bfloat16)


def correlate_kernel(plan, *refs):
    mine_refs = refs[: plan.near]
    other_refs = refs[plan.near : 2 * plan.near]
    kept_ref, sent_ref, rows_ref, toeplitz_ref, columns_ref = refs[2 * plan.near :]
    span = plan.span
    me = lax.axis_index("blk")
    targets = [me, me ^ plan.near]
    filled = plan.coarse * plan.channels
    if filled < LANES:
        columns_ref[filled:, :] = jnp.zeros((LANES - filled, columns_ref.shape[1]), jnp.bfloat16)
    filler = jnp.zeros((plan.channels, span - plan.segment), jnp.float32)
    for hop in range(plan.near):
        mine = mine_refs[hop][...].astype(jnp.float32)
        other = other_refs[hop][...].astype(jnp.float32)
        rows_ref[hop] = mine
        for window in range(plan.windows):
            start = (hop * plan.windows + window) * span
            at = slice(start, start + span)
            half = slice(window * plan.half, (window + 1) * plan.half)
            both = jnp.concatenate([mine[half], other[half]], axis=0)
            both = jnp.concatenate([both, filler], axis=1)
            for step in range(plan.coarse):
                moved = pltpu.roll(both, step * plan.fine, 1) if step else both
                columns_ref[step * plan.channels : (step + 1) * plan.channels, at] = moved.astype(jnp.bfloat16)
            for place, target in enumerate(targets):
                for member in range(plan.own):
                    channel = window * plan.half + target * plan.own + member
                    row = rows_ref[hop, pl.ds(channel, 1), :]
                    row = jnp.concatenate([row, filler[:1]], axis=1)
                    row = jnp.broadcast_to(row, (GROUP, span))
                    pieces = [
                        pltpu.roll(row, (MAXLAG - plan.fine + 1 + lag) % span, 1, stride=1, stride_axis=0)
                        for lag in range(0, plan.fine_padded, GROUP)
                    ]
                    first = place * plan.height + member * plan.fine_padded
                    toeplitz_ref[first : first + plan.fine_padded, at] = jnp.concatenate(pieces, axis=0).astype(
                        jnp.bfloat16
                    )
    products = lax.dot_general(
        toeplitz_ref[...],
        columns_ref[...],
        (((1,), (1,)), ((), ())),
        preferred_element_type=jnp.float32,
    ).reshape(len(targets), plan.own, plan.fine_padded, LANES)
    packed = []
    for place in range(len(targets)):
        part = products[place]
        pieces = [part[member, : plan.whole_groups] for member in range(plan.own)]
        if plan.rest:
            pieces += [part[member, plan.whole_groups : plan.fine] for member in range(plan.own)]
        if plan.rows > plan.own * plan.fine:
            pieces.append(jnp.zeros((plan.rows - plan.own * plan.fine, LANES), jnp.float32))
        packed.append(jnp.concatenate(pieces, axis=0))
    sent_ref[...] = packed[1].astype(jnp.bfloat16)
    kept_ref[...] = packed[0]


def halves(values):
    high = values.astype(jnp.bfloat16)
    return high, (values - high.astype(jnp.float32)).astype(jnp.bfloat16)


def expand_kernel(plan, chosen_ref, kept_ref, arrived_ref, out_ref):
    at_row = lax.broadcasted_iota(jnp.int32, (plan.height, plan.rows), 0)
    at_part = lax.broadcasted_iota(jnp.int32, (plan.height, plan.rows), 1)
    order = jnp.zeros((plan.height, plan.rows), jnp.bool_)
    for member in range(plan.own):
        reverse = plan.fine - 1 - (at_row - member * plan.fine_padded)
        whole = (reverse >= 0) & (reverse < plan.whole_groups) & (at_part == member * plan.whole_groups + reverse)
        tail = plan.own * plan.whole_groups + member * plan.rest + reverse - plan.whole_groups
        rest = (reverse >= plan.whole_groups) & (reverse < plan.fine) & (at_part == tail)
        order = order | whole | rest
    order = order.astype(jnp.float32).astype(jnp.bfloat16)
    total = (kept_ref[...] + arrived_ref[...].astype(jnp.float32)) * plan.norm_factor
    ordered = [jnp.dot(order, part, preferred_element_type=jnp.float32) for part in halves(total)]
    lane = lax.broadcasted_iota(jnp.int32, (plan.height, LANES), 1)
    chosen = chosen_ref[...]
    for step in range(plan.coarse):
        inside = (lane >= step * plan.channels) & (lane < (step + 1) * plan.channels)
        expanded = jnp.zeros((plan.height, plan.source_count), jnp.float32)
        for part in ordered:
            kept = jnp.where(inside, part, 0.0).astype(jnp.bfloat16)
            expanded += jnp.dot(kept, chosen, preferred_element_type=jnp.float32)
        count = min(plan.fine, LAG_COUNT - step * plan.fine)
        for member in range(plan.own):
            out_ref[member, step * plan.fine : step * plan.fine + count, :] = expanded[
                member * plan.fine_padded : member * plan.fine_padded + count
            ]


def few_channels(plan, traces, valid_flags, source_index):
    vmem = pl.BlockSpec(memory_space=pltpu.VMEM)
    anywhere = pl.BlockSpec(memory_space=pl.ANY)
    params = pltpu.CompilerParams(vmem_limit_bytes=32 * 1024 * 1024)
    packed_rows = plan.windows * plan.half
    flags = valid_flags.T

    def swap_cores(array):
        return lax.ppermute(array, "src", [(0, 1), (1, 0)])

    def swap_blk(array, hop):
        return lax.ppermute(array, "blk", [(place, place ^ hop) for place in range(plan.blk_size)])

    whitened = pl.pallas_call(
        functools.partial(whiten_kernel, plan),
        out_shape=jax.ShapeDtypeStruct((packed_rows, plan.segment), jnp.bfloat16),
        in_specs=[anywhere] * 2,
        out_specs=vmem,
        scratch_shapes=[
            pltpu.VMEM(traces.shape, jnp.float32),
            pltpu.VMEM(flags.shape, jnp.int32),
            pltpu.SemaphoreType.DMA((2,)),
        ],
        compiler_params=pltpu.CompilerParams(vmem_limit_bytes=60 * 1024 * 1024),
        name="whiten",
    )(traces, flags)
    mine = [whitened] + [swap_blk(whitened, hop) for hop in range(1, plan.near)]
    other = [swap_cores(array) for array in mine]
    chosen = pl.pallas_call(
        functools.partial(choose_kernel, plan),
        out_shape=jax.ShapeDtypeStruct((LANES, plan.source_count), jnp.bfloat16),
        in_specs=[vmem, pl.BlockSpec(memory_space=pl.ANY)],
        out_specs=vmem,
        compiler_params=params,
        name="choose",
    )(source_index.reshape(1, -1), whitened)
    width = plan.near * plan.windows * plan.span
    kept, sent = pl.pallas_call(
        functools.partial(correlate_kernel, plan),
        out_shape=[
            jax.ShapeDtypeStruct((plan.rows, LANES), jnp.float32),
            jax.ShapeDtypeStruct((plan.rows, LANES), jnp.bfloat16),
        ],
        in_specs=[vmem] * (2 * plan.near),
        out_specs=[vmem] * 2,
        scratch_shapes=[
            pltpu.VMEM((plan.near, packed_rows, plan.segment), jnp.float32),
            pltpu.VMEM((2 * plan.height, width), jnp.bfloat16),
            pltpu.VMEM((LANES, width), jnp.bfloat16),
        ],
        compiler_params=params,
        name="correlate",
    )(*mine, *other)
    arrived = swap_blk(sent, plan.near)
    return pl.pallas_call(
        functools.partial(expand_kernel, plan),
        out_shape=jax.ShapeDtypeStruct((plan.own, LAG_COUNT, plan.source_count), jnp.float32),
        in_specs=[vmem] * 3,
        out_specs=vmem,
        compiler_params=params,
        name="expand",
    )(chosen, kept, arrived)


def body(traces, valid_flags, source_index):
    plan = Plan(
        traces.shape[0],
        traces.shape[1],
        traces.shape[2],
        lax.axis_size("blk"),
        lax.axis_size("src"),
        source_index.shape[0],
    )
    if plan.fits():
        return few_channels(plan, traces, valid_flags, source_index)
    return many_channels(traces, valid_flags, source_index)


def solution(mesh):
    in_specs = (P(("fibre", "src"), "blk", None), P(("fibre", "src"), "blk"), P())
    out_specs = P(("fibre", "src", "blk"), None, None)
    return jax.shard_map(body, mesh=mesh, in_specs=in_specs, out_specs=out_specs, check_vma=False)
```

```python
import functools
import math

import jax
import jax.numpy as jnp
from jax import lax
from jax.experimental import pallas as pl
from jax.experimental.pallas import tpu as pltpu
from jax.sharding import PartitionSpec as P

MAXLAG = 64
LAG_COUNT = 2 * MAXLAG + 1
LANES = 256
GROUP = 8


def broadcast(value, axis, source):
    kept = jnp.where(lax.axis_index(axis) == source, value, 0).astype(value.dtype)
    return lax.psum(kept, axis)


def toeplitz_rows(group, lag_count, segment):
    shifted = jnp.stack(
        [group[:, :, lag_step : lag_step + segment] for lag_step in range(lag_count)], axis=1
    )
    return shifted.reshape(group.shape[0] * lag_count, -1)


def many_channels(traces, valid_flags, source_index):
    segment = traces.shape[2]
    centered = traces - jnp.mean(traces, axis=2, keepdims=True)
    mean_power = jnp.mean(centered * centered, axis=2, keepdims=True)
    flag_values = valid_flags[:, :, None].astype(jnp.float32)
    whitened = (centered * lax.rsqrt(mean_power + 1e-05) * flag_values).astype(jnp.bfloat16)
    pieces = []
    for owner in range(lax.axis_size("src")):
        pieces.append(broadcast(whitened, "src", owner))
    everyone = jnp.concatenate(pieces, axis=0)
    sources = jnp.take(everyone, source_index, axis=0)
    source_count = sources.shape[0]
    norm_factor = 1.0 / math.sqrt(traces.shape[1] * lax.axis_size("blk") * segment)
    own_rows = whitened.shape[0] // lax.axis_size("blk")
    flat_sources = sources.reshape(source_count, -1)
    padded = jnp.pad(whitened, ((0, 0), (0, 0), (MAXLAG, MAXLAG)))
    block_rows = math.gcd(lax.axis_size("blk") * own_rows, 16)
    grouped = padded.reshape(
        (lax.axis_size("blk") * own_rows // block_rows, block_rows) + padded.shape[1:]
    )

    def one_block(group):
        toeplitz = toeplitz_rows(group, LAG_COUNT, segment)
        products = lax.dot_general(
            toeplitz, flat_sources, (((1,), (1,)), ((), ())), preferred_element_type=jnp.float32
        )
        return (products * norm_factor).reshape(block_rows, LAG_COUNT, source_count)

    result = lax.map(one_block, grouped)
    return lax.psum_scatter(
        result.reshape(lax.axis_size("blk") * own_rows, LAG_COUNT, source_count),
        "blk",
        scatter_dimension=0,
        tiled=True,
    )


class Plan:
    def __init__(self, half, windows, segment, blk_size, src_size, source_count):
        self.half = half
        self.windows = windows
        self.segment = segment
        self.blk_size = blk_size
        self.src_size = src_size
        self.channels = half * src_size
        self.source_count = source_count
        self.coarse = LANES // self.channels
        if self.coarse == 0:
            return
        self.fine = -(-LAG_COUNT // self.coarse)
        self.fine_padded = -(-self.fine // (2 * GROUP)) * 2 * GROUP
        self.own = half // blk_size
        reach = segment + (self.coarse - 1) * self.fine
        self.span = -(-max(reach, segment + 2 * MAXLAG) // 128) * 128
        self.whole_groups = self.fine // GROUP * GROUP
        self.rest = self.fine - self.whole_groups
        rows = self.own * self.fine
        self.rows = -(-rows // 16) * 16
        self.height = self.own * self.fine_padded
        self.near = blk_size // 2
        self.norm_factor = 1.0 / math.sqrt(windows * blk_size * segment)

    def fits(self):
        return (
            self.coarse >= 2
            and self.src_size == 2
            and self.half % self.blk_size == 0
            and self.half % GROUP == 0
            and self.channels % 16 == 0
            and self.windows * self.half % 16 == 0
            and self.blk_size == 8
        )


def whiten_kernel(plan, traces_hbm, flags_hbm, out_ref, traces_ref, flags_ref, sems):
    copies = [
        pltpu.make_async_copy(traces_hbm, traces_ref, sems.at[0]),
        pltpu.make_async_copy(flags_hbm, flags_ref, sems.at[1]),
    ]
    for copy in copies:
        copy.start()
    for copy in copies:
        copy.wait()
    pieces = []
    for window in range(plan.windows):
        values = traces_ref[:, window, :]
        centered = values - jnp.mean(values, axis=1, keepdims=True)
        mean_power = jnp.mean(centered * centered, axis=1, keepdims=True)
        flag_values = flags_ref[window : window + 1, :].astype(jnp.float32).reshape(plan.half, 1)
        pieces.append(centered * lax.rsqrt(mean_power + 1e-05) * flag_values)
    out_ref[...] = jnp.concatenate(pieces, axis=0).astype(jnp.bfloat16)


def lag_rows(plan, row):
    span = plan.span
    moved = jnp.broadcast_to(pltpu.roll(row, MAXLAG, 1), (GROUP, span))
    sublane = lax.broadcasted_iota(jnp.int32, (GROUP, span), 0)
    bit = 1
    while bit < GROUP:
        moved = jnp.where((sublane & bit) != 0, pltpu.roll(moved, span - bit, 1), moved)
        bit *= 2
    pieces = [moved]
    for lag in range(GROUP, plan.fine_padded, GROUP):
        pieces.append(pltpu.roll(moved, span - lag, 1))
    return jnp.concatenate(pieces, axis=0).astype(jnp.bfloat16)


def correlate_kernel(plan, pairs, prior, last, *refs):
    mine_refs, refs = refs[:pairs], refs[pairs:]
    other_refs, refs = refs[:pairs], refs[pairs:]
    if prior:
        prior_ref, refs = refs[0], refs[1:]
    out_refs, (rows_ref, toeplitz_ref, columns_ref) = refs[:-3], refs[-3:]
    span = plan.span
    me = lax.axis_index("blk")
    targets = [me, me ^ plan.near]
    filled = plan.coarse * plan.channels
    if filled < LANES:
        columns_ref[filled:, :] = jnp.zeros((LANES - filled, columns_ref.shape[1]), jnp.bfloat16)
    filler = jnp.zeros((plan.channels, span - plan.segment), jnp.float32)
    for pair in range(pairs):
        mine = mine_refs[pair][...].astype(jnp.float32)
        other = other_refs[pair][...].astype(jnp.float32)
        rows_ref[pair] = mine
        for window in range(plan.windows):
            start = (pair * plan.windows + window) * span
            at = slice(start, start + span)
            half = slice(window * plan.half, (window + 1) * plan.half)
            both = jnp.concatenate([mine[half], other[half]], axis=0)
            both = jnp.concatenate([both, filler], axis=1)
            for step in range(plan.coarse):
                moved = pltpu.roll(both, step * plan.fine, 1) if step else both
                columns_ref[step * plan.channels : (step + 1) * plan.channels, at] = moved.astype(jnp.bfloat16)
            for place, target in enumerate(targets):
                for member in range(plan.own):
                    channel = window * plan.half + target * plan.own + member
                    row = jnp.concatenate([rows_ref[pair, pl.ds(channel, 1), :], filler[:1]], axis=1)
                    first = place * plan.height + member * plan.fine_padded
                    toeplitz_ref[first : first + plan.fine_padded, at] = lag_rows(plan, row)
    products = lax.dot_general(
        toeplitz_ref[...],
        columns_ref[...],
        (((1,), (1,)), ((), ())),
        preferred_element_type=jnp.float32,
    )
    if prior:
        products = products + prior_ref[...]
    if not last:
        out_refs[0][...] = products
        return
    products = products.reshape(len(targets), plan.own, plan.fine_padded, LANES)
    packed = []
    for place in range(len(targets)):
        part = products[place]
        pieces = [part[member, : plan.whole_groups] for member in range(plan.own)]
        if plan.rest:
            pieces += [part[member, plan.whole_groups : plan.fine] for member in range(plan.own)]
        if plan.rows > plan.own * plan.fine:
            pieces.append(jnp.zeros((plan.rows - plan.own * plan.fine, LANES), jnp.float32))
        packed.append(jnp.concatenate(pieces, axis=0))
    out_refs[1][...] = packed[1].astype(jnp.bfloat16)
    out_refs[0][...] = packed[0]


def inside_step(plan, step, values):
    lane = lax.broadcasted_iota(jnp.int32, values.shape, 1)
    inside = (lane >= step * plan.channels) & (lane < (step + 1) * plan.channels)
    return jnp.where(inside, values, 0.0).astype(jnp.bfloat16)


def prepare_kernel(plan, index_ref, kept_ref, chosen_ref, base_ref):
    first = lax.axis_index("src") * plan.half
    index = index_ref[...] - first
    index = jnp.where(index < 0, index + plan.channels, index)
    at_column = lax.broadcasted_iota(jnp.int32, (LANES, plan.source_count), 0)
    chosen = jnp.zeros((LANES, plan.source_count), jnp.bool_)
    for step in range(plan.coarse):
        chosen = chosen | (at_column == index + step * plan.channels)
    chosen = chosen.astype(jnp.float32).astype(jnp.bfloat16)
    chosen_ref[...] = chosen
    kept = kept_ref[...] * plan.norm_factor
    high = kept.astype(jnp.bfloat16).astype(jnp.float32)
    for step in range(plan.coarse):
        base_ref[step] = sum(
            jnp.dot(inside_step(plan, step, part), chosen, preferred_element_type=jnp.float32)
            for part in (high, kept - high)
        )


def expand_kernel(plan, chosen_ref, base_ref, arrived_ref, out_hbm, out_ref, sems):
    arrived = arrived_ref[...].astype(jnp.float32)
    chosen = chosen_ref[...]
    expanded = []
    for step in range(plan.coarse):
        moved = jnp.dot(inside_step(plan, step, arrived), chosen, preferred_element_type=jnp.float32)
        expanded.append(base_ref[step] + moved * plan.norm_factor)
    copies = []
    for member in range(plan.own):
        for step in range(plan.coarse):
            start = step * plan.fine
            count = min(plan.whole_groups, LAG_COUNT - start)
            first = member * plan.whole_groups
            out_ref[member, start : start + count, :] = expanded[step][first : first + count]
            rest = min(plan.fine, LAG_COUNT - start) - count
            if rest > 0:
                start += plan.whole_groups
                first = plan.own * plan.whole_groups + member * plan.rest
                out_ref[member, start : start + rest, :] = expanded[step][first : first + rest]
        copies.append(pltpu.make_async_copy(out_ref.at[member], out_hbm.at[member], sems.at[member]))
        copies[-1].start()
    for copy in copies:
        copy.wait()


def few_channels(plan, traces, valid_flags, source_index):
    vmem = pl.BlockSpec(memory_space=pltpu.VMEM)
    params = pltpu.CompilerParams(vmem_limit_bytes=32 * 1024 * 1024)
    packed_rows = plan.windows * plan.half

    def swap_cores(array):
        return lax.ppermute(array, "src", [(0, 1), (1, 0)])

    def swap_blk(array, hops):
        pairs = []
        for place in range(plan.blk_size):
            for core in range(plan.src_size):
                pairs.append((place * plan.src_size + core, (place ^ hops[core]) * plan.src_size + core))
        return lax.ppermute(array, ("blk", "src"), pairs)

    flags = valid_flags.T
    whitened = pl.pallas_call(
        functools.partial(whiten_kernel, plan),
        out_shape=jax.ShapeDtypeStruct((packed_rows, plan.segment), jnp.bfloat16),
        in_specs=[pl.BlockSpec(memory_space=pl.ANY)] * 2,
        out_specs=vmem,
        scratch_shapes=[
            pltpu.VMEM(traces.shape, jnp.float32),
            pltpu.VMEM(flags.shape, jnp.int32),
            pltpu.SemaphoreType.DMA((2,)),
        ],
        compiler_params=pltpu.CompilerParams(vmem_limit_bytes=60 * 1024 * 1024),
        name="whiten",
    )(traces, flags)

    def correlate(mine, other, prior=None, last=False):
        pairs = len(mine)
        width = pairs * plan.windows * plan.span
        height = 2 * plan.height
        if last:
            shapes = [((plan.rows, LANES), jnp.float32), ((plan.rows, LANES), jnp.bfloat16)]
        else:
            shapes = [((height, LANES), jnp.float32)]
        operands = list(mine) + list(other) + ([] if prior is None else [prior])
        results = pl.pallas_call(
            functools.partial(correlate_kernel, plan, pairs, prior is not None, last),
            out_shape=[jax.ShapeDtypeStruct(*shape) for shape in shapes],
            in_specs=[vmem] * len(operands),
            out_specs=[vmem] * len(shapes),
            scratch_shapes=[
                pltpu.VMEM((pairs, packed_rows, plan.segment), jnp.float32),
                pltpu.VMEM((height, width), jnp.bfloat16),
                pltpu.VMEM((LANES, width), jnp.bfloat16),
            ],
            compiler_params=params,
            cost_estimate=pl.CostEstimate(
                flops=2 * height * width * LANES, bytes_accessed=4 * packed_rows * width, transcendentals=0
            ),
            name="correlate",
        )(*operands)
        return results if last else results[0]

    first = swap_blk(whitened, (1, 2))
    second = swap_blk(whitened, (2, 1))
    both = swap_blk(first, (2, 1))
    total = correlate([whitened], [swap_cores(whitened)])
    both, total = lax.optimization_barrier((both, total))
    total = correlate([first, second], [swap_cores(second), swap_cores(first)], total)
    kept, sent = correlate([both], [swap_cores(both)], total, last=True)
    arrived = swap_blk(sent, (4, 4))
    chosen, base = pl.pallas_call(
        functools.partial(prepare_kernel, plan),
        out_shape=[
            jax.ShapeDtypeStruct((LANES, plan.source_count), jnp.bfloat16),
            jax.ShapeDtypeStruct((plan.coarse, plan.rows, plan.source_count), jnp.float32),
        ],
        in_specs=[vmem] * 2,
        out_specs=[vmem] * 2,
        compiler_params=params,
        name="prepare",
    )(source_index.reshape(1, -1), kept)
    out_shape = (plan.own, LAG_COUNT, plan.source_count)
    return pl.pallas_call(
        functools.partial(expand_kernel, plan),
        out_shape=jax.ShapeDtypeStruct(out_shape, jnp.float32),
        in_specs=[vmem] * 3,
        out_specs=pl.BlockSpec(memory_space=pl.ANY),
        scratch_shapes=[pltpu.VMEM(out_shape, jnp.float32), pltpu.SemaphoreType.DMA((plan.own,))],
        compiler_params=params,
        name="expand",
    )(chosen, base, arrived)


def body(traces, valid_flags, source_index):
    plan = Plan(
        traces.shape[0],
        traces.shape[1],
        traces.shape[2],
        lax.axis_size("blk"),
        lax.axis_size("src"),
        source_index.shape[0],
    )
    if plan.fits():
        return few_channels(plan, traces, valid_flags, source_index)
    return many_channels(traces, valid_flags, source_index)


def solution(mesh):
    in_specs = (P(("fibre", "src"), "blk", None), P(("fibre", "src"), "blk"), P())
    out_specs = P(("fibre", "src", "blk"), None, None)
    return jax.shard_map(body, mesh=mesh, in_specs=in_specs, out_specs=out_specs, check_vma=False)
```

```python
import functools
import math

import jax
import jax.numpy as jnp
from jax import lax
from jax.experimental import pallas as pl
from jax.experimental.pallas import tpu as pltpu
from jax.sharding import PartitionSpec as P

MAXLAG = 64
LAG_COUNT = 2 * MAXLAG + 1
LANES = 256
GROUP = 8


def broadcast(value, axis, source):
    kept = jnp.where(lax.axis_index(axis) == source, value, 0).astype(value.dtype)
    return lax.psum(kept, axis)


def toeplitz_rows(group, lag_count, segment):
    shifted = jnp.stack(
        [group[:, :, lag_step : lag_step + segment] for lag_step in range(lag_count)], axis=1
    )
    return shifted.reshape(group.shape[0] * lag_count, -1)


def many_channels(traces, valid_flags, source_index):
    segment = traces.shape[2]
    centered = traces - jnp.mean(traces, axis=2, keepdims=True)
    mean_power = jnp.mean(centered * centered, axis=2, keepdims=True)
    flag_values = valid_flags[:, :, None].astype(jnp.float32)
    whitened = (centered * lax.rsqrt(mean_power + 1e-05) * flag_values).astype(jnp.bfloat16)
    pieces = []
    for owner in range(lax.axis_size("src")):
        pieces.append(broadcast(whitened, "src", owner))
    everyone = jnp.concatenate(pieces, axis=0)
    sources = jnp.take(everyone, source_index, axis=0)
    source_count = sources.shape[0]
    norm_factor = 1.0 / math.sqrt(traces.shape[1] * lax.axis_size("blk") * segment)
    own_rows = whitened.shape[0] // lax.axis_size("blk")
    flat_sources = sources.reshape(source_count, -1)
    padded = jnp.pad(whitened, ((0, 0), (0, 0), (MAXLAG, MAXLAG)))
    block_rows = math.gcd(lax.axis_size("blk") * own_rows, 16)
    grouped = padded.reshape(
        (lax.axis_size("blk") * own_rows // block_rows, block_rows) + padded.shape[1:]
    )

    def one_block(group):
        toeplitz = toeplitz_rows(group, LAG_COUNT, segment)
        products = lax.dot_general(
            toeplitz, flat_sources, (((1,), (1,)), ((), ())), preferred_element_type=jnp.float32
        )
        return (products * norm_factor).reshape(block_rows, LAG_COUNT, source_count)

    result = lax.map(one_block, grouped)
    return lax.psum_scatter(
        result.reshape(lax.axis_size("blk") * own_rows, LAG_COUNT, source_count),
        "blk",
        scatter_dimension=0,
        tiled=True,
    )


class Plan:
    def __init__(self, half, windows, segment, blk_size, src_size, source_count):
        self.half = half
        self.windows = windows
        self.segment = segment
        self.blk_size = blk_size
        self.src_size = src_size
        self.channels = half * src_size
        self.source_count = source_count
        self.coarse = LANES // self.channels
        if self.coarse == 0:
            return
        self.fine = -(-LAG_COUNT // self.coarse)
        self.fine_padded = -(-self.fine // (2 * GROUP)) * 2 * GROUP
        self.own = half // blk_size
        reach = segment + (self.coarse - 1) * self.fine
        self.span = -(-max(reach, segment + 2 * MAXLAG) // 128) * 128
        self.whole_groups = self.fine // GROUP * GROUP
        self.rest = self.fine - self.whole_groups
        rows = self.own * self.fine
        self.rows = -(-rows // 16) * 16
        self.height = self.own * self.fine_padded
        self.near = blk_size // 2
        self.norm_factor = 1.0 / math.sqrt(windows * blk_size * segment)

    def fits(self):
        return (
            self.coarse >= 2
            and self.src_size == 2
            and self.half % self.blk_size == 0
            and self.half % GROUP == 0
            and self.channels % 16 == 0
            and self.windows * self.half % 16 == 0
            and self.blk_size == 8
        )


def whiten_kernel(plan, traces_hbm, flags_hbm, out_ref, traces_ref, flags_ref, sems):
    copies = [
        pltpu.make_async_copy(traces_hbm, traces_ref, sems.at[0]),
        pltpu.make_async_copy(flags_hbm, flags_ref, sems.at[1]),
    ]
    for copy in copies:
        copy.start()
    for copy in copies:
        copy.wait()
    pieces = []
    for window in range(plan.windows):
        values = traces_ref[:, window, :]
        centered = values - jnp.mean(values, axis=1, keepdims=True)
        mean_power = jnp.mean(centered * centered, axis=1, keepdims=True)
        flag_values = flags_ref[window : window + 1, :].astype(jnp.float32).reshape(plan.half, 1)
        pieces.append(centered * lax.rsqrt(mean_power + 1e-05) * flag_values)
    whitened = jnp.concatenate(pieces, axis=0).astype(jnp.bfloat16)
    for part in range(plan.near):
        out_ref[part] = whitened


def correlate_kernel(plan, mine_ref, other_ref, kept_ref, sent_ref, rows_ref, toeplitz_ref, columns_ref):
    span = plan.span
    me = lax.axis_index("blk")
    targets = [me, me ^ plan.near]
    filled = plan.coarse * plan.channels
    if filled < LANES:
        columns_ref[filled:, :] = jnp.zeros((LANES - filled, columns_ref.shape[1]), jnp.bfloat16)
    filler = jnp.zeros((plan.channels, span - plan.segment), jnp.float32)
    for part in range(plan.near):
        mine = mine_ref[part].astype(jnp.float32)
        other = other_ref[part].astype(jnp.float32)
        rows_ref[part] = mine
        for window in range(plan.windows):
            start = (part * plan.windows + window) * span
            at = slice(start, start + span)
            half = slice(window * plan.half, (window + 1) * plan.half)
            both = jnp.concatenate([mine[half], other[half]], axis=0)
            both = jnp.concatenate([both, filler], axis=1)
            for step in range(plan.coarse):
                moved = pltpu.roll(both, step * plan.fine, 1) if step else both
                columns_ref[step * plan.channels : (step + 1) * plan.channels, at] = moved.astype(jnp.bfloat16)
            for place, target in enumerate(targets):
                for member in range(plan.own):
                    channel = window * plan.half + target * plan.own + member
                    row = jnp.concatenate([rows_ref[part, pl.ds(channel, 1), :], filler[:1]], axis=1)
                    row = jnp.broadcast_to(row, (GROUP, span))
                    pieces = [
                        pltpu.roll(row, (MAXLAG - plan.fine + 1 + lag) % span, 1, stride=1, stride_axis=0)
                        for lag in range(0, plan.fine_padded, GROUP)
                    ]
                    first = place * plan.height + member * plan.fine_padded
                    toeplitz_ref[first : first + plan.fine_padded, at] = jnp.concatenate(pieces, axis=0).astype(
                        jnp.bfloat16
                    )
    products = lax.dot_general(
        toeplitz_ref[...],
        columns_ref[...],
        (((1,), (1,)), ((), ())),
        preferred_element_type=jnp.float32,
    ).reshape(len(targets), plan.own, plan.fine_padded, LANES)
    packed = []
    for place in range(len(targets)):
        part = products[place]
        pieces = [part[member, : plan.whole_groups] for member in range(plan.own)]
        if plan.rest:
            pieces += [part[member, plan.whole_groups : plan.fine] for member in range(plan.own)]
        if plan.rows > plan.own * plan.fine:
            pieces.append(jnp.zeros((plan.rows - plan.own * plan.fine, LANES), jnp.float32))
        packed.append(jnp.concatenate(pieces, axis=0))
    sent_ref[...] = packed[1].astype(jnp.bfloat16)
    kept_ref[...] = packed[0]


def order_matrix(plan):
    at_row = lax.broadcasted_iota(jnp.int32, (plan.height, plan.rows), 0)
    at_part = lax.broadcasted_iota(jnp.int32, (plan.height, plan.rows), 1)
    order = jnp.zeros((plan.height, plan.rows), jnp.bool_)
    for member in range(plan.own):
        reverse = plan.fine - 1 - (at_row - member * plan.fine_padded)
        whole = (reverse >= 0) & (reverse < plan.whole_groups) & (at_part == member * plan.whole_groups + reverse)
        tail = plan.own * plan.whole_groups + member * plan.rest + reverse - plan.whole_groups
        rest = (reverse >= plan.whole_groups) & (reverse < plan.fine) & (at_part == tail)
        order = order | whole | rest
    return order.astype(jnp.float32).astype(jnp.bfloat16)


def inside_step(plan, step, values):
    lane = lax.broadcasted_iota(jnp.int32, values.shape, 1)
    inside = (lane >= step * plan.channels) & (lane < (step + 1) * plan.channels)
    return jnp.where(inside, values, 0.0).astype(jnp.bfloat16)


def prepare_kernel(plan, index_ref, kept_ref, order_ref, chosen_ref, base_ref):
    first = lax.axis_index("src") * plan.half
    index = index_ref[...] - first
    index = jnp.where(index < 0, index + plan.channels, index)
    at_column = lax.broadcasted_iota(jnp.int32, (LANES, plan.source_count), 0)
    chosen = jnp.zeros((LANES, plan.source_count), jnp.bool_)
    for step in range(plan.coarse):
        chosen = chosen | (at_column == index + step * plan.channels)
    chosen = chosen.astype(jnp.float32).astype(jnp.bfloat16)
    chosen_ref[...] = chosen
    order = order_matrix(plan)
    order_ref[...] = order
    kept = kept_ref[...] * plan.norm_factor
    high = kept.astype(jnp.bfloat16)
    low = (kept - high.astype(jnp.float32)).astype(jnp.bfloat16)
    parts = [jnp.dot(order, part, preferred_element_type=jnp.float32) for part in (high, low)]
    for step in range(plan.coarse):
        base_ref[step] = sum(
            jnp.dot(inside_step(plan, step, part), chosen, preferred_element_type=jnp.float32) for part in parts
        )


def expand_kernel(plan, order_ref, chosen_ref, base_ref, arrived_ref, out_hbm, out_ref, sems):
    arrived = jnp.dot(order_ref[...], arrived_ref[...], preferred_element_type=jnp.float32)
    chosen = chosen_ref[...]
    expanded = []
    for step in range(plan.coarse):
        moved = jnp.dot(inside_step(plan, step, arrived), chosen, preferred_element_type=jnp.float32)
        expanded.append(base_ref[step] + moved * plan.norm_factor)
    copies = []
    for member in range(plan.own):
        for step in range(plan.coarse):
            start = step * plan.fine
            count = min(plan.fine, LAG_COUNT - start)
            first = member * plan.fine_padded
            out_ref[member, start : start + count, :] = expanded[step][first : first + count]
        copies.append(pltpu.make_async_copy(out_ref.at[member], out_hbm.at[member], sems.at[member]))
        copies[-1].start()
    for copy in copies:
        copy.wait()


def few_channels(plan, traces, valid_flags, source_index):
    vmem = pl.BlockSpec(memory_space=pltpu.VMEM)
    params = pltpu.CompilerParams(vmem_limit_bytes=32 * 1024 * 1024)
    packed_rows = plan.windows * plan.half
    flags = valid_flags.T
    copies = pl.pallas_call(
        functools.partial(whiten_kernel, plan),
        out_shape=jax.ShapeDtypeStruct((plan.near, packed_rows, plan.segment), jnp.bfloat16),
        in_specs=[pl.BlockSpec(memory_space=pl.ANY)] * 2,
        out_specs=vmem,
        scratch_shapes=[
            pltpu.VMEM(traces.shape, jnp.float32),
            pltpu.VMEM(flags.shape, jnp.int32),
            pltpu.SemaphoreType.DMA((2,)),
        ],
        compiler_params=pltpu.CompilerParams(vmem_limit_bytes=60 * 1024 * 1024),
        name="whiten",
    )(traces, flags)
    sides = [list(range(plan.near)), list(range(plan.near, plan.blk_size))]
    mine = lax.all_to_all(copies, "blk", 0, 0, axis_index_groups=sides, tiled=True)
    other = lax.ppermute(mine, "src", [(0, 1), (1, 0)])
    height = 2 * plan.height
    width = plan.near * plan.windows * plan.span
    kept, sent = pl.pallas_call(
        functools.partial(correlate_kernel, plan),
        out_shape=[
            jax.ShapeDtypeStruct((plan.rows, LANES), jnp.float32),
            jax.ShapeDtypeStruct((plan.rows, LANES), jnp.bfloat16),
        ],
        in_specs=[vmem] * 2,
        out_specs=[vmem] * 2,
        scratch_shapes=[
            pltpu.VMEM((plan.near, packed_rows, plan.segment), jnp.float32),
            pltpu.VMEM((height, width), jnp.bfloat16),
            pltpu.VMEM((LANES, width), jnp.bfloat16),
        ],
        compiler_params=params,
        name="correlate",
    )(mine, other)
    pairs = [(place, place ^ plan.near) for place in range(plan.blk_size)]
    arrived = lax.ppermute(sent, "blk", pairs)
    order, chosen, base = pl.pallas_call(
        functools.partial(prepare_kernel, plan),
        out_shape=[
            jax.ShapeDtypeStruct((plan.height, plan.rows), jnp.bfloat16),
            jax.ShapeDtypeStruct((LANES, plan.source_count), jnp.bfloat16),
            jax.ShapeDtypeStruct((plan.coarse, plan.height, plan.source_count), jnp.float32),
        ],
        in_specs=[vmem] * 2,
        out_specs=[vmem] * 3,
        compiler_params=params,
        name="prepare",
    )(source_index.reshape(1, -1), kept)
    out_shape = (plan.own, LAG_COUNT, plan.source_count)
    return pl.pallas_call(
        functools.partial(expand_kernel, plan),
        out_shape=jax.ShapeDtypeStruct(out_shape, jnp.float32),
        in_specs=[vmem] * 4,
        out_specs=pl.BlockSpec(memory_space=pl.ANY),
        scratch_shapes=[pltpu.VMEM(out_shape, jnp.float32), pltpu.SemaphoreType.DMA((plan.own,))],
        compiler_params=params,
        name="expand",
    )(order, chosen, base, arrived)


def body(traces, valid_flags, source_index):
    plan = Plan(
        traces.shape[0],
        traces.shape[1],
        traces.shape[2],
        lax.axis_size("blk"),
        lax.axis_size("src"),
        source_index.shape[0],
    )
    if plan.fits():
        return few_channels(plan, traces, valid_flags, source_index)
    return many_channels(traces, valid_flags, source_index)


def solution(mesh):
    in_specs = (P(("fibre", "src"), "blk", None), P(("fibre", "src"), "blk"), P())
    out_specs = P(("fibre", "src", "blk"), None, None)
    return jax.shard_map(body, mesh=mesh, in_specs=in_specs, out_specs=out_specs, check_vma=False)
```

```python
import functools
import math

import jax
import jax.numpy as jnp
from jax import lax
from jax.experimental import pallas as pl
from jax.experimental.pallas import tpu as pltpu
from jax.sharding import PartitionSpec as P

MAXLAG = 64
LAG_COUNT = 2 * MAXLAG + 1
LANES = 256
GROUP = 8


def broadcast(value, axis, source):
    kept = jnp.where(lax.axis_index(axis) == source, value, 0).astype(value.dtype)
    return lax.psum(kept, axis)


def toeplitz_rows(group, lag_count, segment):
    shifted = jnp.stack(
        [group[:, :, lag_step : lag_step + segment] for lag_step in range(lag_count)], axis=1
    )
    return shifted.reshape(group.shape[0] * lag_count, -1)


def many_channels(traces, valid_flags, source_index):
    segment = traces.shape[2]
    centered = traces - jnp.mean(traces, axis=2, keepdims=True)
    mean_power = jnp.mean(centered * centered, axis=2, keepdims=True)
    flag_values = valid_flags[:, :, None].astype(jnp.float32)
    whitened = (centered * lax.rsqrt(mean_power + 1e-05) * flag_values).astype(jnp.bfloat16)
    pieces = []
    for owner in range(lax.axis_size("src")):
        pieces.append(broadcast(whitened, "src", owner))
    everyone = jnp.concatenate(pieces, axis=0)
    sources = jnp.take(everyone, source_index, axis=0)
    source_count = sources.shape[0]
    norm_factor = 1.0 / math.sqrt(traces.shape[1] * lax.axis_size("blk") * segment)
    own_rows = whitened.shape[0] // lax.axis_size("blk")
    flat_sources = sources.reshape(source_count, -1)
    padded = jnp.pad(whitened, ((0, 0), (0, 0), (MAXLAG, MAXLAG)))
    block_rows = math.gcd(lax.axis_size("blk") * own_rows, 16)
    grouped = padded.reshape(
        (lax.axis_size("blk") * own_rows // block_rows, block_rows) + padded.shape[1:]
    )

    def one_block(group):
        toeplitz = toeplitz_rows(group, LAG_COUNT, segment)
        products = lax.dot_general(
            toeplitz, flat_sources, (((1,), (1,)), ((), ())), preferred_element_type=jnp.float32
        )
        return (products * norm_factor).reshape(block_rows, LAG_COUNT, source_count)

    result = lax.map(one_block, grouped)
    return lax.psum_scatter(
        result.reshape(lax.axis_size("blk") * own_rows, LAG_COUNT, source_count),
        "blk",
        scatter_dimension=0,
        tiled=True,
    )


class Plan:
    def __init__(self, half, windows, segment, blk_size, src_size, source_count):
        self.half = half
        self.windows = windows
        self.segment = segment
        self.blk_size = blk_size
        self.src_size = src_size
        self.channels = half * src_size
        self.source_count = source_count
        self.coarse = LANES // self.channels
        if self.coarse == 0:
            return
        self.fine = -(-LAG_COUNT // self.coarse)
        self.fine_padded = -(-self.fine // (2 * GROUP)) * 2 * GROUP
        self.own = half // blk_size
        reach = segment + (self.coarse - 1) * self.fine
        self.span = -(-max(reach, segment + 2 * MAXLAG) // 128) * 128
        self.whole_groups = self.fine // GROUP * GROUP
        self.rest = self.fine - self.whole_groups
        rows = self.own * self.fine
        self.rows = -(-rows // 16) * 16
        self.height = self.own * self.fine_padded
        self.columns = 2
        self.targets = blk_size // self.columns
        self.norm_factor = 1.0 / math.sqrt(windows * blk_size * segment)

    def fits(self):
        return (
            self.coarse >= 2
            and self.src_size == 2
            and self.half % self.blk_size == 0
            and self.half % GROUP == 0
            and self.channels % 16 == 0
            and self.windows * self.half % 16 == 0
            and self.blk_size == 8
        )


def whiten_kernel(plan, traces_hbm, flags_hbm, out_ref, traces_ref, flags_ref, sems):
    copies = [
        pltpu.make_async_copy(traces_hbm, traces_ref, sems.at[0]),
        pltpu.make_async_copy(flags_hbm, flags_ref, sems.at[1]),
    ]
    for copy in copies:
        copy.start()
    for copy in copies:
        copy.wait()
    pieces = []
    for window in range(plan.windows):
        values = traces_ref[:, window, :]
        centered = values - jnp.mean(values, axis=1, keepdims=True)
        mean_power = jnp.mean(centered * centered, axis=1, keepdims=True)
        flag_values = flags_ref[window : window + 1, :].astype(jnp.float32).reshape(plan.half, 1)
        pieces.append(centered * lax.rsqrt(mean_power + 1e-05) * flag_values)
    out_ref[...] = jnp.concatenate(pieces, axis=0).astype(jnp.bfloat16)


def correlate_kernel(plan, last, mine_ref, other_ref, *refs):
    if last:
        prior_ref, *out_refs, rows_ref, toeplitz_ref, columns_ref = refs
    else:
        sum_ref, rows_ref, toeplitz_ref, columns_ref = refs
    span = plan.span
    me = lax.axis_index("blk")
    filled = plan.coarse * plan.channels
    if filled < LANES:
        columns_ref[filled:, :] = jnp.zeros((LANES - filled, columns_ref.shape[1]), jnp.bfloat16)
    filler = jnp.zeros((plan.channels, span - plan.segment), jnp.float32)
    mine = mine_ref[...].astype(jnp.float32)
    other = other_ref[...].astype(jnp.float32)
    rows_ref[...] = mine
    for window in range(plan.windows):
        at = slice(window * span, (window + 1) * span)
        half = slice(window * plan.half, (window + 1) * plan.half)
        both = jnp.concatenate([mine[half], other[half]], axis=0)
        both = jnp.concatenate([both, filler], axis=1)
        for step in range(plan.coarse):
            moved = pltpu.roll(both, step * plan.fine, 1) if step else both
            columns_ref[step * plan.channels : (step + 1) * plan.channels, at] = moved.astype(jnp.bfloat16)
        for hop in range(plan.targets):
            target = me ^ (hop * plan.columns)
            for member in range(plan.own):
                channel = window * plan.half + target * plan.own + member
                row = jnp.concatenate([rows_ref[pl.ds(channel, 1), :], filler[:1]], axis=1)
                row = jnp.broadcast_to(row, (GROUP, span))
                pieces = [
                    pltpu.roll(row, (MAXLAG - plan.fine + 1 + lag) % span, 1, stride=1, stride_axis=0)
                    for lag in range(0, plan.fine_padded, GROUP)
                ]
                first = hop * plan.height + member * plan.fine_padded
                toeplitz_ref[first : first + plan.fine_padded, at] = jnp.concatenate(pieces, axis=0).astype(
                    jnp.bfloat16
                )
    products = lax.dot_general(
        toeplitz_ref[...],
        columns_ref[...],
        (((1,), (1,)), ((), ())),
        preferred_element_type=jnp.float32,
    )
    if not last:
        sum_ref[...] = products
        return
    products = (products + prior_ref[...]).reshape(plan.targets, plan.own, plan.fine_padded, LANES)
    for hop in range(plan.targets):
        part = products[hop]
        pieces = [part[member, : plan.whole_groups] for member in range(plan.own)]
        if plan.rest:
            pieces += [part[member, plan.whole_groups : plan.fine] for member in range(plan.own)]
        if plan.rows > plan.own * plan.fine:
            pieces.append(jnp.zeros((plan.rows - plan.own * plan.fine, LANES), jnp.float32))
        packed = jnp.concatenate(pieces, axis=0)
        out_refs[hop][...] = packed.astype(out_refs[hop].dtype)


def order_matrix(plan):
    at_row = lax.broadcasted_iota(jnp.int32, (plan.height, plan.rows), 0)
    at_part = lax.broadcasted_iota(jnp.int32, (plan.height, plan.rows), 1)
    order = jnp.zeros((plan.height, plan.rows), jnp.bool_)
    for member in range(plan.own):
        reverse = plan.fine - 1 - (at_row - member * plan.fine_padded)
        whole = (reverse >= 0) & (reverse < plan.whole_groups) & (at_part == member * plan.whole_groups + reverse)
        tail = plan.own * plan.whole_groups + member * plan.rest + reverse - plan.whole_groups
        rest = (reverse >= plan.whole_groups) & (reverse < plan.fine) & (at_part == tail)
        order = order | whole | rest
    return order.astype(jnp.float32).astype(jnp.bfloat16)


def inside_step(plan, step, values):
    lane = lax.broadcasted_iota(jnp.int32, values.shape, 1)
    inside = (lane >= step * plan.channels) & (lane < (step + 1) * plan.channels)
    return jnp.where(inside, values, 0.0).astype(jnp.bfloat16)


def prepare_kernel(plan, index_ref, kept_ref, order_ref, chosen_ref, base_ref):
    first = lax.axis_index("src") * plan.half
    index = index_ref[...] - first
    index = jnp.where(index < 0, index + plan.channels, index)
    at_column = lax.broadcasted_iota(jnp.int32, (LANES, plan.source_count), 0)
    chosen = jnp.zeros((LANES, plan.source_count), jnp.bool_)
    for step in range(plan.coarse):
        chosen = chosen | (at_column == index + step * plan.channels)
    chosen = chosen.astype(jnp.float32).astype(jnp.bfloat16)
    chosen_ref[...] = chosen
    order = order_matrix(plan)
    order_ref[...] = order
    kept = kept_ref[...] * plan.norm_factor
    high = kept.astype(jnp.bfloat16)
    low = (kept - high.astype(jnp.float32)).astype(jnp.bfloat16)
    parts = [jnp.dot(order, part, preferred_element_type=jnp.float32) for part in (high, low)]
    for step in range(plan.coarse):
        base_ref[step] = sum(
            jnp.dot(inside_step(plan, step, part), chosen, preferred_element_type=jnp.float32) for part in parts
        )


def expand_kernel(plan, order_ref, chosen_ref, base_ref, *refs):
    *arrived_refs, out_hbm, out_ref, sems = refs
    order = order_ref[...]
    arrived = sum(jnp.dot(order, ref[...], preferred_element_type=jnp.float32) for ref in arrived_refs)
    high = arrived.astype(jnp.bfloat16).astype(jnp.float32)
    chosen = chosen_ref[...]
    expanded = []
    for step in range(plan.coarse):
        moved = sum(
            jnp.dot(inside_step(plan, step, part), chosen, preferred_element_type=jnp.float32)
            for part in (high, arrived - high)
        )
        expanded.append(base_ref[step] + moved * plan.norm_factor)
    copies = []
    for member in range(plan.own):
        for step in range(plan.coarse):
            start = step * plan.fine
            count = min(plan.fine, LAG_COUNT - start)
            first = member * plan.fine_padded
            out_ref[member, start : start + count, :] = expanded[step][first : first + count]
        copies.append(pltpu.make_async_copy(out_ref.at[member], out_hbm.at[member], sems.at[member]))
        copies[-1].start()
    for copy in copies:
        copy.wait()


def few_channels(plan, traces, valid_flags, source_index):
    vmem = pl.BlockSpec(memory_space=pltpu.VMEM)
    params = pltpu.CompilerParams(vmem_limit_bytes=32 * 1024 * 1024)
    packed_rows = plan.windows * plan.half
    flags = valid_flags.T

    def swap_cores(array):
        return lax.ppermute(array, "src", [(0, 1), (1, 0)])

    def swap_blk(array, hop):
        return lax.ppermute(array, "blk", [(place, place ^ hop) for place in range(plan.blk_size)])

    whitened = pl.pallas_call(
        functools.partial(whiten_kernel, plan),
        out_shape=jax.ShapeDtypeStruct((packed_rows, plan.segment), jnp.bfloat16),
        in_specs=[pl.BlockSpec(memory_space=pl.ANY)] * 2,
        out_specs=vmem,
        scratch_shapes=[
            pltpu.VMEM(traces.shape, jnp.float32),
            pltpu.VMEM(flags.shape, jnp.int32),
            pltpu.SemaphoreType.DMA((2,)),
        ],
        compiler_params=pltpu.CompilerParams(vmem_limit_bytes=60 * 1024 * 1024),
        name="whiten",
    )(traces, flags)

    height = plan.targets * plan.height
    width = plan.windows * plan.span

    def correlate(mine, other, prior=None):
        last = prior is not None
        if last:
            types = [jnp.float32] + [jnp.bfloat16] * (plan.targets - 1)
            shapes = [jax.ShapeDtypeStruct((plan.rows, LANES), dtype) for dtype in types]
        else:
            shapes = [jax.ShapeDtypeStruct((height, LANES), jnp.float32)]
        operands = [mine, other] + ([prior] if last else [])
        results = pl.pallas_call(
            functools.partial(correlate_kernel, plan, last),
            out_shape=shapes,
            in_specs=[vmem] * len(operands),
            out_specs=[vmem] * len(shapes),
            scratch_shapes=[
                pltpu.VMEM((packed_rows, plan.segment), jnp.float32),
                pltpu.VMEM((height, width), jnp.bfloat16),
                pltpu.VMEM((LANES, width), jnp.bfloat16),
            ],
            compiler_params=params,
            cost_estimate=pl.CostEstimate(
                flops=2 * height * width * LANES, bytes_accessed=4 * packed_rows * plan.segment, transcendentals=0
            ),
            name="correlate",
        )(*operands)
        return results if last else results[0]

    beside = swap_blk(whitened, 1)
    total = correlate(whitened, swap_cores(whitened))
    beside, total = lax.optimization_barrier((beside, total))
    kept, *sent = correlate(beside, swap_cores(beside), total)
    arrived = [swap_blk(sent[hop - 1], hop * plan.columns) for hop in reversed(range(1, plan.targets))]
    order, chosen, base = pl.pallas_call(
        functools.partial(prepare_kernel, plan),
        out_shape=[
            jax.ShapeDtypeStruct((plan.height, plan.rows), jnp.bfloat16),
            jax.ShapeDtypeStruct((LANES, plan.source_count), jnp.bfloat16),
            jax.ShapeDtypeStruct((plan.coarse, plan.height, plan.source_count), jnp.float32),
        ],
        in_specs=[vmem] * 2,
        out_specs=[vmem] * 3,
        compiler_params=params,
        name="prepare",
    )(source_index.reshape(1, -1), kept)
    out_shape = (plan.own, LAG_COUNT, plan.source_count)
    return pl.pallas_call(
        functools.partial(expand_kernel, plan),
        out_shape=jax.ShapeDtypeStruct(out_shape, jnp.float32),
        in_specs=[vmem] * (3 + len(arrived)),
        out_specs=pl.BlockSpec(memory_space=pl.ANY),
        scratch_shapes=[pltpu.VMEM(out_shape, jnp.float32), pltpu.SemaphoreType.DMA((plan.own,))],
        compiler_params=params,
        name="expand",
    )(order, chosen, base, *arrived)


def body(traces, valid_flags, source_index):
    plan = Plan(
        traces.shape[0],
        traces.shape[1],
        traces.shape[2],
        lax.axis_size("blk"),
        lax.axis_size("src"),
        source_index.shape[0],
    )
    if plan.fits():
        return few_channels(plan, traces, valid_flags, source_index)
    return many_channels(traces, valid_flags, source_index)


def solution(mesh):
    in_specs = (P(("fibre", "src"), "blk", None), P(("fibre", "src"), "blk"), P())
    out_specs = P(("fibre", "src", "blk"), None, None)
    return jax.shard_map(body, mesh=mesh, in_specs=in_specs, out_specs=out_specs, check_vma=False)
```

```python
import functools
import math

import jax
import jax.numpy as jnp
from jax import lax
from jax.experimental import pallas as pl
from jax.experimental.pallas import tpu as pltpu
from jax.sharding import PartitionSpec as P

MAXLAG = 64
LAG_COUNT = 2 * MAXLAG + 1
LANES = 256
GROUP = 8


def broadcast(value, axis, source):
    kept = jnp.where(lax.axis_index(axis) == source, value, 0).astype(value.dtype)
    return lax.psum(kept, axis)


def toeplitz_rows(group, lag_count, segment):
    shifted = jnp.stack(
        [group[:, :, lag_step : lag_step + segment] for lag_step in range(lag_count)], axis=1
    )
    return shifted.reshape(group.shape[0] * lag_count, -1)


def many_channels(traces, valid_flags, source_index):
    segment = traces.shape[2]
    centered = traces - jnp.mean(traces, axis=2, keepdims=True)
    mean_power = jnp.mean(centered * centered, axis=2, keepdims=True)
    flag_values = valid_flags[:, :, None].astype(jnp.float32)
    whitened = (centered * lax.rsqrt(mean_power + 1e-05) * flag_values).astype(jnp.bfloat16)
    pieces = []
    for owner in range(lax.axis_size("src")):
        pieces.append(broadcast(whitened, "src", owner))
    everyone = jnp.concatenate(pieces, axis=0)
    sources = jnp.take(everyone, source_index, axis=0)
    source_count = sources.shape[0]
    norm_factor = 1.0 / math.sqrt(traces.shape[1] * lax.axis_size("blk") * segment)
    own_rows = whitened.shape[0] // lax.axis_size("blk")
    flat_sources = sources.reshape(source_count, -1)
    padded = jnp.pad(whitened, ((0, 0), (0, 0), (MAXLAG, MAXLAG)))
    block_rows = math.gcd(lax.axis_size("blk") * own_rows, 16)
    grouped = padded.reshape(
        (lax.axis_size("blk") * own_rows // block_rows, block_rows) + padded.shape[1:]
    )

    def one_block(group):
        toeplitz = toeplitz_rows(group, LAG_COUNT, segment)
        products = lax.dot_general(
            toeplitz, flat_sources, (((1,), (1,)), ((), ())), preferred_element_type=jnp.float32
        )
        return (products * norm_factor).reshape(block_rows, LAG_COUNT, source_count)

    result = lax.map(one_block, grouped)
    return lax.psum_scatter(
        result.reshape(lax.axis_size("blk") * own_rows, LAG_COUNT, source_count),
        "blk",
        scatter_dimension=0,
        tiled=True,
    )


class Plan:
    def __init__(self, half, windows, segment, blk_size, src_size, source_count):
        self.half = half
        self.windows = windows
        self.segment = segment
        self.blk_size = blk_size
        self.src_size = src_size
        self.channels = half * src_size
        self.source_count = source_count
        self.coarse = LANES // self.channels
        if self.coarse == 0:
            return
        self.fine = -(-LAG_COUNT // self.coarse)
        self.fine_padded = -(-self.fine // (2 * GROUP)) * 2 * GROUP
        self.own = half // blk_size
        reach = segment + (self.coarse - 1) * self.fine
        self.span = -(-max(reach, segment + 2 * MAXLAG) // 128) * 128
        self.whole_groups = self.fine // GROUP * GROUP
        self.rest = self.fine - self.whole_groups
        rows = self.own * self.fine
        self.rows = -(-rows // 16) * 16
        self.height = self.own * self.fine_padded
        self.columns = 2
        self.targets = blk_size // self.columns
        self.norm_factor = 1.0 / math.sqrt(windows * blk_size * segment)

    def fits(self):
        return (
            self.coarse >= 2
            and self.src_size == 2
            and self.half % self.blk_size == 0
            and self.half % GROUP == 0
            and self.channels % 16 == 0
            and self.windows * self.half % 16 == 0
            and self.blk_size == 8
        )


def whiten_kernel(plan, traces_hbm, flags_hbm, out_ref, traces_ref, flags_ref, sems):
    copies = [
        pltpu.make_async_copy(traces_hbm, traces_ref, sems.at[0]),
        pltpu.make_async_copy(flags_hbm, flags_ref, sems.at[1]),
    ]
    for copy in copies:
        copy.start()
    for copy in copies:
        copy.wait()
    pieces = []
    for window in range(plan.windows):
        values = traces_ref[:, window, :]
        centered = values - jnp.mean(values, axis=1, keepdims=True)
        mean_power = jnp.mean(centered * centered, axis=1, keepdims=True)
        flag_values = flags_ref[window : window + 1, :].astype(jnp.float32).reshape(plan.half, 1)
        pieces.append(centered * lax.rsqrt(mean_power + 1e-05) * flag_values)
    out_ref[...] = jnp.concatenate(pieces, axis=0).astype(jnp.bfloat16)


def correlate_kernel(plan, last, mine_ref, other_ref, *refs):
    if last:
        prior_ref, *out_refs, rows_ref, toeplitz_ref, columns_ref = refs
    else:
        sum_ref, rows_ref, toeplitz_ref, columns_ref = refs
    span = plan.span
    me = lax.axis_index("blk")
    filled = plan.coarse * plan.channels
    if filled < LANES:
        columns_ref[filled:, :] = jnp.zeros((LANES - filled, columns_ref.shape[1]), jnp.bfloat16)
    filler = jnp.zeros((plan.channels, span - plan.segment), jnp.float32)
    mine = mine_ref[...].astype(jnp.float32)
    other = other_ref[...].astype(jnp.float32)
    rows_ref[...] = mine
    for window in range(plan.windows):
        at = slice(window * span, (window + 1) * span)
        half = slice(window * plan.half, (window + 1) * plan.half)
        both = jnp.concatenate([mine[half], other[half]], axis=0)
        both = jnp.concatenate([both, filler], axis=1)
        for step in range(plan.coarse):
            moved = pltpu.roll(both, step * plan.fine, 1) if step else both
            columns_ref[step * plan.channels : (step + 1) * plan.channels, at] = moved.astype(jnp.bfloat16)
        for hop in range(plan.targets):
            target = me ^ (hop * plan.columns)
            for member in range(plan.own):
                channel = window * plan.half + target * plan.own + member
                row = jnp.concatenate([rows_ref[pl.ds(channel, 1), :], filler[:1]], axis=1)
                row = jnp.broadcast_to(row, (GROUP, span))
                pieces = [
                    pltpu.roll(row, (MAXLAG - plan.fine + 1 + lag) % span, 1, stride=1, stride_axis=0)
                    for lag in range(0, plan.fine_padded, GROUP)
                ]
                first = hop * plan.height + member * plan.fine_padded
                toeplitz_ref[first : first + plan.fine_padded, at] = jnp.concatenate(pieces, axis=0).astype(
                    jnp.bfloat16
                )
    products = lax.dot_general(
        toeplitz_ref[...],
        columns_ref[...],
        (((1,), (1,)), ((), ())),
        preferred_element_type=jnp.float32,
    )
    if not last:
        sum_ref[...] = products
        return
    products = (products + prior_ref[...]).reshape(plan.targets, plan.own, plan.fine_padded, LANES)
    for hop in range(plan.targets):
        part = products[hop]
        pieces = [part[member, : plan.whole_groups] for member in range(plan.own)]
        if plan.rest:
            pieces += [part[member, plan.whole_groups : plan.fine] for member in range(plan.own)]
        if plan.rows > plan.own * plan.fine:
            pieces.append(jnp.zeros((plan.rows - plan.own * plan.fine, LANES), jnp.float32))
        packed = jnp.concatenate(pieces, axis=0)
        out_refs[hop][...] = packed.astype(out_refs[hop].dtype)


def order_matrix(plan):
    at_row = lax.broadcasted_iota(jnp.int32, (plan.height, plan.rows), 0)
    at_part = lax.broadcasted_iota(jnp.int32, (plan.height, plan.rows), 1)
    order = jnp.zeros((plan.height, plan.rows), jnp.bool_)
    for member in range(plan.own):
        reverse = plan.fine - 1 - (at_row - member * plan.fine_padded)
        whole = (reverse >= 0) & (reverse < plan.whole_groups) & (at_part == member * plan.whole_groups + reverse)
        tail = plan.own * plan.whole_groups + member * plan.rest + reverse - plan.whole_groups
        rest = (reverse >= plan.whole_groups) & (reverse < plan.fine) & (at_part == tail)
        order = order | whole | rest
    return order.astype(jnp.float32).astype(jnp.bfloat16)


def inside_step(plan, step, values):
    lane = lax.broadcasted_iota(jnp.int32, values.shape, 1)
    inside = (lane >= step * plan.channels) & (lane < (step + 1) * plan.channels)
    return jnp.where(inside, values, 0.0).astype(jnp.bfloat16)


def prepare_kernel(plan, index_ref, kept_ref, order_ref, chosen_ref, base_ref):
    first = lax.axis_index("src") * plan.half
    index = index_ref[...] - first
    index = jnp.where(index < 0, index + plan.channels, index)
    at_column = lax.broadcasted_iota(jnp.int32, (LANES, plan.source_count), 0)
    chosen = jnp.zeros((LANES, plan.source_count), jnp.bool_)
    for step in range(plan.coarse):
        chosen = chosen | (at_column == index + step * plan.channels)
    chosen = chosen.astype(jnp.float32).astype(jnp.bfloat16)
    chosen_ref[...] = chosen
    order = order_matrix(plan)
    order_ref[...] = order
    kept = kept_ref[...] * plan.norm_factor
    high = kept.astype(jnp.bfloat16)
    low = (kept - high.astype(jnp.float32)).astype(jnp.bfloat16)
    parts = [jnp.dot(order, part, preferred_element_type=jnp.float32) for part in (high, low)]
    for step in range(plan.coarse):
        base_ref[step] = sum(
            jnp.dot(inside_step(plan, step, part), chosen, preferred_element_type=jnp.float32) for part in parts
        )


def expand_kernel(plan, order_ref, chosen_ref, base_ref, *refs):
    *arrived_refs, out_hbm, out_ref, sems = refs
    order = order_ref[...]
    arrived = sum(jnp.dot(order, ref[...], preferred_element_type=jnp.float32) for ref in arrived_refs)
    high = arrived.astype(jnp.bfloat16).astype(jnp.float32)
    chosen = chosen_ref[...]
    expanded = []
    for step in range(plan.coarse):
        moved = sum(
            jnp.dot(inside_step(plan, step, part), chosen, preferred_element_type=jnp.float32)
            for part in (high, arrived - high)
        )
        expanded.append(base_ref[step] + moved * plan.norm_factor)
    copies = []
    for member in range(plan.own):
        for step in range(plan.coarse):
            start = step * plan.fine
            count = min(plan.fine, LAG_COUNT - start)
            first = member * plan.fine_padded
            out_ref[member, start : start + count, :] = expanded[step][first : first + count]
        copies.append(pltpu.make_async_copy(out_ref.at[member], out_hbm.at[member], sems.at[member]))
        copies[-1].start()
    for copy in copies:
        copy.wait()


def few_channels(plan, traces, valid_flags, source_index):
    vmem = pl.BlockSpec(memory_space=pltpu.VMEM)
    params = pltpu.CompilerParams(vmem_limit_bytes=32 * 1024 * 1024)
    packed_rows = plan.windows * plan.half
    flags = valid_flags.T

    def swap_cores(array):
        return lax.ppermute(array, "src", [(0, 1), (1, 0)])

    def swap_blk(array, hop):
        return lax.ppermute(array, "blk", [(place, place ^ hop) for place in range(plan.blk_size)])

    whitened = pl.pallas_call(
        functools.partial(whiten_kernel, plan),
        out_shape=pltpu.VMEM((packed_rows, plan.segment), jnp.bfloat16),
        in_specs=[pl.BlockSpec(memory_space=pl.ANY)] * 2,
        out_specs=vmem,
        scratch_shapes=[
            pltpu.VMEM(traces.shape, jnp.float32),
            pltpu.VMEM(flags.shape, jnp.int32),
            pltpu.SemaphoreType.DMA((2,)),
        ],
        compiler_params=pltpu.CompilerParams(vmem_limit_bytes=60 * 1024 * 1024),
        name="whiten",
    )(traces, flags)

    height = plan.targets * plan.height
    width = plan.windows * plan.span

    def correlate(mine, other, prior=None):
        last = prior is not None
        if last:
            types = [jnp.float32] + [jnp.bfloat16] * (plan.targets - 1)
            shapes = [jax.ShapeDtypeStruct((plan.rows, LANES), dtype) for dtype in types]
        else:
            shapes = [jax.ShapeDtypeStruct((height, LANES), jnp.float32)]
        operands = [mine, other] + ([prior] if last else [])
        results = pl.pallas_call(
            functools.partial(correlate_kernel, plan, last),
            out_shape=shapes,
            in_specs=[vmem] * len(operands),
            out_specs=[vmem] * len(shapes),
            scratch_shapes=[
                pltpu.VMEM((packed_rows, plan.segment), jnp.float32),
                pltpu.VMEM((height, width), jnp.bfloat16),
                pltpu.VMEM((LANES, width), jnp.bfloat16),
            ],
            compiler_params=params,
            cost_estimate=pl.CostEstimate(
                flops=2 * height * width * LANES, bytes_accessed=4 * packed_rows * plan.segment, transcendentals=0
            ),
            name="correlate",
        )(*operands)
        return results if last else results[0]

    beside = swap_blk(whitened, 1)
    total = correlate(whitened, swap_cores(whitened))
    beside, total = lax.optimization_barrier((beside, total))
    kept, *sent = correlate(beside, swap_cores(beside), total)
    arrived = [swap_blk(sent[hop - 1], hop * plan.columns) for hop in (2, 3, 1)]
    order, chosen, base = pl.pallas_call(
        functools.partial(prepare_kernel, plan),
        out_shape=[
            jax.ShapeDtypeStruct((plan.height, plan.rows), jnp.bfloat16),
            jax.ShapeDtypeStruct((LANES, plan.source_count), jnp.bfloat16),
            jax.ShapeDtypeStruct((plan.coarse, plan.height, plan.source_count), jnp.float32),
        ],
        in_specs=[vmem] * 2,
        out_specs=[vmem] * 3,
        compiler_params=params,
        name="prepare",
    )(source_index.reshape(1, -1), kept)
    out_shape = (plan.own, LAG_COUNT, plan.source_count)
    return pl.pallas_call(
        functools.partial(expand_kernel, plan),
        out_shape=jax.ShapeDtypeStruct(out_shape, jnp.float32),
        in_specs=[vmem] * (3 + len(arrived)),
        out_specs=pl.BlockSpec(memory_space=pl.ANY),
        scratch_shapes=[pltpu.VMEM(out_shape, jnp.float32), pltpu.SemaphoreType.DMA((plan.own,))],
        compiler_params=params,
        name="expand",
    )(order, chosen, base, *arrived)


def body(traces, valid_flags, source_index):
    plan = Plan(
        traces.shape[0],
        traces.shape[1],
        traces.shape[2],
        lax.axis_size("blk"),
        lax.axis_size("src"),
        source_index.shape[0],
    )
    if plan.fits():
        return few_channels(plan, traces, valid_flags, source_index)
    return many_channels(traces, valid_flags, source_index)


def solution(mesh):
    in_specs = (P(("fibre", "src"), "blk", None), P(("fibre", "src"), "blk"), P())
    out_specs = P(("fibre", "src", "blk"), None, None)
    return jax.shard_map(body, mesh=mesh, in_specs=in_specs, out_specs=out_specs, check_vma=False)
```

```python
import functools
import math

import jax
import jax.numpy as jnp
from jax import lax
from jax.experimental import pallas as pl
from jax.experimental.pallas import tpu as pltpu
from jax.sharding import PartitionSpec as P

MAXLAG = 64
LAG_COUNT = 2 * MAXLAG + 1
LANES = 256
GROUP = 8


def broadcast(value, axis, source):
    kept = jnp.where(lax.axis_index(axis) == source, value, 0).astype(value.dtype)
    return lax.psum(kept, axis)


def toeplitz_rows(group, lag_count, segment):
    shifted = jnp.stack(
        [group[:, :, lag_step : lag_step + segment] for lag_step in range(lag_count)], axis=1
    )
    return shifted.reshape(group.shape[0] * lag_count, -1)


def many_channels(traces, valid_flags, source_index):
    segment = traces.shape[2]
    centered = traces - jnp.mean(traces, axis=2, keepdims=True)
    mean_power = jnp.mean(centered * centered, axis=2, keepdims=True)
    flag_values = valid_flags[:, :, None].astype(jnp.float32)
    whitened = (centered * lax.rsqrt(mean_power + 1e-05) * flag_values).astype(jnp.bfloat16)
    pieces = []
    for owner in range(lax.axis_size("src")):
        pieces.append(broadcast(whitened, "src", owner))
    everyone = jnp.concatenate(pieces, axis=0)
    sources = jnp.take(everyone, source_index, axis=0)
    source_count = sources.shape[0]
    norm_factor = 1.0 / math.sqrt(traces.shape[1] * lax.axis_size("blk") * segment)
    own_rows = whitened.shape[0] // lax.axis_size("blk")
    flat_sources = sources.reshape(source_count, -1)
    padded = jnp.pad(whitened, ((0, 0), (0, 0), (MAXLAG, MAXLAG)))
    block_rows = math.gcd(lax.axis_size("blk") * own_rows, 16)
    grouped = padded.reshape(
        (lax.axis_size("blk") * own_rows // block_rows, block_rows) + padded.shape[1:]
    )

    def one_block(group):
        toeplitz = toeplitz_rows(group, LAG_COUNT, segment)
        products = lax.dot_general(
            toeplitz, flat_sources, (((1,), (1,)), ((), ())), preferred_element_type=jnp.float32
        )
        return (products * norm_factor).reshape(block_rows, LAG_COUNT, source_count)

    result = lax.map(one_block, grouped)
    return lax.psum_scatter(
        result.reshape(lax.axis_size("blk") * own_rows, LAG_COUNT, source_count),
        "blk",
        scatter_dimension=0,
        tiled=True,
    )


class Plan:
    def __init__(self, half, windows, segment, blk_size, src_size, source_count):
        self.half = half
        self.windows = windows
        self.segment = segment
        self.blk_size = blk_size
        self.src_size = src_size
        self.channels = half * src_size
        self.source_count = source_count
        self.coarse = LANES // self.channels
        if self.coarse == 0:
            return
        self.fine = -(-LAG_COUNT // self.coarse)
        self.fine_padded = -(-self.fine // (2 * GROUP)) * 2 * GROUP
        self.own = half // blk_size
        reach = segment + (self.coarse - 1) * self.fine
        self.span = -(-max(reach, segment + 2 * MAXLAG) // 128) * 128
        self.whole_groups = self.fine // GROUP * GROUP
        self.rest = self.fine - self.whole_groups
        rows = self.own * self.fine
        self.rows = -(-rows // 16) * 16
        self.height = self.own * self.fine_padded
        self.columns = 2
        self.targets = blk_size // self.columns
        self.norm_factor = 1.0 / math.sqrt(windows * blk_size * segment)

    def fits(self):
        return (
            self.coarse >= 2
            and self.src_size == 2
            and self.half % self.blk_size == 0
            and self.half % GROUP == 0
            and self.channels % 16 == 0
            and self.windows * self.half % 16 == 0
            and self.blk_size == 8
        )


def whiten_kernel(plan, traces_hbm, flags_hbm, out_ref, traces_ref, flags_ref, sems):
    copies = [
        pltpu.make_async_copy(traces_hbm, traces_ref, sems.at[0]),
        pltpu.make_async_copy(flags_hbm, flags_ref, sems.at[1]),
    ]
    for copy in copies:
        copy.start()
    for copy in copies:
        copy.wait()
    pieces = []
    for window in range(plan.windows):
        values = traces_ref[:, window, :]
        centered = values - jnp.mean(values, axis=1, keepdims=True)
        mean_power = jnp.mean(centered * centered, axis=1, keepdims=True)
        flag_values = flags_ref[window : window + 1, :].astype(jnp.float32).reshape(plan.half, 1)
        pieces.append(centered * lax.rsqrt(mean_power + 1e-05) * flag_values)
    out_ref[...] = jnp.concatenate(pieces, axis=0).astype(jnp.bfloat16)


def correlate_kernel(plan, last, mine_ref, other_ref, *refs):
    if last:
        prior_ref, *out_refs, rows_ref, toeplitz_ref, columns_ref = refs
    else:
        sum_ref, rows_ref, toeplitz_ref, columns_ref = refs
    span = plan.span
    me = lax.axis_index("blk")
    filled = plan.coarse * plan.channels
    if filled < LANES:
        columns_ref[filled:, :] = jnp.zeros((LANES - filled, columns_ref.shape[1]), jnp.bfloat16)
    filler = jnp.zeros((plan.channels, span - plan.segment), jnp.float32)
    mine = mine_ref[...].astype(jnp.float32)
    other = other_ref[...].astype(jnp.float32)
    rows_ref[...] = mine
    for window in range(plan.windows):
        at = slice(window * span, (window + 1) * span)
        half = slice(window * plan.half, (window + 1) * plan.half)
        both = jnp.concatenate([mine[half], other[half]], axis=0)
        both = jnp.concatenate([both, filler], axis=1)
        for step in range(plan.coarse):
            moved = pltpu.roll(both, step * plan.fine, 1) if step else both
            columns_ref[step * plan.channels : (step + 1) * plan.channels, at] = moved.astype(jnp.bfloat16)
        for hop in range(plan.targets):
            target = me ^ (hop * plan.columns)
            for member in range(plan.own):
                channel = window * plan.half + target * plan.own + member
                row = jnp.concatenate([rows_ref[pl.ds(channel, 1), :], filler[:1]], axis=1)
                row = jnp.broadcast_to(row, (GROUP, span))
                pieces = [
                    pltpu.roll(row, (MAXLAG - plan.fine + 1 + lag) % span, 1, stride=1, stride_axis=0)
                    for lag in range(0, plan.fine_padded, GROUP)
                ]
                first = hop * plan.height + member * plan.fine_padded
                toeplitz_ref[first : first + plan.fine_padded, at] = jnp.concatenate(pieces, axis=0).astype(
                    jnp.bfloat16
                )
    products = lax.dot_general(
        toeplitz_ref[...],
        columns_ref[...],
        (((1,), (1,)), ((), ())),
        preferred_element_type=jnp.float32,
    )
    if not last:
        sum_ref[...] = products
        return
    products = (products + prior_ref[...]).reshape(plan.targets, plan.own, plan.fine_padded, LANES)
    for hop in range(plan.targets):
        part = products[hop]
        pieces = [part[member, : plan.whole_groups] for member in range(plan.own)]
        if plan.rest:
            pieces += [part[member, plan.whole_groups : plan.fine] for member in range(plan.own)]
        if plan.rows > plan.own * plan.fine:
            pieces.append(jnp.zeros((plan.rows - plan.own * plan.fine, LANES), jnp.float32))
        packed = jnp.concatenate(pieces, axis=0)
        out_refs[hop][...] = packed.astype(out_refs[hop].dtype)
        if hop == plan.targets - 1:
            out_refs[hop + 1][...] = packed.astype(out_refs[hop + 1].dtype)


def order_matrix(plan):
    at_row = lax.broadcasted_iota(jnp.int32, (plan.height, plan.rows), 0)
    at_part = lax.broadcasted_iota(jnp.int32, (plan.height, plan.rows), 1)
    order = jnp.zeros((plan.height, plan.rows), jnp.bool_)
    for member in range(plan.own):
        reverse = plan.fine - 1 - (at_row - member * plan.fine_padded)
        whole = (reverse >= 0) & (reverse < plan.whole_groups) & (at_part == member * plan.whole_groups + reverse)
        tail = plan.own * plan.whole_groups + member * plan.rest + reverse - plan.whole_groups
        rest = (reverse >= plan.whole_groups) & (reverse < plan.fine) & (at_part == tail)
        order = order | whole | rest
    return order.astype(jnp.float32).astype(jnp.bfloat16)


def inside_step(plan, step, values):
    lane = lax.broadcasted_iota(jnp.int32, values.shape, 1)
    inside = (lane >= step * plan.channels) & (lane < (step + 1) * plan.channels)
    return jnp.where(inside, values, 0.0).astype(jnp.bfloat16)


def prepare_kernel(plan, index_ref, kept_ref, order_ref, chosen_ref, base_ref):
    first = lax.axis_index("src") * plan.half
    index = index_ref[...] - first
    index = jnp.where(index < 0, index + plan.channels, index)
    at_column = lax.broadcasted_iota(jnp.int32, (LANES, plan.source_count), 0)
    chosen = jnp.zeros((LANES, plan.source_count), jnp.bool_)
    for step in range(plan.coarse):
        chosen = chosen | (at_column == index + step * plan.channels)
    chosen = chosen.astype(jnp.float32).astype(jnp.bfloat16)
    chosen_ref[...] = chosen
    order = order_matrix(plan)
    order_ref[...] = order
    kept = kept_ref[...] * plan.norm_factor
    high = kept.astype(jnp.bfloat16)
    low = (kept - high.astype(jnp.float32)).astype(jnp.bfloat16)
    parts = [jnp.dot(order, part, preferred_element_type=jnp.float32) for part in (high, low)]
    for step in range(plan.coarse):
        base_ref[step] = sum(
            jnp.dot(inside_step(plan, step, part), chosen, preferred_element_type=jnp.float32) for part in parts
        )


def expand_kernel(plan, order_ref, chosen_ref, base_ref, *refs):
    inner_ref, *arrived_refs, outer_ref, out_hbm, out_ref, sems = refs
    order = order_ref[...]
    line = lax.axis_index("blk") // plan.columns
    is_outer = (line == 0) | (line == plan.targets - 1)
    blocks = [ref[...] for ref in arrived_refs] + [jnp.where(is_outer, outer_ref[...], inner_ref[...])]
    arrived = sum(jnp.dot(order, block, preferred_element_type=jnp.float32) for block in blocks)
    high = arrived.astype(jnp.bfloat16).astype(jnp.float32)
    chosen = chosen_ref[...]
    expanded = []
    for step in range(plan.coarse):
        moved = sum(
            jnp.dot(inside_step(plan, step, part), chosen, preferred_element_type=jnp.float32)
            for part in (high, arrived - high)
        )
        expanded.append(base_ref[step] + moved * plan.norm_factor)
    copies = []
    for member in range(plan.own):
        for step in range(plan.coarse):
            start = step * plan.fine
            count = min(plan.fine, LAG_COUNT - start)
            first = member * plan.fine_padded
            out_ref[member, start : start + count, :] = expanded[step][first : first + count]
        copies.append(pltpu.make_async_copy(out_ref.at[member], out_hbm.at[member], sems.at[member]))
        copies[-1].start()
    for copy in copies:
        copy.wait()


def few_channels(plan, traces, valid_flags, source_index):
    vmem = pl.BlockSpec(memory_space=pltpu.VMEM)
    params = pltpu.CompilerParams(vmem_limit_bytes=32 * 1024 * 1024)
    packed_rows = plan.windows * plan.half
    flags = valid_flags.T

    def swap_cores(array):
        return lax.ppermute(array, "src", [(0, 1), (1, 0)])

    def swap_blk(array, hop, places):
        pairs = [(place, place ^ hop if place in places else place) for place in range(plan.blk_size)]
        return lax.ppermute(array, "blk", pairs)

    whitened = pl.pallas_call(
        functools.partial(whiten_kernel, plan),
        out_shape=pltpu.VMEM((packed_rows, plan.segment), jnp.bfloat16),
        in_specs=[pl.BlockSpec(memory_space=pl.ANY)] * 2,
        out_specs=vmem,
        scratch_shapes=[
            pltpu.VMEM(traces.shape, jnp.float32),
            pltpu.VMEM(flags.shape, jnp.int32),
            pltpu.SemaphoreType.DMA((2,)),
        ],
        compiler_params=pltpu.CompilerParams(vmem_limit_bytes=60 * 1024 * 1024),
        name="whiten",
    )(traces, flags)

    height = plan.targets * plan.height
    width = plan.windows * plan.span

    def correlate(mine, other, prior=None):
        last = prior is not None
        if last:
            types = [jnp.float32] + [jnp.bfloat16] * plan.targets
            shapes = [jax.ShapeDtypeStruct((plan.rows, LANES), dtype) for dtype in types]
        else:
            shapes = [jax.ShapeDtypeStruct((height, LANES), jnp.float32)]
        operands = [mine, other] + ([prior] if last else [])
        results = pl.pallas_call(
            functools.partial(correlate_kernel, plan, last),
            out_shape=shapes,
            in_specs=[vmem] * len(operands),
            out_specs=[vmem] * len(shapes),
            scratch_shapes=[
                pltpu.VMEM((packed_rows, plan.segment), jnp.float32),
                pltpu.VMEM((height, width), jnp.bfloat16),
                pltpu.VMEM((LANES, width), jnp.bfloat16),
            ],
            compiler_params=params,
            cost_estimate=pl.CostEstimate(
                flops=2 * height * width * LANES, bytes_accessed=4 * packed_rows * plan.segment, transcendentals=0
            ),
            name="correlate",
        )(*operands)
        return results if last else results[0]

    beside = swap_blk(whitened, 1, range(plan.blk_size))
    total = correlate(whitened, swap_cores(whitened))
    beside, total = lax.optimization_barrier((beside, total))
    kept, *sent = correlate(beside, swap_cores(beside), total)
    every = range(plan.blk_size)
    outer = [place for place in every if place // plan.columns in (0, plan.targets - 1)]
    inner = [place for place in every if place not in outer]
    steps = [(sent[3], 3, inner), (sent[1], 2, every), (sent[0], 1, every), (sent[2], 3, outer)]
    arrived = [swap_blk(array, hop * plan.columns, who) for array, hop, who in steps]
    order, chosen, base = pl.pallas_call(
        functools.partial(prepare_kernel, plan),
        out_shape=[
            jax.ShapeDtypeStruct((plan.height, plan.rows), jnp.bfloat16),
            jax.ShapeDtypeStruct((LANES, plan.source_count), jnp.bfloat16),
            jax.ShapeDtypeStruct((plan.coarse, plan.height, plan.source_count), jnp.float32),
        ],
        in_specs=[vmem] * 2,
        out_specs=[vmem] * 3,
        compiler_params=params,
        name="prepare",
    )(source_index.reshape(1, -1), kept)
    out_shape = (plan.own, LAG_COUNT, plan.source_count)
    return pl.pallas_call(
        functools.partial(expand_kernel, plan),
        out_shape=jax.ShapeDtypeStruct(out_shape, jnp.float32),
        in_specs=[vmem] * (3 + len(arrived)),
        out_specs=pl.BlockSpec(memory_space=pl.ANY),
        scratch_shapes=[pltpu.VMEM(out_shape, jnp.float32), pltpu.SemaphoreType.DMA((plan.own,))],
        compiler_params=params,
        name="expand",
    )(order, chosen, base, *arrived)


def body(traces, valid_flags, source_index):
    plan = Plan(
        traces.shape[0],
        traces.shape[1],
        traces.shape[2],
        lax.axis_size("blk"),
        lax.axis_size("src"),
        source_index.shape[0],
    )
    if plan.fits():
        return few_channels(plan, traces, valid_flags, source_index)
    return many_channels(traces, valid_flags, source_index)


def solution(mesh):
    in_specs = (P(("fibre", "src"), "blk", None), P(("fibre", "src"), "blk"), P())
    out_specs = P(("fibre", "src", "blk"), None, None)
    return jax.shard_map(body, mesh=mesh, in_specs=in_specs, out_specs=out_specs, check_vma=False)
```

```python
import functools
import math

import jax
import jax.numpy as jnp
from jax import lax
from jax.experimental import pallas as pl
from jax.experimental.pallas import tpu as pltpu
from jax.sharding import PartitionSpec as P

MAXLAG = 64
LAG_COUNT = 2 * MAXLAG + 1
LANES = 256
GROUP = 8


def broadcast(value, axis, source):
    kept = jnp.where(lax.axis_index(axis) == source, value, 0).astype(value.dtype)
    return lax.psum(kept, axis)


def toeplitz_rows(group, lag_count, segment):
    shifted = jnp.stack(
        [group[:, :, lag_step : lag_step + segment] for lag_step in range(lag_count)], axis=1
    )
    return shifted.reshape(group.shape[0] * lag_count, -1)


def many_channels(traces, valid_flags, source_index):
    segment = traces.shape[2]
    centered = traces - jnp.mean(traces, axis=2, keepdims=True)
    mean_power = jnp.mean(centered * centered, axis=2, keepdims=True)
    flag_values = valid_flags[:, :, None].astype(jnp.float32)
    whitened = (centered * lax.rsqrt(mean_power + 1e-05) * flag_values).astype(jnp.bfloat16)
    pieces = []
    for owner in range(lax.axis_size("src")):
        pieces.append(broadcast(whitened, "src", owner))
    everyone = jnp.concatenate(pieces, axis=0)
    sources = jnp.take(everyone, source_index, axis=0)
    source_count = sources.shape[0]
    norm_factor = 1.0 / math.sqrt(traces.shape[1] * lax.axis_size("blk") * segment)
    own_rows = whitened.shape[0] // lax.axis_size("blk")
    flat_sources = sources.reshape(source_count, -1)
    padded = jnp.pad(whitened, ((0, 0), (0, 0), (MAXLAG, MAXLAG)))
    block_rows = math.gcd(lax.axis_size("blk") * own_rows, 16)
    grouped = padded.reshape(
        (lax.axis_size("blk") * own_rows // block_rows, block_rows) + padded.shape[1:]
    )

    def one_block(group):
        toeplitz = toeplitz_rows(group, LAG_COUNT, segment)
        products = lax.dot_general(
            toeplitz, flat_sources, (((1,), (1,)), ((), ())), preferred_element_type=jnp.float32
        )
        return (products * norm_factor).reshape(block_rows, LAG_COUNT, source_count)

    result = lax.map(one_block, grouped)
    return lax.psum_scatter(
        result.reshape(lax.axis_size("blk") * own_rows, LAG_COUNT, source_count),
        "blk",
        scatter_dimension=0,
        tiled=True,
    )


class Plan:
    def __init__(self, half, windows, segment, blk_size, src_size, source_count):
        self.half = half
        self.windows = windows
        self.segment = segment
        self.blk_size = blk_size
        self.src_size = src_size
        self.channels = half * src_size
        self.source_count = source_count
        self.coarse = LANES // self.channels
        if self.coarse == 0:
            return
        self.fine = -(-LAG_COUNT // self.coarse)
        self.fine_padded = -(-self.fine // (2 * GROUP)) * 2 * GROUP
        self.own = half // blk_size
        reach = segment + (self.coarse - 1) * self.fine
        self.span = -(-max(reach, segment + 2 * MAXLAG) // 128) * 128
        self.whole_groups = self.fine // GROUP * GROUP
        self.rest = self.fine - self.whole_groups
        rows = self.own * self.fine
        self.rows = -(-rows // 16) * 16
        self.height = self.own * self.fine_padded
        self.columns = 2
        self.targets = blk_size // self.columns
        self.norm_factor = 1.0 / math.sqrt(windows * blk_size * segment)

    def fits(self):
        return (
            self.coarse >= 2
            and self.src_size == 2
            and self.half % self.blk_size == 0
            and self.half % GROUP == 0
            and self.channels % 16 == 0
            and self.windows * self.half % 16 == 0
            and self.blk_size == 8
        )


def whiten_kernel(plan, traces_hbm, flags_hbm, out_ref, traces_ref, flags_ref, sems):
    copies = [
        pltpu.make_async_copy(traces_hbm, traces_ref, sems.at[0]),
        pltpu.make_async_copy(flags_hbm, flags_ref, sems.at[1]),
    ]
    for copy in copies:
        copy.start()
    for copy in copies:
        copy.wait()
    pieces = []
    for window in range(plan.windows):
        values = traces_ref[:, window, :]
        centered = values - jnp.mean(values, axis=1, keepdims=True)
        mean_power = jnp.mean(centered * centered, axis=1, keepdims=True)
        flag_values = flags_ref[window : window + 1, :].astype(jnp.float32).reshape(plan.half, 1)
        pieces.append(centered * lax.rsqrt(mean_power + 1e-05) * flag_values)
    out_ref[...] = jnp.concatenate(pieces, axis=0).astype(jnp.bfloat16)


def correlate_kernel(plan, last, mine_ref, other_ref, *refs):
    if last:
        prior_ref, *out_refs, rows_ref, toeplitz_ref, columns_ref = refs
    else:
        sum_ref, rows_ref, toeplitz_ref, columns_ref = refs
    span = plan.span
    me = lax.axis_index("blk")
    filled = plan.coarse * plan.channels
    if filled < LANES:
        columns_ref[filled:, :] = jnp.zeros((LANES - filled, columns_ref.shape[1]), jnp.bfloat16)
    filler = jnp.zeros((plan.channels, span - plan.segment), jnp.float32)
    mine = mine_ref[...].astype(jnp.float32)
    other = other_ref[...].astype(jnp.float32)
    rows_ref[...] = mine
    for window in range(plan.windows):
        at = slice(window * span, (window + 1) * span)
        half = slice(window * plan.half, (window + 1) * plan.half)
        both = jnp.concatenate([mine[half], other[half]], axis=0)
        both = jnp.concatenate([both, filler], axis=1)
        for step in range(plan.coarse):
            moved = pltpu.roll(both, step * plan.fine, 1) if step else both
            columns_ref[step * plan.channels : (step + 1) * plan.channels, at] = moved.astype(jnp.bfloat16)
        for hop in range(plan.targets):
            target = me ^ (hop * plan.columns)
            for member in range(plan.own):
                channel = window * plan.half + target * plan.own + member
                row = jnp.concatenate([rows_ref[pl.ds(channel, 1), :], filler[:1]], axis=1)
                row = jnp.broadcast_to(row, (GROUP, span))
                pieces = [
                    pltpu.roll(row, (MAXLAG - plan.fine + 1 + lag) % span, 1, stride=1, stride_axis=0)
                    for lag in range(0, plan.fine_padded, GROUP)
                ]
                first = hop * plan.height + member * plan.fine_padded
                toeplitz_ref[first : first + plan.fine_padded, at] = jnp.concatenate(pieces, axis=0).astype(
                    jnp.bfloat16
                )
    products = lax.dot_general(
        toeplitz_ref[...],
        columns_ref[...],
        (((1,), (1,)), ((), ())),
        preferred_element_type=jnp.float32,
    )
    if not last:
        sum_ref[...] = products
        return
    products = (products + prior_ref[...]).reshape(plan.targets, plan.own, plan.fine_padded, LANES)
    for hop in range(plan.targets):
        part = products[hop]
        pieces = [part[member, : plan.whole_groups] for member in range(plan.own)]
        if plan.rest:
            pieces += [part[member, plan.whole_groups : plan.fine] for member in range(plan.own)]
        if plan.rows > plan.own * plan.fine:
            pieces.append(jnp.zeros((plan.rows - plan.own * plan.fine, LANES), jnp.float32))
        packed = jnp.concatenate(pieces, axis=0)
        out_refs[hop][...] = packed.astype(out_refs[hop].dtype)
        if hop == plan.targets - 1:
            out_refs[hop + 1][...] = packed.astype(out_refs[hop + 1].dtype)


def order_matrix(plan):
    at_row = lax.broadcasted_iota(jnp.int32, (plan.height, plan.rows), 0)
    at_part = lax.broadcasted_iota(jnp.int32, (plan.height, plan.rows), 1)
    order = jnp.zeros((plan.height, plan.rows), jnp.bool_)
    for member in range(plan.own):
        reverse = plan.fine - 1 - (at_row - member * plan.fine_padded)
        whole = (reverse >= 0) & (reverse < plan.whole_groups) & (at_part == member * plan.whole_groups + reverse)
        tail = plan.own * plan.whole_groups + member * plan.rest + reverse - plan.whole_groups
        rest = (reverse >= plan.whole_groups) & (reverse < plan.fine) & (at_part == tail)
        order = order | whole | rest
    return order.astype(jnp.float32).astype(jnp.bfloat16)


def inside_step(plan, step, values):
    lane = lax.broadcasted_iota(jnp.int32, values.shape, 1)
    inside = (lane >= step * plan.channels) & (lane < (step + 1) * plan.channels)
    return jnp.where(inside, values, 0.0).astype(jnp.bfloat16)


def prepare_kernel(plan, index_ref, kept_ref, order_ref, chosen_ref, base_ref):
    first = lax.axis_index("src") * plan.half
    index = index_ref[...] - first
    index = jnp.where(index < 0, index + plan.channels, index)
    at_column = lax.broadcasted_iota(jnp.int32, (LANES, plan.source_count), 0)
    chosen = jnp.zeros((LANES, plan.source_count), jnp.bool_)
    for step in range(plan.coarse):
        chosen = chosen | (at_column == index + step * plan.channels)
    chosen = chosen.astype(jnp.float32).astype(jnp.bfloat16)
    chosen_ref[...] = chosen
    order = order_matrix(plan)
    order_ref[...] = order
    kept = kept_ref[...] * plan.norm_factor
    high = kept.astype(jnp.bfloat16)
    low = (kept - high.astype(jnp.float32)).astype(jnp.bfloat16)
    parts = [jnp.dot(order, part, preferred_element_type=jnp.float32) for part in (high, low)]
    for step in range(plan.coarse):
        base_ref[step] = sum(
            jnp.dot(inside_step(plan, step, part), chosen, preferred_element_type=jnp.float32) for part in parts
        )


def expand_kernel(plan, order_ref, chosen_ref, base_ref, *refs):
    inner_ref, *arrived_refs, outer_ref, out_hbm, out_ref, sems = refs
    order = order_ref[...]
    line = lax.axis_index("blk") // plan.columns
    is_outer = (line == 0) | (line == plan.targets - 1)
    blocks = [ref[...] for ref in arrived_refs] + [jnp.where(is_outer, outer_ref[...], inner_ref[...])]
    arrived = sum(jnp.dot(order, block, preferred_element_type=jnp.float32) for block in blocks)
    high = arrived.astype(jnp.bfloat16).astype(jnp.float32)
    chosen = chosen_ref[...]
    expanded = []
    for step in range(plan.coarse):
        moved = sum(
            jnp.dot(inside_step(plan, step, part), chosen, preferred_element_type=jnp.float32)
            for part in (high, arrived - high)
        )
        expanded.append(base_ref[step] + moved * plan.norm_factor)
    copies = []
    for member in range(plan.own):
        for step in range(plan.coarse):
            start = step * plan.fine
            count = min(plan.fine, LAG_COUNT - start)
            first = member * plan.fine_padded
            out_ref[member, start : start + count, :] = expanded[step][first : first + count]
        copies.append(pltpu.make_async_copy(out_ref.at[member], out_hbm.at[member], sems.at[member]))
        copies[-1].start()
    for copy in copies:
        copy.wait()


def few_channels(plan, traces, valid_flags, source_index):
    vmem = pl.BlockSpec(memory_space=pltpu.VMEM)
    params = pltpu.CompilerParams(vmem_limit_bytes=32 * 1024 * 1024)
    packed_rows = plan.windows * plan.half
    flags = valid_flags.T

    def swap_cores(array):
        return lax.ppermute(array, "src", [(0, 1), (1, 0)])

    def swap_blk(array, hop, places):
        return lax.ppermute(array, "blk", [(place, place ^ hop) for place in places])

    whitened = pl.pallas_call(
        functools.partial(whiten_kernel, plan),
        out_shape=pltpu.VMEM((packed_rows, plan.segment), jnp.bfloat16),
        in_specs=[pl.BlockSpec(memory_space=pl.ANY)] * 2,
        out_specs=vmem,
        scratch_shapes=[
            pltpu.VMEM(traces.shape, jnp.float32),
            pltpu.VMEM(flags.shape, jnp.int32),
            pltpu.SemaphoreType.DMA((2,)),
        ],
        compiler_params=pltpu.CompilerParams(vmem_limit_bytes=60 * 1024 * 1024),
        name="whiten",
    )(traces, flags)

    height = plan.targets * plan.height
    width = plan.windows * plan.span

    def correlate(mine, other, prior=None):
        last = prior is not None
        if last:
            types = [jnp.float32] + [jnp.bfloat16] * plan.targets
            shapes = [jax.ShapeDtypeStruct((plan.rows, LANES), dtype) for dtype in types]
        else:
            shapes = [jax.ShapeDtypeStruct((height, LANES), jnp.float32)]
        operands = [mine, other] + ([prior] if last else [])
        results = pl.pallas_call(
            functools.partial(correlate_kernel, plan, last),
            out_shape=shapes,
            in_specs=[vmem] * len(operands),
            out_specs=[vmem] * len(shapes),
            scratch_shapes=[
                pltpu.VMEM((packed_rows, plan.segment), jnp.float32),
                pltpu.VMEM((height, width), jnp.bfloat16),
                pltpu.VMEM((LANES, width), jnp.bfloat16),
            ],
            compiler_params=params,
            cost_estimate=pl.CostEstimate(
                flops=2 * height * width * LANES, bytes_accessed=4 * packed_rows * plan.segment, transcendentals=0
            ),
            name="correlate",
        )(*operands)
        return results if last else results[0]

    beside = swap_blk(whitened, 1, range(plan.blk_size))
    total = correlate(whitened, swap_cores(whitened))
    beside, total = lax.optimization_barrier((beside, total))
    kept, *sent = correlate(beside, swap_cores(beside), total)
    every = range(plan.blk_size)
    outer = [place for place in every if place // plan.columns in (0, plan.targets - 1)]
    inner = [place for place in every if place not in outer]
    steps = [(sent[3], 3, inner), (sent[1], 2, every), (sent[0], 1, every), (sent[2], 3, outer)]
    arrived = [swap_blk(array, hop * plan.columns, who) for array, hop, who in steps]
    order, chosen, base = pl.pallas_call(
        functools.partial(prepare_kernel, plan),
        out_shape=[
            jax.ShapeDtypeStruct((plan.height, plan.rows), jnp.bfloat16),
            jax.ShapeDtypeStruct((LANES, plan.source_count), jnp.bfloat16),
            jax.ShapeDtypeStruct((plan.coarse, plan.height, plan.source_count), jnp.float32),
        ],
        in_specs=[vmem] * 2,
        out_specs=[vmem] * 3,
        compiler_params=params,
        name="prepare",
    )(source_index.reshape(1, -1), kept)
    out_shape = (plan.own, LAG_COUNT, plan.source_count)
    return pl.pallas_call(
        functools.partial(expand_kernel, plan),
        out_shape=jax.ShapeDtypeStruct(out_shape, jnp.float32),
        in_specs=[vmem] * (3 + len(arrived)),
        out_specs=pl.BlockSpec(memory_space=pl.ANY),
        scratch_shapes=[pltpu.VMEM(out_shape, jnp.float32), pltpu.SemaphoreType.DMA((plan.own,))],
        compiler_params=params,
        name="expand",
    )(order, chosen, base, *arrived)


def body(traces, valid_flags, source_index):
    plan = Plan(
        traces.shape[0],
        traces.shape[1],
        traces.shape[2],
        lax.axis_size("blk"),
        lax.axis_size("src"),
        source_index.shape[0],
    )
    if plan.fits():
        return few_channels(plan, traces, valid_flags, source_index)
    return many_channels(traces, valid_flags, source_index)


def solution(mesh):
    in_specs = (P(("fibre", "src"), "blk", None), P(("fibre", "src"), "blk"), P())
    out_specs = P(("fibre", "src", "blk"), None, None)
    return jax.shard_map(body, mesh=mesh, in_specs=in_specs, out_specs=out_specs, check_vma=False)
```

```python
import functools
import math

import jax
import jax.numpy as jnp
from jax import lax
from jax.experimental import pallas as pl
from jax.experimental.pallas import tpu as pltpu
from jax.sharding import PartitionSpec as P

MAXLAG = 64
LAG_COUNT = 2 * MAXLAG + 1
LANES = 256
GROUP = 8


def broadcast(value, axis, source):
    kept = jnp.where(lax.axis_index(axis) == source, value, 0).astype(value.dtype)
    return lax.psum(kept, axis)


def toeplitz_rows(group, lag_count, segment):
    shifted = jnp.stack(
        [group[:, :, lag_step : lag_step + segment] for lag_step in range(lag_count)], axis=1
    )
    return shifted.reshape(group.shape[0] * lag_count, -1)


def many_channels(traces, valid_flags, source_index):
    segment = traces.shape[2]
    centered = traces - jnp.mean(traces, axis=2, keepdims=True)
    mean_power = jnp.mean(centered * centered, axis=2, keepdims=True)
    flag_values = valid_flags[:, :, None].astype(jnp.float32)
    whitened = (centered * lax.rsqrt(mean_power + 1e-05) * flag_values).astype(jnp.bfloat16)
    pieces = []
    for owner in range(lax.axis_size("src")):
        pieces.append(broadcast(whitened, "src", owner))
    everyone = jnp.concatenate(pieces, axis=0)
    sources = jnp.take(everyone, source_index, axis=0)
    source_count = sources.shape[0]
    norm_factor = 1.0 / math.sqrt(traces.shape[1] * lax.axis_size("blk") * segment)
    own_rows = whitened.shape[0] // lax.axis_size("blk")
    flat_sources = sources.reshape(source_count, -1)
    padded = jnp.pad(whitened, ((0, 0), (0, 0), (MAXLAG, MAXLAG)))
    block_rows = math.gcd(lax.axis_size("blk") * own_rows, 16)
    grouped = padded.reshape(
        (lax.axis_size("blk") * own_rows // block_rows, block_rows) + padded.shape[1:]
    )

    def one_block(group):
        toeplitz = toeplitz_rows(group, LAG_COUNT, segment)
        products = lax.dot_general(
            toeplitz, flat_sources, (((1,), (1,)), ((), ())), preferred_element_type=jnp.float32
        )
        return (products * norm_factor).reshape(block_rows, LAG_COUNT, source_count)

    result = lax.map(one_block, grouped)
    return lax.psum_scatter(
        result.reshape(lax.axis_size("blk") * own_rows, LAG_COUNT, source_count),
        "blk",
        scatter_dimension=0,
        tiled=True,
    )


class Plan:
    def __init__(self, half, windows, segment, blk_size, src_size, source_count):
        self.half = half
        self.windows = windows
        self.segment = segment
        self.blk_size = blk_size
        self.src_size = src_size
        self.channels = half * src_size
        self.source_count = source_count
        self.coarse = LANES // self.channels
        if self.coarse == 0:
            return
        self.fine = -(-LAG_COUNT // self.coarse)
        self.fine_padded = -(-self.fine // (2 * GROUP)) * 2 * GROUP
        self.own = half // blk_size
        reach = segment + (self.coarse - 1) * self.fine
        self.span = -(-max(reach, segment + 2 * MAXLAG) // 128) * 128
        self.whole_groups = self.fine // GROUP * GROUP
        self.rest = self.fine - self.whole_groups
        rows = self.own * self.fine
        self.rows = -(-rows // 16) * 16
        self.height = self.own * self.fine_padded
        self.far = blk_size // 2
        self.targets = 2
        self.norm_factor = 1.0 / math.sqrt(windows * blk_size * segment)

    def fits(self):
        return (
            self.coarse >= 2
            and self.src_size == 2
            and self.half % self.blk_size == 0
            and self.half % GROUP == 0
            and self.channels % 16 == 0
            and self.windows * self.half % 16 == 0
            and self.blk_size == 8
        )


def whiten_kernel(plan, traces_hbm, flags_hbm, out_ref, traces_ref, flags_ref, sems):
    copies = [
        pltpu.make_async_copy(traces_hbm, traces_ref, sems.at[0]),
        pltpu.make_async_copy(flags_hbm, flags_ref, sems.at[1]),
    ]
    for copy in copies:
        copy.start()
    for copy in copies:
        copy.wait()
    pieces = []
    for window in range(plan.windows):
        values = traces_ref[:, window, :]
        centered = values - jnp.mean(values, axis=1, keepdims=True)
        mean_power = jnp.mean(centered * centered, axis=1, keepdims=True)
        flag_values = flags_ref[window : window + 1, :].astype(jnp.float32).reshape(plan.half, 1)
        pieces.append(centered * lax.rsqrt(mean_power + 1e-05) * flag_values)
    out_ref[...] = jnp.concatenate(pieces, axis=0).astype(jnp.bfloat16)


def correlate_kernel(plan, prior, last, mine_ref, other_ref, *refs):
    if prior:
        prior_ref, *refs = refs
    *out_refs, rows_ref, toeplitz_ref, columns_ref = refs
    span = plan.span
    me = lax.axis_index("blk")
    filled = plan.coarse * plan.channels
    if filled < LANES:
        columns_ref[filled:, :] = jnp.zeros((LANES - filled, columns_ref.shape[1]), jnp.bfloat16)
    filler = jnp.zeros((plan.channels, span - plan.segment), jnp.float32)
    mine = mine_ref[...].astype(jnp.float32)
    other = other_ref[...].astype(jnp.float32)
    rows_ref[...] = mine
    for window in range(plan.windows):
        at = slice(window * span, (window + 1) * span)
        half = slice(window * plan.half, (window + 1) * plan.half)
        both = jnp.concatenate([mine[half], other[half]], axis=0)
        both = jnp.concatenate([both, filler], axis=1)
        for step in range(plan.coarse):
            moved = pltpu.roll(both, step * plan.fine, 1) if step else both
            columns_ref[step * plan.channels : (step + 1) * plan.channels, at] = moved.astype(jnp.bfloat16)
        for hop in range(plan.targets):
            target = me ^ (hop * plan.far)
            for member in range(plan.own):
                channel = window * plan.half + target * plan.own + member
                row = jnp.concatenate([rows_ref[pl.ds(channel, 1), :], filler[:1]], axis=1)
                row = jnp.broadcast_to(row, (GROUP, span))
                pieces = [
                    pltpu.roll(row, (MAXLAG - plan.fine + 1 + lag) % span, 1, stride=1, stride_axis=0)
                    for lag in range(0, plan.fine_padded, GROUP)
                ]
                first = hop * plan.height + member * plan.fine_padded
                toeplitz_ref[first : first + plan.fine_padded, at] = jnp.concatenate(pieces, axis=0).astype(
                    jnp.bfloat16
                )
    products = lax.dot_general(
        toeplitz_ref[...],
        columns_ref[...],
        (((1,), (1,)), ((), ())),
        preferred_element_type=jnp.float32,
    )
    if prior:
        products = products + prior_ref[...]
    if not last:
        out_refs[0][...] = products
        return
    products = products.reshape(plan.targets, plan.own, plan.fine_padded, LANES)
    for hop in range(plan.targets):
        part = products[hop]
        pieces = [part[member, : plan.whole_groups] for member in range(plan.own)]
        if plan.rest:
            pieces += [part[member, plan.whole_groups : plan.fine] for member in range(plan.own)]
        if plan.rows > plan.own * plan.fine:
            pieces.append(jnp.zeros((plan.rows - plan.own * plan.fine, LANES), jnp.float32))
        packed = jnp.concatenate(pieces, axis=0)
        out_refs[hop][...] = packed.astype(out_refs[hop].dtype)


def order_matrix(plan):
    at_row = lax.broadcasted_iota(jnp.int32, (plan.height, plan.rows), 0)
    at_part = lax.broadcasted_iota(jnp.int32, (plan.height, plan.rows), 1)
    order = jnp.zeros((plan.height, plan.rows), jnp.bool_)
    for member in range(plan.own):
        reverse = plan.fine - 1 - (at_row - member * plan.fine_padded)
        whole = (reverse >= 0) & (reverse < plan.whole_groups) & (at_part == member * plan.whole_groups + reverse)
        tail = plan.own * plan.whole_groups + member * plan.rest + reverse - plan.whole_groups
        rest = (reverse >= plan.whole_groups) & (reverse < plan.fine) & (at_part == tail)
        order = order | whole | rest
    return order.astype(jnp.float32).astype(jnp.bfloat16)


def inside_step(plan, step, values):
    lane = lax.broadcasted_iota(jnp.int32, values.shape, 1)
    inside = (lane >= step * plan.channels) & (lane < (step + 1) * plan.channels)
    return jnp.where(inside, values, 0.0).astype(jnp.bfloat16)


def prepare_kernel(plan, index_ref, kept_ref, order_ref, chosen_ref, base_ref):
    first = lax.axis_index("src") * plan.half
    index = index_ref[...] - first
    index = jnp.where(index < 0, index + plan.channels, index)
    at_column = lax.broadcasted_iota(jnp.int32, (LANES, plan.source_count), 0)
    chosen = jnp.zeros((LANES, plan.source_count), jnp.bool_)
    for step in range(plan.coarse):
        chosen = chosen | (at_column == index + step * plan.channels)
    chosen = chosen.astype(jnp.float32).astype(jnp.bfloat16)
    chosen_ref[...] = chosen
    order = order_matrix(plan)
    order_ref[...] = order
    kept = kept_ref[...] * plan.norm_factor
    high = kept.astype(jnp.bfloat16)
    low = (kept - high.astype(jnp.float32)).astype(jnp.bfloat16)
    parts = [jnp.dot(order, part, preferred_element_type=jnp.float32) for part in (high, low)]
    for step in range(plan.coarse):
        base_ref[step] = sum(
            jnp.dot(inside_step(plan, step, part), chosen, preferred_element_type=jnp.float32) for part in parts
        )


def expand_kernel(plan, order_ref, chosen_ref, base_ref, arrived_ref, out_hbm, out_ref, sems):
    arrived = jnp.dot(order_ref[...], arrived_ref[...], preferred_element_type=jnp.float32)
    chosen = chosen_ref[...]
    expanded = []
    for step in range(plan.coarse):
        moved = jnp.dot(inside_step(plan, step, arrived), chosen, preferred_element_type=jnp.float32)
        expanded.append(base_ref[step] + moved * plan.norm_factor)
    copies = []
    for member in range(plan.own):
        for step in range(plan.coarse):
            start = step * plan.fine
            count = min(plan.fine, LAG_COUNT - start)
            first = member * plan.fine_padded
            out_ref[member, start : start + count, :] = expanded[step][first : first + count]
        copies.append(pltpu.make_async_copy(out_ref.at[member], out_hbm.at[member], sems.at[member]))
        copies[-1].start()
    for copy in copies:
        copy.wait()


def few_channels(plan, traces, valid_flags, source_index):
    vmem = pl.BlockSpec(memory_space=pltpu.VMEM)
    params = pltpu.CompilerParams(vmem_limit_bytes=32 * 1024 * 1024)
    packed_rows = plan.windows * plan.half
    flags = valid_flags.T

    def swap_cores(array):
        return lax.ppermute(array, "src", [(0, 1), (1, 0)])

    def swap_blk(array, hop):
        return lax.ppermute(array, "blk", [(place, place ^ hop) for place in range(plan.blk_size)])

    whitened = pl.pallas_call(
        functools.partial(whiten_kernel, plan),
        out_shape=pltpu.VMEM((packed_rows, plan.segment), jnp.bfloat16),
        in_specs=[pl.BlockSpec(memory_space=pl.ANY)] * 2,
        out_specs=vmem,
        scratch_shapes=[
            pltpu.VMEM(traces.shape, jnp.float32),
            pltpu.VMEM(flags.shape, jnp.int32),
            pltpu.SemaphoreType.DMA((2,)),
        ],
        compiler_params=pltpu.CompilerParams(vmem_limit_bytes=60 * 1024 * 1024),
        name="whiten",
    )(traces, flags)

    height = plan.targets * plan.height
    width = plan.windows * plan.span

    def correlate(mine, other, prior=None, last=False):
        if last:
            shapes = [jax.ShapeDtypeStruct((plan.rows, LANES), dtype) for dtype in (jnp.float32, jnp.bfloat16)]
        else:
            shapes = [jax.ShapeDtypeStruct((height, LANES), jnp.float32)]
        operands = [mine, other] + ([] if prior is None else [prior])
        results = pl.pallas_call(
            functools.partial(correlate_kernel, plan, prior is not None, last),
            out_shape=shapes,
            in_specs=[vmem] * len(operands),
            out_specs=[vmem] * len(shapes),
            scratch_shapes=[
                pltpu.VMEM((packed_rows, plan.segment), jnp.float32),
                pltpu.VMEM((height, width), jnp.bfloat16),
                pltpu.VMEM((LANES, width), jnp.bfloat16),
            ],
            compiler_params=params,
            cost_estimate=pl.CostEstimate(
                flops=2 * height * width * LANES, bytes_accessed=4 * packed_rows * plan.segment, transcendentals=0
            ),
            name="correlate",
        )(*operands)
        return results if last else results[0]

    diagonal, along, beside = [swap_blk(whitened, hop) for hop in (3, 2, 1)]
    total = correlate(whitened, swap_cores(whitened))
    beside, along, total = lax.optimization_barrier((beside, along, total))
    other_beside, other_along = swap_cores(beside), swap_cores(along)
    diagonal, other_beside = lax.optimization_barrier((diagonal, other_beside))
    total = correlate(beside, other_beside, total)
    total = correlate(along, other_along, total)
    kept, sent = correlate(diagonal, swap_cores(diagonal), total, last=True)
    arrived = swap_blk(sent, plan.far)
    order, chosen, base = pl.pallas_call(
        functools.partial(prepare_kernel, plan),
        out_shape=[
            jax.ShapeDtypeStruct((plan.height, plan.rows), jnp.bfloat16),
            jax.ShapeDtypeStruct((LANES, plan.source_count), jnp.bfloat16),
            jax.ShapeDtypeStruct((plan.coarse, plan.height, plan.source_count), jnp.float32),
        ],
        in_specs=[vmem] * 2,
        out_specs=[vmem] * 3,
        compiler_params=params,
        name="prepare",
    )(source_index.reshape(1, -1), kept)
    out_shape = (plan.own, LAG_COUNT, plan.source_count)
    return pl.pallas_call(
        functools.partial(expand_kernel, plan),
        out_shape=jax.ShapeDtypeStruct(out_shape, jnp.float32),
        in_specs=[vmem] * 4,
        out_specs=pl.BlockSpec(memory_space=pl.ANY),
        scratch_shapes=[pltpu.VMEM(out_shape, jnp.float32), pltpu.SemaphoreType.DMA((plan.own,))],
        compiler_params=params,
        name="expand",
    )(order, chosen, base, arrived)


def body(traces, valid_flags, source_index):
    plan = Plan(
        traces.shape[0],
        traces.shape[1],
        traces.shape[2],
        lax.axis_size("blk"),
        lax.axis_size("src"),
        source_index.shape[0],
    )
    if plan.fits():
        return few_channels(plan, traces, valid_flags, source_index)
    return many_channels(traces, valid_flags, source_index)


def solution(mesh):
    in_specs = (P(("fibre", "src"), "blk", None), P(("fibre", "src"), "blk"), P())
    out_specs = P(("fibre", "src", "blk"), None, None)
    return jax.shard_map(body, mesh=mesh, in_specs=in_specs, out_specs=out_specs, check_vma=False)
```

```python
import functools
import math

import jax
import jax.numpy as jnp
from jax import lax
from jax.experimental import pallas as pl
from jax.experimental.pallas import tpu as pltpu
from jax.sharding import PartitionSpec as P

MAXLAG = 64
LAG_COUNT = 2 * MAXLAG + 1
LANES = 256
GROUP = 8


def broadcast(value, axis, source):
    kept = jnp.where(lax.axis_index(axis) == source, value, 0).astype(value.dtype)
    return lax.psum(kept, axis)


def toeplitz_rows(group, lag_count, segment):
    shifted = jnp.stack(
        [group[:, :, lag_step : lag_step + segment] for lag_step in range(lag_count)], axis=1
    )
    return shifted.reshape(group.shape[0] * lag_count, -1)


def many_channels(traces, valid_flags, source_index):
    segment = traces.shape[2]
    centered = traces - jnp.mean(traces, axis=2, keepdims=True)
    mean_power = jnp.mean(centered * centered, axis=2, keepdims=True)
    flag_values = valid_flags[:, :, None].astype(jnp.float32)
    whitened = (centered * lax.rsqrt(mean_power + 1e-05) * flag_values).astype(jnp.bfloat16)
    pieces = []
    for owner in range(lax.axis_size("src")):
        pieces.append(broadcast(whitened, "src", owner))
    everyone = jnp.concatenate(pieces, axis=0)
    sources = jnp.take(everyone, source_index, axis=0)
    source_count = sources.shape[0]
    norm_factor = 1.0 / math.sqrt(traces.shape[1] * lax.axis_size("blk") * segment)
    own_rows = whitened.shape[0] // lax.axis_size("blk")
    flat_sources = sources.reshape(source_count, -1)
    padded = jnp.pad(whitened, ((0, 0), (0, 0), (MAXLAG, MAXLAG)))
    block_rows = math.gcd(lax.axis_size("blk") * own_rows, 16)
    grouped = padded.reshape(
        (lax.axis_size("blk") * own_rows // block_rows, block_rows) + padded.shape[1:]
    )

    def one_block(group):
        toeplitz = toeplitz_rows(group, LAG_COUNT, segment)
        products = lax.dot_general(
            toeplitz, flat_sources, (((1,), (1,)), ((), ())), preferred_element_type=jnp.float32
        )
        return (products * norm_factor).reshape(block_rows, LAG_COUNT, source_count)

    result = lax.map(one_block, grouped)
    return lax.psum_scatter(
        result.reshape(lax.axis_size("blk") * own_rows, LAG_COUNT, source_count),
        "blk",
        scatter_dimension=0,
        tiled=True,
    )


class Plan:
    def __init__(self, half, windows, segment, blk_size, src_size, source_count):
        self.half = half
        self.windows = windows
        self.segment = segment
        self.blk_size = blk_size
        self.src_size = src_size
        self.channels = half * src_size
        self.source_count = source_count
        self.coarse = LANES // self.channels
        if self.coarse == 0:
            return
        self.fine = -(-LAG_COUNT // self.coarse)
        self.fine_padded = -(-self.fine // (2 * GROUP)) * 2 * GROUP
        self.own = half // blk_size
        reach = segment + (self.coarse - 1) * self.fine
        self.span = -(-max(reach, segment + 2 * MAXLAG) // 128) * 128
        self.whole_groups = self.fine // GROUP * GROUP
        self.rest = self.fine - self.whole_groups
        rows = self.own * self.fine
        self.rows = -(-rows // 16) * 16
        self.height = self.own * self.fine_padded
        self.targets = blk_size // 2
        self.norm_factor = 1.0 / math.sqrt(windows * blk_size * segment)

    def fits(self):
        return (
            self.coarse >= 2
            and self.src_size == 2
            and self.half % self.blk_size == 0
            and self.half % GROUP == 0
            and self.channels % 16 == 0
            and self.windows * self.half % 16 == 0
            and self.blk_size == 8
        )


def whiten_kernel(plan, traces_hbm, flags_hbm, out_ref, traces_ref, flags_ref, sems):
    copies = [
        pltpu.make_async_copy(traces_hbm, traces_ref, sems.at[0]),
        pltpu.make_async_copy(flags_hbm, flags_ref, sems.at[1]),
    ]
    for copy in copies:
        copy.start()
    for copy in copies:
        copy.wait()
    pieces = []
    for window in range(plan.windows):
        values = traces_ref[:, window, :]
        centered = values - jnp.mean(values, axis=1, keepdims=True)
        mean_power = jnp.mean(centered * centered, axis=1, keepdims=True)
        flag_values = flags_ref[window : window + 1, :].astype(jnp.float32).reshape(plan.half, 1)
        pieces.append(centered * lax.rsqrt(mean_power + 1e-05) * flag_values)
    out_ref[...] = jnp.concatenate(pieces, axis=0).astype(jnp.bfloat16)


def correlate_kernel(plan, last, mine_ref, other_ref, *refs):
    if last:
        prior_ref, *out_refs, rows_ref, toeplitz_ref, columns_ref = refs
    else:
        sum_ref, rows_ref, toeplitz_ref, columns_ref = refs
    span = plan.span
    me = lax.axis_index("blk")
    filled = plan.coarse * plan.channels
    if filled < LANES:
        columns_ref[filled:, :] = jnp.zeros((LANES - filled, columns_ref.shape[1]), jnp.bfloat16)
    filler = jnp.zeros((plan.channels, span - plan.segment), jnp.float32)
    mine = mine_ref[...].astype(jnp.float32)
    other = other_ref[...].astype(jnp.float32)
    rows_ref[...] = mine
    for window in range(plan.windows):
        at = slice(window * span, (window + 1) * span)
        half = slice(window * plan.half, (window + 1) * plan.half)
        both = jnp.concatenate([mine[half], other[half]], axis=0)
        both = jnp.concatenate([both, filler], axis=1)
        for step in range(plan.coarse):
            moved = pltpu.roll(both, step * plan.fine, 1) if step else both
            columns_ref[step * plan.channels : (step + 1) * plan.channels, at] = moved.astype(jnp.bfloat16)
        for hop in range(plan.targets):
            target = me ^ hop
            for member in range(plan.own):
                channel = window * plan.half + target * plan.own + member
                row = jnp.concatenate([rows_ref[pl.ds(channel, 1), :], filler[:1]], axis=1)
                row = jnp.broadcast_to(row, (GROUP, span))
                pieces = [
                    pltpu.roll(row, (MAXLAG - plan.fine + 1 + lag) % span, 1, stride=1, stride_axis=0)
                    for lag in range(0, plan.fine_padded, GROUP)
                ]
                first = hop * plan.height + member * plan.fine_padded
                toeplitz_ref[first : first + plan.fine_padded, at] = jnp.concatenate(pieces, axis=0).astype(
                    jnp.bfloat16
                )
    products = lax.dot_general(
        toeplitz_ref[...],
        columns_ref[...],
        (((1,), (1,)), ((), ())),
        preferred_element_type=jnp.float32,
    )
    if not last:
        sum_ref[...] = products
        return
    products = (products + prior_ref[...]).reshape(plan.targets, plan.own, plan.fine_padded, LANES)
    for hop in range(plan.targets):
        part = products[hop]
        pieces = [part[member, : plan.whole_groups] for member in range(plan.own)]
        if plan.rest:
            pieces += [part[member, plan.whole_groups : plan.fine] for member in range(plan.own)]
        if plan.rows > plan.own * plan.fine:
            pieces.append(jnp.zeros((plan.rows - plan.own * plan.fine, LANES), jnp.float32))
        packed = jnp.concatenate(pieces, axis=0)
        out_refs[hop][...] = packed.astype(out_refs[hop].dtype)


def order_matrix(plan):
    at_row = lax.broadcasted_iota(jnp.int32, (plan.height, plan.rows), 0)
    at_part = lax.broadcasted_iota(jnp.int32, (plan.height, plan.rows), 1)
    order = jnp.zeros((plan.height, plan.rows), jnp.bool_)
    for member in range(plan.own):
        reverse = plan.fine - 1 - (at_row - member * plan.fine_padded)
        whole = (reverse >= 0) & (reverse < plan.whole_groups) & (at_part == member * plan.whole_groups + reverse)
        tail = plan.own * plan.whole_groups + member * plan.rest + reverse - plan.whole_groups
        rest = (reverse >= plan.whole_groups) & (reverse < plan.fine) & (at_part == tail)
        order = order | whole | rest
    return order.astype(jnp.float32).astype(jnp.bfloat16)


def inside_step(plan, step, values):
    lane = lax.broadcasted_iota(jnp.int32, values.shape, 1)
    inside = (lane >= step * plan.channels) & (lane < (step + 1) * plan.channels)
    return jnp.where(inside, values, 0.0).astype(jnp.bfloat16)


def prepare_kernel(plan, index_ref, kept_ref, order_ref, chosen_ref, base_ref):
    first = lax.axis_index("src") * plan.half
    index = index_ref[...] - first
    index = jnp.where(index < 0, index + plan.channels, index)
    at_column = lax.broadcasted_iota(jnp.int32, (LANES, plan.source_count), 0)
    chosen = jnp.zeros((LANES, plan.source_count), jnp.bool_)
    for step in range(plan.coarse):
        chosen = chosen | (at_column == index + step * plan.channels)
    chosen = chosen.astype(jnp.float32).astype(jnp.bfloat16)
    chosen_ref[...] = chosen
    order = order_matrix(plan)
    order_ref[...] = order
    kept = kept_ref[...] * plan.norm_factor
    high = kept.astype(jnp.bfloat16)
    low = (kept - high.astype(jnp.float32)).astype(jnp.bfloat16)
    parts = [jnp.dot(order, part, preferred_element_type=jnp.float32) for part in (high, low)]
    for step in range(plan.coarse):
        base_ref[step] = sum(
            jnp.dot(inside_step(plan, step, part), chosen, preferred_element_type=jnp.float32) for part in parts
        )


def expand_kernel(plan, order_ref, chosen_ref, base_ref, *refs):
    *arrived_refs, out_hbm, out_ref, sems = refs
    order = order_ref[...]
    arrived = sum(jnp.dot(order, ref[...], preferred_element_type=jnp.float32) for ref in arrived_refs)
    high = arrived.astype(jnp.bfloat16).astype(jnp.float32)
    chosen = chosen_ref[...]
    expanded = []
    for step in range(plan.coarse):
        moved = sum(
            jnp.dot(inside_step(plan, step, part), chosen, preferred_element_type=jnp.float32)
            for part in (high, arrived - high)
        )
        expanded.append(base_ref[step] + moved * plan.norm_factor)
    copies = []
    for member in range(plan.own):
        for step in range(plan.coarse):
            start = step * plan.fine
            count = min(plan.fine, LAG_COUNT - start)
            first = member * plan.fine_padded
            out_ref[member, start : start + count, :] = expanded[step][first : first + count]
        copies.append(pltpu.make_async_copy(out_ref.at[member], out_hbm.at[member], sems.at[member]))
        copies[-1].start()
    for copy in copies:
        copy.wait()


def few_channels(plan, traces, valid_flags, source_index):
    vmem = pl.BlockSpec(memory_space=pltpu.VMEM)
    params = pltpu.CompilerParams(vmem_limit_bytes=32 * 1024 * 1024)
    packed_rows = plan.windows * plan.half
    flags = valid_flags.T

    def swap_cores(array):
        return lax.ppermute(array, "src", [(0, 1), (1, 0)])

    def swap_blk(array, hop):
        return lax.ppermute(array, "blk", [(place, place ^ hop) for place in range(plan.blk_size)])

    whitened = pl.pallas_call(
        functools.partial(whiten_kernel, plan),
        out_shape=pltpu.VMEM((packed_rows, plan.segment), jnp.bfloat16),
        in_specs=[pl.BlockSpec(memory_space=pl.ANY)] * 2,
        out_specs=vmem,
        scratch_shapes=[
            pltpu.VMEM(traces.shape, jnp.float32),
            pltpu.VMEM(flags.shape, jnp.int32),
            pltpu.SemaphoreType.DMA((2,)),
        ],
        compiler_params=pltpu.CompilerParams(vmem_limit_bytes=60 * 1024 * 1024),
        name="whiten",
    )(traces, flags)

    height = plan.targets * plan.height
    width = plan.windows * plan.span

    def correlate(mine, other, prior=None):
        last = prior is not None
        if last:
            types = [jnp.float32] + [jnp.bfloat16] * (plan.targets - 1)
            shapes = [jax.ShapeDtypeStruct((plan.rows, LANES), dtype) for dtype in types]
        else:
            shapes = [jax.ShapeDtypeStruct((height, LANES), jnp.float32)]
        operands = [mine, other] + ([prior] if last else [])
        results = pl.pallas_call(
            functools.partial(correlate_kernel, plan, last),
            out_shape=shapes,
            in_specs=[vmem] * len(operands),
            out_specs=[vmem] * len(shapes),
            scratch_shapes=[
                pltpu.VMEM((packed_rows, plan.segment), jnp.float32),
                pltpu.VMEM((height, width), jnp.bfloat16),
                pltpu.VMEM((LANES, width), jnp.bfloat16),
            ],
            compiler_params=params,
            cost_estimate=pl.CostEstimate(
                flops=2 * height * width * LANES, bytes_accessed=4 * packed_rows * plan.segment, transcendentals=0
            ),
            name="correlate",
        )(*operands)
        return results if last else results[0]

    other = swap_cores(whitened)
    across = swap_blk(whitened, plan.targets)
    total = correlate(whitened, other)
    kept, *sent = correlate(across, swap_cores(across), total)
    arrived = [swap_blk(sent[hop - 1], hop) for hop in reversed(range(1, plan.targets))]
    order, chosen, base = pl.pallas_call(
        functools.partial(prepare_kernel, plan),
        out_shape=[
            jax.ShapeDtypeStruct((plan.height, plan.rows), jnp.bfloat16),
            jax.ShapeDtypeStruct((LANES, plan.source_count), jnp.bfloat16),
            jax.ShapeDtypeStruct((plan.coarse, plan.height, plan.source_count), jnp.float32),
        ],
        in_specs=[vmem] * 2,
        out_specs=[vmem] * 3,
        compiler_params=params,
        name="prepare",
    )(source_index.reshape(1, -1), kept)
    out_shape = (plan.own, LAG_COUNT, plan.source_count)
    return pl.pallas_call(
        functools.partial(expand_kernel, plan),
        out_shape=jax.ShapeDtypeStruct(out_shape, jnp.float32),
        in_specs=[vmem] * (3 + len(arrived)),
        out_specs=pl.BlockSpec(memory_space=pl.ANY),
        scratch_shapes=[pltpu.VMEM(out_shape, jnp.float32), pltpu.SemaphoreType.DMA((plan.own,))],
        compiler_params=params,
        name="expand",
    )(order, chosen, base, *arrived)


def body(traces, valid_flags, source_index):
    plan = Plan(
        traces.shape[0],
        traces.shape[1],
        traces.shape[2],
        lax.axis_size("blk"),
        lax.axis_size("src"),
        source_index.shape[0],
    )
    if plan.fits():
        return few_channels(plan, traces, valid_flags, source_index)
    return many_channels(traces, valid_flags, source_index)


def solution(mesh):
    in_specs = (P(("fibre", "src"), "blk", None), P(("fibre", "src"), "blk"), P())
    out_specs = P(("fibre", "src", "blk"), None, None)
    return jax.shard_map(body, mesh=mesh, in_specs=in_specs, out_specs=out_specs, check_vma=False)
```

```python
import functools
import math

import jax
import jax.numpy as jnp
from jax import lax
from jax.experimental import pallas as pl
from jax.experimental.pallas import tpu as pltpu
from jax.sharding import PartitionSpec as P

MAXLAG = 64
LAG_COUNT = 2 * MAXLAG + 1
LANES = 256
GROUP = 8


def broadcast(value, axis, source):
    kept = jnp.where(lax.axis_index(axis) == source, value, 0).astype(value.dtype)
    return lax.psum(kept, axis)


def toeplitz_rows(group, lag_count, segment):
    shifted = jnp.stack(
        [group[:, :, lag_step : lag_step + segment] for lag_step in range(lag_count)], axis=1
    )
    return shifted.reshape(group.shape[0] * lag_count, -1)


def many_channels(traces, valid_flags, source_index):
    segment = traces.shape[2]
    centered = traces - jnp.mean(traces, axis=2, keepdims=True)
    mean_power = jnp.mean(centered * centered, axis=2, keepdims=True)
    flag_values = valid_flags[:, :, None].astype(jnp.float32)
    whitened = (centered * lax.rsqrt(mean_power + 1e-05) * flag_values).astype(jnp.bfloat16)
    pieces = []
    for owner in range(lax.axis_size("src")):
        pieces.append(broadcast(whitened, "src", owner))
    everyone = jnp.concatenate(pieces, axis=0)
    sources = jnp.take(everyone, source_index, axis=0)
    source_count = sources.shape[0]
    norm_factor = 1.0 / math.sqrt(traces.shape[1] * lax.axis_size("blk") * segment)
    own_rows = whitened.shape[0] // lax.axis_size("blk")
    flat_sources = sources.reshape(source_count, -1)
    padded = jnp.pad(whitened, ((0, 0), (0, 0), (MAXLAG, MAXLAG)))
    block_rows = math.gcd(lax.axis_size("blk") * own_rows, 16)
    grouped = padded.reshape(
        (lax.axis_size("blk") * own_rows // block_rows, block_rows) + padded.shape[1:]
    )

    def one_block(group):
        toeplitz = toeplitz_rows(group, LAG_COUNT, segment)
        products = lax.dot_general(
            toeplitz, flat_sources, (((1,), (1,)), ((), ())), preferred_element_type=jnp.float32
        )
        return (products * norm_factor).reshape(block_rows, LAG_COUNT, source_count)

    result = lax.map(one_block, grouped)
    return lax.psum_scatter(
        result.reshape(lax.axis_size("blk") * own_rows, LAG_COUNT, source_count),
        "blk",
        scatter_dimension=0,
        tiled=True,
    )


class Plan:
    def __init__(self, half, windows, segment, blk_size, src_size, source_count):
        self.half = half
        self.windows = windows
        self.segment = segment
        self.blk_size = blk_size
        self.src_size = src_size
        self.channels = half * src_size
        self.source_count = source_count
        self.coarse = LANES // self.channels
        if self.coarse == 0:
            return
        self.fine = -(-LAG_COUNT // self.coarse)
        self.fine_padded = -(-self.fine // (2 * GROUP)) * 2 * GROUP
        self.own = half // blk_size
        reach = segment + (self.coarse - 1) * self.fine
        self.span = -(-max(reach, segment + 2 * MAXLAG) // 128) * 128
        self.whole_groups = self.fine // GROUP * GROUP
        self.rest = self.fine - self.whole_groups
        rows = self.own * self.fine
        self.rows = -(-rows // 16) * 16
        self.height = self.own * self.fine_padded
        self.targets = blk_size // 2
        self.norm_factor = 1.0 / math.sqrt(windows * blk_size * segment)

    def fits(self):
        return (
            self.coarse >= 2
            and self.src_size == 2
            and self.half % self.blk_size == 0
            and self.half % GROUP == 0
            and self.channels % 16 == 0
            and self.windows * self.half % 16 == 0
            and self.blk_size == 8
        )


def whiten_kernel(plan, traces_hbm, flags_hbm, out_ref, traces_ref, flags_ref, sems):
    copies = [
        pltpu.make_async_copy(traces_hbm, traces_ref, sems.at[0]),
        pltpu.make_async_copy(flags_hbm, flags_ref, sems.at[1]),
    ]
    for copy in copies:
        copy.start()
    for copy in copies:
        copy.wait()
    pieces = []
    for window in range(plan.windows):
        values = traces_ref[:, window, :]
        centered = values - jnp.mean(values, axis=1, keepdims=True)
        mean_power = jnp.mean(centered * centered, axis=1, keepdims=True)
        flag_values = flags_ref[window : window + 1, :].astype(jnp.float32).reshape(plan.half, 1)
        pieces.append(centered * lax.rsqrt(mean_power + 1e-05) * flag_values)
    out_ref[...] = jnp.concatenate(pieces, axis=0).astype(jnp.bfloat16)


def correlate_kernel(plan, last, mine_ref, other_ref, *refs):
    if last:
        prior_ref, *out_refs, rows_ref, toeplitz_ref, columns_ref = refs
    else:
        sum_ref, rows_ref, toeplitz_ref, columns_ref = refs
    span = plan.span
    me = lax.axis_index("blk")
    filled = plan.coarse * plan.channels
    if filled < LANES:
        columns_ref[filled:, :] = jnp.zeros((LANES - filled, columns_ref.shape[1]), jnp.bfloat16)
    filler = jnp.zeros((plan.channels, span - plan.segment), jnp.float32)
    mine = mine_ref[...].astype(jnp.float32)
    other = other_ref[...].astype(jnp.float32)
    rows_ref[...] = mine
    for window in range(plan.windows):
        at = slice(window * span, (window + 1) * span)
        half = slice(window * plan.half, (window + 1) * plan.half)
        both = jnp.concatenate([mine[half], other[half]], axis=0)
        both = jnp.concatenate([both, filler], axis=1)
        for step in range(plan.coarse):
            moved = pltpu.roll(both, step * plan.fine, 1) if step else both
            columns_ref[step * plan.channels : (step + 1) * plan.channels, at] = moved.astype(jnp.bfloat16)
        for hop in range(plan.targets):
            target = me ^ hop
            for member in range(plan.own):
                channel = window * plan.half + target * plan.own + member
                row = jnp.concatenate([rows_ref[pl.ds(channel, 1), :], filler[:1]], axis=1)
                row = jnp.broadcast_to(row, (GROUP, span))
                pieces = [
                    pltpu.roll(row, (MAXLAG - plan.fine + 1 + lag) % span, 1, stride=1, stride_axis=0)
                    for lag in range(0, plan.fine_padded, GROUP)
                ]
                first = hop * plan.height + member * plan.fine_padded
                toeplitz_ref[first : first + plan.fine_padded, at] = jnp.concatenate(pieces, axis=0).astype(
                    jnp.bfloat16
                )
    products = lax.dot_general(
        toeplitz_ref[...],
        columns_ref[...],
        (((1,), (1,)), ((), ())),
        preferred_element_type=jnp.float32,
    )
    if not last:
        sum_ref[...] = products
        return
    products = (products + prior_ref[...]).reshape(plan.targets, plan.own, plan.fine_padded, LANES)
    for hop in range(plan.targets):
        part = products[hop]
        pieces = [part[member, : plan.whole_groups] for member in range(plan.own)]
        if plan.rest:
            pieces += [part[member, plan.whole_groups : plan.fine] for member in range(plan.own)]
        if plan.rows > plan.own * plan.fine:
            pieces.append(jnp.zeros((plan.rows - plan.own * plan.fine, LANES), jnp.float32))
        packed = jnp.concatenate(pieces, axis=0)
        out_refs[hop][...] = packed.astype(out_refs[hop].dtype)


def order_matrix(plan):
    at_row = lax.broadcasted_iota(jnp.int32, (plan.height, plan.rows), 0)
    at_part = lax.broadcasted_iota(jnp.int32, (plan.height, plan.rows), 1)
    order = jnp.zeros((plan.height, plan.rows), jnp.bool_)
    for member in range(plan.own):
        reverse = plan.fine - 1 - (at_row - member * plan.fine_padded)
        whole = (reverse >= 0) & (reverse < plan.whole_groups) & (at_part == member * plan.whole_groups + reverse)
        tail = plan.own * plan.whole_groups + member * plan.rest + reverse - plan.whole_groups
        rest = (reverse >= plan.whole_groups) & (reverse < plan.fine) & (at_part == tail)
        order = order | whole | rest
    return order.astype(jnp.float32).astype(jnp.bfloat16)


def inside_step(plan, step, values):
    lane = lax.broadcasted_iota(jnp.int32, values.shape, 1)
    inside = (lane >= step * plan.channels) & (lane < (step + 1) * plan.channels)
    return jnp.where(inside, values, 0.0).astype(jnp.bfloat16)


def prepare_kernel(plan, index_ref, kept_ref, order_ref, chosen_ref, base_ref):
    first = lax.axis_index("src") * plan.half
    index = index_ref[...] - first
    index = jnp.where(index < 0, index + plan.channels, index)
    at_column = lax.broadcasted_iota(jnp.int32, (LANES, plan.source_count), 0)
    chosen = jnp.zeros((LANES, plan.source_count), jnp.bool_)
    for step in range(plan.coarse):
        chosen = chosen | (at_column == index + step * plan.channels)
    chosen = chosen.astype(jnp.float32).astype(jnp.bfloat16)
    chosen_ref[...] = chosen
    order = order_matrix(plan)
    for block in range(plan.targets - 1):
        order_ref[:, block * plan.rows : (block + 1) * plan.rows] = order
    kept = kept_ref[...] * plan.norm_factor
    high = kept.astype(jnp.bfloat16)
    low = (kept - high.astype(jnp.float32)).astype(jnp.bfloat16)
    parts = [jnp.dot(order, part, preferred_element_type=jnp.float32) for part in (high, low)]
    for step in range(plan.coarse):
        base_ref[step] = sum(
            jnp.dot(inside_step(plan, step, part), chosen, preferred_element_type=jnp.float32) for part in parts
        )


def expand_kernel(plan, order_ref, chosen_ref, base_ref, *refs):
    *arrived_refs, out_hbm, out_ref, sems = refs
    blocks = jnp.concatenate([ref[...] for ref in arrived_refs], axis=0)
    arrived = jnp.dot(order_ref[...], blocks, preferred_element_type=jnp.float32) * plan.norm_factor
    high = arrived.astype(jnp.bfloat16).astype(jnp.float32)
    steps = [inside_step(plan, step, part) for part in (high, arrived - high) for step in range(plan.coarse)]
    moved = jnp.dot(jnp.concatenate(steps, axis=0), chosen_ref[...], preferred_element_type=jnp.float32)
    moved = moved.reshape(2, plan.coarse, plan.height, plan.source_count)
    expanded = [base_ref[step] + (moved[0, step] + moved[1, step]) for step in range(plan.coarse)]
    copies = []
    for member in range(plan.own):
        for step in range(plan.coarse):
            start = step * plan.fine
            count = min(plan.fine, LAG_COUNT - start)
            first = member * plan.fine_padded
            out_ref[member, start : start + count, :] = expanded[step][first : first + count]
        copies.append(pltpu.make_async_copy(out_ref.at[member], out_hbm.at[member], sems.at[member]))
        copies[-1].start()
    for copy in copies:
        copy.wait()


def few_channels(plan, traces, valid_flags, source_index):
    vmem = pl.BlockSpec(memory_space=pltpu.VMEM)
    params = pltpu.CompilerParams(vmem_limit_bytes=32 * 1024 * 1024)
    packed_rows = plan.windows * plan.half
    flags = valid_flags.T

    def swap_cores(array):
        return lax.ppermute(array, "src", [(0, 1), (1, 0)])

    def swap_blk(array, hop):
        return lax.ppermute(array, "blk", [(place, place ^ hop) for place in range(plan.blk_size)])

    whitened = pl.pallas_call(
        functools.partial(whiten_kernel, plan),
        out_shape=pltpu.VMEM((packed_rows, plan.segment), jnp.bfloat16),
        in_specs=[pl.BlockSpec(memory_space=pl.ANY)] * 2,
        out_specs=vmem,
        scratch_shapes=[
            pltpu.VMEM(traces.shape, jnp.float32),
            pltpu.VMEM(flags.shape, jnp.int32),
            pltpu.SemaphoreType.DMA((2,)),
        ],
        compiler_params=pltpu.CompilerParams(vmem_limit_bytes=60 * 1024 * 1024),
        name="whiten",
    )(traces, flags)

    height = plan.targets * plan.height
    width = plan.windows * plan.span

    def correlate(mine, other, prior=None):
        last = prior is not None
        if last:
            types = [jnp.float32] + [jnp.bfloat16] * (plan.targets - 1)
            shapes = [jax.ShapeDtypeStruct((plan.rows, LANES), dtype) for dtype in types]
        else:
            shapes = [jax.ShapeDtypeStruct((height, LANES), jnp.float32)]
        operands = [mine, other] + ([prior] if last else [])
        results = pl.pallas_call(
            functools.partial(correlate_kernel, plan, last),
            out_shape=shapes,
            in_specs=[vmem] * len(operands),
            out_specs=[vmem] * len(shapes),
            scratch_shapes=[
                pltpu.VMEM((packed_rows, plan.segment), jnp.float32),
                pltpu.VMEM((height, width), jnp.bfloat16),
                pltpu.VMEM((LANES, width), jnp.bfloat16),
            ],
            compiler_params=params,
            cost_estimate=pl.CostEstimate(
                flops=2 * height * width * LANES, bytes_accessed=4 * packed_rows * plan.segment, transcendentals=0
            ),
            name="correlate",
        )(*operands)
        return results if last else results[0]

    other = swap_cores(whitened)
    across = swap_blk(whitened, plan.targets)
    total = correlate(whitened, other)
    kept, *sent = correlate(across, swap_cores(across), total)
    arrived = [swap_blk(sent[hop - 1], hop) for hop in (3, 1, 2)]
    order, chosen, base = pl.pallas_call(
        functools.partial(prepare_kernel, plan),
        out_shape=[
            jax.ShapeDtypeStruct((plan.height, (plan.targets - 1) * plan.rows), jnp.bfloat16),
            jax.ShapeDtypeStruct((LANES, plan.source_count), jnp.bfloat16),
            jax.ShapeDtypeStruct((plan.coarse, plan.height, plan.source_count), jnp.float32),
        ],
        in_specs=[vmem] * 2,
        out_specs=[vmem] * 3,
        compiler_params=params,
        name="prepare",
    )(source_index.reshape(1, -1), kept)
    out_shape = (plan.own, LAG_COUNT, plan.source_count)
    return pl.pallas_call(
        functools.partial(expand_kernel, plan),
        out_shape=jax.ShapeDtypeStruct(out_shape, jnp.float32),
        in_specs=[vmem] * (3 + len(arrived)),
        out_specs=pl.BlockSpec(memory_space=pl.ANY),
        scratch_shapes=[pltpu.VMEM(out_shape, jnp.float32), pltpu.SemaphoreType.DMA((plan.own,))],
        compiler_params=params,
        name="expand",
    )(order, chosen, base, *arrived)


def body(traces, valid_flags, source_index):
    plan = Plan(
        traces.shape[0],
        traces.shape[1],
        traces.shape[2],
        lax.axis_size("blk"),
        lax.axis_size("src"),
        source_index.shape[0],
    )
    if plan.fits():
        return few_channels(plan, traces, valid_flags, source_index)
    return many_channels(traces, valid_flags, source_index)


def solution(mesh):
    in_specs = (P(("fibre", "src"), "blk", None), P(("fibre", "src"), "blk"), P())
    out_specs = P(("fibre", "src", "blk"), None, None)
    return jax.shard_map(body, mesh=mesh, in_specs=in_specs, out_specs=out_specs, check_vma=False)
```

```python
import functools
import math

import jax
import jax.numpy as jnp
from jax import lax
from jax.experimental import pallas as pl
from jax.experimental.pallas import tpu as pltpu
from jax.sharding import PartitionSpec as P

MAXLAG = 64
LAG_COUNT = 2 * MAXLAG + 1
LANES = 256
GROUP = 8


def broadcast(value, axis, source):
    kept = jnp.where(lax.axis_index(axis) == source, value, 0).astype(value.dtype)
    return lax.psum(kept, axis)


def toeplitz_rows(group, lag_count, segment):
    shifted = jnp.stack(
        [group[:, :, lag_step : lag_step + segment] for lag_step in range(lag_count)], axis=1
    )
    return shifted.reshape(group.shape[0] * lag_count, -1)


def many_channels(traces, valid_flags, source_index):
    segment = traces.shape[2]
    centered = traces - jnp.mean(traces, axis=2, keepdims=True)
    mean_power = jnp.mean(centered * centered, axis=2, keepdims=True)
    flag_values = valid_flags[:, :, None].astype(jnp.float32)
    whitened = (centered * lax.rsqrt(mean_power + 1e-05) * flag_values).astype(jnp.bfloat16)
    pieces = []
    for owner in range(lax.axis_size("src")):
        pieces.append(broadcast(whitened, "src", owner))
    everyone = jnp.concatenate(pieces, axis=0)
    sources = jnp.take(everyone, source_index, axis=0)
    source_count = sources.shape[0]
    norm_factor = 1.0 / math.sqrt(traces.shape[1] * lax.axis_size("blk") * segment)
    own_rows = whitened.shape[0] // lax.axis_size("blk")
    flat_sources = sources.reshape(source_count, -1)
    padded = jnp.pad(whitened, ((0, 0), (0, 0), (MAXLAG, MAXLAG)))
    block_rows = math.gcd(lax.axis_size("blk") * own_rows, 16)
    grouped = padded.reshape(
        (lax.axis_size("blk") * own_rows // block_rows, block_rows) + padded.shape[1:]
    )

    def one_block(group):
        toeplitz = toeplitz_rows(group, LAG_COUNT, segment)
        products = lax.dot_general(
            toeplitz, flat_sources, (((1,), (1,)), ((), ())), preferred_element_type=jnp.float32
        )
        return (products * norm_factor).reshape(block_rows, LAG_COUNT, source_count)

    result = lax.map(one_block, grouped)
    return lax.psum_scatter(
        result.reshape(lax.axis_size("blk") * own_rows, LAG_COUNT, source_count),
        "blk",
        scatter_dimension=0,
        tiled=True,
    )


class Plan:
    def __init__(self, half, windows, segment, blk_size, src_size, source_count):
        self.half = half
        self.windows = windows
        self.segment = segment
        self.blk_size = blk_size
        self.src_size = src_size
        self.channels = half * src_size
        self.source_count = source_count
        self.coarse = LANES // self.channels
        if self.coarse == 0:
            return
        self.fine = -(-LAG_COUNT // self.coarse)
        self.fine_padded = -(-self.fine // (2 * GROUP)) * 2 * GROUP
        self.own = half // blk_size
        reach = segment + (self.coarse - 1) * self.fine
        self.span = -(-max(reach, segment + 2 * MAXLAG) // 128) * 128
        self.whole_groups = self.fine // GROUP * GROUP
        self.rest = self.fine - self.whole_groups
        rows = self.own * self.fine
        self.rows = -(-rows // 16) * 16
        self.height = self.own * self.fine_padded
        self.targets = blk_size // 2
        self.norm_factor = 1.0 / math.sqrt(windows * blk_size * segment)

    def fits(self):
        return (
            self.coarse >= 2
            and self.src_size == 2
            and self.half % self.blk_size == 0
            and self.half % GROUP == 0
            and self.channels % 16 == 0
            and self.windows * self.half % 16 == 0
            and self.blk_size == 8
        )


def whiten_kernel(plan, traces_hbm, flags_hbm, out_ref, traces_ref, flags_ref, sems):
    copies = [
        pltpu.make_async_copy(traces_hbm, traces_ref, sems.at[0]),
        pltpu.make_async_copy(flags_hbm, flags_ref, sems.at[1]),
    ]
    for copy in copies:
        copy.start()
    for copy in copies:
        copy.wait()
    pieces = []
    for window in range(plan.windows):
        values = traces_ref[:, window, :]
        centered = values - jnp.mean(values, axis=1, keepdims=True)
        mean_power = jnp.mean(centered * centered, axis=1, keepdims=True)
        flag_values = flags_ref[window : window + 1, :].astype(jnp.float32).reshape(plan.half, 1)
        pieces.append(centered * lax.rsqrt(mean_power + 1e-05) * flag_values)
    out_ref[...] = jnp.concatenate(pieces, axis=0).astype(jnp.bfloat16)


def correlate_kernel(plan, last, mine_ref, other_ref, *refs):
    if last:
        prior_ref, *out_refs, rows_ref, toeplitz_ref, columns_ref = refs
    else:
        sum_ref, rows_ref, toeplitz_ref, columns_ref = refs
    span = plan.span
    me = lax.axis_index("blk")
    filled = plan.coarse * plan.channels
    if filled < LANES:
        columns_ref[filled:, :] = jnp.zeros((LANES - filled, columns_ref.shape[1]), jnp.bfloat16)
    filler = jnp.zeros((plan.channels, span - plan.segment), jnp.float32)
    mine = mine_ref[...].astype(jnp.float32)
    other = other_ref[...].astype(jnp.float32)
    rows_ref[...] = mine
    for window in range(plan.windows):
        at = slice(window * span, (window + 1) * span)
        half = slice(window * plan.half, (window + 1) * plan.half)
        both = jnp.concatenate([mine[half], other[half]], axis=0)
        both = jnp.concatenate([both, filler], axis=1)
        for step in range(plan.coarse):
            moved = pltpu.roll(both, step * plan.fine, 1) if step else both
            columns_ref[step * plan.channels : (step + 1) * plan.channels, at] = moved.astype(jnp.bfloat16)
        for hop in range(plan.targets):
            target = me ^ hop
            for member in range(plan.own):
                channel = window * plan.half + target * plan.own + member
                row = jnp.concatenate([rows_ref[pl.ds(channel, 1), :], filler[:1]], axis=1)
                row = jnp.broadcast_to(row, (GROUP, span))
                pieces = [
                    pltpu.roll(row, (MAXLAG - plan.fine + 1 + lag) % span, 1, stride=1, stride_axis=0)
                    for lag in range(0, plan.fine_padded, GROUP)
                ]
                first = hop * plan.height + member * plan.fine_padded
                toeplitz_ref[first : first + plan.fine_padded, at] = jnp.concatenate(pieces, axis=0).astype(
                    jnp.bfloat16
                )
    products = lax.dot_general(
        toeplitz_ref[...],
        columns_ref[...],
        (((1,), (1,)), ((), ())),
        preferred_element_type=jnp.float32,
    )
    if not last:
        sum_ref[...] = products
        return
    products = (products + prior_ref[...]).reshape(plan.targets, plan.own, plan.fine_padded, LANES)
    for hop in range(plan.targets):
        part = products[hop]
        pieces = [part[member, : plan.whole_groups] for member in range(plan.own)]
        if plan.rest:
            pieces += [part[member, plan.whole_groups : plan.fine] for member in range(plan.own)]
        if plan.rows > plan.own * plan.fine:
            pieces.append(jnp.zeros((plan.rows - plan.own * plan.fine, LANES), jnp.float32))
        packed = jnp.concatenate(pieces, axis=0)
        out_refs[hop][...] = packed.astype(out_refs[hop].dtype)


def order_matrix(plan):
    at_row = lax.broadcasted_iota(jnp.int32, (plan.height, plan.rows), 0)
    at_part = lax.broadcasted_iota(jnp.int32, (plan.height, plan.rows), 1)
    order = jnp.zeros((plan.height, plan.rows), jnp.bool_)
    for member in range(plan.own):
        reverse = plan.fine - 1 - (at_row - member * plan.fine_padded)
        whole = (reverse >= 0) & (reverse < plan.whole_groups) & (at_part == member * plan.whole_groups + reverse)
        tail = plan.own * plan.whole_groups + member * plan.rest + reverse - plan.whole_groups
        rest = (reverse >= plan.whole_groups) & (reverse < plan.fine) & (at_part == tail)
        order = order | whole | rest
    return order.astype(jnp.float32).astype(jnp.bfloat16)


def inside_step(plan, step, values):
    lane = lax.broadcasted_iota(jnp.int32, values.shape, 1)
    inside = (lane >= step * plan.channels) & (lane < (step + 1) * plan.channels)
    return jnp.where(inside, values, 0.0).astype(jnp.bfloat16)


def prepare_kernel(plan, index_ref, kept_ref, order_ref, chosen_ref, base_ref):
    first = lax.axis_index("src") * plan.half
    index = index_ref[...] - first
    index = jnp.where(index < 0, index + plan.channels, index)
    at_column = lax.broadcasted_iota(jnp.int32, (LANES, plan.source_count), 0)
    chosen = jnp.zeros((LANES, plan.source_count), jnp.bool_)
    for step in range(plan.coarse):
        chosen = chosen | (at_column == index + step * plan.channels)
    chosen = chosen.astype(jnp.float32).astype(jnp.bfloat16)
    chosen_ref[...] = chosen
    order = order_matrix(plan)
    for block in range(plan.targets - 1):
        order_ref[:, block * plan.rows : (block + 1) * plan.rows] = order
    kept = kept_ref[...] * plan.norm_factor
    high = kept.astype(jnp.bfloat16)
    low = (kept - high.astype(jnp.float32)).astype(jnp.bfloat16)
    parts = [jnp.dot(order, part, preferred_element_type=jnp.float32) for part in (high, low)]
    for step in range(plan.coarse):
        base_ref[step] = sum(
            jnp.dot(inside_step(plan, step, part), chosen, preferred_element_type=jnp.float32) for part in parts
        )


def expand_kernel(plan, order_ref, chosen_ref, base_ref, *refs):
    *arrived_refs, out_hbm, out_ref, sems = refs
    blocks = jnp.concatenate([ref[...] for ref in arrived_refs], axis=0)
    arrived = jnp.dot(order_ref[...], blocks, preferred_element_type=jnp.float32) * plan.norm_factor
    high = arrived.astype(jnp.bfloat16).astype(jnp.float32)
    steps = [inside_step(plan, step, part) for part in (high, arrived - high) for step in range(plan.coarse)]
    moved = jnp.dot(jnp.concatenate(steps, axis=0), chosen_ref[...], preferred_element_type=jnp.float32)
    moved = moved.reshape(2, plan.coarse, plan.height, plan.source_count)
    expanded = [base_ref[step] + (moved[0, step] + moved[1, step]) for step in range(plan.coarse)]
    copies = []
    for member in range(plan.own):
        for step in range(plan.coarse):
            start = step * plan.fine
            count = min(plan.fine, LAG_COUNT - start)
            first = member * plan.fine_padded
            out_ref[member, start : start + count, :] = expanded[step][first : first + count]
        copies.append(pltpu.make_async_copy(out_ref.at[member], out_hbm.at[member], sems.at[member]))
        copies[-1].start()
    for copy in copies:
        copy.wait()


def few_channels(plan, traces, valid_flags, source_index):
    vmem = pl.BlockSpec(memory_space=pltpu.VMEM)
    params = pltpu.CompilerParams(vmem_limit_bytes=32 * 1024 * 1024)
    packed_rows = plan.windows * plan.half
    flags = valid_flags.T

    def swap_cores(array):
        return lax.ppermute(array, "src", [(0, 1), (1, 0)])

    def swap_blk(array, hop):
        return lax.ppermute(array, "blk", [(place, place ^ hop) for place in range(plan.blk_size)])

    whitened = pl.pallas_call(
        functools.partial(whiten_kernel, plan),
        out_shape=pltpu.VMEM((packed_rows, plan.segment), jnp.bfloat16),
        in_specs=[pl.BlockSpec(memory_space=pl.ANY)] * 2,
        out_specs=vmem,
        scratch_shapes=[
            pltpu.VMEM(traces.shape, jnp.float32),
            pltpu.VMEM(flags.shape, jnp.int32),
            pltpu.SemaphoreType.DMA((2,)),
        ],
        compiler_params=pltpu.CompilerParams(vmem_limit_bytes=60 * 1024 * 1024),
        name="whiten",
    )(traces, flags)

    height = plan.targets * plan.height
    width = plan.windows * plan.span

    def correlate(mine, other, prior=None):
        last = prior is not None
        if last:
            types = [jnp.float32] + [jnp.bfloat16] * (plan.targets - 1)
            shapes = [jax.ShapeDtypeStruct((plan.rows, LANES), dtype) for dtype in types]
        else:
            shapes = [jax.ShapeDtypeStruct((height, LANES), jnp.float32)]
        operands = [mine, other] + ([prior] if last else [])
        results = pl.pallas_call(
            functools.partial(correlate_kernel, plan, last),
            out_shape=shapes,
            in_specs=[vmem] * len(operands),
            out_specs=[vmem] * len(shapes),
            scratch_shapes=[
                pltpu.VMEM((packed_rows, plan.segment), jnp.float32),
                pltpu.VMEM((height, width), jnp.bfloat16),
                pltpu.VMEM((LANES, width), jnp.bfloat16),
            ],
            compiler_params=params,
            cost_estimate=pl.CostEstimate(
                flops=2 * height * width * LANES, bytes_accessed=4 * packed_rows * plan.segment, transcendentals=0
            ),
            name="correlate",
        )(*operands)
        return results if last else results[0]

    other = swap_cores(whitened)
    across = swap_blk(whitened, plan.targets)
    total = correlate(whitened, other)
    kept, *sent = correlate(across, swap_cores(across), total)
    arrived = [swap_blk(sent[hop - 1], hop) for hop in (1, 3, 2)]
    order, chosen, base = pl.pallas_call(
        functools.partial(prepare_kernel, plan),
        out_shape=[
            jax.ShapeDtypeStruct((plan.height, (plan.targets - 1) * plan.rows), jnp.bfloat16),
            jax.ShapeDtypeStruct((LANES, plan.source_count), jnp.bfloat16),
            jax.ShapeDtypeStruct((plan.coarse, plan.height, plan.source_count), jnp.float32),
        ],
        in_specs=[vmem] * 2,
        out_specs=[vmem] * 3,
        compiler_params=params,
        name="prepare",
    )(source_index.reshape(1, -1), kept)
    out_shape = (plan.own, LAG_COUNT, plan.source_count)
    return pl.pallas_call(
        functools.partial(expand_kernel, plan),
        out_shape=jax.ShapeDtypeStruct(out_shape, jnp.float32),
        in_specs=[vmem] * (3 + len(arrived)),
        out_specs=pl.BlockSpec(memory_space=pl.ANY),
        scratch_shapes=[pltpu.VMEM(out_shape, jnp.float32), pltpu.SemaphoreType.DMA((plan.own,))],
        compiler_params=params,
        name="expand",
    )(order, chosen, base, *arrived)


def body(traces, valid_flags, source_index):
    plan = Plan(
        traces.shape[0],
        traces.shape[1],
        traces.shape[2],
        lax.axis_size("blk"),
        lax.axis_size("src"),
        source_index.shape[0],
    )
    if plan.fits():
        return few_channels(plan, traces, valid_flags, source_index)
    return many_channels(traces, valid_flags, source_index)


def solution(mesh):
    in_specs = (P(("fibre", "src"), "blk", None), P(("fibre", "src"), "blk"), P())
    out_specs = P(("fibre", "src", "blk"), None, None)
    return jax.shard_map(body, mesh=mesh, in_specs=in_specs, out_specs=out_specs, check_vma=False)
```

```python
import functools
import math

import jax
import jax.numpy as jnp
from jax import lax
from jax.experimental import pallas as pl
from jax.experimental.pallas import tpu as pltpu
from jax.sharding import PartitionSpec as P

MAXLAG = 64
LAG_COUNT = 2 * MAXLAG + 1
LANES = 256
GROUP = 8


def broadcast(value, axis, source):
    kept = jnp.where(lax.axis_index(axis) == source, value, 0).astype(value.dtype)
    return lax.psum(kept, axis)


def toeplitz_rows(group, lag_count, segment):
    shifted = jnp.stack(
        [group[:, :, lag_step : lag_step + segment] for lag_step in range(lag_count)], axis=1
    )
    return shifted.reshape(group.shape[0] * lag_count, -1)


def many_channels(traces, valid_flags, source_index):
    segment = traces.shape[2]
    centered = traces - jnp.mean(traces, axis=2, keepdims=True)
    mean_power = jnp.mean(centered * centered, axis=2, keepdims=True)
    flag_values = valid_flags[:, :, None].astype(jnp.float32)
    whitened = (centered * lax.rsqrt(mean_power + 1e-05) * flag_values).astype(jnp.bfloat16)
    pieces = []
    for owner in range(lax.axis_size("src")):
        pieces.append(broadcast(whitened, "src", owner))
    everyone = jnp.concatenate(pieces, axis=0)
    sources = jnp.take(everyone, source_index, axis=0)
    source_count = sources.shape[0]
    norm_factor = 1.0 / math.sqrt(traces.shape[1] * lax.axis_size("blk") * segment)
    own_rows = whitened.shape[0] // lax.axis_size("blk")
    flat_sources = sources.reshape(source_count, -1)
    padded = jnp.pad(whitened, ((0, 0), (0, 0), (MAXLAG, MAXLAG)))
    block_rows = math.gcd(lax.axis_size("blk") * own_rows, 16)
    grouped = padded.reshape(
        (lax.axis_size("blk") * own_rows // block_rows, block_rows) + padded.shape[1:]
    )

    def one_block(group):
        toeplitz = toeplitz_rows(group, LAG_COUNT, segment)
        products = lax.dot_general(
            toeplitz, flat_sources, (((1,), (1,)), ((), ())), preferred_element_type=jnp.float32
        )
        return (products * norm_factor).reshape(block_rows, LAG_COUNT, source_count)

    result = lax.map(one_block, grouped)
    return lax.psum_scatter(
        result.reshape(lax.axis_size("blk") * own_rows, LAG_COUNT, source_count),
        "blk",
        scatter_dimension=0,
        tiled=True,
    )


class Plan:
    def __init__(self, half, windows, segment, blk_size, src_size, source_count):
        self.half = half
        self.windows = windows
        self.segment = segment
        self.blk_size = blk_size
        self.src_size = src_size
        self.channels = half * src_size
        self.source_count = source_count
        self.half_lanes = LANES // 2
        self.coarse = self.half_lanes // half
        if self.coarse == 0:
            return
        self.fine = -(-LAG_COUNT // self.coarse)
        self.fine_padded = -(-self.fine // (2 * GROUP)) * 2 * GROUP
        self.own = half // blk_size
        reach = segment + (self.coarse - 1) * self.fine
        self.span = -(-max(reach, segment + 2 * MAXLAG) // 128) * 128
        self.whole_groups = self.fine // GROUP * GROUP
        self.rest = self.fine - self.whole_groups
        rows = self.own * self.fine
        self.rows = -(-rows // 16) * 16
        self.height = self.own * self.fine_padded
        self.targets = blk_size // 2
        self.norm_factor = 1.0 / math.sqrt(windows * blk_size * segment)

    def fits(self):
        return (
            self.coarse >= 2
            and self.src_size == 2
            and self.half % self.blk_size == 0
            and self.half % GROUP == 0
            and self.channels % 16 == 0
            and self.windows * self.half % 16 == 0
            and self.blk_size == 8
        )


def whiten_kernel(plan, traces_hbm, flags_hbm, out_ref, traces_ref, flags_ref, sems):
    copies = [
        pltpu.make_async_copy(traces_hbm, traces_ref, sems.at[0]),
        pltpu.make_async_copy(flags_hbm, flags_ref, sems.at[1]),
    ]
    for copy in copies:
        copy.start()
    for copy in copies:
        copy.wait()
    pieces = []
    for window in range(plan.windows):
        values = traces_ref[:, window, :]
        centered = values - jnp.mean(values, axis=1, keepdims=True)
        mean_power = jnp.mean(centered * centered, axis=1, keepdims=True)
        flag_values = flags_ref[window : window + 1, :].astype(jnp.float32).reshape(plan.half, 1)
        pieces.append(centered * lax.rsqrt(mean_power + 1e-05) * flag_values)
    out_ref[...] = jnp.concatenate(pieces, axis=0).astype(jnp.bfloat16)


def lag_rows(plan, rows_ref, toeplitz_ref):
    span = plan.span
    me = lax.axis_index("blk")
    filler = jnp.zeros((1, span - plan.segment), jnp.float32)
    for window in range(plan.windows):
        at = slice(window * span, (window + 1) * span)
        for hop in range(plan.targets):
            for member in range(plan.own):
                channel = window * plan.half + (me ^ hop) * plan.own + member
                row = jnp.concatenate([rows_ref[pl.ds(channel, 1), :], filler], axis=1)
                row = jnp.broadcast_to(row, (GROUP, span))
                pieces = [
                    pltpu.roll(row, (MAXLAG - plan.fine + 1 + lag) % span, 1, stride=1, stride_axis=0)
                    for lag in range(0, plan.fine_padded, GROUP)
                ]
                first = hop * plan.height + member * plan.fine_padded
                toeplitz_ref[first : first + plan.fine_padded, at] = jnp.concatenate(pieces, axis=0).astype(
                    jnp.bfloat16
                )


def half_product(plan, values, toeplitz_ref, columns_ref):
    span = plan.span
    filled = plan.coarse * plan.half
    if filled < plan.half_lanes:
        columns_ref[filled:, :] = jnp.zeros((plan.half_lanes - filled, columns_ref.shape[1]), jnp.bfloat16)
    filler = jnp.zeros((plan.half, span - plan.segment), jnp.float32)
    for window in range(plan.windows):
        at = slice(window * span, (window + 1) * span)
        rows = jnp.concatenate([values[window * plan.half : (window + 1) * plan.half], filler], axis=1)
        for step in range(plan.coarse):
            moved = pltpu.roll(rows, step * plan.fine, 1) if step else rows
            columns_ref[step * plan.half : (step + 1) * plan.half, at] = moved.astype(jnp.bfloat16)
    return lax.dot_general(
        toeplitz_ref[...], columns_ref[...], (((1,), (1,)), ((), ())), preferred_element_type=jnp.float32
    )


def near_kernel(plan, mine_ref, other_ref, sum_ref, rows_ref, toeplitz_ref, columns_ref):
    rows_ref[...] = mine_ref[...].astype(jnp.float32)
    lag_rows(plan, rows_ref, toeplitz_ref)
    other = other_ref[...].astype(jnp.float32)
    sum_ref[:, : plan.half_lanes] = half_product(plan, rows_ref[...], toeplitz_ref, columns_ref.at[0])
    sum_ref[:, plan.half_lanes :] = half_product(plan, other, toeplitz_ref, columns_ref.at[1])


def across_kernel(plan, mine_ref, prior_ref, toeplitz_ref, sum_ref, rows_ref, columns_ref):
    rows_ref[...] = mine_ref[...].astype(jnp.float32)
    lag_rows(plan, rows_ref, toeplitz_ref)
    sum_ref[:, : plan.half_lanes] = prior_ref[:, : plan.half_lanes] + half_product(
        plan, rows_ref[...], toeplitz_ref, columns_ref
    )
    sum_ref[:, plan.half_lanes :] = prior_ref[:, plan.half_lanes :]


def finish_kernel(plan, other_ref, toeplitz_ref, prior_ref, *refs):
    *out_refs, columns_ref = refs
    right = prior_ref[:, plan.half_lanes :] + half_product(
        plan, other_ref[...].astype(jnp.float32), toeplitz_ref, columns_ref
    )
    products = jnp.concatenate([prior_ref[:, : plan.half_lanes], right], axis=1)
    products = products.reshape(plan.targets, plan.own, plan.fine_padded, LANES)
    for hop in range(plan.targets):
        part = products[hop]
        pieces = [part[member, : plan.whole_groups] for member in range(plan.own)]
        if plan.rest:
            pieces += [part[member, plan.whole_groups : plan.fine] for member in range(plan.own)]
        if plan.rows > plan.own * plan.fine:
            pieces.append(jnp.zeros((plan.rows - plan.own * plan.fine, LANES), jnp.float32))
        packed = jnp.concatenate(pieces, axis=0)
        out_refs[hop][...] = packed.astype(out_refs[hop].dtype)


def order_matrix(plan):
    at_row = lax.broadcasted_iota(jnp.int32, (plan.height, plan.rows), 0)
    at_part = lax.broadcasted_iota(jnp.int32, (plan.height, plan.rows), 1)
    order = jnp.zeros((plan.height, plan.rows), jnp.bool_)
    for member in range(plan.own):
        reverse = plan.fine - 1 - (at_row - member * plan.fine_padded)
        whole = (reverse >= 0) & (reverse < plan.whole_groups) & (at_part == member * plan.whole_groups + reverse)
        tail = plan.own * plan.whole_groups + member * plan.rest + reverse - plan.whole_groups
        rest = (reverse >= plan.whole_groups) & (reverse < plan.fine) & (at_part == tail)
        order = order | whole | rest
    return order.astype(jnp.float32).astype(jnp.bfloat16)


def inside_step(plan, step, values):
    lane = lax.broadcasted_iota(jnp.int32, values.shape, 1)
    lane = jnp.where(lane >= plan.half_lanes, lane - plan.half_lanes, lane)
    inside = (lane >= step * plan.half) & (lane < (step + 1) * plan.half)
    return jnp.where(inside, values, 0.0).astype(jnp.bfloat16)


def choose_kernel(plan, index_ref, whitened_ref, order_ref, chosen_ref, same_ref):
    first = lax.axis_index("src") * plan.half
    index = index_ref[...] - first
    index = jnp.where(index < 0, index + plan.channels, index)
    lane = jnp.where(index >= plan.half, index - plan.half + plan.half_lanes, index)
    at_column = lax.broadcasted_iota(jnp.int32, (LANES, plan.source_count), 0)
    chosen = jnp.zeros((LANES, plan.source_count), jnp.bool_)
    for step in range(plan.coarse):
        chosen = chosen | (at_column == lane + step * plan.half)
    chosen_ref[...] = chosen.astype(jnp.float32).astype(jnp.bfloat16)
    order = order_matrix(plan)
    for block in range(plan.targets - 1):
        order_ref[:, block * plan.rows : (block + 1) * plan.rows] = order
    same_ref[...] = whitened_ref[...]


def prepare_kernel(plan, order_ref, chosen_ref, kept_ref, base_ref):
    order = order_ref[:, : plan.rows]
    chosen = chosen_ref[...]
    kept = kept_ref[...] * plan.norm_factor
    high = kept.astype(jnp.bfloat16)
    low = (kept - high.astype(jnp.float32)).astype(jnp.bfloat16)
    parts = [jnp.dot(order, part, preferred_element_type=jnp.float32) for part in (high, low)]
    for step in range(plan.coarse):
        base_ref[step] = sum(
            jnp.dot(inside_step(plan, step, part), chosen, preferred_element_type=jnp.float32) for part in parts
        )


def expand_kernel(plan, order_ref, chosen_ref, base_ref, *refs):
    *arrived_refs, out_hbm, out_ref, sems = refs
    blocks = jnp.concatenate([ref[...] for ref in arrived_refs], axis=0)
    arrived = jnp.dot(order_ref[...], blocks, preferred_element_type=jnp.float32) * plan.norm_factor
    high = arrived.astype(jnp.bfloat16).astype(jnp.float32)
    steps = [inside_step(plan, step, part) for part in (high, arrived - high) for step in range(plan.coarse)]
    moved = jnp.dot(jnp.concatenate(steps, axis=0), chosen_ref[...], preferred_element_type=jnp.float32)
    moved = moved.reshape(2, plan.coarse, plan.height, plan.source_count)
    expanded = [base_ref[step] + (moved[0, step] + moved[1, step]) for step in range(plan.coarse)]
    copies = []
    for member in range(plan.own):
        for step in range(plan.coarse):
            start = step * plan.fine
            count = min(plan.fine, LAG_COUNT - start)
            first = member * plan.fine_padded
            out_ref[member, start : start + count, :] = expanded[step][first : first + count]
        copies.append(pltpu.make_async_copy(out_ref.at[member], out_hbm.at[member], sems.at[member]))
        copies[-1].start()
    for copy in copies:
        copy.wait()


def few_channels(plan, traces, valid_flags, source_index):
    vmem = pl.BlockSpec(memory_space=pltpu.VMEM)
    params = pltpu.CompilerParams(vmem_limit_bytes=32 * 1024 * 1024)
    packed_rows = plan.windows * plan.half
    flags = valid_flags.T

    def swap_cores(array):
        return lax.ppermute(array, "src", [(0, 1), (1, 0)])

    def swap_blk(array, hop):
        return lax.ppermute(array, "blk", [(place, place ^ hop) for place in range(plan.blk_size)])

    whitened = pl.pallas_call(
        functools.partial(whiten_kernel, plan),
        out_shape=pltpu.VMEM((packed_rows, plan.segment), jnp.bfloat16),
        in_specs=[pl.BlockSpec(memory_space=pl.ANY)] * 2,
        out_specs=vmem,
        scratch_shapes=[
            pltpu.VMEM(traces.shape, jnp.float32),
            pltpu.VMEM(flags.shape, jnp.int32),
            pltpu.SemaphoreType.DMA((2,)),
        ],
        compiler_params=pltpu.CompilerParams(vmem_limit_bytes=60 * 1024 * 1024),
        name="whiten",
    )(traces, flags)

    height = plan.targets * plan.height
    width = plan.windows * plan.span
    rows = pltpu.VMEM((packed_rows, plan.segment), jnp.float32)
    toeplitz = (height, width)
    columns = (plan.half_lanes, width)
    sums = jax.ShapeDtypeStruct((height, LANES), jnp.float32)

    def call(kernel, name, operands, outputs, scratch=()):
        return pl.pallas_call(
            functools.partial(kernel, plan),
            out_shape=outputs,
            in_specs=[vmem] * len(operands),
            out_specs=[vmem] * len(outputs),
            scratch_shapes=scratch,
            compiler_params=params,
            name=name,
        )(*operands)

    across = swap_blk(whitened, plan.targets)
    order, chosen, same = call(
        choose_kernel,
        "choose",
        (source_index.reshape(1, -1), whitened),
        (
            jax.ShapeDtypeStruct((plan.height, (plan.targets - 1) * plan.rows), jnp.bfloat16),
            jax.ShapeDtypeStruct((LANES, plan.source_count), jnp.bfloat16),
            jax.ShapeDtypeStruct(whitened.shape, whitened.dtype),
        ),
    )
    (total,) = call(
        near_kernel,
        "near",
        (whitened, swap_cores(same)),
        (sums,),
        (rows, pltpu.VMEM(toeplitz, jnp.bfloat16), pltpu.VMEM((2,) + columns, jnp.bfloat16)),
    )
    across_other = swap_cores(across)
    lagged, total = call(
        across_kernel,
        "across",
        (across, total),
        (jax.ShapeDtypeStruct(toeplitz, jnp.bfloat16), sums),
        (rows, pltpu.VMEM(columns, jnp.bfloat16)),
    )
    kept, *sent = call(
        finish_kernel,
        "finish",
        (across_other, lagged, total),
        tuple(
            jax.ShapeDtypeStruct((plan.rows, LANES), jnp.bfloat16 if hop else jnp.float32)
            for hop in range(plan.targets)
        ),
        (pltpu.VMEM(columns, jnp.bfloat16),),
    )
    arrived = [swap_blk(sent[hop - 1], hop) for hop in (1, 3, 2)]
    (base,) = call(
        prepare_kernel,
        "prepare",
        (order, chosen, kept),
        (jax.ShapeDtypeStruct((plan.coarse, plan.height, plan.source_count), jnp.float32),),
    )
    out_shape = (plan.own, LAG_COUNT, plan.source_count)
    return pl.pallas_call(
        functools.partial(expand_kernel, plan),
        out_shape=jax.ShapeDtypeStruct(out_shape, jnp.float32),
        in_specs=[vmem] * (3 + len(arrived)),
        out_specs=pl.BlockSpec(memory_space=pl.ANY),
        scratch_shapes=[pltpu.VMEM(out_shape, jnp.float32), pltpu.SemaphoreType.DMA((plan.own,))],
        compiler_params=params,
        name="expand",
    )(order, chosen, base, *arrived)


def body(traces, valid_flags, source_index):
    plan = Plan(
        traces.shape[0],
        traces.shape[1],
        traces.shape[2],
        lax.axis_size("blk"),
        lax.axis_size("src"),
        source_index.shape[0],
    )
    if plan.fits():
        return few_channels(plan, traces, valid_flags, source_index)
    return many_channels(traces, valid_flags, source_index)


def solution(mesh):
    in_specs = (P(("fibre", "src"), "blk", None), P(("fibre", "src"), "blk"), P())
    out_specs = P(("fibre", "src", "blk"), None, None)
    return jax.shard_map(body, mesh=mesh, in_specs=in_specs, out_specs=out_specs, check_vma=False)
```

```python
import functools
import math

import jax
import jax.numpy as jnp
from jax import lax
from jax.experimental import pallas as pl
from jax.experimental.pallas import tpu as pltpu
from jax.sharding import PartitionSpec as P

MAXLAG = 64
LAG_COUNT = 2 * MAXLAG + 1
LANES = 256
GROUP = 8
HOPS = ((3, 2), (1, 3), (2, 1))


def broadcast(value, axis, source):
    kept = jnp.where(lax.axis_index(axis) == source, value, 0).astype(value.dtype)
    return lax.psum(kept, axis)


def toeplitz_rows(group, lag_count, segment):
    shifted = jnp.stack(
        [group[:, :, lag_step : lag_step + segment] for lag_step in range(lag_count)], axis=1
    )
    return shifted.reshape(group.shape[0] * lag_count, -1)


def many_channels(traces, valid_flags, source_index):
    segment = traces.shape[2]
    centered = traces - jnp.mean(traces, axis=2, keepdims=True)
    mean_power = jnp.mean(centered * centered, axis=2, keepdims=True)
    flag_values = valid_flags[:, :, None].astype(jnp.float32)
    whitened = (centered * lax.rsqrt(mean_power + 1e-05) * flag_values).astype(jnp.bfloat16)
    pieces = []
    for owner in range(lax.axis_size("src")):
        pieces.append(broadcast(whitened, "src", owner))
    everyone = jnp.concatenate(pieces, axis=0)
    sources = jnp.take(everyone, source_index, axis=0)
    source_count = sources.shape[0]
    norm_factor = 1.0 / math.sqrt(traces.shape[1] * lax.axis_size("blk") * segment)
    own_rows = whitened.shape[0] // lax.axis_size("blk")
    flat_sources = sources.reshape(source_count, -1)
    padded = jnp.pad(whitened, ((0, 0), (0, 0), (MAXLAG, MAXLAG)))
    block_rows = math.gcd(lax.axis_size("blk") * own_rows, 16)
    grouped = padded.reshape(
        (lax.axis_size("blk") * own_rows // block_rows, block_rows) + padded.shape[1:]
    )

    def one_block(group):
        toeplitz = toeplitz_rows(group, LAG_COUNT, segment)
        products = lax.dot_general(
            toeplitz, flat_sources, (((1,), (1,)), ((), ())), preferred_element_type=jnp.float32
        )
        return (products * norm_factor).reshape(block_rows, LAG_COUNT, source_count)

    result = lax.map(one_block, grouped)
    return lax.psum_scatter(
        result.reshape(lax.axis_size("blk") * own_rows, LAG_COUNT, source_count),
        "blk",
        scatter_dimension=0,
        tiled=True,
    )


class Plan:
    def __init__(self, half, windows, segment, blk_size, src_size, source_count):
        self.half = half
        self.windows = windows
        self.segment = segment
        self.blk_size = blk_size
        self.src_size = src_size
        self.channels = half * src_size
        self.source_count = source_count
        self.half_lanes = LANES // 2
        self.coarse = self.half_lanes // half
        if self.coarse == 0:
            return
        self.fine = -(-LAG_COUNT // self.coarse)
        self.fine_padded = -(-self.fine // (2 * GROUP)) * 2 * GROUP
        self.own = half // blk_size
        reach = segment + (self.coarse - 1) * self.fine
        self.span = -(-max(reach, segment + 2 * MAXLAG) // 128) * 128
        self.whole_groups = self.fine // GROUP * GROUP
        self.rest = self.fine - self.whole_groups
        rows = self.own * self.fine
        self.rows = -(-rows // 16) * 16
        self.height = self.own * self.fine_padded
        self.targets = blk_size // 2
        self.norm_factor = 1.0 / math.sqrt(windows * blk_size * segment)

    def fits(self):
        return (
            self.coarse >= 2
            and self.src_size == 2
            and self.half % self.blk_size == 0
            and self.half % GROUP == 0
            and self.channels % 16 == 0
            and self.windows * self.half % 16 == 0
            and self.blk_size == 8
        )


def whiten_kernel(plan, traces_hbm, flags_hbm, out_ref, traces_ref, flags_ref, sems):
    copies = [
        pltpu.make_async_copy(traces_hbm, traces_ref, sems.at[0]),
        pltpu.make_async_copy(flags_hbm, flags_ref, sems.at[1]),
    ]
    for copy in copies:
        copy.start()
    for copy in copies:
        copy.wait()
    pieces = []
    for window in range(plan.windows):
        values = traces_ref[:, window, :]
        centered = values - jnp.mean(values, axis=1, keepdims=True)
        mean_power = jnp.mean(centered * centered, axis=1, keepdims=True)
        flag_values = flags_ref[window : window + 1, :].astype(jnp.float32).reshape(plan.half, 1)
        pieces.append(centered * lax.rsqrt(mean_power + 1e-05) * flag_values)
    out_ref[...] = jnp.concatenate(pieces, axis=0).astype(jnp.bfloat16)


def lag_rows(plan, rows_ref, toeplitz_ref):
    span = plan.span
    me = lax.axis_index("blk")
    on_first = lax.axis_index("src") == 0
    hops = [0] + [jnp.where(on_first, *pair) for pair in HOPS]
    filler = jnp.zeros((1, span - plan.segment), jnp.float32)
    for window in range(plan.windows):
        at = slice(window * span, (window + 1) * span)
        for place, hop in enumerate(hops):
            for member in range(plan.own):
                channel = window * plan.half + (me ^ hop) * plan.own + member
                row = jnp.concatenate([rows_ref[pl.ds(channel, 1), :], filler], axis=1)
                row = jnp.broadcast_to(row, (GROUP, span))
                pieces = [
                    pltpu.roll(row, (MAXLAG - plan.fine + 1 + lag) % span, 1, stride=1, stride_axis=0)
                    for lag in range(0, plan.fine_padded, GROUP)
                ]
                first = place * plan.height + member * plan.fine_padded
                toeplitz_ref[first : first + plan.fine_padded, at] = jnp.concatenate(pieces, axis=0).astype(
                    jnp.bfloat16
                )


def half_product(plan, values, toeplitz_ref, columns_ref):
    span = plan.span
    filled = plan.coarse * plan.half
    if filled < plan.half_lanes:
        columns_ref[filled:, :] = jnp.zeros((plan.half_lanes - filled, columns_ref.shape[1]), jnp.bfloat16)
    filler = jnp.zeros((plan.half, span - plan.segment), jnp.float32)
    for window in range(plan.windows):
        at = slice(window * span, (window + 1) * span)
        rows = jnp.concatenate([values[window * plan.half : (window + 1) * plan.half], filler], axis=1)
        for step in range(plan.coarse):
            moved = pltpu.roll(rows, step * plan.fine, 1) if step else rows
            columns_ref[step * plan.half : (step + 1) * plan.half, at] = moved.astype(jnp.bfloat16)
    return lax.dot_general(
        toeplitz_ref[...], columns_ref[...], (((1,), (1,)), ((), ())), preferred_element_type=jnp.float32
    )


def near_kernel(plan, mine_ref, other_ref, sum_ref, rows_ref, toeplitz_ref, columns_ref):
    rows_ref[...] = mine_ref[...].astype(jnp.float32)
    lag_rows(plan, rows_ref, toeplitz_ref)
    other = other_ref[...].astype(jnp.float32)
    sum_ref[:, : plan.half_lanes] = half_product(plan, rows_ref[...], toeplitz_ref, columns_ref.at[0])
    sum_ref[:, plan.half_lanes :] = half_product(plan, other, toeplitz_ref, columns_ref.at[1])


def across_kernel(plan, mine_ref, prior_ref, toeplitz_ref, sum_ref, rows_ref, columns_ref):
    rows_ref[...] = mine_ref[...].astype(jnp.float32)
    lag_rows(plan, rows_ref, toeplitz_ref)
    sum_ref[:, : plan.half_lanes] = prior_ref[:, : plan.half_lanes] + half_product(
        plan, rows_ref[...], toeplitz_ref, columns_ref
    )
    sum_ref[:, plan.half_lanes :] = prior_ref[:, plan.half_lanes :]


def finish_kernel(plan, other_ref, toeplitz_ref, prior_ref, *refs):
    *out_refs, columns_ref = refs
    right = prior_ref[:, plan.half_lanes :] + half_product(
        plan, other_ref[...].astype(jnp.float32), toeplitz_ref, columns_ref
    )
    products = jnp.concatenate([prior_ref[:, : plan.half_lanes], right], axis=1)
    products = products.reshape(plan.targets, plan.own, plan.fine_padded, LANES)
    for hop in range(plan.targets):
        part = products[hop]
        pieces = [part[member, : plan.whole_groups] for member in range(plan.own)]
        if plan.rest:
            pieces += [part[member, plan.whole_groups : plan.fine] for member in range(plan.own)]
        if plan.rows > plan.own * plan.fine:
            pieces.append(jnp.zeros((plan.rows - plan.own * plan.fine, LANES), jnp.float32))
        packed = jnp.concatenate(pieces, axis=0)
        out_refs[hop][...] = packed.astype(out_refs[hop].dtype)


def order_matrix(plan):
    at_row = lax.broadcasted_iota(jnp.int32, (plan.height, plan.rows), 0)
    at_part = lax.broadcasted_iota(jnp.int32, (plan.height, plan.rows), 1)
    order = jnp.zeros((plan.height, plan.rows), jnp.bool_)
    for member in range(plan.own):
        reverse = plan.fine - 1 - (at_row - member * plan.fine_padded)
        whole = (reverse >= 0) & (reverse < plan.whole_groups) & (at_part == member * plan.whole_groups + reverse)
        tail = plan.own * plan.whole_groups + member * plan.rest + reverse - plan.whole_groups
        rest = (reverse >= plan.whole_groups) & (reverse < plan.fine) & (at_part == tail)
        order = order | whole | rest
    return order.astype(jnp.float32).astype(jnp.bfloat16)


def inside_step(plan, step, values):
    lane = lax.broadcasted_iota(jnp.int32, values.shape, 1)
    lane = jnp.where(lane >= plan.half_lanes, lane - plan.half_lanes, lane)
    inside = (lane >= step * plan.half) & (lane < (step + 1) * plan.half)
    return jnp.where(inside, values, 0.0).astype(jnp.bfloat16)


def choose_kernel(plan, index_ref, whitened_ref, order_ref, chosen_ref, same_ref):
    first = lax.axis_index("src") * plan.half
    index = index_ref[...] - first
    index = jnp.where(index < 0, index + plan.channels, index)
    lane = jnp.where(index >= plan.half, index - plan.half + plan.half_lanes, index)
    at_column = lax.broadcasted_iota(jnp.int32, (LANES, plan.source_count), 0)
    chosen = jnp.zeros((LANES, plan.source_count), jnp.bool_)
    for step in range(plan.coarse):
        chosen = chosen | (at_column == lane + step * plan.half)
    chosen_ref[...] = chosen.astype(jnp.float32).astype(jnp.bfloat16)
    order = order_matrix(plan)
    for block in range(plan.targets - 1):
        order_ref[:, block * plan.rows : (block + 1) * plan.rows] = order
    same_ref[...] = whitened_ref[...]


def prepare_kernel(plan, order_ref, chosen_ref, kept_ref, base_ref):
    order = order_ref[:, : plan.rows]
    chosen = chosen_ref[...]
    kept = kept_ref[...] * plan.norm_factor
    high = kept.astype(jnp.bfloat16)
    low = (kept - high.astype(jnp.float32)).astype(jnp.bfloat16)
    parts = [jnp.dot(order, part, preferred_element_type=jnp.float32) for part in (high, low)]
    for step in range(plan.coarse):
        base_ref[step] = sum(
            jnp.dot(inside_step(plan, step, part), chosen, preferred_element_type=jnp.float32) for part in parts
        )


def expand_kernel(plan, order_ref, chosen_ref, base_ref, *refs):
    *arrived_refs, out_hbm, out_ref, sems = refs
    blocks = jnp.concatenate([ref[...] for ref in arrived_refs], axis=0)
    arrived = jnp.dot(order_ref[...], blocks, preferred_element_type=jnp.float32) * plan.norm_factor
    high = arrived.astype(jnp.bfloat16).astype(jnp.float32)
    steps = [inside_step(plan, step, part) for part in (high, arrived - high) for step in range(plan.coarse)]
    moved = jnp.dot(jnp.concatenate(steps, axis=0), chosen_ref[...], preferred_element_type=jnp.float32)
    moved = moved.reshape(2, plan.coarse, plan.height, plan.source_count)
    expanded = [base_ref[step] + (moved[0, step] + moved[1, step]) for step in range(plan.coarse)]
    copies = []
    for member in range(plan.own):
        for step in range(plan.coarse):
            start = step * plan.fine
            count = min(plan.fine, LAG_COUNT - start)
            first = member * plan.fine_padded
            out_ref[member, start : start + count, :] = expanded[step][first : first + count]
        copies.append(pltpu.make_async_copy(out_ref.at[member], out_hbm.at[member], sems.at[member]))
        copies[-1].start()
    for copy in copies:
        copy.wait()


def few_channels(plan, traces, valid_flags, source_index):
    vmem = pl.BlockSpec(memory_space=pltpu.VMEM)
    params = pltpu.CompilerParams(vmem_limit_bytes=32 * 1024 * 1024)
    packed_rows = plan.windows * plan.half
    flags = valid_flags.T

    def swap_cores(array):
        return lax.ppermute(array, "src", [(0, 1), (1, 0)])

    def swap_blk(array, hops):
        pairs = [
            (place * plan.src_size + core, (place ^ hops[core]) * plan.src_size + core)
            for place in range(plan.blk_size)
            for core in range(plan.src_size)
        ]
        return lax.ppermute(array, ("blk", "src"), pairs)

    whitened = pl.pallas_call(
        functools.partial(whiten_kernel, plan),
        out_shape=pltpu.VMEM((packed_rows, plan.segment), jnp.bfloat16),
        in_specs=[pl.BlockSpec(memory_space=pl.ANY)] * 2,
        out_specs=vmem,
        scratch_shapes=[
            pltpu.VMEM(traces.shape, jnp.float32),
            pltpu.VMEM(flags.shape, jnp.int32),
            pltpu.SemaphoreType.DMA((2,)),
        ],
        compiler_params=pltpu.CompilerParams(vmem_limit_bytes=60 * 1024 * 1024),
        name="whiten",
    )(traces, flags)

    height = plan.targets * plan.height
    width = plan.windows * plan.span
    rows = pltpu.VMEM((packed_rows, plan.segment), jnp.float32)
    toeplitz = (height, width)
    columns = (plan.half_lanes, width)
    sums = jax.ShapeDtypeStruct((height, LANES), jnp.float32)

    def call(kernel, name, operands, outputs, scratch=()):
        return pl.pallas_call(
            functools.partial(kernel, plan),
            out_shape=outputs,
            in_specs=[vmem] * len(operands),
            out_specs=[vmem] * len(outputs),
            scratch_shapes=scratch,
            compiler_params=params,
            name=name,
        )(*operands)

    across = swap_blk(whitened, (plan.targets, plan.targets))
    order, chosen, same = call(
        choose_kernel,
        "choose",
        (source_index.reshape(1, -1), whitened),
        (
            jax.ShapeDtypeStruct((plan.height, (plan.targets - 1) * plan.rows), jnp.bfloat16),
            jax.ShapeDtypeStruct((LANES, plan.source_count), jnp.bfloat16),
            jax.ShapeDtypeStruct(whitened.shape, whitened.dtype),
        ),
    )
    (total,) = call(
        near_kernel,
        "near",
        (whitened, swap_cores(same)),
        (sums,),
        (rows, pltpu.VMEM(toeplitz, jnp.bfloat16), pltpu.VMEM((2,) + columns, jnp.bfloat16)),
    )
    across_other = swap_cores(across)
    lagged, total = call(
        across_kernel,
        "across",
        (across, total),
        (jax.ShapeDtypeStruct(toeplitz, jnp.bfloat16), sums),
        (rows, pltpu.VMEM(columns, jnp.bfloat16)),
    )
    kept, *sent = call(
        finish_kernel,
        "finish",
        (across_other, lagged, total),
        tuple(
            jax.ShapeDtypeStruct((plan.rows, LANES), jnp.bfloat16 if hop else jnp.float32)
            for hop in range(plan.targets)
        ),
        (pltpu.VMEM(columns, jnp.bfloat16),),
    )
    arrived = [swap_blk(array, hops) for array, hops in zip(sent, HOPS)]
    (base,) = call(
        prepare_kernel,
        "prepare",
        (order, chosen, kept),
        (jax.ShapeDtypeStruct((plan.coarse, plan.height, plan.source_count), jnp.float32),),
    )
    out_shape = (plan.own, LAG_COUNT, plan.source_count)
    return pl.pallas_call(
        functools.partial(expand_kernel, plan),
        out_shape=jax.ShapeDtypeStruct(out_shape, jnp.float32),
        in_specs=[vmem] * (3 + len(arrived)),
        out_specs=pl.BlockSpec(memory_space=pl.ANY),
        scratch_shapes=[pltpu.VMEM(out_shape, jnp.float32), pltpu.SemaphoreType.DMA((plan.own,))],
        compiler_params=params,
        name="expand",
    )(order, chosen, base, *arrived)


def body(traces, valid_flags, source_index):
    plan = Plan(
        traces.shape[0],
        traces.shape[1],
        traces.shape[2],
        lax.axis_size("blk"),
        lax.axis_size("src"),
        source_index.shape[0],
    )
    if plan.fits():
        return few_channels(plan, traces, valid_flags, source_index)
    return many_channels(traces, valid_flags, source_index)


def solution(mesh):
    in_specs = (P(("fibre", "src"), "blk", None), P(("fibre", "src"), "blk"), P())
    out_specs = P(("fibre", "src", "blk"), None, None)
    return jax.shard_map(body, mesh=mesh, in_specs=in_specs, out_specs=out_specs, check_vma=False)
```

```python
import functools
import math

import jax
import jax.numpy as jnp
from jax import lax
from jax.experimental import pallas as pl
from jax.experimental.pallas import tpu as pltpu
from jax.sharding import PartitionSpec as P

MAXLAG = 64
LAG_COUNT = 2 * MAXLAG + 1
LANES = 256
GROUP = 8
HOPS = ((3, 2), (1, 3), (2, 1))


def broadcast(value, axis, source):
    kept = jnp.where(lax.axis_index(axis) == source, value, 0).astype(value.dtype)
    return lax.psum(kept, axis)


def toeplitz_rows(group, lag_count, segment):
    shifted = jnp.stack(
        [group[:, :, lag_step : lag_step + segment] for lag_step in range(lag_count)], axis=1
    )
    return shifted.reshape(group.shape[0] * lag_count, -1)


def many_channels(traces, valid_flags, source_index):
    segment = traces.shape[2]
    centered = traces - jnp.mean(traces, axis=2, keepdims=True)
    mean_power = jnp.mean(centered * centered, axis=2, keepdims=True)
    flag_values = valid_flags[:, :, None].astype(jnp.float32)
    whitened = (centered * lax.rsqrt(mean_power + 1e-05) * flag_values).astype(jnp.bfloat16)
    pieces = []
    for owner in range(lax.axis_size("src")):
        pieces.append(broadcast(whitened, "src", owner))
    everyone = jnp.concatenate(pieces, axis=0)
    sources = jnp.take(everyone, source_index, axis=0)
    source_count = sources.shape[0]
    norm_factor = 1.0 / math.sqrt(traces.shape[1] * lax.axis_size("blk") * segment)
    own_rows = whitened.shape[0] // lax.axis_size("blk")
    flat_sources = sources.reshape(source_count, -1)
    padded = jnp.pad(whitened, ((0, 0), (0, 0), (MAXLAG, MAXLAG)))
    block_rows = math.gcd(lax.axis_size("blk") * own_rows, 16)
    grouped = padded.reshape(
        (lax.axis_size("blk") * own_rows // block_rows, block_rows) + padded.shape[1:]
    )

    def one_block(group):
        toeplitz = toeplitz_rows(group, LAG_COUNT, segment)
        products = lax.dot_general(
            toeplitz, flat_sources, (((1,), (1,)), ((), ())), preferred_element_type=jnp.float32
        )
        return (products * norm_factor).reshape(block_rows, LAG_COUNT, source_count)

    result = lax.map(one_block, grouped)
    return lax.psum_scatter(
        result.reshape(lax.axis_size("blk") * own_rows, LAG_COUNT, source_count),
        "blk",
        scatter_dimension=0,
        tiled=True,
    )


class Plan:
    def __init__(self, half, windows, segment, blk_size, src_size, source_count):
        self.half = half
        self.windows = windows
        self.segment = segment
        self.blk_size = blk_size
        self.src_size = src_size
        self.channels = half * src_size
        self.source_count = source_count
        self.half_lanes = LANES // 2
        self.coarse = self.half_lanes // half
        if self.coarse == 0:
            return
        self.fine = -(-LAG_COUNT // self.coarse)
        self.fine_padded = -(-self.fine // (2 * GROUP)) * 2 * GROUP
        self.own = half // blk_size
        reach = segment + (self.coarse - 1) * self.fine
        self.span = -(-max(reach, segment + 2 * MAXLAG) // 128) * 128
        self.whole_groups = self.fine // GROUP * GROUP
        self.rest = self.fine - self.whole_groups
        rows = self.own * self.fine
        self.rows = -(-rows // 16) * 16
        self.height = self.own * self.fine_padded
        self.targets = blk_size // 2
        self.norm_factor = 1.0 / math.sqrt(windows * blk_size * segment)

    def fits(self):
        return (
            self.coarse >= 2
            and self.src_size == 2
            and self.half % self.blk_size == 0
            and self.half % GROUP == 0
            and self.channels % 16 == 0
            and self.windows * self.half % 16 == 0
            and self.blk_size == 8
        )


def whiten_kernel(plan, traces_hbm, flags_hbm, out_ref, traces_ref, flags_ref, sems):
    copies = [
        pltpu.make_async_copy(traces_hbm, traces_ref, sems.at[0]),
        pltpu.make_async_copy(flags_hbm, flags_ref, sems.at[1]),
    ]
    for copy in copies:
        copy.start()
    for copy in copies:
        copy.wait()
    pieces = []
    for window in range(plan.windows):
        values = traces_ref[:, window, :]
        centered = values - jnp.mean(values, axis=1, keepdims=True)
        mean_power = jnp.mean(centered * centered, axis=1, keepdims=True)
        flag_values = flags_ref[window : window + 1, :].astype(jnp.float32).reshape(plan.half, 1)
        pieces.append(centered * lax.rsqrt(mean_power + 1e-05) * flag_values)
    out_ref[...] = jnp.concatenate(pieces, axis=0).astype(jnp.bfloat16)


def lag_rows(plan, rows_ref, toeplitz_ref):
    span = plan.span
    me = lax.axis_index("blk")
    on_first = lax.axis_index("src") == 0
    hops = [0] + [jnp.where(on_first, *pair) for pair in HOPS]
    filler = jnp.zeros((1, span - plan.segment), jnp.float32)
    for window in range(plan.windows):
        at = slice(window * span, (window + 1) * span)
        for place, hop in enumerate(hops):
            for member in range(plan.own):
                channel = window * plan.half + (me ^ hop) * plan.own + member
                row = jnp.concatenate([rows_ref[pl.ds(channel, 1), :], filler], axis=1)
                row = jnp.broadcast_to(row, (GROUP, span))
                pieces = [
                    pltpu.roll(row, (MAXLAG - plan.fine + 1 + lag) % span, 1, stride=1, stride_axis=0)
                    for lag in range(0, plan.fine_padded, GROUP)
                ]
                first = place * plan.height + member * plan.fine_padded
                toeplitz_ref[first : first + plan.fine_padded, at] = jnp.concatenate(pieces, axis=0).astype(
                    jnp.bfloat16
                )


def half_product(plan, values, toeplitz_ref, columns_ref):
    span = plan.span
    filled = plan.coarse * plan.half
    if filled < plan.half_lanes:
        columns_ref[filled:, :] = jnp.zeros((plan.half_lanes - filled, columns_ref.shape[1]), jnp.bfloat16)
    filler = jnp.zeros((plan.half, span - plan.segment), jnp.float32)
    for window in range(plan.windows):
        at = slice(window * span, (window + 1) * span)
        rows = jnp.concatenate([values[window * plan.half : (window + 1) * plan.half], filler], axis=1)
        for step in range(plan.coarse):
            moved = pltpu.roll(rows, step * plan.fine, 1) if step else rows
            columns_ref[step * plan.half : (step + 1) * plan.half, at] = moved.astype(jnp.bfloat16)
    return lax.dot_general(
        toeplitz_ref[...], columns_ref[...], (((1,), (1,)), ((), ())), preferred_element_type=jnp.float32
    )


def near_kernel(plan, other_ref, toeplitz_ref, prior_ref, sum_ref, columns_ref):
    other = other_ref[...].astype(jnp.float32)
    sum_ref[:, : plan.half_lanes] = prior_ref[...]
    sum_ref[:, plan.half_lanes :] = half_product(plan, other, toeplitz_ref, columns_ref)


def across_kernel(plan, mine_ref, prior_ref, toeplitz_ref, sum_ref, rows_ref, columns_ref):
    rows_ref[...] = mine_ref[...].astype(jnp.float32)
    lag_rows(plan, rows_ref, toeplitz_ref)
    sum_ref[:, : plan.half_lanes] = prior_ref[:, : plan.half_lanes] + half_product(
        plan, rows_ref[...], toeplitz_ref, columns_ref
    )
    sum_ref[:, plan.half_lanes :] = prior_ref[:, plan.half_lanes :]


def finish_kernel(plan, other_ref, toeplitz_ref, prior_ref, *refs):
    *out_refs, columns_ref = refs
    right = prior_ref[:, plan.half_lanes :] + half_product(
        plan, other_ref[...].astype(jnp.float32), toeplitz_ref, columns_ref
    )
    products = jnp.concatenate([prior_ref[:, : plan.half_lanes], right], axis=1)
    products = products.reshape(plan.targets, plan.own, plan.fine_padded, LANES)
    for hop in range(plan.targets):
        part = products[hop]
        pieces = [part[member, : plan.whole_groups] for member in range(plan.own)]
        if plan.rest:
            pieces += [part[member, plan.whole_groups : plan.fine] for member in range(plan.own)]
        if plan.rows > plan.own * plan.fine:
            pieces.append(jnp.zeros((plan.rows - plan.own * plan.fine, LANES), jnp.float32))
        packed = jnp.concatenate(pieces, axis=0)
        out_refs[hop][...] = packed.astype(out_refs[hop].dtype)


def order_matrix(plan):
    at_row = lax.broadcasted_iota(jnp.int32, (plan.rows, plan.rows), 0)
    at_part = lax.broadcasted_iota(jnp.int32, (plan.rows, plan.rows), 1)
    order = jnp.zeros((plan.rows, plan.rows), jnp.bool_)
    for member in range(plan.own):
        reverse = plan.fine - 1 - (at_row - member * plan.fine)
        whole = (reverse >= 0) & (reverse < plan.whole_groups) & (at_part == member * plan.whole_groups + reverse)
        tail = plan.own * plan.whole_groups + member * plan.rest + reverse - plan.whole_groups
        rest = (reverse >= plan.whole_groups) & (reverse < plan.fine) & (at_part == tail)
        order = order | whole | rest
    return order.astype(jnp.float32).astype(jnp.bfloat16)


def spread(plan, values):
    high = values.astype(jnp.bfloat16).astype(jnp.float32)
    low = values - high
    lane = lax.broadcasted_iota(jnp.int32, values.shape, 1)
    lane = jnp.where(lane >= plan.half_lanes, lane - plan.half_lanes, lane)
    up = pltpu.roll(low, plan.half, 1)
    down = pltpu.roll(low, LANES - plan.half, 1)
    pieces = []
    for step in range(plan.coarse):
        beside, moved = (step + 1, up) if step + 1 < plan.coarse else (step - 1, down)
        kept = jnp.where((lane >= step * plan.half) & (lane < (step + 1) * plan.half), high, 0.0)
        there = (lane >= beside * plan.half) & (lane < (beside + 1) * plan.half)
        pieces.append(jnp.where(there, moved, kept).astype(jnp.bfloat16))
    return jnp.concatenate(pieces, axis=0)


def first_kernel(
    plan, index_ref, mine_ref, order_ref, chosen_ref, same_ref, toeplitz_ref, sum_ref, rows_ref, columns_ref
):
    same_ref[...] = mine_ref[...]
    rows_ref[...] = mine_ref[...].astype(jnp.float32)
    lag_rows(plan, rows_ref, toeplitz_ref)
    sum_ref[...] = half_product(plan, rows_ref[...], toeplitz_ref, columns_ref)
    first = lax.axis_index("src") * plan.half
    index = index_ref[...] - first
    index = jnp.where(index < 0, index + plan.channels, index)
    lane = jnp.where(index >= plan.half, index - plan.half + plan.half_lanes, index)
    at_column = lax.broadcasted_iota(jnp.int32, (LANES, plan.source_count), 0)
    chosen = jnp.zeros((LANES, plan.source_count), jnp.bool_)
    for step in range(plan.coarse):
        chosen = chosen | (at_column == lane + step * plan.half)
    chosen_ref[...] = chosen.astype(jnp.float32).astype(jnp.bfloat16)
    order = order_matrix(plan)
    for block in range(plan.targets - 1):
        order_ref[:, block * plan.rows : (block + 1) * plan.rows] = order


def prepare_kernel(plan, order_ref, chosen_ref, kept_ref, base_ref):
    kept = kept_ref[...] * plan.norm_factor
    high = kept.astype(jnp.bfloat16)
    low = (kept - high.astype(jnp.float32)).astype(jnp.bfloat16)
    order = order_ref[:, : plan.rows]
    ordered = sum(jnp.dot(order, part, preferred_element_type=jnp.float32) for part in (high, low))
    base_ref[...] = jnp.dot(spread(plan, ordered), chosen_ref[...], preferred_element_type=jnp.float32)


def expand_kernel(plan, order_ref, chosen_ref, base_ref, *refs):
    *arrived_refs, out_hbm, out_ref, sems = refs
    blocks = jnp.concatenate([ref[...] for ref in arrived_refs], axis=0)
    arrived = jnp.dot(order_ref[...], blocks, preferred_element_type=jnp.float32) * plan.norm_factor
    expanded = base_ref[...] + jnp.dot(spread(plan, arrived), chosen_ref[...], preferred_element_type=jnp.float32)
    copies = []
    for member in range(plan.own):
        for step in range(plan.coarse):
            start = step * plan.fine
            count = min(plan.fine, LAG_COUNT - start)
            first = step * plan.rows + member * plan.fine
            out_ref[member, start : start + count, :] = expanded[first : first + count]
        copies.append(pltpu.make_async_copy(out_ref.at[member], out_hbm.at[member], sems.at[member]))
        copies[-1].start()
    for copy in copies:
        copy.wait()


def few_channels(plan, traces, valid_flags, source_index):
    vmem = pl.BlockSpec(memory_space=pltpu.VMEM)
    params = pltpu.CompilerParams(vmem_limit_bytes=32 * 1024 * 1024)
    packed_rows = plan.windows * plan.half
    flags = valid_flags.T

    def swap_cores(array):
        return lax.ppermute(array, "src", [(0, 1), (1, 0)])

    def swap_blk(array, hops):
        pairs = [
            (place * plan.src_size + core, (place ^ hops[core]) * plan.src_size + core)
            for place in range(plan.blk_size)
            for core in range(plan.src_size)
        ]
        return lax.ppermute(array, ("blk", "src"), pairs)

    whitened = pl.pallas_call(
        functools.partial(whiten_kernel, plan),
        out_shape=pltpu.VMEM((packed_rows, plan.segment), jnp.bfloat16),
        in_specs=[pl.BlockSpec(memory_space=pl.ANY)] * 2,
        out_specs=vmem,
        scratch_shapes=[
            pltpu.VMEM(traces.shape, jnp.float32),
            pltpu.VMEM(flags.shape, jnp.int32),
            pltpu.SemaphoreType.DMA((2,)),
        ],
        compiler_params=pltpu.CompilerParams(vmem_limit_bytes=60 * 1024 * 1024),
        name="whiten",
    )(traces, flags)

    height = plan.targets * plan.height
    width = plan.windows * plan.span
    rows = pltpu.VMEM((packed_rows, plan.segment), jnp.float32)
    toeplitz = (height, width)
    columns = (plan.half_lanes, width)
    sums = jax.ShapeDtypeStruct((height, LANES), jnp.float32)

    def call(kernel, name, operands, outputs, scratch=()):
        return pl.pallas_call(
            functools.partial(kernel, plan),
            out_shape=outputs,
            in_specs=[vmem] * len(operands),
            out_specs=[vmem] * len(outputs),
            scratch_shapes=scratch,
            compiler_params=params,
            name=name,
        )(*operands)

    across = swap_blk(whitened, (plan.targets, plan.targets))
    order, chosen, same, lagged, total = call(
        first_kernel,
        "first",
        (source_index.reshape(1, -1), whitened),
        (
            jax.ShapeDtypeStruct((plan.rows, (plan.targets - 1) * plan.rows), jnp.bfloat16),
            jax.ShapeDtypeStruct((LANES, plan.source_count), jnp.bfloat16),
            jax.ShapeDtypeStruct(whitened.shape, whitened.dtype),
            jax.ShapeDtypeStruct(toeplitz, jnp.bfloat16),
            jax.ShapeDtypeStruct((height, plan.half_lanes), jnp.float32),
        ),
        (rows, pltpu.VMEM(columns, jnp.bfloat16)),
    )
    (total,) = call(
        near_kernel, "near", (swap_cores(same), lagged, total), (sums,), (pltpu.VMEM(columns, jnp.bfloat16),)
    )
    across_other = swap_cores(across)
    lagged, total = call(
        across_kernel,
        "across",
        (across, total),
        (jax.ShapeDtypeStruct(toeplitz, jnp.bfloat16), sums),
        (rows, pltpu.VMEM(columns, jnp.bfloat16)),
    )
    kept, *sent = call(
        finish_kernel,
        "finish",
        (across_other, lagged, total),
        tuple(
            jax.ShapeDtypeStruct((plan.rows, LANES), jnp.bfloat16 if hop else jnp.float32)
            for hop in range(plan.targets)
        ),
        (pltpu.VMEM(columns, jnp.bfloat16),),
    )
    arrived = [swap_blk(array, hops) for array, hops in zip(sent, HOPS)]
    (base,) = call(
        prepare_kernel,
        "prepare",
        (order, chosen, kept),
        (jax.ShapeDtypeStruct((plan.coarse * plan.rows, plan.source_count), jnp.float32),),
    )
    out_shape = (plan.own, LAG_COUNT, plan.source_count)
    return pl.pallas_call(
        functools.partial(expand_kernel, plan),
        out_shape=jax.ShapeDtypeStruct(out_shape, jnp.float32),
        in_specs=[vmem] * (3 + len(arrived)),
        out_specs=pl.BlockSpec(memory_space=pl.ANY),
        scratch_shapes=[pltpu.VMEM(out_shape, jnp.float32), pltpu.SemaphoreType.DMA((plan.own,))],
        compiler_params=params,
        name="expand",
    )(order, chosen, base, *arrived)


def body(traces, valid_flags, source_index):
    plan = Plan(
        traces.shape[0],
        traces.shape[1],
        traces.shape[2],
        lax.axis_size("blk"),
        lax.axis_size("src"),
        source_index.shape[0],
    )
    if plan.fits():
        return few_channels(plan, traces, valid_flags, source_index)
    return many_channels(traces, valid_flags, source_index)


def solution(mesh):
    in_specs = (P(("fibre", "src"), "blk", None), P(("fibre", "src"), "blk"), P())
    out_specs = P(("fibre", "src", "blk"), None, None)
    return jax.shard_map(body, mesh=mesh, in_specs=in_specs, out_specs=out_specs, check_vma=False)
```

```python
import functools
import math

import jax
import jax.numpy as jnp
from jax import lax
from jax.experimental import pallas as pl
from jax.experimental.pallas import tpu as pltpu
from jax.sharding import PartitionSpec as P

MAXLAG = 64
LAG_COUNT = 2 * MAXLAG + 1
LANES = 256
GROUP = 8
FIRST_HOP = (1, 2)
SECOND_HOP = (2, 1)
BOTH_HOPS = (3, 3)
ARRIVALS = 2
TARGETS = (SECOND_HOP, BOTH_HOPS, FIRST_HOP)


def broadcast(value, axis, source):
    kept = jnp.where(lax.axis_index(axis) == source, value, 0).astype(value.dtype)
    return lax.psum(kept, axis)


def toeplitz_rows(group, lag_count, segment):
    shifted = jnp.stack(
        [group[:, :, lag_step : lag_step + segment] for lag_step in range(lag_count)], axis=1
    )
    return shifted.reshape(group.shape[0] * lag_count, -1)


def many_channels(traces, valid_flags, source_index):
    segment = traces.shape[2]
    centered = traces - jnp.mean(traces, axis=2, keepdims=True)
    mean_power = jnp.mean(centered * centered, axis=2, keepdims=True)
    flag_values = valid_flags[:, :, None].astype(jnp.float32)
    whitened = (centered * lax.rsqrt(mean_power + 1e-05) * flag_values).astype(jnp.bfloat16)
    pieces = []
    for owner in range(lax.axis_size("src")):
        pieces.append(broadcast(whitened, "src", owner))
    everyone = jnp.concatenate(pieces, axis=0)
    sources = jnp.take(everyone, source_index, axis=0)
    source_count = sources.shape[0]
    norm_factor = 1.0 / math.sqrt(traces.shape[1] * lax.axis_size("blk") * segment)
    own_rows = whitened.shape[0] // lax.axis_size("blk")
    flat_sources = sources.reshape(source_count, -1)
    padded = jnp.pad(whitened, ((0, 0), (0, 0), (MAXLAG, MAXLAG)))
    block_rows = math.gcd(lax.axis_size("blk") * own_rows, 16)
    grouped = padded.reshape(
        (lax.axis_size("blk") * own_rows // block_rows, block_rows) + padded.shape[1:]
    )

    def one_block(group):
        toeplitz = toeplitz_rows(group, LAG_COUNT, segment)
        products = lax.dot_general(
            toeplitz, flat_sources, (((1,), (1,)), ((), ())), preferred_element_type=jnp.float32
        )
        return (products * norm_factor).reshape(block_rows, LAG_COUNT, source_count)

    result = lax.map(one_block, grouped)
    return lax.psum_scatter(
        result.reshape(lax.axis_size("blk") * own_rows, LAG_COUNT, source_count),
        "blk",
        scatter_dimension=0,
        tiled=True,
    )


class Plan:
    def __init__(self, half, windows, segment, blk_size, src_size, source_count):
        self.half = half
        self.windows = windows
        self.segment = segment
        self.blk_size = blk_size
        self.src_size = src_size
        self.channels = half * src_size
        self.source_count = source_count
        self.half_lanes = LANES // 2
        self.coarse = self.half_lanes // half
        if self.coarse == 0:
            return
        self.fine = -(-LAG_COUNT // self.coarse)
        self.fine_padded = -(-self.fine // (2 * GROUP)) * 2 * GROUP
        self.own = half // blk_size
        reach = segment + (self.coarse - 1) * self.fine
        self.span = -(-max(reach, segment + 2 * MAXLAG) // 128) * 128
        self.whole_groups = self.fine // GROUP * GROUP
        self.rest = self.fine - self.whole_groups
        rows = self.own * self.fine
        self.rows = -(-rows // 16) * 16
        self.height = self.own * self.fine_padded
        self.targets = blk_size // 2
        self.norm_factor = 1.0 / math.sqrt(windows * blk_size * segment)

    def fits(self):
        return (
            self.coarse >= 2
            and self.src_size == 2
            and self.half % self.blk_size == 0
            and self.half % GROUP == 0
            and self.channels % 16 == 0
            and self.windows * self.half % 16 == 0
            and self.blk_size == 8
        )


def whiten_kernel(plan, traces_hbm, flags_hbm, out_ref, traces_ref, flags_ref, sems):
    copies = [
        pltpu.make_async_copy(traces_hbm, traces_ref, sems.at[0]),
        pltpu.make_async_copy(flags_hbm, flags_ref, sems.at[1]),
    ]
    for copy in copies:
        copy.start()
    for copy in copies:
        copy.wait()
    pieces = []
    for window in range(plan.windows):
        values = traces_ref[:, window, :]
        centered = values - jnp.mean(values, axis=1, keepdims=True)
        mean_power = jnp.mean(centered * centered, axis=1, keepdims=True)
        flag_values = flags_ref[window : window + 1, :].astype(jnp.float32).reshape(plan.half, 1)
        pieces.append(centered * lax.rsqrt(mean_power + 1e-05) * flag_values)
    out_ref[...] = jnp.concatenate(pieces, axis=0).astype(jnp.bfloat16)


def lag_rows(plan, rows_ref, toeplitz_ref):
    span = plan.span
    me = lax.axis_index("blk")
    on_first = lax.axis_index("src") == 0
    hops = [0] + [jnp.where(on_first, *pair) for pair in TARGETS]
    filler = jnp.zeros((1, span - plan.segment), jnp.float32)
    for window in range(plan.windows):
        at = slice(window * span, (window + 1) * span)
        for place, hop in enumerate(hops):
            for member in range(plan.own):
                channel = window * plan.half + (me ^ hop) * plan.own + member
                row = jnp.concatenate([rows_ref[pl.ds(channel, 1), :], filler], axis=1)
                row = jnp.broadcast_to(row, (GROUP, span))
                pieces = [
                    pltpu.roll(row, (MAXLAG - plan.fine + 1 + lag) % span, 1, stride=1, stride_axis=0)
                    for lag in range(0, plan.fine_padded, GROUP)
                ]
                first = place * plan.height + member * plan.fine_padded
                toeplitz_ref[first : first + plan.fine_padded, at] = jnp.concatenate(pieces, axis=0).astype(
                    jnp.bfloat16
                )


def half_product(plan, values, toeplitz_ref, columns_ref):
    span = plan.span
    filled = plan.coarse * plan.half
    if filled < plan.half_lanes:
        columns_ref[filled:, :] = jnp.zeros((plan.half_lanes - filled, columns_ref.shape[1]), jnp.bfloat16)
    filler = jnp.zeros((plan.half, span - plan.segment), jnp.float32)
    for window in range(plan.windows):
        at = slice(window * span, (window + 1) * span)
        rows = jnp.concatenate([values[window * plan.half : (window + 1) * plan.half], filler], axis=1)
        for step in range(plan.coarse):
            moved = pltpu.roll(rows, step * plan.fine, 1) if step else rows
            columns_ref[step * plan.half : (step + 1) * plan.half, at] = moved.astype(jnp.bfloat16)
    return lax.dot_general(
        toeplitz_ref[...], columns_ref[...], (((1,), (1,)), ((), ())), preferred_element_type=jnp.float32
    )


def near_kernel(plan, other_ref, toeplitz_ref, prior_ref, sum_ref, columns_ref):
    other = other_ref[...].astype(jnp.float32)
    sum_ref[:, : plan.half_lanes] = prior_ref[...]
    sum_ref[:, plan.half_lanes :] = half_product(plan, other, toeplitz_ref, columns_ref)


def across_kernel(plan, mine_ref, prior_ref, toeplitz_ref, sum_ref, rows_ref, columns_ref):
    rows_ref[...] = mine_ref[...].astype(jnp.float32)
    lag_rows(plan, rows_ref, toeplitz_ref)
    sum_ref[:, : plan.half_lanes] = prior_ref[:, : plan.half_lanes] + half_product(
        plan, rows_ref[...], toeplitz_ref, columns_ref
    )
    sum_ref[:, plan.half_lanes :] = prior_ref[:, plan.half_lanes :]


def finish_kernel(plan, other_ref, toeplitz_ref, prior_ref, *refs):
    *out_refs, columns_ref = refs
    right = prior_ref[:, plan.half_lanes :] + half_product(
        plan, other_ref[...].astype(jnp.float32), toeplitz_ref, columns_ref
    )
    products = jnp.concatenate([prior_ref[:, : plan.half_lanes], right], axis=1)
    products = products.reshape(plan.targets, plan.own, plan.fine_padded, LANES)
    for hop in range(plan.targets):
        part = products[hop]
        pieces = [part[member, : plan.whole_groups] for member in range(plan.own)]
        if plan.rest:
            pieces += [part[member, plan.whole_groups : plan.fine] for member in range(plan.own)]
        if plan.rows > plan.own * plan.fine:
            pieces.append(jnp.zeros((plan.rows - plan.own * plan.fine, LANES), jnp.float32))
        packed = jnp.concatenate(pieces, axis=0)
        out_refs[hop][...] = packed.astype(out_refs[hop].dtype)


def complete_kernel(plan, part_ref, passed_ref, out_ref):
    out_ref[...] = (part_ref[...] + passed_ref[...].astype(jnp.float32)).astype(jnp.bfloat16)


def order_matrix(plan):
    at_row = lax.broadcasted_iota(jnp.int32, (plan.rows, plan.rows), 0)
    at_part = lax.broadcasted_iota(jnp.int32, (plan.rows, plan.rows), 1)
    order = jnp.zeros((plan.rows, plan.rows), jnp.bool_)
    for member in range(plan.own):
        reverse = plan.fine - 1 - (at_row - member * plan.fine)
        whole = (reverse >= 0) & (reverse < plan.whole_groups) & (at_part == member * plan.whole_groups + reverse)
        tail = plan.own * plan.whole_groups + member * plan.rest + reverse - plan.whole_groups
        rest = (reverse >= plan.whole_groups) & (reverse < plan.fine) & (at_part == tail)
        order = order | whole | rest
    return order.astype(jnp.float32).astype(jnp.bfloat16)


def spread(plan, values):
    high = values.astype(jnp.bfloat16).astype(jnp.float32)
    low = values - high
    lane = lax.broadcasted_iota(jnp.int32, values.shape, 1)
    lane = jnp.where(lane >= plan.half_lanes, lane - plan.half_lanes, lane)
    up = pltpu.roll(low, plan.half, 1)
    down = pltpu.roll(low, LANES - plan.half, 1)
    pieces = []
    for step in range(plan.coarse):
        beside, moved = (step + 1, up) if step + 1 < plan.coarse else (step - 1, down)
        kept = jnp.where((lane >= step * plan.half) & (lane < (step + 1) * plan.half), high, 0.0)
        there = (lane >= beside * plan.half) & (lane < (beside + 1) * plan.half)
        pieces.append(jnp.where(there, moved, kept).astype(jnp.bfloat16))
    return jnp.concatenate(pieces, axis=0)


def first_kernel(
    plan, index_ref, mine_ref, order_ref, chosen_ref, same_ref, toeplitz_ref, sum_ref, rows_ref, columns_ref
):
    same_ref[...] = mine_ref[...]
    rows_ref[...] = mine_ref[...].astype(jnp.float32)
    lag_rows(plan, rows_ref, toeplitz_ref)
    sum_ref[...] = half_product(plan, rows_ref[...], toeplitz_ref, columns_ref)
    first = lax.axis_index("src") * plan.half
    index = index_ref[...] - first
    index = jnp.where(index < 0, index + plan.channels, index)
    lane = jnp.where(index >= plan.half, index - plan.half + plan.half_lanes, index)
    at_column = lax.broadcasted_iota(jnp.int32, (LANES, plan.source_count), 0)
    chosen = jnp.zeros((LANES, plan.source_count), jnp.bool_)
    for step in range(plan.coarse):
        chosen = chosen | (at_column == lane + step * plan.half)
    chosen_ref[...] = chosen.astype(jnp.float32).astype(jnp.bfloat16)
    order = order_matrix(plan)
    for block in range(ARRIVALS):
        order_ref[:, block * plan.rows : (block + 1) * plan.rows] = order


def prepare_kernel(plan, order_ref, chosen_ref, kept_ref, base_ref):
    kept = kept_ref[...] * plan.norm_factor
    high = kept.astype(jnp.bfloat16)
    low = (kept - high.astype(jnp.float32)).astype(jnp.bfloat16)
    order = order_ref[:, : plan.rows]
    ordered = sum(jnp.dot(order, part, preferred_element_type=jnp.float32) for part in (high, low))
    base_ref[...] = jnp.dot(spread(plan, ordered), chosen_ref[...], preferred_element_type=jnp.float32)


def expand_kernel(plan, order_ref, chosen_ref, base_ref, *refs):
    *arrived_refs, out_hbm, out_ref, sems = refs
    blocks = jnp.concatenate([ref[...] for ref in arrived_refs], axis=0)
    arrived = jnp.dot(order_ref[...], blocks, preferred_element_type=jnp.float32) * plan.norm_factor
    expanded = base_ref[...] + jnp.dot(spread(plan, arrived), chosen_ref[...], preferred_element_type=jnp.float32)
    copies = []
    for member in range(plan.own):
        for step in range(plan.coarse):
            start = step * plan.fine
            count = min(plan.fine, LAG_COUNT - start)
            first = step * plan.rows + member * plan.fine
            out_ref[member, start : start + count, :] = expanded[first : first + count]
        copies.append(pltpu.make_async_copy(out_ref.at[member], out_hbm.at[member], sems.at[member]))
        copies[-1].start()
    for copy in copies:
        copy.wait()


def few_channels(plan, traces, valid_flags, source_index):
    vmem = pl.BlockSpec(memory_space=pltpu.VMEM)
    params = pltpu.CompilerParams(vmem_limit_bytes=32 * 1024 * 1024)
    packed_rows = plan.windows * plan.half
    flags = valid_flags.T

    def swap_cores(array):
        return lax.ppermute(array, "src", [(0, 1), (1, 0)])

    def swap_blk(array, hops):
        pairs = [
            (place * plan.src_size + core, (place ^ hops[core]) * plan.src_size + core)
            for place in range(plan.blk_size)
            for core in range(plan.src_size)
        ]
        return lax.ppermute(array, ("blk", "src"), pairs)

    whitened = pl.pallas_call(
        functools.partial(whiten_kernel, plan),
        out_shape=pltpu.VMEM((packed_rows, plan.segment), jnp.bfloat16),
        in_specs=[pl.BlockSpec(memory_space=pl.ANY)] * 2,
        out_specs=vmem,
        scratch_shapes=[
            pltpu.VMEM(traces.shape, jnp.float32),
            pltpu.VMEM(flags.shape, jnp.int32),
            pltpu.SemaphoreType.DMA((2,)),
        ],
        compiler_params=pltpu.CompilerParams(vmem_limit_bytes=60 * 1024 * 1024),
        name="whiten",
    )(traces, flags)

    height = plan.targets * plan.height
    width = plan.windows * plan.span
    rows = pltpu.VMEM((packed_rows, plan.segment), jnp.float32)
    toeplitz = (height, width)
    columns = (plan.half_lanes, width)
    sums = jax.ShapeDtypeStruct((height, LANES), jnp.float32)

    def call(kernel, name, operands, outputs, scratch=()):
        return pl.pallas_call(
            functools.partial(kernel, plan),
            out_shape=outputs,
            in_specs=[vmem] * len(operands),
            out_specs=[vmem] * len(outputs),
            scratch_shapes=scratch,
            compiler_params=params,
            name=name,
        )(*operands)

    across = swap_blk(whitened, (plan.targets, plan.targets))
    order, chosen, same, lagged, total = call(
        first_kernel,
        "first",
        (source_index.reshape(1, -1), whitened),
        (
            jax.ShapeDtypeStruct((plan.rows, ARRIVALS * plan.rows), jnp.bfloat16),
            jax.ShapeDtypeStruct((LANES, plan.source_count), jnp.bfloat16),
            jax.ShapeDtypeStruct(whitened.shape, whitened.dtype),
            jax.ShapeDtypeStruct(toeplitz, jnp.bfloat16),
            jax.ShapeDtypeStruct((height, plan.half_lanes), jnp.float32),
        ),
        (rows, pltpu.VMEM(columns, jnp.bfloat16)),
    )
    (total,) = call(
        near_kernel, "near", (swap_cores(same), lagged, total), (sums,), (pltpu.VMEM(columns, jnp.bfloat16),)
    )
    across_other = swap_cores(across)
    lagged, total = call(
        across_kernel,
        "across",
        (across, total),
        (jax.ShapeDtypeStruct(toeplitz, jnp.bfloat16), sums),
        (rows, pltpu.VMEM(columns, jnp.bfloat16)),
    )
    kept, *sent = call(
        finish_kernel,
        "finish",
        (across_other, lagged, total),
        tuple(
            jax.ShapeDtypeStruct((plan.rows, LANES), dtype)
            for dtype in (jnp.float32, jnp.float32, jnp.bfloat16, jnp.bfloat16)
        ),
        (pltpu.VMEM(columns, jnp.bfloat16),),
    )
    to_complete, to_pass_on, first_sent = sent
    passed_on = swap_blk(to_pass_on, FIRST_HOP)
    first_arrived = swap_blk(first_sent, FIRST_HOP)
    (completed,) = call(
        complete_kernel, "complete", (to_complete, passed_on), (jax.ShapeDtypeStruct(passed_on.shape, jnp.bfloat16),)
    )
    arrived = [first_arrived, swap_blk(completed, SECOND_HOP)]
    (base,) = call(
        prepare_kernel,
        "prepare",
        (order, chosen, kept),
        (jax.ShapeDtypeStruct((plan.coarse * plan.rows, plan.source_count), jnp.float32),),
    )
    out_shape = (plan.own, LAG_COUNT, plan.source_count)
    return pl.pallas_call(
        functools.partial(expand_kernel, plan),
        out_shape=jax.ShapeDtypeStruct(out_shape, jnp.float32),
        in_specs=[vmem] * (3 + len(arrived)),
        out_specs=pl.BlockSpec(memory_space=pl.ANY),
        scratch_shapes=[pltpu.VMEM(out_shape, jnp.float32), pltpu.SemaphoreType.DMA((plan.own,))],
        compiler_params=params,
        name="expand",
    )(order, chosen, base, *arrived)


def body(traces, valid_flags, source_index):
    plan = Plan(
        traces.shape[0],
        traces.shape[1],
        traces.shape[2],
        lax.axis_size("blk"),
        lax.axis_size("src"),
        source_index.shape[0],
    )
    if plan.fits():
        return few_channels(plan, traces, valid_flags, source_index)
    return many_channels(traces, valid_flags, source_index)


def solution(mesh):
    in_specs = (P(("fibre", "src"), "blk", None), P(("fibre", "src"), "blk"), P())
    out_specs = P(("fibre", "src", "blk"), None, None)
    return jax.shard_map(body, mesh=mesh, in_specs=in_specs, out_specs=out_specs, check_vma=False)
```

```python
import functools
import math

import jax
import jax.numpy as jnp
from jax import lax
from jax.experimental import pallas as pl
from jax.experimental.pallas import tpu as pltpu
from jax.sharding import PartitionSpec as P

MAXLAG = 64
LAG_COUNT = 2 * MAXLAG + 1
LANES = 256
GROUP = 8
HOPS = ((3, 2), (1, 3), (2, 1))


def broadcast(value, axis, source):
    kept = jnp.where(lax.axis_index(axis) == source, value, 0).astype(value.dtype)
    return lax.psum(kept, axis)


def toeplitz_rows(group, lag_count, segment):
    shifted = jnp.stack(
        [group[:, :, lag_step : lag_step + segment] for lag_step in range(lag_count)], axis=1
    )
    return shifted.reshape(group.shape[0] * lag_count, -1)


def many_channels(traces, valid_flags, source_index):
    segment = traces.shape[2]
    centered = traces - jnp.mean(traces, axis=2, keepdims=True)
    mean_power = jnp.mean(centered * centered, axis=2, keepdims=True)
    flag_values = valid_flags[:, :, None].astype(jnp.float32)
    whitened = (centered * lax.rsqrt(mean_power + 1e-05) * flag_values).astype(jnp.bfloat16)
    pieces = []
    for owner in range(lax.axis_size("src")):
        pieces.append(broadcast(whitened, "src", owner))
    everyone = jnp.concatenate(pieces, axis=0)
    sources = jnp.take(everyone, source_index, axis=0)
    source_count = sources.shape[0]
    norm_factor = 1.0 / math.sqrt(traces.shape[1] * lax.axis_size("blk") * segment)
    own_rows = whitened.shape[0] // lax.axis_size("blk")
    flat_sources = sources.reshape(source_count, -1)
    padded = jnp.pad(whitened, ((0, 0), (0, 0), (MAXLAG, MAXLAG)))
    block_rows = math.gcd(lax.axis_size("blk") * own_rows, 16)
    grouped = padded.reshape(
        (lax.axis_size("blk") * own_rows // block_rows, block_rows) + padded.shape[1:]
    )

    def one_block(group):
        toeplitz = toeplitz_rows(group, LAG_COUNT, segment)
        products = lax.dot_general(
            toeplitz, flat_sources, (((1,), (1,)), ((), ())), preferred_element_type=jnp.float32
        )
        return (products * norm_factor).reshape(block_rows, LAG_COUNT, source_count)

    result = lax.map(one_block, grouped)
    return lax.psum_scatter(
        result.reshape(lax.axis_size("blk") * own_rows, LAG_COUNT, source_count),
        "blk",
        scatter_dimension=0,
        tiled=True,
    )


class Plan:
    def __init__(self, half, windows, segment, blk_size, src_size, source_count):
        self.half = half
        self.windows = windows
        self.segment = segment
        self.blk_size = blk_size
        self.src_size = src_size
        self.channels = half * src_size
        self.source_count = source_count
        self.half_lanes = LANES // 2
        self.coarse = self.half_lanes // half
        if self.coarse == 0:
            return
        self.fine = -(-LAG_COUNT // self.coarse)
        self.fine_padded = -(-self.fine // (2 * GROUP)) * 2 * GROUP
        self.own = half // blk_size
        reach = segment + (self.coarse - 1) * self.fine
        self.span = -(-max(reach, segment + 2 * MAXLAG) // 128) * 128
        self.whole_groups = self.fine // GROUP * GROUP
        self.rest = self.fine - self.whole_groups
        rows = self.own * self.fine
        self.rows = -(-rows // 16) * 16
        self.height = self.own * self.fine_padded
        self.targets = blk_size // 2
        self.norm_factor = 1.0 / math.sqrt(windows * blk_size * segment)

    def fits(self):
        return (
            self.coarse >= 2
            and self.src_size == 2
            and self.half % self.blk_size == 0
            and self.half % GROUP == 0
            and self.channels % 16 == 0
            and self.windows * self.half % 16 == 0
            and self.blk_size == 8
        )


def whiten_kernel(plan, traces_hbm, flags_hbm, *refs):
    *out_refs, traces_ref, flags_ref, sems = refs
    copies = [
        pltpu.make_async_copy(traces_hbm, traces_ref, sems.at[0]),
        pltpu.make_async_copy(flags_hbm, flags_ref, sems.at[1]),
    ]
    for copy in copies:
        copy.start()
    for copy in copies:
        copy.wait()
    for window in range(plan.windows):
        values = traces_ref[:, window, :]
        centered = values - jnp.mean(values, axis=1, keepdims=True)
        mean_power = jnp.mean(centered * centered, axis=1, keepdims=True)
        flag_values = flags_ref[window : window + 1, :].astype(jnp.float32).reshape(plan.half, 1)
        out_refs[window][...] = (centered * lax.rsqrt(mean_power + 1e-05) * flag_values).astype(jnp.bfloat16)


def lag_rows(plan, rows_ref, toeplitz_ref):
    span = plan.span
    me = lax.axis_index("blk")
    on_first = lax.axis_index("src") == 0
    hops = [0] + [jnp.where(on_first, *pair) for pair in HOPS]
    filler = jnp.zeros((1, span - plan.segment), jnp.float32)
    for window in range(plan.windows):
        at = slice(window * span, (window + 1) * span)
        for place, hop in enumerate(hops):
            for member in range(plan.own):
                channel = window * plan.half + (me ^ hop) * plan.own + member
                row = jnp.concatenate([rows_ref[pl.ds(channel, 1), :], filler], axis=1)
                row = jnp.broadcast_to(row, (GROUP, span))
                pieces = [
                    pltpu.roll(row, (MAXLAG - plan.fine + 1 + lag) % span, 1, stride=1, stride_axis=0)
                    for lag in range(0, plan.fine_padded, GROUP)
                ]
                first = place * plan.height + member * plan.fine_padded
                toeplitz_ref[first : first + plan.fine_padded, at] = jnp.concatenate(pieces, axis=0).astype(
                    jnp.bfloat16
                )


def half_product(plan, values, toeplitz_ref, columns_ref):
    span = plan.span
    filled = plan.coarse * plan.half
    if filled < plan.half_lanes:
        columns_ref[filled:, :] = jnp.zeros((plan.half_lanes - filled, columns_ref.shape[1]), jnp.bfloat16)
    filler = jnp.zeros((plan.half, span - plan.segment), jnp.float32)
    for window in range(plan.windows):
        at = slice(window * span, (window + 1) * span)
        rows = jnp.concatenate([values[window].astype(jnp.float32), filler], axis=1)
        for step in range(plan.coarse):
            moved = pltpu.roll(rows, step * plan.fine, 1) if step else rows
            columns_ref[step * plan.half : (step + 1) * plan.half, at] = moved.astype(jnp.bfloat16)
    return lax.dot_general(
        toeplitz_ref[...], columns_ref[...], (((1,), (1,)), ((), ())), preferred_element_type=jnp.float32
    )


def load_rows(plan, refs, rows_ref):
    values = [ref[...].astype(jnp.float32) for ref in refs]
    for window, array in enumerate(values):
        rows_ref[window * plan.half : (window + 1) * plan.half, :] = array
    return values


def near_kernel(plan, other_ref, toeplitz_ref, sum_ref, columns_ref):
    packed = other_ref[...].astype(jnp.float32)
    other = [packed[window * plan.half : (window + 1) * plan.half] for window in range(plan.windows)]
    sum_ref[...] = half_product(plan, other, toeplitz_ref, columns_ref)


def across_kernel(plan, *refs):
    mine_refs, (prior_ref, toeplitz_ref, sum_ref, rows_ref, columns_ref) = refs[: plan.windows], refs[plan.windows :]
    mine = load_rows(plan, mine_refs, rows_ref)
    lag_rows(plan, rows_ref, toeplitz_ref)
    sum_ref[...] = prior_ref[...] + half_product(plan, mine, toeplitz_ref, columns_ref)


def finish_kernel(plan, *refs):
    other_refs, refs = refs[: plan.windows], refs[plan.windows :]
    toeplitz_ref, left_ref, right_ref, *out_refs, columns_ref = refs
    right = right_ref[...] + half_product(plan, [ref[...] for ref in other_refs], toeplitz_ref, columns_ref)
    products = jnp.concatenate([left_ref[...], right], axis=1)
    products = products.reshape(plan.targets, plan.own, plan.fine_padded, LANES)
    for hop in range(plan.targets):
        part = products[hop]
        pieces = [part[member, : plan.whole_groups] for member in range(plan.own)]
        if plan.rest:
            pieces += [part[member, plan.whole_groups : plan.fine] for member in range(plan.own)]
        if plan.rows > plan.own * plan.fine:
            pieces.append(jnp.zeros((plan.rows - plan.own * plan.fine, LANES), jnp.float32))
        packed = jnp.concatenate(pieces, axis=0)
        out_refs[hop][...] = packed.astype(out_refs[hop].dtype)


def order_matrix(plan):
    at_row = lax.broadcasted_iota(jnp.int32, (plan.rows, plan.rows), 0)
    at_part = lax.broadcasted_iota(jnp.int32, (plan.rows, plan.rows), 1)
    order = jnp.zeros((plan.rows, plan.rows), jnp.bool_)
    for member in range(plan.own):
        reverse = plan.fine - 1 - (at_row - member * plan.fine)
        whole = (reverse >= 0) & (reverse < plan.whole_groups) & (at_part == member * plan.whole_groups + reverse)
        tail = plan.own * plan.whole_groups + member * plan.rest + reverse - plan.whole_groups
        rest = (reverse >= plan.whole_groups) & (reverse < plan.fine) & (at_part == tail)
        order = order | whole | rest
    return order.astype(jnp.float32).astype(jnp.bfloat16)


def spread(plan, values):
    high = values.astype(jnp.bfloat16).astype(jnp.float32)
    low = values - high
    lane = lax.broadcasted_iota(jnp.int32, values.shape, 1)
    lane = jnp.where(lane >= plan.half_lanes, lane - plan.half_lanes, lane)
    up = pltpu.roll(low, plan.half, 1)
    down = pltpu.roll(low, LANES - plan.half, 1)
    pieces = []
    for step in range(plan.coarse):
        beside, moved = (step + 1, up) if step + 1 < plan.coarse else (step - 1, down)
        kept = jnp.where((lane >= step * plan.half) & (lane < (step + 1) * plan.half), high, 0.0)
        there = (lane >= beside * plan.half) & (lane < (beside + 1) * plan.half)
        pieces.append(jnp.where(there, moved, kept).astype(jnp.bfloat16))
    return jnp.concatenate(pieces, axis=0)


def first_kernel(plan, index_ref, *refs):
    mine_refs, refs = refs[: plan.windows], refs[plan.windows :]
    order_ref, chosen_ref, same_ref, toeplitz_ref, sum_ref, rows_ref, columns_ref = refs
    mine = load_rows(plan, mine_refs, rows_ref)
    same_ref[...] = rows_ref[...].astype(jnp.bfloat16)
    lag_rows(plan, rows_ref, toeplitz_ref)
    sum_ref[...] = half_product(plan, mine, toeplitz_ref, columns_ref)
    first = lax.axis_index("src") * plan.half
    index = index_ref[...] - first
    index = jnp.where(index < 0, index + plan.channels, index)
    lane = jnp.where(index >= plan.half, index - plan.half + plan.half_lanes, index)
    at_column = lax.broadcasted_iota(jnp.int32, (LANES, plan.source_count), 0)
    chosen = jnp.zeros((LANES, plan.source_count), jnp.bool_)
    for step in range(plan.coarse):
        chosen = chosen | (at_column == lane + step * plan.half)
    chosen_ref[...] = chosen.astype(jnp.float32).astype(jnp.bfloat16)
    order = order_matrix(plan)
    for block in range(plan.targets - 1):
        order_ref[:, block * plan.rows : (block + 1) * plan.rows] = order


def prepare_kernel(plan, order_ref, chosen_ref, kept_ref, base_ref):
    kept = kept_ref[...] * plan.norm_factor
    high = kept.astype(jnp.bfloat16)
    low = (kept - high.astype(jnp.float32)).astype(jnp.bfloat16)
    order = order_ref[:, : plan.rows]
    ordered = sum(jnp.dot(order, part, preferred_element_type=jnp.float32) for part in (high, low))
    base_ref[...] = jnp.dot(spread(plan, ordered), chosen_ref[...], preferred_element_type=jnp.float32)


def expand_kernel(plan, order_ref, chosen_ref, base_ref, *refs):
    *arrived_refs, out_hbm, out_ref, sems = refs
    blocks = jnp.concatenate([ref[...] for ref in arrived_refs], axis=0)
    arrived = jnp.dot(order_ref[...], blocks, preferred_element_type=jnp.float32) * plan.norm_factor
    expanded = base_ref[...] + jnp.dot(spread(plan, arrived), chosen_ref[...], preferred_element_type=jnp.float32)
    copies = []
    for member in range(plan.own):
        for step in range(plan.coarse):
            start = step * plan.fine
            count = min(plan.fine, LAG_COUNT - start)
            first = step * plan.rows + member * plan.fine
            out_ref[member, start : start + count, :] = expanded[first : first + count]
        copies.append(pltpu.make_async_copy(out_ref.at[member], out_hbm.at[member], sems.at[member]))
        copies[-1].start()
    for copy in copies:
        copy.wait()


def few_channels(plan, traces, valid_flags, source_index):
    vmem = pl.BlockSpec(memory_space=pltpu.VMEM)
    params = pltpu.CompilerParams(vmem_limit_bytes=32 * 1024 * 1024)
    packed_rows = plan.windows * plan.half
    flags = valid_flags.T

    def swap_cores(array):
        return lax.ppermute(array, "src", [(0, 1), (1, 0)])

    def swap_blk(array, hops):
        pairs = [
            (place * plan.src_size + core, (place ^ hops[core]) * plan.src_size + core)
            for place in range(plan.blk_size)
            for core in range(plan.src_size)
        ]
        return lax.ppermute(array, ("blk", "src"), pairs)

    whitened = pl.pallas_call(
        functools.partial(whiten_kernel, plan),
        out_shape=[pltpu.VMEM((plan.half, plan.segment), jnp.bfloat16)] * plan.windows,
        in_specs=[pl.BlockSpec(memory_space=pl.ANY)] * 2,
        out_specs=[vmem] * plan.windows,
        scratch_shapes=[
            pltpu.VMEM(traces.shape, jnp.float32),
            pltpu.VMEM(flags.shape, jnp.int32),
            pltpu.SemaphoreType.DMA((2,)),
        ],
        compiler_params=pltpu.CompilerParams(vmem_limit_bytes=60 * 1024 * 1024),
        name="whiten",
    )(traces, flags)

    height = plan.targets * plan.height
    width = plan.windows * plan.span
    rows = pltpu.VMEM((packed_rows, plan.segment), jnp.float32)
    toeplitz = (height, width)
    columns = (plan.half_lanes, width)
    sums = jax.ShapeDtypeStruct((height, plan.half_lanes), jnp.float32)

    def call(kernel, name, operands, outputs, scratch=()):
        return pl.pallas_call(
            functools.partial(kernel, plan),
            out_shape=outputs,
            in_specs=[vmem] * len(operands),
            out_specs=[vmem] * len(outputs),
            scratch_shapes=scratch,
            compiler_params=params,
            name=name,
        )(*operands)

    across = [swap_blk(array, (plan.targets, plan.targets)) for array in whitened]
    order, chosen, same, lagged, left = call(
        first_kernel,
        "first",
        (source_index.reshape(1, -1), *whitened),
        (
            jax.ShapeDtypeStruct((plan.rows, (plan.targets - 1) * plan.rows), jnp.bfloat16),
            jax.ShapeDtypeStruct((LANES, plan.source_count), jnp.bfloat16),
            jax.ShapeDtypeStruct((packed_rows, plan.segment), jnp.bfloat16),
            jax.ShapeDtypeStruct(toeplitz, jnp.bfloat16),
            sums,
        ),
        (rows, pltpu.VMEM(columns, jnp.bfloat16)),
    )
    *across, same = lax.optimization_barrier((*across, same))
    (right,) = call(near_kernel, "near", (swap_cores(same), lagged), (sums,), (pltpu.VMEM(columns, jnp.bfloat16),))
    across_other = [swap_cores(array) for array in across]
    lagged, left = call(
        across_kernel,
        "across",
        (*across, left),
        (jax.ShapeDtypeStruct(toeplitz, jnp.bfloat16), sums),
        (rows, pltpu.VMEM(columns, jnp.bfloat16)),
    )
    kept, *sent = call(
        finish_kernel,
        "finish",
        (*across_other, lagged, left, right),
        tuple(
            jax.ShapeDtypeStruct((plan.rows, LANES), jnp.bfloat16 if hop else jnp.float32)
            for hop in range(plan.targets)
        ),
        (pltpu.VMEM(columns, jnp.bfloat16),),
    )
    arrived = [swap_blk(array, hops) for array, hops in zip(sent, HOPS)]
    (base,) = call(
        prepare_kernel,
        "prepare",
        (order, chosen, kept),
        (jax.ShapeDtypeStruct((plan.coarse * plan.rows, plan.source_count), jnp.float32),),
    )
    out_shape = (plan.own, LAG_COUNT, plan.source_count)
    return pl.pallas_call(
        functools.partial(expand_kernel, plan),
        out_shape=jax.ShapeDtypeStruct(out_shape, jnp.float32),
        in_specs=[vmem] * (3 + len(arrived)),
        out_specs=pl.BlockSpec(memory_space=pl.ANY),
        scratch_shapes=[pltpu.VMEM(out_shape, jnp.float32), pltpu.SemaphoreType.DMA((plan.own,))],
        compiler_params=params,
        name="expand",
    )(order, chosen, base, *arrived)


def body(traces, valid_flags, source_index):
    plan = Plan(
        traces.shape[0],
        traces.shape[1],
        traces.shape[2],
        lax.axis_size("blk"),
        lax.axis_size("src"),
        source_index.shape[0],
    )
    if plan.fits():
        return few_channels(plan, traces, valid_flags, source_index)
    return many_channels(traces, valid_flags, source_index)


def solution(mesh):
    in_specs = (P(("fibre", "src"), "blk", None), P(("fibre", "src"), "blk"), P())
    out_specs = P(("fibre", "src", "blk"), None, None)
    return jax.shard_map(body, mesh=mesh, in_specs=in_specs, out_specs=out_specs, check_vma=False)
```

```python
import functools
import math

import jax
import jax.numpy as jnp
from jax import lax
from jax.experimental import pallas as pl
from jax.experimental.pallas import tpu as pltpu
from jax.sharding import PartitionSpec as P

MAXLAG = 64
LAG_COUNT = 2 * MAXLAG + 1
LANES = 256
GROUP = 8
HOPS = (3, 1, 2)


def broadcast(value, axis, source):
    kept = jnp.where(lax.axis_index(axis) == source, value, 0).astype(value.dtype)
    return lax.psum(kept, axis)


def toeplitz_rows(group, lag_count, segment):
    shifted = jnp.stack(
        [group[:, :, lag_step : lag_step + segment] for lag_step in range(lag_count)], axis=1
    )
    return shifted.reshape(group.shape[0] * lag_count, -1)


def many_channels(traces, valid_flags, source_index):
    segment = traces.shape[2]
    centered = traces - jnp.mean(traces, axis=2, keepdims=True)
    mean_power = jnp.mean(centered * centered, axis=2, keepdims=True)
    flag_values = valid_flags[:, :, None].astype(jnp.float32)
    whitened = (centered * lax.rsqrt(mean_power + 1e-05) * flag_values).astype(jnp.bfloat16)
    pieces = []
    for owner in range(lax.axis_size("src")):
        pieces.append(broadcast(whitened, "src", owner))
    everyone = jnp.concatenate(pieces, axis=0)
    sources = jnp.take(everyone, source_index, axis=0)
    source_count = sources.shape[0]
    norm_factor = 1.0 / math.sqrt(traces.shape[1] * lax.axis_size("blk") * segment)
    own_rows = whitened.shape[0] // lax.axis_size("blk")
    flat_sources = sources.reshape(source_count, -1)
    padded = jnp.pad(whitened, ((0, 0), (0, 0), (MAXLAG, MAXLAG)))
    block_rows = math.gcd(lax.axis_size("blk") * own_rows, 16)
    grouped = padded.reshape(
        (lax.axis_size("blk") * own_rows // block_rows, block_rows) + padded.shape[1:]
    )

    def one_block(group):
        toeplitz = toeplitz_rows(group, LAG_COUNT, segment)
        products = lax.dot_general(
            toeplitz, flat_sources, (((1,), (1,)), ((), ())), preferred_element_type=jnp.float32
        )
        return (products * norm_factor).reshape(block_rows, LAG_COUNT, source_count)

    result = lax.map(one_block, grouped)
    return lax.psum_scatter(
        result.reshape(lax.axis_size("blk") * own_rows, LAG_COUNT, source_count),
        "blk",
        scatter_dimension=0,
        tiled=True,
    )


class Plan:
    def __init__(self, half, windows, segment, blk_size, src_size, source_count):
        self.half = half
        self.windows = windows
        self.segment = segment
        self.blk_size = blk_size
        self.src_size = src_size
        self.channels = half * src_size
        self.source_count = source_count
        self.half_lanes = LANES // 2
        self.coarse = self.half_lanes // half
        if self.coarse == 0:
            return
        self.fine = -(-LAG_COUNT // self.coarse)
        self.fine_padded = -(-self.fine // (2 * GROUP)) * 2 * GROUP
        self.own = half // blk_size
        reach = segment + (self.coarse - 1) * self.fine
        self.span = -(-max(reach, segment + 2 * MAXLAG) // 128) * 128
        self.whole_groups = self.fine // GROUP * GROUP
        self.rest = self.fine - self.whole_groups
        rows = self.own * self.fine
        self.rows = -(-rows // 16) * 16
        self.height = self.own * self.fine_padded
        self.targets = blk_size // 2
        self.norm_factor = 1.0 / math.sqrt(windows * blk_size * segment)

    def fits(self):
        return (
            self.coarse >= 2
            and self.src_size == 2
            and self.half % self.blk_size == 0
            and self.half % GROUP == 0
            and self.channels % 16 == 0
            and self.windows * self.half % 16 == 0
            and self.blk_size == 8
        )


def whiten_kernel(plan, traces_hbm, flags_hbm, out_ref, traces_ref, flags_ref, sems):
    copies = [
        pltpu.make_async_copy(traces_hbm, traces_ref, sems.at[0]),
        pltpu.make_async_copy(flags_hbm, flags_ref, sems.at[1]),
    ]
    for copy in copies:
        copy.start()
    for copy in copies:
        copy.wait()
    pieces = []
    for window in range(plan.windows):
        values = traces_ref[:, window, :]
        centered = values - jnp.mean(values, axis=1, keepdims=True)
        mean_power = jnp.mean(centered * centered, axis=1, keepdims=True)
        flag_values = flags_ref[window : window + 1, :].astype(jnp.float32).reshape(plan.half, 1)
        pieces.append(centered * lax.rsqrt(mean_power + 1e-05) * flag_values)
    out_ref[...] = jnp.concatenate(pieces, axis=0).astype(jnp.bfloat16)


def lag_rows(plan, rows_ref, toeplitz_ref):
    span = plan.span
    me = lax.axis_index("blk")
    hops = (0,) + HOPS
    filler = jnp.zeros((1, span - plan.segment), jnp.float32)
    for window in range(plan.windows):
        at = slice(window * span, (window + 1) * span)
        for place, hop in enumerate(hops):
            for member in range(plan.own):
                channel = window * plan.half + (me ^ hop) * plan.own + member
                row = jnp.concatenate([rows_ref[pl.ds(channel, 1), :], filler], axis=1)
                row = jnp.broadcast_to(row, (GROUP, span))
                pieces = [
                    pltpu.roll(row, (MAXLAG - plan.fine + 1 + lag) % span, 1, stride=1, stride_axis=0)
                    for lag in range(0, plan.fine_padded, GROUP)
                ]
                first = place * plan.height + member * plan.fine_padded
                toeplitz_ref[first : first + plan.fine_padded, at] = jnp.concatenate(pieces, axis=0).astype(
                    jnp.bfloat16
                )


def half_product(plan, values, toeplitz_ref, columns_ref):
    span = plan.span
    filled = plan.coarse * plan.half
    if filled < plan.half_lanes:
        columns_ref[filled:, :] = jnp.zeros((plan.half_lanes - filled, columns_ref.shape[1]), jnp.bfloat16)
    filler = jnp.zeros((plan.half, span - plan.segment), jnp.float32)
    for window in range(plan.windows):
        at = slice(window * span, (window + 1) * span)
        rows = jnp.concatenate([values[window * plan.half : (window + 1) * plan.half], filler], axis=1)
        for step in range(plan.coarse):
            moved = pltpu.roll(rows, step * plan.fine, 1) if step else rows
            columns_ref[step * plan.half : (step + 1) * plan.half, at] = moved.astype(jnp.bfloat16)
    return lax.dot_general(
        toeplitz_ref[...], columns_ref[...], (((1,), (1,)), ((), ())), preferred_element_type=jnp.float32
    )


def near_kernel(plan, mine_ref, other_ref, sum_ref, rows_ref, toeplitz_ref, columns_ref):
    rows_ref[...] = mine_ref[...].astype(jnp.float32)
    lag_rows(plan, rows_ref, toeplitz_ref)
    other = other_ref[...].astype(jnp.float32)
    sum_ref[:, : plan.half_lanes] = half_product(plan, rows_ref[...], toeplitz_ref, columns_ref.at[0])
    sum_ref[:, plan.half_lanes :] = half_product(plan, other, toeplitz_ref, columns_ref.at[1])


def across_kernel(plan, mine_ref, prior_ref, toeplitz_ref, sum_ref, rows_ref, columns_ref):
    rows_ref[...] = mine_ref[...].astype(jnp.float32)
    lag_rows(plan, rows_ref, toeplitz_ref)
    sum_ref[:, : plan.half_lanes] = prior_ref[:, : plan.half_lanes] + half_product(
        plan, rows_ref[...], toeplitz_ref, columns_ref
    )
    sum_ref[:, plan.half_lanes :] = prior_ref[:, plan.half_lanes :]


def finish_kernel(plan, other_ref, toeplitz_ref, prior_ref, *refs):
    *out_refs, columns_ref = refs
    right = prior_ref[:, plan.half_lanes :] + half_product(
        plan, other_ref[...].astype(jnp.float32), toeplitz_ref, columns_ref
    )
    products = jnp.concatenate([prior_ref[:, : plan.half_lanes], right], axis=1)
    products = products.reshape(plan.targets, plan.own, plan.fine_padded, LANES)
    for hop in range(plan.targets):
        part = products[hop]
        pieces = [part[member, : plan.whole_groups] for member in range(plan.own)]
        if plan.rest:
            pieces += [part[member, plan.whole_groups : plan.fine] for member in range(plan.own)]
        if plan.rows > plan.own * plan.fine:
            pieces.append(jnp.zeros((plan.rows - plan.own * plan.fine, LANES), jnp.float32))
        packed = jnp.concatenate(pieces, axis=0)
        out_refs[hop][...] = packed.astype(out_refs[hop].dtype)


def order_matrix(plan):
    at_row = lax.broadcasted_iota(jnp.int32, (plan.rows, plan.rows), 0)
    at_part = lax.broadcasted_iota(jnp.int32, (plan.rows, plan.rows), 1)
    order = jnp.zeros((plan.rows, plan.rows), jnp.bool_)
    for member in range(plan.own):
        reverse = plan.fine - 1 - (at_row - member * plan.fine)
        whole = (reverse >= 0) & (reverse < plan.whole_groups) & (at_part == member * plan.whole_groups + reverse)
        tail = plan.own * plan.whole_groups + member * plan.rest + reverse - plan.whole_groups
        rest = (reverse >= plan.whole_groups) & (reverse < plan.fine) & (at_part == tail)
        order = order | whole | rest
    return order.astype(jnp.float32).astype(jnp.bfloat16)


def spread(plan, values):
    high = values.astype(jnp.bfloat16).astype(jnp.float32)
    low = values - high
    lane = lax.broadcasted_iota(jnp.int32, values.shape, 1)
    lane = jnp.where(lane >= plan.half_lanes, lane - plan.half_lanes, lane)
    up = pltpu.roll(low, plan.half, 1)
    down = pltpu.roll(low, LANES - plan.half, 1)
    pieces = []
    for step in range(plan.coarse):
        beside, moved = (step + 1, up) if step + 1 < plan.coarse else (step - 1, down)
        kept = jnp.where((lane >= step * plan.half) & (lane < (step + 1) * plan.half), high, 0.0)
        there = (lane >= beside * plan.half) & (lane < (beside + 1) * plan.half)
        pieces.append(jnp.where(there, moved, kept).astype(jnp.bfloat16))
    return jnp.concatenate(pieces, axis=0)


def choose_kernel(plan, index_ref, whitened_ref, order_ref, chosen_ref, same_ref):
    same_ref[...] = whitened_ref[...]
    first = lax.axis_index("src") * plan.half
    index = index_ref[...] - first
    index = jnp.where(index < 0, index + plan.channels, index)
    lane = jnp.where(index >= plan.half, index - plan.half + plan.half_lanes, index)
    at_column = lax.broadcasted_iota(jnp.int32, (LANES, plan.source_count), 0)
    chosen = jnp.zeros((LANES, plan.source_count), jnp.bool_)
    for step in range(plan.coarse):
        chosen = chosen | (at_column == lane + step * plan.half)
    chosen_ref[...] = chosen.astype(jnp.float32).astype(jnp.bfloat16)
    order = order_matrix(plan)
    for block in range(plan.targets - 1):
        order_ref[:, block * plan.rows : (block + 1) * plan.rows] = order


def prepare_kernel(plan, order_ref, chosen_ref, kept_ref, base_ref):
    kept = kept_ref[...] * plan.norm_factor
    high = kept.astype(jnp.bfloat16)
    low = (kept - high.astype(jnp.float32)).astype(jnp.bfloat16)
    order = order_ref[:, : plan.rows]
    ordered = sum(jnp.dot(order, part, preferred_element_type=jnp.float32) for part in (high, low))
    base_ref[...] = jnp.dot(spread(plan, ordered), chosen_ref[...], preferred_element_type=jnp.float32)


def expand_kernel(plan, order_ref, chosen_ref, base_ref, *refs):
    *arrived_refs, out_hbm, out_ref, sems = refs
    blocks = jnp.concatenate([ref[...] for ref in arrived_refs], axis=0)
    arrived = jnp.dot(order_ref[...], blocks, preferred_element_type=jnp.float32) * plan.norm_factor
    expanded = base_ref[...] + jnp.dot(spread(plan, arrived), chosen_ref[...], preferred_element_type=jnp.float32)
    copies = []
    for member in range(plan.own):
        for step in range(plan.coarse):
            start = step * plan.fine
            count = min(plan.fine, LAG_COUNT - start)
            first = step * plan.rows + member * plan.fine
            out_ref[member, start : start + count, :] = expanded[first : first + count]
        copies.append(pltpu.make_async_copy(out_ref.at[member], out_hbm.at[member], sems.at[member]))
        copies[-1].start()
    for copy in copies:
        copy.wait()


def few_channels(plan, traces, valid_flags, source_index):
    vmem = pl.BlockSpec(memory_space=pltpu.VMEM)
    params = pltpu.CompilerParams(vmem_limit_bytes=32 * 1024 * 1024)
    packed_rows = plan.windows * plan.half
    flags = valid_flags.T

    def swap_cores(array):
        return lax.ppermute(array, "src", [(0, 1), (1, 0)])

    def swap_blk(array, hop):
        pairs = [
            (place * plan.src_size + core, (place ^ hop) * plan.src_size + 1 - core)
            for place in range(plan.blk_size)
            for core in range(plan.src_size)
        ]
        return lax.ppermute(array, ("blk", "src"), pairs)

    whitened = pl.pallas_call(
        functools.partial(whiten_kernel, plan),
        out_shape=pltpu.VMEM((packed_rows, plan.segment), jnp.bfloat16),
        in_specs=[pl.BlockSpec(memory_space=pl.ANY)] * 2,
        out_specs=vmem,
        scratch_shapes=[
            pltpu.VMEM(traces.shape, jnp.float32),
            pltpu.VMEM(flags.shape, jnp.int32),
            pltpu.SemaphoreType.DMA((2,)),
        ],
        compiler_params=pltpu.CompilerParams(vmem_limit_bytes=60 * 1024 * 1024),
        name="whiten",
    )(traces, flags)

    height = plan.targets * plan.height
    width = plan.windows * plan.span
    rows = pltpu.VMEM((packed_rows, plan.segment), jnp.float32)
    toeplitz = (height, width)
    columns = (plan.half_lanes, width)
    sums = jax.ShapeDtypeStruct((height, LANES), jnp.float32)

    def call(kernel, name, operands, outputs, scratch=()):
        return pl.pallas_call(
            functools.partial(kernel, plan),
            out_shape=outputs,
            in_specs=[vmem] * len(operands),
            out_specs=[vmem] * len(outputs),
            scratch_shapes=scratch,
            compiler_params=params,
            name=name,
        )(*operands)

    across = swap_blk(whitened, plan.targets)
    order, chosen, same = call(
        choose_kernel,
        "choose",
        (source_index.reshape(1, -1), whitened),
        (
            jax.ShapeDtypeStruct((plan.rows, (plan.targets - 1) * plan.rows), jnp.bfloat16),
            jax.ShapeDtypeStruct((LANES, plan.source_count), jnp.bfloat16),
            jax.ShapeDtypeStruct(whitened.shape, whitened.dtype),
        ),
    )
    (total,) = call(
        near_kernel,
        "near",
        (swap_cores(same), whitened),
        (sums,),
        (rows, pltpu.VMEM(toeplitz, jnp.bfloat16), pltpu.VMEM((2,) + columns, jnp.bfloat16)),
    )
    across_other = swap_cores(across)
    lagged, total = call(
        across_kernel,
        "across",
        (across, total),
        (jax.ShapeDtypeStruct(toeplitz, jnp.bfloat16), sums),
        (rows, pltpu.VMEM(columns, jnp.bfloat16)),
    )
    kept, *sent = call(
        finish_kernel,
        "finish",
        (across_other, lagged, total),
        tuple(
            jax.ShapeDtypeStruct((plan.rows, LANES), jnp.bfloat16 if hop else jnp.float32)
            for hop in range(plan.targets)
        ),
        (pltpu.VMEM(columns, jnp.bfloat16),),
    )
    arrived = [swap_blk(array, hop) for array, hop in zip(sent, HOPS)]
    kept = swap_cores(kept)
    (base,) = call(
        prepare_kernel,
        "prepare",
        (order, chosen, kept),
        (jax.ShapeDtypeStruct((plan.coarse * plan.rows, plan.source_count), jnp.float32),),
    )
    out_shape = (plan.own, LAG_COUNT, plan.source_count)
    return pl.pallas_call(
        functools.partial(expand_kernel, plan),
        out_shape=jax.ShapeDtypeStruct(out_shape, jnp.float32),
        in_specs=[vmem] * (3 + len(arrived)),
        out_specs=pl.BlockSpec(memory_space=pl.ANY),
        scratch_shapes=[pltpu.VMEM(out_shape, jnp.float32), pltpu.SemaphoreType.DMA((plan.own,))],
        compiler_params=params,
        name="expand",
    )(order, chosen, base, *arrived)


def body(traces, valid_flags, source_index):
    plan = Plan(
        traces.shape[0],
        traces.shape[1],
        traces.shape[2],
        lax.axis_size("blk"),
        lax.axis_size("src"),
        source_index.shape[0],
    )
    if plan.fits():
        return few_channels(plan, traces, valid_flags, source_index)
    return many_channels(traces, valid_flags, source_index)


def solution(mesh):
    in_specs = (P(("fibre", "src"), "blk", None), P(("fibre", "src"), "blk"), P())
    out_specs = P(("fibre", "src", "blk"), None, None)
    return jax.shard_map(body, mesh=mesh, in_specs=in_specs, out_specs=out_specs, check_vma=False)
```

```python
import functools
import math

import jax
import jax.numpy as jnp
from jax import lax
from jax.experimental import pallas as pl
from jax.experimental.pallas import tpu as pltpu
from jax.sharding import PartitionSpec as P

MAXLAG = 64
LAG_COUNT = 2 * MAXLAG + 1
LANES = 256
GROUP = 8
HOPS = (3, 1, 2, 0)


def broadcast(value, axis, source):
    kept = jnp.where(lax.axis_index(axis) == source, value, 0).astype(value.dtype)
    return lax.psum(kept, axis)


def toeplitz_rows(group, lag_count, segment):
    shifted = jnp.stack(
        [group[:, :, lag_step : lag_step + segment] for lag_step in range(lag_count)], axis=1
    )
    return shifted.reshape(group.shape[0] * lag_count, -1)


def many_channels(traces, valid_flags, source_index):
    segment = traces.shape[2]
    centered = traces - jnp.mean(traces, axis=2, keepdims=True)
    mean_power = jnp.mean(centered * centered, axis=2, keepdims=True)
    flag_values = valid_flags[:, :, None].astype(jnp.float32)
    whitened = (centered * lax.rsqrt(mean_power + 1e-05) * flag_values).astype(jnp.bfloat16)
    pieces = []
    for owner in range(lax.axis_size("src")):
        pieces.append(broadcast(whitened, "src", owner))
    everyone = jnp.concatenate(pieces, axis=0)
    sources = jnp.take(everyone, source_index, axis=0)
    source_count = sources.shape[0]
    norm_factor = 1.0 / math.sqrt(traces.shape[1] * lax.axis_size("blk") * segment)
    own_rows = whitened.shape[0] // lax.axis_size("blk")
    flat_sources = sources.reshape(source_count, -1)
    padded = jnp.pad(whitened, ((0, 0), (0, 0), (MAXLAG, MAXLAG)))
    block_rows = math.gcd(lax.axis_size("blk") * own_rows, 16)
    grouped = padded.reshape(
        (lax.axis_size("blk") * own_rows // block_rows, block_rows) + padded.shape[1:]
    )

    def one_block(group):
        toeplitz = toeplitz_rows(group, LAG_COUNT, segment)
        products = lax.dot_general(
            toeplitz, flat_sources, (((1,), (1,)), ((), ())), preferred_element_type=jnp.float32
        )
        return (products * norm_factor).reshape(block_rows, LAG_COUNT, source_count)

    result = lax.map(one_block, grouped)
    return lax.psum_scatter(
        result.reshape(lax.axis_size("blk") * own_rows, LAG_COUNT, source_count),
        "blk",
        scatter_dimension=0,
        tiled=True,
    )


class Plan:
    def __init__(self, half, windows, segment, blk_size, src_size, source_count):
        self.half = half
        self.windows = windows
        self.segment = segment
        self.blk_size = blk_size
        self.src_size = src_size
        self.channels = half * src_size
        self.source_count = source_count
        self.half_lanes = LANES // 2
        self.coarse = self.half_lanes // half
        if self.coarse == 0:
            return
        self.fine = -(-LAG_COUNT // self.coarse)
        self.fine_padded = -(-self.fine // (2 * GROUP)) * 2 * GROUP
        self.own = half // blk_size
        reach = segment + (self.coarse - 1) * self.fine
        self.span = -(-max(reach, segment + 2 * MAXLAG) // 128) * 128
        self.whole_groups = self.fine // GROUP * GROUP
        self.rest = self.fine - self.whole_groups
        rows = self.own * self.fine
        self.rows = -(-rows // 16) * 16
        self.height = self.own * self.fine_padded
        self.targets = blk_size // 2
        self.norm_factor = 1.0 / math.sqrt(windows * blk_size * segment)

    def fits(self):
        return (
            self.coarse >= 2
            and self.src_size == 2
            and self.half % self.blk_size == 0
            and self.half % GROUP == 0
            and self.channels % 16 == 0
            and self.windows * self.half % 16 == 0
            and self.blk_size == 8
        )


def whiten_kernel(plan, traces_hbm, flags_hbm, out_ref, traces_ref, flags_ref, sems):
    copies = [
        pltpu.make_async_copy(traces_hbm, traces_ref, sems.at[0]),
        pltpu.make_async_copy(flags_hbm, flags_ref, sems.at[1]),
    ]
    for copy in copies:
        copy.start()
    for copy in copies:
        copy.wait()
    pieces = []
    for window in range(plan.windows):
        values = traces_ref[:, window, :]
        centered = values - jnp.mean(values, axis=1, keepdims=True)
        mean_power = jnp.mean(centered * centered, axis=1, keepdims=True)
        flag_values = flags_ref[window : window + 1, :].astype(jnp.float32).reshape(plan.half, 1)
        pieces.append(centered * lax.rsqrt(mean_power + 1e-05) * flag_values)
    out_ref[...] = jnp.concatenate(pieces, axis=0).astype(jnp.bfloat16)


def lag_rows(plan, rows_ref, toeplitz_ref):
    span = plan.span
    me = lax.axis_index("blk")
    filler = jnp.zeros((1, span - plan.segment), jnp.float32)
    for window in range(plan.windows):
        at = slice(window * span, (window + 1) * span)
        for place, hop in enumerate(HOPS):
            for member in range(plan.own):
                channel = window * plan.half + (me ^ hop) * plan.own + member
                row = jnp.concatenate([rows_ref[pl.ds(channel, 1), :], filler], axis=1)
                row = jnp.broadcast_to(row, (GROUP, span))
                pieces = [
                    pltpu.roll(row, (MAXLAG - plan.fine + 1 + lag) % span, 1, stride=1, stride_axis=0)
                    for lag in range(0, plan.fine_padded, GROUP)
                ]
                first = place * plan.height + member * plan.fine_padded
                toeplitz_ref[first : first + plan.fine_padded, at] = jnp.concatenate(pieces, axis=0).astype(
                    jnp.bfloat16
                )


def fill_columns(plan, values, columns_ref):
    span = plan.span
    filled = plan.coarse * plan.half
    if filled < plan.half_lanes:
        columns_ref[filled:, :] = jnp.zeros((plan.half_lanes - filled, columns_ref.shape[1]), jnp.bfloat16)
    filler = jnp.zeros((plan.half, span - plan.segment), jnp.float32)
    for window in range(plan.windows):
        at = slice(window * span, (window + 1) * span)
        rows = jnp.concatenate([values[window * plan.half : (window + 1) * plan.half], filler], axis=1)
        for step in range(plan.coarse):
            moved = pltpu.roll(rows, step * plan.fine, 1) if step else rows
            columns_ref[step * plan.half : (step + 1) * plan.half, at] = moved.astype(jnp.bfloat16)


def product(toeplitz_ref, columns_ref):
    return lax.dot_general(
        toeplitz_ref[...], columns_ref[...], (((1,), (1,)), ((), ())), preferred_element_type=jnp.float32
    )


def near_kernel(plan, mine_ref, other_ref, sum_ref, rows_ref, toeplitz_ref, columns_ref):
    rows_ref[...] = mine_ref[...].astype(jnp.float32)
    lag_rows(plan, rows_ref, toeplitz_ref)
    fill_columns(plan, rows_ref[...], columns_ref.at[: plan.half_lanes])
    fill_columns(plan, other_ref[...].astype(jnp.float32), columns_ref.at[plan.half_lanes :])
    sum_ref[...] = product(toeplitz_ref, columns_ref)


def across_kernel(plan, mine_ref, prior_ref, toeplitz_ref, sum_ref, rows_ref, columns_ref):
    rows_ref[...] = mine_ref[...].astype(jnp.float32)
    lag_rows(plan, rows_ref, toeplitz_ref)
    fill_columns(plan, rows_ref[...], columns_ref)
    sum_ref[:, : plan.half_lanes] = prior_ref[:, : plan.half_lanes] + product(toeplitz_ref, columns_ref)
    sum_ref[:, plan.half_lanes :] = prior_ref[:, plan.half_lanes :]


def finish_kernel(plan, other_ref, toeplitz_ref, prior_ref, *refs):
    *out_refs, columns_ref = refs
    fill_columns(plan, other_ref[...].astype(jnp.float32), columns_ref)
    right = prior_ref[:, plan.half_lanes :] + product(toeplitz_ref, columns_ref)
    products = jnp.concatenate([prior_ref[:, : plan.half_lanes], right], axis=1)
    products = products.reshape(plan.targets, plan.own, plan.fine_padded, LANES)
    for hop in range(plan.targets):
        part = products[hop]
        pieces = [part[member, : plan.whole_groups] for member in range(plan.own)]
        if plan.rest:
            pieces += [part[member, plan.whole_groups : plan.fine] for member in range(plan.own)]
        if plan.rows > plan.own * plan.fine:
            pieces.append(jnp.zeros((plan.rows - plan.own * plan.fine, LANES), jnp.float32))
        packed = jnp.concatenate(pieces, axis=0)
        out_refs[hop][...] = packed.astype(out_refs[hop].dtype)


def order_matrix(plan):
    at_row = lax.broadcasted_iota(jnp.int32, (plan.rows, plan.rows), 0)
    at_part = lax.broadcasted_iota(jnp.int32, (plan.rows, plan.rows), 1)
    order = jnp.zeros((plan.rows, plan.rows), jnp.bool_)
    for member in range(plan.own):
        reverse = plan.fine - 1 - (at_row - member * plan.fine)
        whole = (reverse >= 0) & (reverse < plan.whole_groups) & (at_part == member * plan.whole_groups + reverse)
        tail = plan.own * plan.whole_groups + member * plan.rest + reverse - plan.whole_groups
        rest = (reverse >= plan.whole_groups) & (reverse < plan.fine) & (at_part == tail)
        order = order | whole | rest
    return order.astype(jnp.float32).astype(jnp.bfloat16)


def spread(plan, values):
    high = values.astype(jnp.bfloat16).astype(jnp.float32)
    low = values - high
    lane = lax.broadcasted_iota(jnp.int32, values.shape, 1)
    lane = jnp.where(lane >= plan.half_lanes, lane - plan.half_lanes, lane)
    up = pltpu.roll(low, plan.half, 1)
    down = pltpu.roll(low, LANES - plan.half, 1)
    pieces = []
    for step in range(plan.coarse):
        beside, moved = (step + 1, up) if step + 1 < plan.coarse else (step - 1, down)
        kept = jnp.where((lane >= step * plan.half) & (lane < (step + 1) * plan.half), high, 0.0)
        there = (lane >= beside * plan.half) & (lane < (beside + 1) * plan.half)
        pieces.append(jnp.where(there, moved, kept).astype(jnp.bfloat16))
    return jnp.concatenate(pieces, axis=0)


def choose_kernel(plan, index_ref, whitened_ref, order_ref, chosen_ref, same_ref):
    same_ref[...] = whitened_ref[...]
    first = lax.axis_index("src") * plan.half
    index = index_ref[...] - first
    index = jnp.where(index < 0, index + plan.channels, index)
    lane = jnp.where(index >= plan.half, index - plan.half + plan.half_lanes, index)
    at_column = lax.broadcasted_iota(jnp.int32, (LANES, plan.source_count), 0)
    chosen = jnp.zeros((LANES, plan.source_count), jnp.bool_)
    for step in range(plan.coarse):
        chosen = chosen | (at_column == lane + step * plan.half)
    chosen_ref[...] = chosen.astype(jnp.float32).astype(jnp.bfloat16)
    order = order_matrix(plan)
    for block in range(plan.targets):
        order_ref[:, block * plan.rows : (block + 1) * plan.rows] = order


def expand_kernel(plan, order_ref, chosen_ref, *refs):
    *arrived_refs, out_hbm, out_ref, sems = refs
    blocks = jnp.concatenate([ref[...] for ref in arrived_refs], axis=0)
    total = jnp.dot(order_ref[...], blocks, preferred_element_type=jnp.float32) * plan.norm_factor
    expanded = jnp.dot(spread(plan, total), chosen_ref[...], preferred_element_type=jnp.float32)
    copies = []
    for member in range(plan.own):
        for step in range(plan.coarse):
            start = step * plan.fine
            count = min(plan.fine, LAG_COUNT - start)
            first = step * plan.rows + member * plan.fine
            out_ref[member, start : start + count, :] = expanded[first : first + count]
        copies.append(pltpu.make_async_copy(out_ref.at[member], out_hbm.at[member], sems.at[member]))
        copies[-1].start()
    for copy in copies:
        copy.wait()


def few_channels(plan, traces, valid_flags, source_index):
    vmem = pl.BlockSpec(memory_space=pltpu.VMEM)
    params = pltpu.CompilerParams(vmem_limit_bytes=32 * 1024 * 1024)
    packed_rows = plan.windows * plan.half
    flags = valid_flags.T

    def swap_cores(array):
        return lax.ppermute(array, "src", [(0, 1), (1, 0)])

    def swap_blk(array, hop):
        pairs = [
            (place * plan.src_size + core, (place ^ hop) * plan.src_size + 1 - core)
            for place in range(plan.blk_size)
            for core in range(plan.src_size)
        ]
        return lax.ppermute(array, ("blk", "src"), pairs)

    whitened = pl.pallas_call(
        functools.partial(whiten_kernel, plan),
        out_shape=pltpu.VMEM((packed_rows, plan.segment), jnp.bfloat16),
        in_specs=[pl.BlockSpec(memory_space=pl.ANY)] * 2,
        out_specs=vmem,
        scratch_shapes=[
            pltpu.VMEM(traces.shape, jnp.float32),
            pltpu.VMEM(flags.shape, jnp.int32),
            pltpu.SemaphoreType.DMA((2,)),
        ],
        compiler_params=pltpu.CompilerParams(vmem_limit_bytes=60 * 1024 * 1024),
        name="whiten",
    )(traces, flags)

    height = plan.targets * plan.height
    width = plan.windows * plan.span
    rows = pltpu.VMEM((packed_rows, plan.segment), jnp.float32)
    toeplitz = (height, width)
    columns = (plan.half_lanes, width)
    sums = jax.ShapeDtypeStruct((height, LANES), jnp.float32)

    def call(kernel, name, operands, outputs, scratch=()):
        return pl.pallas_call(
            functools.partial(kernel, plan),
            out_shape=outputs,
            in_specs=[vmem] * len(operands),
            out_specs=[vmem] * len(outputs),
            scratch_shapes=scratch,
            compiler_params=params,
            name=name,
        )(*operands)

    across = swap_blk(whitened, plan.targets)
    order, chosen, same = call(
        choose_kernel,
        "choose",
        (source_index.reshape(1, -1), whitened),
        (
            jax.ShapeDtypeStruct((plan.rows, plan.targets * plan.rows), jnp.bfloat16),
            jax.ShapeDtypeStruct((LANES, plan.source_count), jnp.bfloat16),
            jax.ShapeDtypeStruct(whitened.shape, whitened.dtype),
        ),
    )
    (total,) = call(
        near_kernel,
        "near",
        (swap_cores(same), whitened),
        (sums,),
        (rows, pltpu.VMEM(toeplitz, jnp.bfloat16), pltpu.VMEM((LANES, width), jnp.bfloat16)),
    )
    across_other = swap_cores(across)
    lagged, total = call(
        across_kernel,
        "across",
        (across, total),
        (jax.ShapeDtypeStruct(toeplitz, jnp.bfloat16), sums),
        (rows, pltpu.VMEM(columns, jnp.bfloat16)),
    )
    sent = call(
        finish_kernel,
        "finish",
        (across_other, lagged, total),
        (jax.ShapeDtypeStruct((plan.rows, LANES), jnp.bfloat16),) * plan.targets,
        (pltpu.VMEM(columns, jnp.bfloat16),),
    )
    arrived = [swap_blk(array, hop) for array, hop in zip(sent, HOPS)]
    out_shape = (plan.own, LAG_COUNT, plan.source_count)
    return pl.pallas_call(
        functools.partial(expand_kernel, plan),
        out_shape=jax.ShapeDtypeStruct(out_shape, jnp.float32),
        in_specs=[vmem] * (2 + len(arrived)),
        out_specs=pl.BlockSpec(memory_space=pl.ANY),
        scratch_shapes=[pltpu.VMEM(out_shape, jnp.float32), pltpu.SemaphoreType.DMA((plan.own,))],
        compiler_params=params,
        name="expand",
    )(order, chosen, *arrived)


def body(traces, valid_flags, source_index):
    plan = Plan(
        traces.shape[0],
        traces.shape[1],
        traces.shape[2],
        lax.axis_size("blk"),
        lax.axis_size("src"),
        source_index.shape[0],
    )
    if plan.fits():
        return few_channels(plan, traces, valid_flags, source_index)
    return many_channels(traces, valid_flags, source_index)


def solution(mesh):
    in_specs = (P(("fibre", "src"), "blk", None), P(("fibre", "src"), "blk"), P())
    out_specs = P(("fibre", "src", "blk"), None, None)
    return jax.shard_map(body, mesh=mesh, in_specs=in_specs, out_specs=out_specs, check_vma=False)
```

```python
import functools
import math

import jax
import jax.numpy as jnp
from jax import lax
from jax.experimental import pallas as pl
from jax.experimental.pallas import tpu as pltpu
from jax.sharding import PartitionSpec as P

MAXLAG = 64
LAG_COUNT = 2 * MAXLAG + 1
LANES = 256
GROUP = 8
HOPS = (3, 1, 2, 0)


def broadcast(value, axis, source):
    kept = jnp.where(lax.axis_index(axis) == source, value, 0).astype(value.dtype)
    return lax.psum(kept, axis)


def toeplitz_rows(group, lag_count, segment):
    shifted = jnp.stack(
        [group[:, :, lag_step : lag_step + segment] for lag_step in range(lag_count)], axis=1
    )
    return shifted.reshape(group.shape[0] * lag_count, -1)


def many_channels(traces, valid_flags, source_index):
    segment = traces.shape[2]
    centered = traces - jnp.mean(traces, axis=2, keepdims=True)
    mean_power = jnp.mean(centered * centered, axis=2, keepdims=True)
    flag_values = valid_flags[:, :, None].astype(jnp.float32)
    whitened = (centered * lax.rsqrt(mean_power + 1e-05) * flag_values).astype(jnp.bfloat16)
    pieces = []
    for owner in range(lax.axis_size("src")):
        pieces.append(broadcast(whitened, "src", owner))
    everyone = jnp.concatenate(pieces, axis=0)
    sources = jnp.take(everyone, source_index, axis=0)
    source_count = sources.shape[0]
    norm_factor = 1.0 / math.sqrt(traces.shape[1] * lax.axis_size("blk") * segment)
    own_rows = whitened.shape[0] // lax.axis_size("blk")
    flat_sources = sources.reshape(source_count, -1)
    padded = jnp.pad(whitened, ((0, 0), (0, 0), (MAXLAG, MAXLAG)))
    block_rows = math.gcd(lax.axis_size("blk") * own_rows, 16)
    grouped = padded.reshape(
        (lax.axis_size("blk") * own_rows // block_rows, block_rows) + padded.shape[1:]
    )

    def one_block(group):
        toeplitz = toeplitz_rows(group, LAG_COUNT, segment)
        products = lax.dot_general(
            toeplitz, flat_sources, (((1,), (1,)), ((), ())), preferred_element_type=jnp.float32
        )
        return (products * norm_factor).reshape(block_rows, LAG_COUNT, source_count)

    result = lax.map(one_block, grouped)
    return lax.psum_scatter(
        result.reshape(lax.axis_size("blk") * own_rows, LAG_COUNT, source_count),
        "blk",
        scatter_dimension=0,
        tiled=True,
    )


class Plan:
    def __init__(self, half, windows, segment, blk_size, src_size, source_count):
        self.half = half
        self.windows = windows
        self.segment = segment
        self.blk_size = blk_size
        self.src_size = src_size
        self.channels = half * src_size
        self.source_count = source_count
        self.half_lanes = LANES // 2
        self.coarse = self.half_lanes // half
        if self.coarse == 0:
            return
        self.fine = -(-LAG_COUNT // self.coarse)
        self.fine_padded = -(-self.fine // (2 * GROUP)) * 2 * GROUP
        self.own = half // blk_size
        reach = segment + (self.coarse - 1) * self.fine
        self.span = -(-max(reach, segment + 2 * MAXLAG) // 128) * 128
        self.whole_groups = self.fine // GROUP * GROUP
        self.rest = self.fine - self.whole_groups
        rows = self.own * self.fine
        self.rows = -(-rows // 16) * 16
        self.height = self.own * self.fine_padded
        self.targets = blk_size // 2
        self.norm_factor = 1.0 / math.sqrt(windows * blk_size * segment)

    def fits(self):
        return (
            self.coarse >= 2
            and self.src_size == 2
            and self.half % self.blk_size == 0
            and self.half % GROUP == 0
            and self.channels % 16 == 0
            and self.windows * self.half % 16 == 0
            and self.blk_size == 8
        )


def whiten_kernel(plan, traces_hbm, flags_hbm, out_ref, traces_ref, flags_ref, sems):
    copies = [
        pltpu.make_async_copy(traces_hbm, traces_ref, sems.at[0]),
        pltpu.make_async_copy(flags_hbm, flags_ref, sems.at[1]),
    ]
    for copy in copies:
        copy.start()
    for copy in copies:
        copy.wait()
    pieces = []
    for window in range(plan.windows):
        values = traces_ref[:, window, :]
        centered = values - jnp.mean(values, axis=1, keepdims=True)
        mean_power = jnp.mean(centered * centered, axis=1, keepdims=True)
        flag_values = flags_ref[window : window + 1, :].astype(jnp.float32).reshape(plan.half, 1)
        pieces.append(centered * lax.rsqrt(mean_power + 1e-05) * flag_values)
    out_ref[...] = jnp.concatenate(pieces, axis=0).astype(jnp.bfloat16)


def lag_rows(plan, rows_ref, toeplitz_ref):
    span = plan.span
    me = lax.axis_index("blk")
    filler = jnp.zeros((1, span - plan.segment), jnp.float32)
    for window in range(plan.windows):
        at = slice(window * span, (window + 1) * span)
        for place, hop in enumerate(HOPS):
            for member in range(plan.own):
                channel = window * plan.half + (me ^ hop) * plan.own + member
                row = jnp.concatenate([rows_ref[pl.ds(channel, 1), :], filler], axis=1)
                row = jnp.broadcast_to(row, (GROUP, span))
                pieces = [
                    pltpu.roll(row, (MAXLAG - plan.fine + 1 + lag) % span, 1, stride=1, stride_axis=0)
                    for lag in range(0, plan.fine_padded, GROUP)
                ]
                first = place * plan.height + member * plan.fine_padded
                toeplitz_ref[first : first + plan.fine_padded, at] = jnp.concatenate(pieces, axis=0).astype(
                    jnp.bfloat16
                )


def fill_columns(plan, values, columns_ref):
    span = plan.span
    filled = plan.coarse * plan.half
    if filled < plan.half_lanes:
        columns_ref[filled:, :] = jnp.zeros((plan.half_lanes - filled, columns_ref.shape[1]), jnp.bfloat16)
    filler = jnp.zeros((plan.half, span - plan.segment), jnp.float32)
    for window in range(plan.windows):
        at = slice(window * span, (window + 1) * span)
        rows = jnp.concatenate([values[window * plan.half : (window + 1) * plan.half], filler], axis=1)
        for step in range(plan.coarse):
            moved = pltpu.roll(rows, step * plan.fine, 1) if step else rows
            columns_ref[step * plan.half : (step + 1) * plan.half, at] = moved.astype(jnp.bfloat16)


def product(toeplitz_ref, columns_ref):
    return lax.dot_general(
        toeplitz_ref[...], columns_ref[...], (((1,), (1,)), ((), ())), preferred_element_type=jnp.float32
    )


def near_kernel(plan, mine_ref, other_ref, sum_ref, rows_ref, toeplitz_ref, columns_ref):
    rows_ref[...] = mine_ref[...].astype(jnp.float32)
    lag_rows(plan, rows_ref, toeplitz_ref)
    fill_columns(plan, rows_ref[...], columns_ref.at[: plan.half_lanes])
    fill_columns(plan, other_ref[...].astype(jnp.float32), columns_ref.at[plan.half_lanes :])
    sum_ref[...] = product(toeplitz_ref, columns_ref)


def across_kernel(plan, mine_ref, prior_ref, toeplitz_ref, sum_ref, rows_ref, columns_ref):
    rows_ref[...] = mine_ref[...].astype(jnp.float32)
    lag_rows(plan, rows_ref, toeplitz_ref)
    fill_columns(plan, rows_ref[...], columns_ref)
    sum_ref[:, : plan.half_lanes] = prior_ref[:, : plan.half_lanes] + product(toeplitz_ref, columns_ref)
    sum_ref[:, plan.half_lanes :] = prior_ref[:, plan.half_lanes :]


def finish_kernel(plan, other_ref, toeplitz_ref, prior_ref, *refs):
    *out_refs, columns_ref = refs
    fill_columns(plan, other_ref[...].astype(jnp.float32), columns_ref)
    right = prior_ref[:, plan.half_lanes :] + product(toeplitz_ref, columns_ref)
    products = jnp.concatenate([prior_ref[:, : plan.half_lanes], right], axis=1)
    products = products.reshape(plan.targets, plan.own, plan.fine_padded, LANES)
    for hop in range(plan.targets):
        part = products[hop]
        pieces = [part[member, : plan.whole_groups] for member in range(plan.own)]
        if plan.rest:
            pieces += [part[member, plan.whole_groups : plan.fine] for member in range(plan.own)]
        if plan.rows > plan.own * plan.fine:
            pieces.append(jnp.zeros((plan.rows - plan.own * plan.fine, LANES), jnp.float32))
        packed = jnp.concatenate(pieces, axis=0)
        out_refs[hop][...] = packed.astype(out_refs[hop].dtype)


def order_matrix(plan):
    at_row = lax.broadcasted_iota(jnp.int32, (plan.height, plan.rows), 0)
    at_part = lax.broadcasted_iota(jnp.int32, (plan.height, plan.rows), 1)
    order = jnp.zeros((plan.height, plan.rows), jnp.bool_)
    for member in range(plan.own):
        reverse = plan.fine - 1 - (at_row - member * plan.fine_padded)
        whole = (reverse >= 0) & (reverse < plan.whole_groups) & (at_part == member * plan.whole_groups + reverse)
        tail = plan.own * plan.whole_groups + member * plan.rest + reverse - plan.whole_groups
        rest = (reverse >= plan.whole_groups) & (reverse < plan.fine) & (at_part == tail)
        order = order | whole | rest
    return order.astype(jnp.float32).astype(jnp.bfloat16)


def spread(plan, values):
    high = values.astype(jnp.bfloat16).astype(jnp.float32)
    low = values - high
    lane = lax.broadcasted_iota(jnp.int32, values.shape, 1)
    lane = jnp.where(lane >= plan.half_lanes, lane - plan.half_lanes, lane)
    up = pltpu.roll(low, plan.half, 1)
    down = pltpu.roll(low, LANES - plan.half, 1)
    pieces = []
    for step in range(plan.coarse):
        beside, moved = (step + 1, up) if step + 1 < plan.coarse else (step - 1, down)
        kept = jnp.where((lane >= step * plan.half) & (lane < (step + 1) * plan.half), high, 0.0)
        there = (lane >= beside * plan.half) & (lane < (beside + 1) * plan.half)
        pieces.append(jnp.where(there, moved, kept).astype(jnp.bfloat16))
    return jnp.concatenate(pieces, axis=0)


def choose_kernel(plan, index_ref, whitened_ref, order_ref, chosen_ref, same_ref):
    same_ref[...] = whitened_ref[...]
    first = lax.axis_index("src") * plan.half
    index = index_ref[...] - first
    index = jnp.where(index < 0, index + plan.channels, index)
    lane = jnp.where(index >= plan.half, index - plan.half + plan.half_lanes, index)
    at_column = lax.broadcasted_iota(jnp.int32, (LANES, plan.source_count), 0)
    chosen = jnp.zeros((LANES, plan.source_count), jnp.bool_)
    for step in range(plan.coarse):
        chosen = chosen | (at_column == lane + step * plan.half)
    chosen_ref[...] = chosen.astype(jnp.float32).astype(jnp.bfloat16)
    order = order_matrix(plan)
    for block in range(plan.targets):
        order_ref[:, block * plan.rows : (block + 1) * plan.rows] = order


def expand_kernel(plan, order_ref, chosen_ref, *refs):
    *arrived_refs, out_hbm, out_ref, sems = refs
    blocks = jnp.concatenate([ref[...] for ref in arrived_refs], axis=0)
    total = jnp.dot(order_ref[...], blocks, preferred_element_type=jnp.float32) * plan.norm_factor
    chosen = chosen_ref[...]
    copies = []
    for member in range(plan.own):
        rows = total[member * plan.fine_padded : (member + 1) * plan.fine_padded]
        expanded = jnp.dot(spread(plan, rows), chosen, preferred_element_type=jnp.float32)
        for step in range(plan.coarse):
            start = step * plan.fine
            count = min(plan.fine, LAG_COUNT - start)
            first = step * plan.fine_padded
            out_ref[member, start : start + count, :] = expanded[first : first + count]
        copies.append(pltpu.make_async_copy(out_ref.at[member], out_hbm.at[member], sems.at[member]))
        copies[-1].start()
    for copy in copies:
        copy.wait()


def few_channels(plan, traces, valid_flags, source_index):
    vmem = pl.BlockSpec(memory_space=pltpu.VMEM)
    params = pltpu.CompilerParams(vmem_limit_bytes=32 * 1024 * 1024)
    packed_rows = plan.windows * plan.half
    flags = valid_flags.T

    def swap_cores(array):
        return lax.ppermute(array, "src", [(0, 1), (1, 0)])

    def swap_blk(array, hop):
        pairs = [
            (place * plan.src_size + core, (place ^ hop) * plan.src_size + 1 - core)
            for place in range(plan.blk_size)
            for core in range(plan.src_size)
        ]
        return lax.ppermute(array, ("blk", "src"), pairs)

    whitened = pl.pallas_call(
        functools.partial(whiten_kernel, plan),
        out_shape=pltpu.VMEM((packed_rows, plan.segment), jnp.bfloat16),
        in_specs=[pl.BlockSpec(memory_space=pl.ANY)] * 2,
        out_specs=vmem,
        scratch_shapes=[
            pltpu.VMEM(traces.shape, jnp.float32),
            pltpu.VMEM(flags.shape, jnp.int32),
            pltpu.SemaphoreType.DMA((2,)),
        ],
        compiler_params=pltpu.CompilerParams(vmem_limit_bytes=60 * 1024 * 1024),
        name="whiten",
    )(traces, flags)

    height = plan.targets * plan.height
    width = plan.windows * plan.span
    rows = pltpu.VMEM((packed_rows, plan.segment), jnp.float32)
    toeplitz = (height, width)
    columns = (plan.half_lanes, width)
    sums = jax.ShapeDtypeStruct((height, LANES), jnp.float32)

    def call(kernel, name, operands, outputs, scratch=()):
        return pl.pallas_call(
            functools.partial(kernel, plan),
            out_shape=outputs,
            in_specs=[vmem] * len(operands),
            out_specs=[vmem] * len(outputs),
            scratch_shapes=scratch,
            compiler_params=params,
            name=name,
        )(*operands)

    across = swap_blk(whitened, plan.targets)
    order, chosen, same = call(
        choose_kernel,
        "choose",
        (source_index.reshape(1, -1), whitened),
        (
            jax.ShapeDtypeStruct((plan.height, plan.targets * plan.rows), jnp.bfloat16),
            jax.ShapeDtypeStruct((LANES, plan.source_count), jnp.bfloat16),
            jax.ShapeDtypeStruct(whitened.shape, whitened.dtype),
        ),
    )
    (total,) = call(
        near_kernel,
        "near",
        (swap_cores(same), whitened),
        (sums,),
        (rows, pltpu.VMEM(toeplitz, jnp.bfloat16), pltpu.VMEM((LANES, width), jnp.bfloat16)),
    )
    across_other = swap_cores(across)
    lagged, total = call(
        across_kernel,
        "across",
        (across, total),
        (jax.ShapeDtypeStruct(toeplitz, jnp.bfloat16), sums),
        (rows, pltpu.VMEM(columns, jnp.bfloat16)),
    )
    sent = call(
        finish_kernel,
        "finish",
        (across_other, lagged, total),
        (jax.ShapeDtypeStruct((plan.rows, LANES), jnp.bfloat16),) * plan.targets,
        (pltpu.VMEM(columns, jnp.bfloat16),),
    )
    arrived = [swap_blk(array, hop) for array, hop in zip(sent, HOPS)]
    out_shape = (plan.own, LAG_COUNT, plan.source_count)
    return pl.pallas_call(
        functools.partial(expand_kernel, plan),
        out_shape=jax.ShapeDtypeStruct(out_shape, jnp.float32),
        in_specs=[vmem] * (2 + len(arrived)),
        out_specs=pl.BlockSpec(memory_space=pl.ANY),
        scratch_shapes=[pltpu.VMEM(out_shape, jnp.float32), pltpu.SemaphoreType.DMA((plan.own,))],
        compiler_params=params,
        name="expand",
    )(order, chosen, *arrived)


def body(traces, valid_flags, source_index):
    plan = Plan(
        traces.shape[0],
        traces.shape[1],
        traces.shape[2],
        lax.axis_size("blk"),
        lax.axis_size("src"),
        source_index.shape[0],
    )
    if plan.fits():
        return few_channels(plan, traces, valid_flags, source_index)
    return many_channels(traces, valid_flags, source_index)


def solution(mesh):
    in_specs = (P(("fibre", "src"), "blk", None), P(("fibre", "src"), "blk"), P())
    out_specs = P(("fibre", "src", "blk"), None, None)
    return jax.shard_map(body, mesh=mesh, in_specs=in_specs, out_specs=out_specs, check_vma=False)
```

```python
import functools
import math

import jax
import jax.numpy as jnp
from jax import lax
from jax.experimental import pallas as pl
from jax.experimental.pallas import tpu as pltpu
from jax.sharding import PartitionSpec as P

MAXLAG = 64
LAG_COUNT = 2 * MAXLAG + 1
LANES = 256
IN_PARTS = 4
OUT_PARTS = 4
OUT_ROWS = 32
GROUP = 8
HOPS = (3, 1, 2, 0)


def broadcast(value, axis, source):
    kept = jnp.where(lax.axis_index(axis) == source, value, 0).astype(value.dtype)
    return lax.psum(kept, axis)


def toeplitz_rows(group, lag_count, segment):
    shifted = jnp.stack(
        [group[:, :, lag_step : lag_step + segment] for lag_step in range(lag_count)], axis=1
    )
    return shifted.reshape(group.shape[0] * lag_count, -1)


def many_channels(traces, valid_flags, source_index):
    segment = traces.shape[2]
    centered = traces - jnp.mean(traces, axis=2, keepdims=True)
    mean_power = jnp.mean(centered * centered, axis=2, keepdims=True)
    flag_values = valid_flags[:, :, None].astype(jnp.float32)
    whitened = (centered * lax.rsqrt(mean_power + 1e-05) * flag_values).astype(jnp.bfloat16)
    pieces = []
    for owner in range(lax.axis_size("src")):
        pieces.append(broadcast(whitened, "src", owner))
    everyone = jnp.concatenate(pieces, axis=0)
    sources = jnp.take(everyone, source_index, axis=0)
    source_count = sources.shape[0]
    norm_factor = 1.0 / math.sqrt(traces.shape[1] * lax.axis_size("blk") * segment)
    own_rows = whitened.shape[0] // lax.axis_size("blk")
    flat_sources = sources.reshape(source_count, -1)
    padded = jnp.pad(whitened, ((0, 0), (0, 0), (MAXLAG, MAXLAG)))
    block_rows = math.gcd(lax.axis_size("blk") * own_rows, 16)
    grouped = padded.reshape(
        (lax.axis_size("blk") * own_rows // block_rows, block_rows) + padded.shape[1:]
    )

    def one_block(group):
        toeplitz = toeplitz_rows(group, LAG_COUNT, segment)
        products = lax.dot_general(
            toeplitz, flat_sources, (((1,), (1,)), ((), ())), preferred_element_type=jnp.float32
        )
        return (products * norm_factor).reshape(block_rows, LAG_COUNT, source_count)

    result = lax.map(one_block, grouped)
    return lax.psum_scatter(
        result.reshape(lax.axis_size("blk") * own_rows, LAG_COUNT, source_count),
        "blk",
        scatter_dimension=0,
        tiled=True,
    )


class Plan:
    def __init__(self, half, windows, segment, blk_size, src_size, source_count):
        self.half = half
        self.windows = windows
        self.segment = segment
        self.blk_size = blk_size
        self.src_size = src_size
        self.channels = half * src_size
        self.source_count = source_count
        self.half_lanes = LANES // 2
        self.coarse = self.half_lanes // half
        if self.coarse == 0:
            return
        self.fine = -(-LAG_COUNT // self.coarse)
        self.fine_padded = -(-self.fine // (2 * GROUP)) * 2 * GROUP
        self.own = half // blk_size
        reach = segment + (self.coarse - 1) * self.fine
        self.span = -(-max(reach, segment + 2 * MAXLAG) // 128) * 128
        self.whole_groups = self.fine // GROUP * GROUP
        self.rest = self.fine - self.whole_groups
        rows = self.own * self.fine
        self.rows = -(-rows // 16) * 16
        self.height = self.own * self.fine_padded
        self.targets = blk_size // 2
        self.norm_factor = 1.0 / math.sqrt(windows * blk_size * segment)

    def fits(self):
        return (
            self.coarse >= 2
            and self.src_size == 2
            and self.half % self.blk_size == 0
            and self.half % GROUP == 0
            and self.channels % 16 == 0
            and self.windows * self.half % 16 == 0
            and self.blk_size == 8
        )


def whiten_kernel(plan, traces_hbm, flags_hbm, out_ref, traces_ref, flags_ref, sems):
    part = plan.half // IN_PARTS
    copies = [pltpu.make_async_copy(flags_hbm, flags_ref, sems.at[IN_PARTS])]
    for index in range(IN_PARTS):
        at = pl.ds(index * part, part)
        copies.append(pltpu.make_async_copy(traces_hbm.at[at], traces_ref.at[at], sems.at[index]))
    for copy in copies:
        copy.start()
    for copy in copies:
        copy.wait()
    pieces = []
    for window in range(plan.windows):
        values = traces_ref[:, window, :]
        centered = values - jnp.mean(values, axis=1, keepdims=True)
        mean_power = jnp.mean(centered * centered, axis=1, keepdims=True)
        flag_values = flags_ref[window : window + 1, :].astype(jnp.float32).reshape(plan.half, 1)
        pieces.append(centered * lax.rsqrt(mean_power + 1e-05) * flag_values)
    out_ref[...] = jnp.concatenate(pieces, axis=0).astype(jnp.bfloat16)


def lag_rows(plan, rows_ref, toeplitz_ref):
    span = plan.span
    me = lax.axis_index("blk")
    filler = jnp.zeros((1, span - plan.segment), jnp.float32)
    for window in range(plan.windows):
        at = slice(window * span, (window + 1) * span)
        for place, hop in enumerate(HOPS):
            for member in range(plan.own):
                channel = window * plan.half + (me ^ hop) * plan.own + member
                row = jnp.concatenate([rows_ref[pl.ds(channel, 1), :], filler], axis=1)
                row = jnp.broadcast_to(row, (GROUP, span))
                pieces = [
                    pltpu.roll(row, (MAXLAG - plan.fine + 1 + lag) % span, 1, stride=1, stride_axis=0)
                    for lag in range(0, plan.fine_padded, GROUP)
                ]
                first = place * plan.height + member * plan.fine_padded
                toeplitz_ref[first : first + plan.fine_padded, at] = jnp.concatenate(pieces, axis=0).astype(
                    jnp.bfloat16
                )


def fill_columns(plan, values, columns_ref):
    span = plan.span
    filled = plan.coarse * plan.half
    if filled < plan.half_lanes:
        columns_ref[filled:, :] = jnp.zeros((plan.half_lanes - filled, columns_ref.shape[1]), jnp.bfloat16)
    filler = jnp.zeros((plan.half, span - plan.segment), jnp.float32)
    for window in range(plan.windows):
        at = slice(window * span, (window + 1) * span)
        rows = jnp.concatenate([values[window * plan.half : (window + 1) * plan.half], filler], axis=1)
        for step in range(plan.coarse):
            moved = pltpu.roll(rows, step * plan.fine, 1) if step else rows
            columns_ref[step * plan.half : (step + 1) * plan.half, at] = moved.astype(jnp.bfloat16)


def product(toeplitz_ref, columns_ref):
    return lax.dot_general(
        toeplitz_ref[...], columns_ref[...], (((1,), (1,)), ((), ())), preferred_element_type=jnp.float32
    )


def near_kernel(plan, mine_ref, other_ref, sum_ref, rows_ref, toeplitz_ref, columns_ref):
    rows_ref[...] = mine_ref[...].astype(jnp.float32)
    lag_rows(plan, rows_ref, toeplitz_ref)
    fill_columns(plan, rows_ref[...], columns_ref.at[: plan.half_lanes])
    fill_columns(plan, other_ref[...].astype(jnp.float32), columns_ref.at[plan.half_lanes :])
    sum_ref[...] = product(toeplitz_ref, columns_ref)


def across_kernel(plan, mine_ref, prior_ref, toeplitz_ref, sum_ref, rows_ref, columns_ref):
    rows_ref[...] = mine_ref[...].astype(jnp.float32)
    lag_rows(plan, rows_ref, toeplitz_ref)
    fill_columns(plan, rows_ref[...], columns_ref)
    sum_ref[:, : plan.half_lanes] = prior_ref[:, : plan.half_lanes] + product(toeplitz_ref, columns_ref)
    sum_ref[:, plan.half_lanes :] = prior_ref[:, plan.half_lanes :]


def finish_kernel(plan, other_ref, toeplitz_ref, prior_ref, *refs):
    *out_refs, columns_ref = refs
    fill_columns(plan, other_ref[...].astype(jnp.float32), columns_ref)
    right = prior_ref[:, plan.half_lanes :] + product(toeplitz_ref, columns_ref)
    products = jnp.concatenate([prior_ref[:, : plan.half_lanes], right], axis=1)
    products = products.reshape(plan.targets, plan.own, plan.fine_padded, LANES)
    for hop in range(plan.targets):
        part = products[hop]
        pieces = [part[member, : plan.whole_groups] for member in range(plan.own)]
        if plan.rest:
            pieces += [part[member, plan.whole_groups : plan.fine] for member in range(plan.own)]
        if plan.rows > plan.own * plan.fine:
            pieces.append(jnp.zeros((plan.rows - plan.own * plan.fine, LANES), jnp.float32))
        packed = jnp.concatenate(pieces, axis=0)
        out_refs[hop][...] = packed.astype(out_refs[hop].dtype)


def order_matrix(plan):
    at_row = lax.broadcasted_iota(jnp.int32, (plan.height, plan.rows), 0)
    at_part = lax.broadcasted_iota(jnp.int32, (plan.height, plan.rows), 1)
    order = jnp.zeros((plan.height, plan.rows), jnp.bool_)
    for member in range(plan.own):
        reverse = plan.fine - 1 - (at_row - member * plan.fine_padded)
        whole = (reverse >= 0) & (reverse < plan.whole_groups) & (at_part == member * plan.whole_groups + reverse)
        tail = plan.own * plan.whole_groups + member * plan.rest + reverse - plan.whole_groups
        rest = (reverse >= plan.whole_groups) & (reverse < plan.fine) & (at_part == tail)
        order = order | whole | rest
    return order.astype(jnp.float32).astype(jnp.bfloat16)


def spread(plan, values):
    high = values.astype(jnp.bfloat16).astype(jnp.float32)
    low = values - high
    lane = lax.broadcasted_iota(jnp.int32, values.shape, 1)
    lane = jnp.where(lane >= plan.half_lanes, lane - plan.half_lanes, lane)
    up = pltpu.roll(low, plan.half, 1)
    down = pltpu.roll(low, LANES - plan.half, 1)
    pieces = []
    for step in range(plan.coarse):
        beside, moved = (step + 1, up) if step + 1 < plan.coarse else (step - 1, down)
        kept = jnp.where((lane >= step * plan.half) & (lane < (step + 1) * plan.half), high, 0.0)
        there = (lane >= beside * plan.half) & (lane < (beside + 1) * plan.half)
        pieces.append(jnp.where(there, moved, kept).astype(jnp.bfloat16))
    return jnp.concatenate(pieces, axis=0)


def choose_kernel(plan, index_ref, whitened_ref, order_ref, chosen_ref, same_ref):
    same_ref[...] = whitened_ref[...]
    first = lax.axis_index("src") * plan.half
    index = index_ref[...] - first
    index = jnp.where(index < 0, index + plan.channels, index)
    lane = jnp.where(index >= plan.half, index - plan.half + plan.half_lanes, index)
    at_column = lax.broadcasted_iota(jnp.int32, (LANES, plan.source_count), 0)
    chosen = jnp.zeros((LANES, plan.source_count), jnp.bool_)
    for step in range(plan.coarse):
        chosen = chosen | (at_column == lane + step * plan.half)
    chosen_ref[...] = chosen.astype(jnp.float32).astype(jnp.bfloat16)
    order = order_matrix(plan)
    for block in range(plan.targets):
        order_ref[:, block * plan.rows : (block + 1) * plan.rows] = order


def expand_kernel(plan, order_ref, chosen_ref, *refs):
    *arrived_refs, out_hbm, out_ref, sems = refs
    blocks = jnp.concatenate([ref[...] for ref in arrived_refs], axis=0)
    total = jnp.dot(order_ref[...], blocks, preferred_element_type=jnp.float32) * plan.norm_factor
    chosen = chosen_ref[...]
    copies = []
    for member in range(plan.own):
        rows = total[member * plan.fine_padded : (member + 1) * plan.fine_padded]
        expanded = jnp.dot(spread(plan, rows), chosen, preferred_element_type=jnp.float32)
        for step in range(plan.coarse):
            start = step * plan.fine
            count = min(plan.fine, LAG_COUNT - start)
            first = step * plan.fine_padded
            out_ref[member, start : start + count, :] = expanded[first : first + count]
        for part in range(OUT_PARTS):
            start = part * OUT_ROWS
            count = OUT_ROWS if part + 1 < OUT_PARTS else LAG_COUNT - start
            at = (member, pl.ds(start, count))
            copies.append(pltpu.make_async_copy(out_ref.at[at], out_hbm.at[at], sems.at[member, part]))
            copies[-1].start()
    for copy in copies:
        copy.wait()


def few_channels(plan, traces, valid_flags, source_index):
    vmem = pl.BlockSpec(memory_space=pltpu.VMEM)
    params = pltpu.CompilerParams(vmem_limit_bytes=32 * 1024 * 1024)
    packed_rows = plan.windows * plan.half
    flags = valid_flags.T

    def swap_cores(array):
        return lax.ppermute(array, "src", [(0, 1), (1, 0)])

    def swap_blk(array, hop):
        pairs = [
            (place * plan.src_size + core, (place ^ hop) * plan.src_size + 1 - core)
            for place in range(plan.blk_size)
            for core in range(plan.src_size)
        ]
        return lax.ppermute(array, ("blk", "src"), pairs)

    whitened = pl.pallas_call(
        functools.partial(whiten_kernel, plan),
        out_shape=pltpu.VMEM((packed_rows, plan.segment), jnp.bfloat16),
        in_specs=[pl.BlockSpec(memory_space=pl.ANY)] * 2,
        out_specs=vmem,
        scratch_shapes=[
            pltpu.VMEM(traces.shape, jnp.float32),
            pltpu.VMEM(flags.shape, jnp.int32),
            pltpu.SemaphoreType.DMA((IN_PARTS + 1,)),
        ],
        compiler_params=pltpu.CompilerParams(vmem_limit_bytes=60 * 1024 * 1024),
        name="whiten",
    )(traces, flags)

    height = plan.targets * plan.height
    width = plan.windows * plan.span
    rows = pltpu.VMEM((packed_rows, plan.segment), jnp.float32)
    toeplitz = (height, width)
    columns = (plan.half_lanes, width)
    sums = jax.ShapeDtypeStruct((height, LANES), jnp.float32)

    def call(kernel, name, operands, outputs, scratch=()):
        return pl.pallas_call(
            functools.partial(kernel, plan),
            out_shape=outputs,
            in_specs=[vmem] * len(operands),
            out_specs=[vmem] * len(outputs),
            scratch_shapes=scratch,
            compiler_params=params,
            name=name,
        )(*operands)

    across = swap_blk(whitened, plan.targets)
    order, chosen, same = call(
        choose_kernel,
        "choose",
        (source_index.reshape(1, -1), whitened),
        (
            jax.ShapeDtypeStruct((plan.height, plan.targets * plan.rows), jnp.bfloat16),
            jax.ShapeDtypeStruct((LANES, plan.source_count), jnp.bfloat16),
            jax.ShapeDtypeStruct(whitened.shape, whitened.dtype),
        ),
    )
    (total,) = call(
        near_kernel,
        "near",
        (swap_cores(same), whitened),
        (sums,),
        (rows, pltpu.VMEM(toeplitz, jnp.bfloat16), pltpu.VMEM((LANES, width), jnp.bfloat16)),
    )
    across_other = swap_cores(across)
    lagged, total = call(
        across_kernel,
        "across",
        (across, total),
        (jax.ShapeDtypeStruct(toeplitz, jnp.bfloat16), sums),
        (rows, pltpu.VMEM(columns, jnp.bfloat16)),
    )
    sent = call(
        finish_kernel,
        "finish",
        (across_other, lagged, total),
        (jax.ShapeDtypeStruct((plan.rows, LANES), jnp.bfloat16),) * plan.targets,
        (pltpu.VMEM(columns, jnp.bfloat16),),
    )
    arrived = [swap_blk(array, hop) for array, hop in zip(sent, HOPS)]
    out_shape = (plan.own, LAG_COUNT, plan.source_count)
    return pl.pallas_call(
        functools.partial(expand_kernel, plan),
        out_shape=jax.ShapeDtypeStruct(out_shape, jnp.float32),
        in_specs=[vmem] * (2 + len(arrived)),
        out_specs=pl.BlockSpec(memory_space=pl.ANY),
        scratch_shapes=[pltpu.VMEM(out_shape, jnp.float32), pltpu.SemaphoreType.DMA((plan.own, OUT_PARTS))],
        compiler_params=params,
        name="expand",
    )(order, chosen, *arrived)


def body(traces, valid_flags, source_index):
    plan = Plan(
        traces.shape[0],
        traces.shape[1],
        traces.shape[2],
        lax.axis_size("blk"),
        lax.axis_size("src"),
        source_index.shape[0],
    )
    if plan.fits():
        return few_channels(plan, traces, valid_flags, source_index)
    return many_channels(traces, valid_flags, source_index)


def solution(mesh):
    in_specs = (P(("fibre", "src"), "blk", None), P(("fibre", "src"), "blk"), P())
    out_specs = P(("fibre", "src", "blk"), None, None)
    return jax.shard_map(body, mesh=mesh, in_specs=in_specs, out_specs=out_specs, check_vma=False)
```

```python
import functools
import math

import jax
import jax.numpy as jnp
from jax import lax
from jax.experimental import pallas as pl
from jax.experimental.pallas import tpu as pltpu
from jax.sharding import PartitionSpec as P

MAXLAG = 64
LAG_COUNT = 2 * MAXLAG + 1
LANES = 256
IN_PARTS = 4
GROUP = 8
HOPS = (3, 1, 2, 0)


def broadcast(value, axis, source):
    kept = jnp.where(lax.axis_index(axis) == source, value, 0).astype(value.dtype)
    return lax.psum(kept, axis)


def toeplitz_rows(group, lag_count, segment):
    shifted = jnp.stack(
        [group[:, :, lag_step : lag_step + segment] for lag_step in range(lag_count)], axis=1
    )
    return shifted.reshape(group.shape[0] * lag_count, -1)


def many_channels(traces, valid_flags, source_index):
    segment = traces.shape[2]
    centered = traces - jnp.mean(traces, axis=2, keepdims=True)
    mean_power = jnp.mean(centered * centered, axis=2, keepdims=True)
    flag_values = valid_flags[:, :, None].astype(jnp.float32)
    whitened = (centered * lax.rsqrt(mean_power + 1e-05) * flag_values).astype(jnp.bfloat16)
    pieces = []
    for owner in range(lax.axis_size("src")):
        pieces.append(broadcast(whitened, "src", owner))
    everyone = jnp.concatenate(pieces, axis=0)
    sources = jnp.take(everyone, source_index, axis=0)
    source_count = sources.shape[0]
    norm_factor = 1.0 / math.sqrt(traces.shape[1] * lax.axis_size("blk") * segment)
    own_rows = whitened.shape[0] // lax.axis_size("blk")
    flat_sources = sources.reshape(source_count, -1)
    padded = jnp.pad(whitened, ((0, 0), (0, 0), (MAXLAG, MAXLAG)))
    block_rows = math.gcd(lax.axis_size("blk") * own_rows, 16)
    grouped = padded.reshape(
        (lax.axis_size("blk") * own_rows // block_rows, block_rows) + padded.shape[1:]
    )

    def one_block(group):
        toeplitz = toeplitz_rows(group, LAG_COUNT, segment)
        products = lax.dot_general(
            toeplitz, flat_sources, (((1,), (1,)), ((), ())), preferred_element_type=jnp.float32
        )
        return (products * norm_factor).reshape(block_rows, LAG_COUNT, source_count)

    result = lax.map(one_block, grouped)
    return lax.psum_scatter(
        result.reshape(lax.axis_size("blk") * own_rows, LAG_COUNT, source_count),
        "blk",
        scatter_dimension=0,
        tiled=True,
    )


class Plan:
    def __init__(self, half, windows, segment, blk_size, src_size, source_count):
        self.half = half
        self.windows = windows
        self.segment = segment
        self.blk_size = blk_size
        self.src_size = src_size
        self.channels = half * src_size
        self.source_count = source_count
        self.half_lanes = LANES // 2
        self.coarse = self.half_lanes // half
        if self.coarse == 0:
            return
        self.fine = -(-LAG_COUNT // self.coarse)
        self.fine_padded = -(-self.fine // (2 * GROUP)) * 2 * GROUP
        self.own = half // blk_size
        reach = segment + (self.coarse - 1) * self.fine
        self.span = -(-max(reach, segment + 2 * MAXLAG) // 128) * 128
        self.whole_groups = self.fine // GROUP * GROUP
        self.rest = self.fine - self.whole_groups
        rows = self.own * self.fine
        self.rows = -(-rows // 16) * 16
        self.height = self.own * self.fine_padded
        self.targets = blk_size // 2
        self.norm_factor = 1.0 / math.sqrt(windows * blk_size * segment)

    def fits(self):
        return (
            self.coarse >= 2
            and self.src_size == 2
            and self.half % self.blk_size == 0
            and self.half % GROUP == 0
            and self.channels % 16 == 0
            and self.windows * self.half % 16 == 0
            and self.blk_size == 8
        )


def whiten_kernel(plan, traces_hbm, flags_hbm, out_ref, traces_ref, flags_ref, sems):
    part = plan.half // IN_PARTS
    copies = [pltpu.make_async_copy(flags_hbm, flags_ref, sems.at[IN_PARTS])]
    for index in range(IN_PARTS):
        at = pl.ds(index * part, part)
        copies.append(pltpu.make_async_copy(traces_hbm.at[at], traces_ref.at[at], sems.at[index]))
    for copy in copies:
        copy.start()
    for copy in copies:
        copy.wait()
    pieces = []
    for window in range(plan.windows):
        values = traces_ref[:, window, :]
        centered = values - jnp.mean(values, axis=1, keepdims=True)
        mean_power = jnp.mean(centered * centered, axis=1, keepdims=True)
        flag_values = flags_ref[window : window + 1, :].astype(jnp.float32).reshape(plan.half, 1)
        pieces.append(centered * lax.rsqrt(mean_power + 1e-05) * flag_values)
    out_ref[...] = jnp.concatenate(pieces, axis=0).astype(jnp.bfloat16)


def lag_rows(plan, rows_ref, toeplitz_ref):
    span = plan.span
    me = lax.axis_index("blk")
    filler = jnp.zeros((1, span - plan.segment), jnp.float32)
    for window in range(plan.windows):
        at = slice(window * span, (window + 1) * span)
        for place, hop in enumerate(HOPS):
            for member in range(plan.own):
                channel = window * plan.half + (me ^ hop) * plan.own + member
                row = jnp.concatenate([rows_ref[pl.ds(channel, 1), :], filler], axis=1)
                row = jnp.broadcast_to(row, (GROUP, span))
                pieces = [
                    pltpu.roll(row, (MAXLAG - plan.fine + 1 + lag) % span, 1, stride=1, stride_axis=0)
                    for lag in range(0, plan.fine_padded, GROUP)
                ]
                first = place * plan.height + member * plan.fine_padded
                toeplitz_ref[first : first + plan.fine_padded, at] = jnp.concatenate(pieces, axis=0).astype(
                    jnp.bfloat16
                )


def fill_columns(plan, values, columns_ref):
    span = plan.span
    filled = plan.coarse * plan.half
    if filled < plan.half_lanes:
        columns_ref[filled:, :] = jnp.zeros((plan.half_lanes - filled, columns_ref.shape[1]), jnp.bfloat16)
    filler = jnp.zeros((plan.half, span - plan.segment), jnp.float32)
    for window in range(plan.windows):
        at = slice(window * span, (window + 1) * span)
        rows = jnp.concatenate([values[window * plan.half : (window + 1) * plan.half], filler], axis=1)
        for step in range(plan.coarse):
            moved = pltpu.roll(rows, step * plan.fine, 1) if step else rows
            columns_ref[step * plan.half : (step + 1) * plan.half, at] = moved.astype(jnp.bfloat16)


def product(toeplitz_ref, columns_ref):
    return lax.dot_general(
        toeplitz_ref[...], columns_ref[...], (((1,), (1,)), ((), ())), preferred_element_type=jnp.float32
    )


def near_kernel(plan, *refs):
    mine_refs, (other_ref, sum_ref, rows_ref, toeplitz_ref, columns_ref) = refs[: plan.windows], refs[plan.windows :]
    for window, mine_ref in enumerate(mine_refs):
        rows_ref[window * plan.half : (window + 1) * plan.half, :] = mine_ref[...].astype(jnp.float32)
    lag_rows(plan, rows_ref, toeplitz_ref)
    fill_columns(plan, rows_ref[...], columns_ref.at[: plan.half_lanes])
    fill_columns(plan, other_ref[...].astype(jnp.float32), columns_ref.at[plan.half_lanes :])
    sum_ref[...] = product(toeplitz_ref, columns_ref)


def across_kernel(plan, mine_ref, prior_ref, toeplitz_ref, sum_ref, rows_ref, columns_ref):
    rows_ref[...] = mine_ref[...].astype(jnp.float32)
    lag_rows(plan, rows_ref, toeplitz_ref)
    fill_columns(plan, rows_ref[...], columns_ref)
    sum_ref[:, : plan.half_lanes] = prior_ref[:, : plan.half_lanes] + product(toeplitz_ref, columns_ref)
    sum_ref[:, plan.half_lanes :] = prior_ref[:, plan.half_lanes :]


def finish_kernel(plan, other_ref, toeplitz_ref, prior_ref, *refs):
    *out_refs, columns_ref = refs
    fill_columns(plan, other_ref[...].astype(jnp.float32), columns_ref)
    right = prior_ref[:, plan.half_lanes :] + product(toeplitz_ref, columns_ref)
    products = jnp.concatenate([prior_ref[:, : plan.half_lanes], right], axis=1)
    products = products.reshape(plan.targets, plan.own, plan.fine_padded, LANES)
    for hop in range(plan.targets):
        part = products[hop]
        pieces = [part[member, : plan.whole_groups] for member in range(plan.own)]
        if plan.rest:
            pieces += [part[member, plan.whole_groups : plan.fine] for member in range(plan.own)]
        if plan.rows > plan.own * plan.fine:
            pieces.append(jnp.zeros((plan.rows - plan.own * plan.fine, LANES), jnp.float32))
        packed = jnp.concatenate(pieces, axis=0)
        out_refs[hop][...] = packed.astype(out_refs[hop].dtype)


def order_matrix(plan):
    at_row = lax.broadcasted_iota(jnp.int32, (plan.height, plan.rows), 0)
    at_part = lax.broadcasted_iota(jnp.int32, (plan.height, plan.rows), 1)
    order = jnp.zeros((plan.height, plan.rows), jnp.bool_)
    for member in range(plan.own):
        reverse = plan.fine - 1 - (at_row - member * plan.fine_padded)
        whole = (reverse >= 0) & (reverse < plan.whole_groups) & (at_part == member * plan.whole_groups + reverse)
        tail = plan.own * plan.whole_groups + member * plan.rest + reverse - plan.whole_groups
        rest = (reverse >= plan.whole_groups) & (reverse < plan.fine) & (at_part == tail)
        order = order | whole | rest
    return order.astype(jnp.float32).astype(jnp.bfloat16)


def spread(plan, values):
    high = values.astype(jnp.bfloat16).astype(jnp.float32)
    low = values - high
    lane = lax.broadcasted_iota(jnp.int32, values.shape, 1)
    lane = jnp.where(lane >= plan.half_lanes, lane - plan.half_lanes, lane)
    up = pltpu.roll(low, plan.half, 1)
    down = pltpu.roll(low, LANES - plan.half, 1)
    pieces = []
    for step in range(plan.coarse):
        beside, moved = (step + 1, up) if step + 1 < plan.coarse else (step - 1, down)
        kept = jnp.where((lane >= step * plan.half) & (lane < (step + 1) * plan.half), high, 0.0)
        there = (lane >= beside * plan.half) & (lane < (beside + 1) * plan.half)
        pieces.append(jnp.where(there, moved, kept).astype(jnp.bfloat16))
    return jnp.concatenate(pieces, axis=0)


def choose_kernel(plan, index_ref, whitened_ref, order_ref, chosen_ref, *same_refs):
    whitened = whitened_ref[...].astype(jnp.float32)
    for window, same_ref in enumerate(same_refs):
        same_ref[...] = whitened[window * plan.half : (window + 1) * plan.half].astype(jnp.bfloat16)
    first = lax.axis_index("src") * plan.half
    index = index_ref[...] - first
    index = jnp.where(index < 0, index + plan.channels, index)
    lane = jnp.where(index >= plan.half, index - plan.half + plan.half_lanes, index)
    at_column = lax.broadcasted_iota(jnp.int32, (LANES, plan.source_count), 0)
    chosen = jnp.zeros((LANES, plan.source_count), jnp.bool_)
    for step in range(plan.coarse):
        chosen = chosen | (at_column == lane + step * plan.half)
    chosen_ref[...] = chosen.astype(jnp.float32).astype(jnp.bfloat16)
    order = order_matrix(plan)
    for block in range(plan.targets):
        order_ref[:, block * plan.rows : (block + 1) * plan.rows] = order


def expand_kernel(plan, order_ref, chosen_ref, *refs):
    *arrived_refs, out_hbm, out_ref, sems = refs
    blocks = jnp.concatenate([ref[...] for ref in arrived_refs], axis=0)
    total = jnp.dot(order_ref[...], blocks, preferred_element_type=jnp.float32) * plan.norm_factor
    chosen = chosen_ref[...]
    copies = []
    for member in range(plan.own):
        rows = total[member * plan.fine_padded : (member + 1) * plan.fine_padded]
        expanded = jnp.dot(spread(plan, rows), chosen, preferred_element_type=jnp.float32)
        for step in range(plan.coarse):
            start = step * plan.fine
            count = min(plan.fine, LAG_COUNT - start)
            first = step * plan.fine_padded
            out_ref[member, start : start + count, :] = expanded[first : first + count]
        copies.append(pltpu.make_async_copy(out_ref.at[member], out_hbm.at[member], sems.at[member]))
        copies[-1].start()
    for copy in copies:
        copy.wait()


def few_channels(plan, traces, valid_flags, source_index):
    vmem = pl.BlockSpec(memory_space=pltpu.VMEM)
    params = pltpu.CompilerParams(vmem_limit_bytes=32 * 1024 * 1024)
    packed_rows = plan.windows * plan.half
    flags = valid_flags.T

    def swap_cores(array):
        return lax.ppermute(array, "src", [(0, 1), (1, 0)])

    def swap_blk(array, hop):
        pairs = [
            (place * plan.src_size + core, (place ^ hop) * plan.src_size + 1 - core)
            for place in range(plan.blk_size)
            for core in range(plan.src_size)
        ]
        return lax.ppermute(array, ("blk", "src"), pairs)

    whitened = pl.pallas_call(
        functools.partial(whiten_kernel, plan),
        out_shape=pltpu.VMEM((packed_rows, plan.segment), jnp.bfloat16),
        in_specs=[pl.BlockSpec(memory_space=pl.ANY)] * 2,
        out_specs=vmem,
        scratch_shapes=[
            pltpu.VMEM(traces.shape, jnp.float32),
            pltpu.VMEM(flags.shape, jnp.int32),
            pltpu.SemaphoreType.DMA((IN_PARTS + 1,)),
        ],
        compiler_params=pltpu.CompilerParams(vmem_limit_bytes=60 * 1024 * 1024),
        name="whiten",
    )(traces, flags)

    height = plan.targets * plan.height
    width = plan.windows * plan.span
    rows = pltpu.VMEM((packed_rows, plan.segment), jnp.float32)
    toeplitz = (height, width)
    columns = (plan.half_lanes, width)
    sums = jax.ShapeDtypeStruct((height, LANES), jnp.float32)

    def call(kernel, name, operands, outputs, scratch=()):
        return pl.pallas_call(
            functools.partial(kernel, plan),
            out_shape=outputs,
            in_specs=[vmem] * len(operands),
            out_specs=[vmem] * len(outputs),
            scratch_shapes=scratch,
            compiler_params=params,
            name=name,
        )(*operands)

    across = swap_blk(whitened, plan.targets)
    order, chosen, *same = call(
        choose_kernel,
        "choose",
        (source_index.reshape(1, -1), whitened),
        (
            jax.ShapeDtypeStruct((plan.height, plan.targets * plan.rows), jnp.bfloat16),
            jax.ShapeDtypeStruct((LANES, plan.source_count), jnp.bfloat16),
            *[jax.ShapeDtypeStruct((plan.half, plan.segment), whitened.dtype)] * plan.windows,
        ),
    )
    (total,) = call(
        near_kernel,
        "near",
        (*[swap_cores(array) for array in same], whitened),
        (sums,),
        (rows, pltpu.VMEM(toeplitz, jnp.bfloat16), pltpu.VMEM((LANES, width), jnp.bfloat16)),
    )
    across, total = lax.optimization_barrier((across, total))
    across_other = swap_cores(across)
    lagged, total = call(
        across_kernel,
        "across",
        (across, total),
        (jax.ShapeDtypeStruct(toeplitz, jnp.bfloat16), sums),
        (rows, pltpu.VMEM(columns, jnp.bfloat16)),
    )
    sent = call(
        finish_kernel,
        "finish",
        (across_other, lagged, total),
        (jax.ShapeDtypeStruct((plan.rows, LANES), jnp.bfloat16),) * plan.targets,
        (pltpu.VMEM(columns, jnp.bfloat16),),
    )
    arrived = [swap_blk(array, hop) for array, hop in zip(sent, HOPS)]
    out_shape = (plan.own, LAG_COUNT, plan.source_count)
    return pl.pallas_call(
        functools.partial(expand_kernel, plan),
        out_shape=jax.ShapeDtypeStruct(out_shape, jnp.float32),
        in_specs=[vmem] * (2 + len(arrived)),
        out_specs=pl.BlockSpec(memory_space=pl.ANY),
        scratch_shapes=[pltpu.VMEM(out_shape, jnp.float32), pltpu.SemaphoreType.DMA((plan.own,))],
        compiler_params=params,
        name="expand",
    )(order, chosen, *arrived)


def body(traces, valid_flags, source_index):
    plan = Plan(
        traces.shape[0],
        traces.shape[1],
        traces.shape[2],
        lax.axis_size("blk"),
        lax.axis_size("src"),
        source_index.shape[0],
    )
    if plan.fits():
        return few_channels(plan, traces, valid_flags, source_index)
    return many_channels(traces, valid_flags, source_index)


def solution(mesh):
    in_specs = (P(("fibre", "src"), "blk", None), P(("fibre", "src"), "blk"), P())
    out_specs = P(("fibre", "src", "blk"), None, None)
    return jax.shard_map(body, mesh=mesh, in_specs=in_specs, out_specs=out_specs, check_vma=False)
```

```python
import functools
import math

import jax
import jax.numpy as jnp
from jax import lax
from jax.experimental import pallas as pl
from jax.experimental.pallas import tpu as pltpu
from jax.sharding import PartitionSpec as P

MAXLAG = 64
LAG_COUNT = 2 * MAXLAG + 1
LANES = 256
IN_PARTS = 4
GROUP = 8
HOPS = (3, 1, 2, 0)


def broadcast(value, axis, source):
    kept = jnp.where(lax.axis_index(axis) == source, value, 0).astype(value.dtype)
    return lax.psum(kept, axis)


def toeplitz_rows(group, lag_count, segment):
    shifted = jnp.stack(
        [group[:, :, lag_step : lag_step + segment] for lag_step in range(lag_count)], axis=1
    )
    return shifted.reshape(group.shape[0] * lag_count, -1)


def many_channels(traces, valid_flags, source_index):
    segment = traces.shape[2]
    centered = traces - jnp.mean(traces, axis=2, keepdims=True)
    mean_power = jnp.mean(centered * centered, axis=2, keepdims=True)
    flag_values = valid_flags[:, :, None].astype(jnp.float32)
    whitened = (centered * lax.rsqrt(mean_power + 1e-05) * flag_values).astype(jnp.bfloat16)
    pieces = []
    for owner in range(lax.axis_size("src")):
        pieces.append(broadcast(whitened, "src", owner))
    everyone = jnp.concatenate(pieces, axis=0)
    sources = jnp.take(everyone, source_index, axis=0)
    source_count = sources.shape[0]
    norm_factor = 1.0 / math.sqrt(traces.shape[1] * lax.axis_size("blk") * segment)
    own_rows = whitened.shape[0] // lax.axis_size("blk")
    flat_sources = sources.reshape(source_count, -1)
    padded = jnp.pad(whitened, ((0, 0), (0, 0), (MAXLAG, MAXLAG)))
    block_rows = math.gcd(lax.axis_size("blk") * own_rows, 16)
    grouped = padded.reshape(
        (lax.axis_size("blk") * own_rows // block_rows, block_rows) + padded.shape[1:]
    )

    def one_block(group):
        toeplitz = toeplitz_rows(group, LAG_COUNT, segment)
        products = lax.dot_general(
            toeplitz, flat_sources, (((1,), (1,)), ((), ())), preferred_element_type=jnp.float32
        )
        return (products * norm_factor).reshape(block_rows, LAG_COUNT, source_count)

    result = lax.map(one_block, grouped)
    return lax.psum_scatter(
        result.reshape(lax.axis_size("blk") * own_rows, LAG_COUNT, source_count),
        "blk",
        scatter_dimension=0,
        tiled=True,
    )


class Plan:
    def __init__(self, half, windows, segment, blk_size, src_size, source_count):
        self.half = half
        self.windows = windows
        self.segment = segment
        self.blk_size = blk_size
        self.src_size = src_size
        self.channels = half * src_size
        self.source_count = source_count
        self.half_lanes = LANES // 2
        self.coarse = self.half_lanes // half
        if self.coarse == 0:
            return
        self.fine = -(-LAG_COUNT // self.coarse)
        self.fine_padded = -(-self.fine // (2 * GROUP)) * 2 * GROUP
        self.own = half // blk_size
        reach = segment + (self.coarse - 1) * self.fine
        self.span = -(-max(reach, segment + 2 * MAXLAG) // 128) * 128
        self.whole_groups = self.fine // GROUP * GROUP
        self.rest = self.fine - self.whole_groups
        rows = self.own * self.fine
        self.rows = -(-rows // 16) * 16
        self.height = self.own * self.fine_padded
        self.targets = blk_size // 2
        self.norm_factor = 1.0 / math.sqrt(windows * blk_size * segment)

    def fits(self):
        return (
            self.coarse >= 2
            and self.src_size == 2
            and self.half % self.blk_size == 0
            and self.half % GROUP == 0
            and self.channels % 16 == 0
            and self.windows * self.half % 16 == 0
            and self.blk_size == 8
        )


def whiten_kernel(plan, traces_hbm, flags_hbm, out_ref, traces_ref, flags_ref, sems):
    part = plan.half // IN_PARTS
    copies = [pltpu.make_async_copy(flags_hbm, flags_ref, sems.at[IN_PARTS])]
    for index in range(IN_PARTS):
        at = pl.ds(index * part, part)
        copies.append(pltpu.make_async_copy(traces_hbm.at[at], traces_ref.at[at], sems.at[index]))
    for copy in copies:
        copy.start()
    for copy in copies:
        copy.wait()
    pieces = []
    for window in range(plan.windows):
        values = traces_ref[:, window, :]
        centered = values - jnp.mean(values, axis=1, keepdims=True)
        mean_power = jnp.mean(centered * centered, axis=1, keepdims=True)
        flag_values = flags_ref[window : window + 1, :].astype(jnp.float32).reshape(plan.half, 1)
        pieces.append(centered * lax.rsqrt(mean_power + 1e-05) * flag_values)
    out_ref[...] = jnp.concatenate(pieces, axis=0).astype(jnp.bfloat16)


def lag_rows(plan, rows_ref, toeplitz_ref):
    span = plan.span
    me = lax.axis_index("blk")
    filler = jnp.zeros((1, span - plan.segment), jnp.float32)
    for window in range(plan.windows):
        at = slice(window * span, (window + 1) * span)
        for place, hop in enumerate(HOPS):
            for member in range(plan.own):
                channel = window * plan.half + (me ^ hop) * plan.own + member
                row = jnp.concatenate([rows_ref[pl.ds(channel, 1), :], filler], axis=1)
                row = jnp.broadcast_to(row, (GROUP, span))
                pieces = [
                    pltpu.roll(row, (MAXLAG - plan.fine_padded + 1 + lag) % span, 1, stride=1, stride_axis=0)
                    for lag in range(0, plan.fine_padded, GROUP)
                ]
                first = place * plan.height + member * plan.fine_padded
                toeplitz_ref[first : first + plan.fine_padded, at] = jnp.concatenate(pieces, axis=0).astype(
                    jnp.bfloat16
                )


def fill_columns(plan, values, columns_ref):
    span = plan.span
    filled = plan.coarse * plan.half
    if filled < plan.half_lanes:
        columns_ref[filled:, :] = jnp.zeros((plan.half_lanes - filled, columns_ref.shape[1]), jnp.bfloat16)
    filler = jnp.zeros((plan.half, span - plan.segment), jnp.float32)
    for window in range(plan.windows):
        at = slice(window * span, (window + 1) * span)
        rows = jnp.concatenate([values[window * plan.half : (window + 1) * plan.half], filler], axis=1)
        for step in range(plan.coarse):
            moved = pltpu.roll(rows, step * plan.fine, 1) if step else rows
            columns_ref[step * plan.half : (step + 1) * plan.half, at] = moved.astype(jnp.bfloat16)


def product(toeplitz_ref, columns_ref):
    return lax.dot_general(
        toeplitz_ref[...], columns_ref[...], (((1,), (1,)), ((), ())), preferred_element_type=jnp.float32
    )


def near_kernel(plan, *refs):
    mine_refs, (other_ref, sum_ref, rows_ref, toeplitz_ref, columns_ref) = refs[: plan.windows], refs[plan.windows :]
    for window, mine_ref in enumerate(mine_refs):
        rows_ref[window * plan.half : (window + 1) * plan.half, :] = mine_ref[...].astype(jnp.float32)
    lag_rows(plan, rows_ref, toeplitz_ref)
    fill_columns(plan, rows_ref[...], columns_ref.at[: plan.half_lanes])
    fill_columns(plan, other_ref[...].astype(jnp.float32), columns_ref.at[plan.half_lanes :])
    sum_ref[...] = product(toeplitz_ref, columns_ref)


def across_kernel(plan, mine_ref, prior_ref, toeplitz_ref, sum_ref, rows_ref, columns_ref):
    rows_ref[...] = mine_ref[...].astype(jnp.float32)
    lag_rows(plan, rows_ref, toeplitz_ref)
    fill_columns(plan, rows_ref[...], columns_ref)
    sum_ref[:, : plan.half_lanes] = prior_ref[:, : plan.half_lanes] + product(toeplitz_ref, columns_ref)
    sum_ref[:, plan.half_lanes :] = prior_ref[:, plan.half_lanes :]


def finish_kernel(plan, other_ref, toeplitz_ref, prior_ref, *refs):
    *out_refs, columns_ref = refs
    fill_columns(plan, other_ref[...].astype(jnp.float32), columns_ref)
    right = prior_ref[:, plan.half_lanes :] + product(toeplitz_ref, columns_ref)
    products = jnp.concatenate([prior_ref[:, : plan.half_lanes], right], axis=1)
    back = GROUP - 1 - lax.broadcasted_iota(jnp.int32, (GROUP, LANES), 0)
    for place in range(plan.targets):
        whole, rest = [], []
        for member in range(plan.own):
            last = place * plan.height + (member + 1) * plan.fine_padded
            tiles = [
                jnp.take_along_axis(products[last - lag - GROUP : last - lag], back, axis=0)
                for lag in range(0, plan.fine, GROUP)
            ]
            whole += tiles[: plan.whole_groups // GROUP]
            if plan.rest:
                rest.append(tiles[-1][: plan.rest])
        pieces = whole + rest
        if plan.rows > plan.own * plan.fine:
            pieces.append(jnp.zeros((plan.rows - plan.own * plan.fine, LANES), jnp.float32))
        out_refs[place][...] = jnp.concatenate(pieces, axis=0).astype(jnp.bfloat16)


def spread(plan, values):
    high = values.astype(jnp.bfloat16).astype(jnp.float32)
    low = values - high
    lane = lax.broadcasted_iota(jnp.int32, values.shape, 1)
    lane = jnp.where(lane >= plan.half_lanes, lane - plan.half_lanes, lane)
    up = pltpu.roll(low, plan.half, 1)
    down = pltpu.roll(low, LANES - plan.half, 1)
    pieces = []
    for step in range(plan.coarse):
        beside, moved = (step + 1, up) if step + 1 < plan.coarse else (step - 1, down)
        kept = jnp.where((lane >= step * plan.half) & (lane < (step + 1) * plan.half), high, 0.0)
        there = (lane >= beside * plan.half) & (lane < (beside + 1) * plan.half)
        pieces.append(jnp.where(there, moved, kept).astype(jnp.bfloat16))
    return jnp.concatenate(pieces, axis=0)


def choose_kernel(plan, index_ref, whitened_ref, chosen_ref, *same_refs):
    whitened = whitened_ref[...].astype(jnp.float32)
    for window, same_ref in enumerate(same_refs):
        same_ref[...] = whitened[window * plan.half : (window + 1) * plan.half].astype(jnp.bfloat16)
    first = lax.axis_index("src") * plan.half
    index = index_ref[...] - first
    index = jnp.where(index < 0, index + plan.channels, index)
    lane = jnp.where(index >= plan.half, index - plan.half + plan.half_lanes, index)
    at_column = lax.broadcasted_iota(jnp.int32, (LANES, plan.source_count), 0)
    chosen = jnp.zeros((LANES, plan.source_count), jnp.bool_)
    for step in range(plan.coarse):
        chosen = chosen | (at_column == lane + step * plan.half)
    chosen_ref[...] = chosen.astype(jnp.float32).astype(jnp.bfloat16)


def expand_kernel(plan, chosen_ref, *refs):
    *arrived_refs, out_hbm, out_ref, sems = refs
    total = sum(ref[...].astype(jnp.float32) for ref in arrived_refs) * plan.norm_factor
    chosen = chosen_ref[...]
    filler = jnp.zeros((plan.fine_padded - plan.fine, LANES), jnp.float32)
    copies = []
    for member in range(plan.own):
        rest = plan.own * plan.whole_groups + member * plan.rest
        rows = jnp.concatenate(
            [
                total[member * plan.whole_groups : (member + 1) * plan.whole_groups],
                total[rest : rest + plan.rest],
                filler,
            ],
            axis=0,
        )
        expanded = jnp.dot(spread(plan, rows), chosen, preferred_element_type=jnp.float32)
        for step in range(plan.coarse):
            start = step * plan.fine
            count = min(plan.fine, LAG_COUNT - start)
            first = step * plan.fine_padded
            out_ref[member, start : start + count, :] = expanded[first : first + count]
        copies.append(pltpu.make_async_copy(out_ref.at[member], out_hbm.at[member], sems.at[member]))
        copies[-1].start()
    for copy in copies:
        copy.wait()


def few_channels(plan, traces, valid_flags, source_index):
    vmem = pl.BlockSpec(memory_space=pltpu.VMEM)
    params = pltpu.CompilerParams(vmem_limit_bytes=32 * 1024 * 1024)
    packed_rows = plan.windows * plan.half
    flags = valid_flags.T

    def swap_cores(array):
        return lax.ppermute(array, "src", [(0, 1), (1, 0)])

    def swap_blk(array, hop):
        pairs = [
            (place * plan.src_size + core, (place ^ hop) * plan.src_size + 1 - core)
            for place in range(plan.blk_size)
            for core in range(plan.src_size)
        ]
        return lax.ppermute(array, ("blk", "src"), pairs)

    whitened = pl.pallas_call(
        functools.partial(whiten_kernel, plan),
        out_shape=pltpu.VMEM((packed_rows, plan.segment), jnp.bfloat16),
        in_specs=[pl.BlockSpec(memory_space=pl.ANY)] * 2,
        out_specs=vmem,
        scratch_shapes=[
            pltpu.VMEM(traces.shape, jnp.float32),
            pltpu.VMEM(flags.shape, jnp.int32),
            pltpu.SemaphoreType.DMA((IN_PARTS + 1,)),
        ],
        compiler_params=pltpu.CompilerParams(vmem_limit_bytes=60 * 1024 * 1024),
        name="whiten",
    )(traces, flags)

    height = plan.targets * plan.height
    width = plan.windows * plan.span
    rows = pltpu.VMEM((packed_rows, plan.segment), jnp.float32)
    toeplitz = (height, width)
    columns = (plan.half_lanes, width)
    sums = jax.ShapeDtypeStruct((height, LANES), jnp.float32)

    def call(kernel, name, operands, outputs, scratch=()):
        return pl.pallas_call(
            functools.partial(kernel, plan),
            out_shape=outputs,
            in_specs=[vmem] * len(operands),
            out_specs=[vmem] * len(outputs),
            scratch_shapes=scratch,
            compiler_params=params,
            name=name,
        )(*operands)

    across = swap_blk(whitened, plan.targets)
    chosen, *same = call(
        choose_kernel,
        "choose",
        (source_index.reshape(1, -1), whitened),
        (
            jax.ShapeDtypeStruct((LANES, plan.source_count), jnp.bfloat16),
            *[jax.ShapeDtypeStruct((plan.half, plan.segment), whitened.dtype)] * plan.windows,
        ),
    )
    (total,) = call(
        near_kernel,
        "near",
        (*[swap_cores(array) for array in same], whitened),
        (sums,),
        (rows, pltpu.VMEM(toeplitz, jnp.bfloat16), pltpu.VMEM((LANES, width), jnp.bfloat16)),
    )
    across, total = lax.optimization_barrier((across, total))
    across_other = swap_cores(across)
    lagged, total = call(
        across_kernel,
        "across",
        (across, total),
        (jax.ShapeDtypeStruct(toeplitz, jnp.bfloat16), sums),
        (rows, pltpu.VMEM(columns, jnp.bfloat16)),
    )
    sent = call(
        finish_kernel,
        "finish",
        (across_other, lagged, total),
        (jax.ShapeDtypeStruct((plan.rows, LANES), jnp.bfloat16),) * plan.targets,
        (pltpu.VMEM(columns, jnp.bfloat16),),
    )
    arrived = [swap_blk(array, hop) for array, hop in zip(sent, HOPS)]
    out_shape = (plan.own, LAG_COUNT, plan.source_count)
    return pl.pallas_call(
        functools.partial(expand_kernel, plan),
        out_shape=jax.ShapeDtypeStruct(out_shape, jnp.float32),
        in_specs=[vmem] * (1 + len(arrived)),
        out_specs=pl.BlockSpec(memory_space=pl.ANY),
        scratch_shapes=[pltpu.VMEM(out_shape, jnp.float32), pltpu.SemaphoreType.DMA((plan.own,))],
        compiler_params=params,
        name="expand",
    )(chosen, *arrived)


def body(traces, valid_flags, source_index):
    plan = Plan(
        traces.shape[0],
        traces.shape[1],
        traces.shape[2],
        lax.axis_size("blk"),
        lax.axis_size("src"),
        source_index.shape[0],
    )
    if plan.fits():
        return few_channels(plan, traces, valid_flags, source_index)
    return many_channels(traces, valid_flags, source_index)


def solution(mesh):
    in_specs = (P(("fibre", "src"), "blk", None), P(("fibre", "src"), "blk"), P())
    out_specs = P(("fibre", "src", "blk"), None, None)
    return jax.shard_map(body, mesh=mesh, in_specs=in_specs, out_specs=out_specs, check_vma=False)
```

```python
import functools
import math

import jax
import jax.numpy as jnp
from jax import lax
from jax.experimental import pallas as pl
from jax.experimental.pallas import tpu as pltpu
from jax.sharding import PartitionSpec as P

MAXLAG = 64
LAG_COUNT = 2 * MAXLAG + 1
LANES = 256
IN_PARTS = 4
GROUP = 8
HOPS = (3, 1, 2, 0)


def broadcast(value, axis, source):
    kept = jnp.where(lax.axis_index(axis) == source, value, 0).astype(value.dtype)
    return lax.psum(kept, axis)


def toeplitz_rows(group, lag_count, segment):
    shifted = jnp.stack(
        [group[:, :, lag_step : lag_step + segment] for lag_step in range(lag_count)], axis=1
    )
    return shifted.reshape(group.shape[0] * lag_count, -1)


def many_channels(traces, valid_flags, source_index):
    segment = traces.shape[2]
    centered = traces - jnp.mean(traces, axis=2, keepdims=True)
    mean_power = jnp.mean(centered * centered, axis=2, keepdims=True)
    flag_values = valid_flags[:, :, None].astype(jnp.float32)
    whitened = (centered * lax.rsqrt(mean_power + 1e-05) * flag_values).astype(jnp.bfloat16)
    pieces = []
    for owner in range(lax.axis_size("src")):
        pieces.append(broadcast(whitened, "src", owner))
    everyone = jnp.concatenate(pieces, axis=0)
    sources = jnp.take(everyone, source_index, axis=0)
    source_count = sources.shape[0]
    norm_factor = 1.0 / math.sqrt(traces.shape[1] * lax.axis_size("blk") * segment)
    own_rows = whitened.shape[0] // lax.axis_size("blk")
    flat_sources = sources.reshape(source_count, -1)
    padded = jnp.pad(whitened, ((0, 0), (0, 0), (MAXLAG, MAXLAG)))
    block_rows = math.gcd(lax.axis_size("blk") * own_rows, 16)
    grouped = padded.reshape(
        (lax.axis_size("blk") * own_rows // block_rows, block_rows) + padded.shape[1:]
    )

    def one_block(group):
        toeplitz = toeplitz_rows(group, LAG_COUNT, segment)
        products = lax.dot_general(
            toeplitz, flat_sources, (((1,), (1,)), ((), ())), preferred_element_type=jnp.float32
        )
        return (products * norm_factor).reshape(block_rows, LAG_COUNT, source_count)

    result = lax.map(one_block, grouped)
    return lax.psum_scatter(
        result.reshape(lax.axis_size("blk") * own_rows, LAG_COUNT, source_count),
        "blk",
        scatter_dimension=0,
        tiled=True,
    )


class Plan:
    def __init__(self, half, windows, segment, blk_size, src_size, source_count):
        self.half = half
        self.windows = windows
        self.segment = segment
        self.blk_size = blk_size
        self.src_size = src_size
        self.channels = half * src_size
        self.source_count = source_count
        self.half_lanes = LANES // 2
        self.coarse = self.half_lanes // half
        if self.coarse == 0:
            return
        self.fine = -(-LAG_COUNT // self.coarse)
        self.fine_padded = -(-self.fine // (2 * GROUP)) * 2 * GROUP
        self.own = half // blk_size
        reach = segment + (self.coarse - 1) * self.fine
        self.span = -(-max(reach, segment + 2 * MAXLAG) // 128) * 128
        self.whole_groups = self.fine // GROUP * GROUP
        self.rest = self.fine - self.whole_groups
        rows = self.own * self.fine
        self.rows = -(-rows // 16) * 16
        self.height = self.own * self.fine_padded
        self.targets = blk_size // 2
        self.norm_factor = 1.0 / math.sqrt(windows * blk_size * segment)

    def fits(self):
        return (
            self.coarse >= 2
            and self.src_size == 2
            and self.half % self.blk_size == 0
            and self.half % GROUP == 0
            and self.channels % 16 == 0
            and self.windows * self.half % 16 == 0
            and self.blk_size == 8
        )


def whiten_kernel(plan, traces_hbm, flags_hbm, out_ref, traces_ref, flags_ref, sems):
    part = plan.half // IN_PARTS
    copies = [pltpu.make_async_copy(flags_hbm, flags_ref, sems.at[IN_PARTS])]
    for index in range(IN_PARTS):
        at = pl.ds(index * part, part)
        copies.append(pltpu.make_async_copy(traces_hbm.at[at], traces_ref.at[at], sems.at[index]))
    for copy in copies:
        copy.start()
    for copy in copies:
        copy.wait()
    pieces = []
    for window in range(plan.windows):
        values = traces_ref[:, window, :]
        centered = values - jnp.mean(values, axis=1, keepdims=True)
        mean_power = jnp.mean(centered * centered, axis=1, keepdims=True)
        flag_values = flags_ref[window : window + 1, :].astype(jnp.float32).reshape(plan.half, 1)
        pieces.append(centered * lax.rsqrt(mean_power + 1e-05) * flag_values)
    out_ref[...] = jnp.concatenate(pieces, axis=0).astype(jnp.bfloat16)


def lag_rows(plan, rows_ref, toeplitz_ref):
    span = plan.span
    me = lax.axis_index("blk")
    filler = jnp.zeros((1, span - plan.segment), jnp.float32)
    for window in range(plan.windows):
        at = slice(window * span, (window + 1) * span)
        for place, hop in enumerate(HOPS):
            for member in range(plan.own):
                channel = window * plan.half + (me ^ hop) * plan.own + member
                row = jnp.concatenate([rows_ref[pl.ds(channel, 1), :], filler], axis=1)
                row = jnp.broadcast_to(row, (GROUP, span))
                pieces = [
                    pltpu.roll(row, (MAXLAG - plan.fine_padded + 1 + lag) % span, 1, stride=1, stride_axis=0)
                    for lag in range(0, plan.fine_padded, GROUP)
                ]
                first = place * plan.height + member * plan.fine_padded
                toeplitz_ref[first : first + plan.fine_padded, at] = jnp.concatenate(pieces, axis=0).astype(
                    jnp.bfloat16
                )


def fill_columns(plan, values, columns_ref):
    span = plan.span
    filled = plan.coarse * plan.half
    if filled < plan.half_lanes:
        columns_ref[filled:, :] = jnp.zeros((plan.half_lanes - filled, columns_ref.shape[1]), jnp.bfloat16)
    filler = jnp.zeros((plan.half, span - plan.segment), jnp.float32)
    for window in range(plan.windows):
        at = slice(window * span, (window + 1) * span)
        rows = jnp.concatenate([values[window * plan.half : (window + 1) * plan.half], filler], axis=1)
        for step in range(plan.coarse):
            moved = pltpu.roll(rows, step * plan.fine, 1) if step else rows
            columns_ref[step * plan.half : (step + 1) * plan.half, at] = moved.astype(jnp.bfloat16)


def product(toeplitz_ref, columns_ref):
    return lax.dot_general(
        toeplitz_ref[...], columns_ref[...], (((1,), (1,)), ((), ())), preferred_element_type=jnp.float32
    )


def near_kernel(plan, *refs):
    mine_refs, (other_ref, sum_ref, rows_ref, toeplitz_ref, columns_ref) = refs[: plan.windows], refs[plan.windows :]
    for window, mine_ref in enumerate(mine_refs):
        rows_ref[window * plan.half : (window + 1) * plan.half, :] = mine_ref[...].astype(jnp.float32)
    lag_rows(plan, rows_ref, toeplitz_ref)
    fill_columns(plan, rows_ref[...], columns_ref.at[: plan.half_lanes])
    fill_columns(plan, other_ref[...].astype(jnp.float32), columns_ref.at[plan.half_lanes :])
    sum_ref[...] = product(toeplitz_ref, columns_ref)


def across_kernel(plan, mine_ref, prior_ref, toeplitz_ref, sum_ref, rows_ref, columns_ref):
    rows_ref[...] = mine_ref[...].astype(jnp.float32)
    lag_rows(plan, rows_ref, toeplitz_ref)
    fill_columns(plan, rows_ref[...], columns_ref)
    sum_ref[:, : plan.half_lanes] = prior_ref[:, : plan.half_lanes] + product(toeplitz_ref, columns_ref)
    sum_ref[:, plan.half_lanes :] = prior_ref[:, plan.half_lanes :]


def finish_kernel(plan, other_ref, toeplitz_ref, prior_ref, *refs):
    *out_refs, columns_ref = refs
    fill_columns(plan, other_ref[...].astype(jnp.float32), columns_ref)
    right = prior_ref[:, plan.half_lanes :] + product(toeplitz_ref, columns_ref)
    products = jnp.concatenate([prior_ref[:, : plan.half_lanes], right], axis=1)
    back = GROUP - 1 - lax.broadcasted_iota(jnp.int32, (GROUP, LANES), 0)
    for place in range(plan.targets):
        whole, rest = [], []
        for member in range(plan.own):
            last = place * plan.height + (member + 1) * plan.fine_padded
            tiles = [
                jnp.take_along_axis(products[last - lag - GROUP : last - lag], back, axis=0)
                for lag in range(0, plan.fine, GROUP)
            ]
            whole += tiles[: plan.whole_groups // GROUP]
            if plan.rest:
                rest.append(tiles[-1][: plan.rest])
        pieces = whole + rest
        if plan.rows > plan.own * plan.fine:
            pieces.append(jnp.zeros((plan.rows - plan.own * plan.fine, LANES), jnp.float32))
        out_refs[place][...] = jnp.concatenate(pieces, axis=0).astype(jnp.bfloat16)


def spread(plan, values):
    high = values.astype(jnp.bfloat16).astype(jnp.float32)
    low = values - high
    lane = lax.broadcasted_iota(jnp.int32, values.shape, 1)
    lane = jnp.where(lane >= plan.half_lanes, lane - plan.half_lanes, lane)
    up = pltpu.roll(low, plan.half, 1)
    down = pltpu.roll(low, LANES - plan.half, 1)
    pieces = []
    for step in range(plan.coarse):
        beside, moved = (step + 1, up) if step + 1 < plan.coarse else (step - 1, down)
        kept = jnp.where((lane >= step * plan.half) & (lane < (step + 1) * plan.half), high, 0.0)
        there = (lane >= beside * plan.half) & (lane < (beside + 1) * plan.half)
        pieces.append(jnp.where(there, moved, kept).astype(jnp.bfloat16))
    return jnp.concatenate(pieces, axis=0)


def choose_kernel(plan, index_ref, whitened_ref, chosen_ref, *same_refs):
    whitened = whitened_ref[...].astype(jnp.float32)
    for window, same_ref in enumerate(same_refs):
        same_ref[...] = whitened[window * plan.half : (window + 1) * plan.half].astype(jnp.bfloat16)
    first = lax.axis_index("src") * plan.half
    index = index_ref[...] - first
    index = jnp.where(index < 0, index + plan.channels, index)
    lane = jnp.where(index >= plan.half, index - plan.half + plan.half_lanes, index)
    at_column = lax.broadcasted_iota(jnp.int32, (LANES, plan.source_count), 0)
    chosen = jnp.zeros((LANES, plan.source_count), jnp.bool_)
    for step in range(plan.coarse):
        chosen = chosen | (at_column == lane + step * plan.half)
    chosen_ref[...] = chosen.astype(jnp.float32).astype(jnp.bfloat16)


def expand_kernel(plan, chosen_ref, *refs):
    *arrived_refs, out_hbm, out_ref, sems = refs
    total = sum(ref[...].astype(jnp.float32) for ref in arrived_refs) * plan.norm_factor
    chosen = chosen_ref[...]
    filler = jnp.zeros((plan.fine_padded - plan.fine, LANES), jnp.float32)
    copies = []
    for member in range(plan.own):
        rest = plan.own * plan.whole_groups + member * plan.rest
        rows = jnp.concatenate(
            [
                total[member * plan.whole_groups : (member + 1) * plan.whole_groups],
                total[rest : rest + plan.rest],
                filler,
            ],
            axis=0,
        )
        expanded = jnp.dot(spread(plan, rows), chosen, preferred_element_type=jnp.float32)
        for step in range(plan.coarse):
            start = step * plan.fine
            count = min(plan.fine, LAG_COUNT - start)
            first = step * plan.fine_padded
            out_ref[member, start : start + count, :] = expanded[first : first + count]
        copies.append(pltpu.make_async_copy(out_ref.at[member], out_hbm.at[member], sems.at[member]))
        copies[-1].start()
    for copy in copies:
        copy.wait()


def few_channels(plan, traces, valid_flags, source_index):
    vmem = pl.BlockSpec(memory_space=pltpu.VMEM)
    params = pltpu.CompilerParams(vmem_limit_bytes=32 * 1024 * 1024)
    packed_rows = plan.windows * plan.half
    flags = valid_flags.T

    def swap_cores(array):
        return lax.ppermute(array, "src", [(0, 1), (1, 0)])

    def swap_blk(array, hop):
        pairs = [
            (place * plan.src_size + core, (place ^ hop) * plan.src_size + 1 - core)
            for place in range(plan.blk_size)
            for core in range(plan.src_size)
        ]
        return lax.ppermute(array, ("blk", "src"), pairs)

    whitened = pl.pallas_call(
        functools.partial(whiten_kernel, plan),
        out_shape=pltpu.VMEM((packed_rows, plan.segment), jnp.bfloat16),
        in_specs=[pl.BlockSpec(memory_space=pl.ANY)] * 2,
        out_specs=vmem,
        scratch_shapes=[
            pltpu.VMEM(traces.shape, jnp.float32),
            pltpu.VMEM(flags.shape, jnp.int32),
            pltpu.SemaphoreType.DMA((IN_PARTS + 1,)),
        ],
        compiler_params=pltpu.CompilerParams(vmem_limit_bytes=60 * 1024 * 1024),
        name="whiten",
    )(traces, flags)

    height = plan.targets * plan.height
    width = plan.windows * plan.span
    rows = pltpu.VMEM((packed_rows, plan.segment), jnp.float32)
    toeplitz = (height, width)
    columns = (plan.half_lanes, width)
    sums = jax.ShapeDtypeStruct((height, LANES), jnp.float32)

    def call(kernel, name, operands, outputs, scratch=()):
        return pl.pallas_call(
            functools.partial(kernel, plan),
            out_shape=outputs,
            in_specs=[vmem] * len(operands),
            out_specs=[vmem] * len(outputs),
            scratch_shapes=scratch,
            compiler_params=params,
            name=name,
        )(*operands)

    across = swap_blk(whitened, plan.blk_size - 2)
    chosen, *same = call(
        choose_kernel,
        "choose",
        (source_index.reshape(1, -1), whitened),
        (
            jax.ShapeDtypeStruct((LANES, plan.source_count), jnp.bfloat16),
            *[jax.ShapeDtypeStruct((plan.half, plan.segment), whitened.dtype)] * plan.windows,
        ),
    )
    (total,) = call(
        near_kernel,
        "near",
        (*[swap_cores(array) for array in same], whitened),
        (sums,),
        (rows, pltpu.VMEM(toeplitz, jnp.bfloat16), pltpu.VMEM((LANES, width), jnp.bfloat16)),
    )
    across, total = lax.optimization_barrier((across, total))
    across_other = swap_cores(across)
    lagged, total = call(
        across_kernel,
        "across",
        (across, total),
        (jax.ShapeDtypeStruct(toeplitz, jnp.bfloat16), sums),
        (rows, pltpu.VMEM(columns, jnp.bfloat16)),
    )
    sent = call(
        finish_kernel,
        "finish",
        (across_other, lagged, total),
        (jax.ShapeDtypeStruct((plan.rows, LANES), jnp.bfloat16),) * plan.targets,
        (pltpu.VMEM(columns, jnp.bfloat16),),
    )
    arrived = [swap_blk(array, hop) for array, hop in zip(sent, HOPS)]
    out_shape = (plan.own, LAG_COUNT, plan.source_count)
    return pl.pallas_call(
        functools.partial(expand_kernel, plan),
        out_shape=jax.ShapeDtypeStruct(out_shape, jnp.float32),
        in_specs=[vmem] * (1 + len(arrived)),
        out_specs=pl.BlockSpec(memory_space=pl.ANY),
        scratch_shapes=[pltpu.VMEM(out_shape, jnp.float32), pltpu.SemaphoreType.DMA((plan.own,))],
        compiler_params=params,
        name="expand",
    )(chosen, *arrived)


def body(traces, valid_flags, source_index):
    plan = Plan(
        traces.shape[0],
        traces.shape[1],
        traces.shape[2],
        lax.axis_size("blk"),
        lax.axis_size("src"),
        source_index.shape[0],
    )
    if plan.fits():
        return few_channels(plan, traces, valid_flags, source_index)
    return many_channels(traces, valid_flags, source_index)


def solution(mesh):
    in_specs = (P(("fibre", "src"), "blk", None), P(("fibre", "src"), "blk"), P())
    out_specs = P(("fibre", "src", "blk"), None, None)
    return jax.shard_map(body, mesh=mesh, in_specs=in_specs, out_specs=out_specs, check_vma=False)
```

```python
import functools
import math

import jax
import jax.numpy as jnp
from jax import lax
from jax.experimental import pallas as pl
from jax.experimental.pallas import tpu as pltpu
from jax.sharding import PartitionSpec as P

MAXLAG = 64
LAG_COUNT = 2 * MAXLAG + 1
LANES = 256
IN_PARTS = 4
GROUP = 8
HOPS = (3, 1, 2, 0)


def broadcast(value, axis, source):
    kept = jnp.where(lax.axis_index(axis) == source, value, 0).astype(value.dtype)
    return lax.psum(kept, axis)


def toeplitz_rows(group, lag_count, segment):
    shifted = jnp.stack(
        [group[:, :, lag_step : lag_step + segment] for lag_step in range(lag_count)], axis=1
    )
    return shifted.reshape(group.shape[0] * lag_count, -1)


def many_channels(traces, valid_flags, source_index):
    segment = traces.shape[2]
    centered = traces - jnp.mean(traces, axis=2, keepdims=True)
    mean_power = jnp.mean(centered * centered, axis=2, keepdims=True)
    flag_values = valid_flags[:, :, None].astype(jnp.float32)
    whitened = (centered * lax.rsqrt(mean_power + 1e-05) * flag_values).astype(jnp.bfloat16)
    pieces = []
    for owner in range(lax.axis_size("src")):
        pieces.append(broadcast(whitened, "src", owner))
    everyone = jnp.concatenate(pieces, axis=0)
    sources = jnp.take(everyone, source_index, axis=0)
    source_count = sources.shape[0]
    norm_factor = 1.0 / math.sqrt(traces.shape[1] * lax.axis_size("blk") * segment)
    own_rows = whitened.shape[0] // lax.axis_size("blk")
    flat_sources = sources.reshape(source_count, -1)
    padded = jnp.pad(whitened, ((0, 0), (0, 0), (MAXLAG, MAXLAG)))
    block_rows = math.gcd(lax.axis_size("blk") * own_rows, 16)
    grouped = padded.reshape(
        (lax.axis_size("blk") * own_rows // block_rows, block_rows) + padded.shape[1:]
    )

    def one_block(group):
        toeplitz = toeplitz_rows(group, LAG_COUNT, segment)
        products = lax.dot_general(
            toeplitz, flat_sources, (((1,), (1,)), ((), ())), preferred_element_type=jnp.float32
        )
        return (products * norm_factor).reshape(block_rows, LAG_COUNT, source_count)

    result = lax.map(one_block, grouped)
    return lax.psum_scatter(
        result.reshape(lax.axis_size("blk") * own_rows, LAG_COUNT, source_count),
        "blk",
        scatter_dimension=0,
        tiled=True,
    )


class Plan:
    def __init__(self, half, windows, segment, blk_size, src_size, source_count):
        self.half = half
        self.windows = windows
        self.segment = segment
        self.blk_size = blk_size
        self.src_size = src_size
        self.channels = half * src_size
        self.source_count = source_count
        self.half_lanes = LANES // 2
        self.coarse = self.half_lanes // half
        if self.coarse == 0:
            return
        self.fine = -(-LAG_COUNT // self.coarse)
        self.fine_padded = -(-self.fine // (2 * GROUP)) * 2 * GROUP
        self.own = half // blk_size
        reach = segment + (self.coarse - 1) * self.fine
        self.span = -(-max(reach, segment + 2 * MAXLAG) // 128) * 128
        self.whole_groups = self.fine // GROUP * GROUP
        self.rest = self.fine - self.whole_groups
        rows = self.own * self.fine
        self.rows = -(-rows // 16) * 16
        self.height = self.own * self.fine_padded
        self.targets = blk_size // 2
        self.norm_factor = 1.0 / math.sqrt(windows * blk_size * segment)

    def fits(self):
        return (
            self.coarse >= 2
            and self.src_size == 2
            and self.half % self.blk_size == 0
            and self.half % GROUP == 0
            and self.channels % 16 == 0
            and self.windows * self.half % 16 == 0
            and self.blk_size == 8
        )


def whiten_kernel(plan, traces_hbm, flags_hbm, out_ref, traces_ref, flags_ref, sems):
    part = plan.half // IN_PARTS
    copies = [pltpu.make_async_copy(flags_hbm, flags_ref, sems.at[IN_PARTS])]
    for index in range(IN_PARTS):
        at = pl.ds(index * part, part)
        copies.append(pltpu.make_async_copy(traces_hbm.at[at], traces_ref.at[at], sems.at[index]))
    for copy in copies:
        copy.start()
    for copy in copies:
        copy.wait()
    pieces = []
    for window in range(plan.windows):
        values = traces_ref[:, window, :]
        centered = values - jnp.mean(values, axis=1, keepdims=True)
        mean_power = jnp.mean(centered * centered, axis=1, keepdims=True)
        flag_values = flags_ref[window : window + 1, :].astype(jnp.float32).reshape(plan.half, 1)
        pieces.append(centered * lax.rsqrt(mean_power + 1e-05) * flag_values)
    out_ref[...] = jnp.concatenate(pieces, axis=0).astype(jnp.bfloat16)


def lag_rows(plan, rows_ref, toeplitz_ref):
    span = plan.span
    me = lax.axis_index("blk")
    filler = jnp.zeros((1, span - plan.segment), jnp.float32)
    for window in range(plan.windows):
        at = slice(window * span, (window + 1) * span)
        for place, hop in enumerate(HOPS):
            for member in range(plan.own):
                channel = window * plan.half + (me ^ hop) * plan.own + member
                row = jnp.concatenate([rows_ref[pl.ds(channel, 1), :], filler], axis=1)
                row = jnp.broadcast_to(row, (GROUP, span))
                pieces = [
                    pltpu.roll(row, (MAXLAG - plan.fine_padded + 1 + lag) % span, 1, stride=1, stride_axis=0)
                    for lag in range(0, plan.fine_padded, GROUP)
                ]
                first = place * plan.height + member * plan.fine_padded
                toeplitz_ref[first : first + plan.fine_padded, at] = jnp.concatenate(pieces, axis=0).astype(
                    jnp.bfloat16
                )


def fill_columns(plan, values, columns_ref):
    span = plan.span
    filler = jnp.zeros((plan.half, span - plan.segment), jnp.float32)
    spare = jnp.zeros((plan.half_lanes - plan.coarse * plan.half, span), jnp.float32)
    for window in range(plan.windows):
        rows = jnp.concatenate([values[window * plan.half : (window + 1) * plan.half], filler], axis=1)
        pieces = [rows] + [pltpu.roll(rows, step * plan.fine, 1) for step in range(1, plan.coarse)]
        if spare.shape[0]:
            pieces.append(spare)
        columns_ref[:, window * span : (window + 1) * span] = jnp.concatenate(pieces, axis=0).astype(jnp.bfloat16)


def product(toeplitz_ref, columns_ref):
    return lax.dot_general(
        toeplitz_ref[...], columns_ref[...], (((1,), (1,)), ((), ())), preferred_element_type=jnp.float32
    )


def near_kernel(plan, *refs):
    mine_refs, (other_ref, sum_ref, rows_ref, toeplitz_ref, columns_ref) = refs[: plan.windows], refs[plan.windows :]
    for window, mine_ref in enumerate(mine_refs):
        rows_ref[window * plan.half : (window + 1) * plan.half, :] = mine_ref[...].astype(jnp.float32)
    lag_rows(plan, rows_ref, toeplitz_ref)
    fill_columns(plan, rows_ref[...], columns_ref.at[: plan.half_lanes])
    fill_columns(plan, other_ref[...].astype(jnp.float32), columns_ref.at[plan.half_lanes :])
    sum_ref[...] = product(toeplitz_ref, columns_ref)


def across_kernel(plan, mine_ref, prior_ref, toeplitz_ref, left_ref, right_ref, rows_ref, columns_ref):
    rows_ref[...] = mine_ref[...].astype(jnp.float32)
    lag_rows(plan, rows_ref, toeplitz_ref)
    fill_columns(plan, rows_ref[...], columns_ref)
    left = prior_ref[:, : plan.half_lanes] + product(toeplitz_ref, columns_ref)
    for place, block in enumerate(pack(plan, left)):
        left_ref[place * plan.rows : (place + 1) * plan.rows, :] = block
    right_ref[...] = prior_ref[:, plan.half_lanes :]


def pack(plan, products):
    width = products.shape[1]
    back = GROUP - 1 - lax.broadcasted_iota(jnp.int32, (GROUP, width), 0)
    packed = []
    for place in range(plan.targets):
        whole, rest = [], []
        for member in range(plan.own):
            last = place * plan.height + (member + 1) * plan.fine_padded
            tiles = [
                jnp.take_along_axis(products[last - lag - GROUP : last - lag], back, axis=0)
                for lag in range(0, plan.fine, GROUP)
            ]
            whole += tiles[: plan.whole_groups // GROUP]
            if plan.rest:
                rest.append(tiles[-1][: plan.rest])
        pieces = whole + rest
        if plan.rows > plan.own * plan.fine:
            pieces.append(jnp.zeros((plan.rows - plan.own * plan.fine, width), jnp.float32))
        packed.append(jnp.concatenate(pieces, axis=0))
    return packed


def finish_kernel(plan, other_ref, toeplitz_ref, left_ref, right_ref, *refs):
    *out_refs, columns_ref = refs
    fill_columns(plan, other_ref[...].astype(jnp.float32), columns_ref)
    right = pack(plan, right_ref[...] + product(toeplitz_ref, columns_ref))
    for place, out_ref in enumerate(out_refs):
        rows = slice(place * plan.rows, (place + 1) * plan.rows)
        out_ref[...] = jnp.concatenate([left_ref[rows, :], right[place]], axis=1).astype(jnp.bfloat16)


def spread(plan, values):
    high = values.astype(jnp.bfloat16).astype(jnp.float32)
    low = values - high
    lane = lax.broadcasted_iota(jnp.int32, values.shape, 1)
    lane = jnp.where(lane >= plan.half_lanes, lane - plan.half_lanes, lane)
    up = pltpu.roll(low, plan.half, 1)
    down = pltpu.roll(low, LANES - plan.half, 1)
    pieces = []
    for step in range(plan.coarse):
        beside, moved = (step + 1, up) if step + 1 < plan.coarse else (step - 1, down)
        kept = jnp.where((lane >= step * plan.half) & (lane < (step + 1) * plan.half), high, 0.0)
        there = (lane >= beside * plan.half) & (lane < (beside + 1) * plan.half)
        pieces.append(jnp.where(there, moved, kept).astype(jnp.bfloat16))
    return jnp.concatenate(pieces, axis=0)


def choose_kernel(plan, index_ref, whitened_ref, chosen_ref, *same_refs):
    whitened = whitened_ref[...].astype(jnp.float32)
    for window, same_ref in enumerate(same_refs):
        same_ref[...] = whitened[window * plan.half : (window + 1) * plan.half].astype(jnp.bfloat16)
    first = lax.axis_index("src") * plan.half
    index = index_ref[...] - first
    index = jnp.where(index < 0, index + plan.channels, index)
    lane = jnp.where(index >= plan.half, index - plan.half + plan.half_lanes, index)
    at_column = lax.broadcasted_iota(jnp.int32, (LANES, plan.source_count), 0)
    chosen = jnp.zeros((LANES, plan.source_count), jnp.bool_)
    for step in range(plan.coarse):
        chosen = chosen | (at_column == lane + step * plan.half)
    chosen_ref[...] = chosen.astype(jnp.float32).astype(jnp.bfloat16)


def expand_kernel(plan, chosen_ref, *refs):
    *arrived_refs, out_hbm, out_ref, sems = refs
    total = sum(ref[...].astype(jnp.float32) for ref in arrived_refs) * plan.norm_factor
    chosen = chosen_ref[...]
    filler = jnp.zeros((plan.fine_padded - plan.fine, LANES), jnp.float32)
    copies = []
    for member in range(plan.own):
        rest = plan.own * plan.whole_groups + member * plan.rest
        rows = jnp.concatenate(
            [
                total[member * plan.whole_groups : (member + 1) * plan.whole_groups],
                total[rest : rest + plan.rest],
                filler,
            ],
            axis=0,
        )
        expanded = jnp.dot(spread(plan, rows), chosen, preferred_element_type=jnp.float32)
        for step in range(plan.coarse):
            start = step * plan.fine
            count = min(plan.fine, LAG_COUNT - start)
            first = step * plan.fine_padded
            out_ref[member, start : start + count, :] = expanded[first : first + count]
        copies.append(pltpu.make_async_copy(out_ref.at[member], out_hbm.at[member], sems.at[member]))
        copies[-1].start()
    for copy in copies:
        copy.wait()


def few_channels(plan, traces, valid_flags, source_index):
    vmem = pl.BlockSpec(memory_space=pltpu.VMEM)
    params = pltpu.CompilerParams(vmem_limit_bytes=32 * 1024 * 1024)
    packed_rows = plan.windows * plan.half
    flags = valid_flags.T

    def swap_cores(array):
        return lax.ppermute(array, "src", [(0, 1), (1, 0)])

    def swap_blk(array, hop):
        pairs = [
            (place * plan.src_size + core, (place ^ hop) * plan.src_size + 1 - core)
            for place in range(plan.blk_size)
            for core in range(plan.src_size)
        ]
        return lax.ppermute(array, ("blk", "src"), pairs)

    whitened = pl.pallas_call(
        functools.partial(whiten_kernel, plan),
        out_shape=pltpu.VMEM((packed_rows, plan.segment), jnp.bfloat16),
        in_specs=[pl.BlockSpec(memory_space=pl.ANY)] * 2,
        out_specs=vmem,
        scratch_shapes=[
            pltpu.VMEM(traces.shape, jnp.float32),
            pltpu.VMEM(flags.shape, jnp.int32),
            pltpu.SemaphoreType.DMA((IN_PARTS + 1,)),
        ],
        compiler_params=pltpu.CompilerParams(vmem_limit_bytes=60 * 1024 * 1024),
        name="whiten",
    )(traces, flags)

    height = plan.targets * plan.height
    width = plan.windows * plan.span
    rows = pltpu.VMEM((packed_rows, plan.segment), jnp.float32)
    toeplitz = (height, width)
    columns = (plan.half_lanes, width)
    sums = jax.ShapeDtypeStruct((height, LANES), jnp.float32)

    def call(kernel, name, operands, outputs, scratch=()):
        return pl.pallas_call(
            functools.partial(kernel, plan),
            out_shape=outputs,
            in_specs=[vmem] * len(operands),
            out_specs=[vmem] * len(outputs),
            scratch_shapes=scratch,
            compiler_params=params,
            name=name,
        )(*operands)

    across = swap_blk(whitened, plan.targets)
    chosen, *same = call(
        choose_kernel,
        "choose",
        (source_index.reshape(1, -1), whitened),
        (
            jax.ShapeDtypeStruct((LANES, plan.source_count), jnp.bfloat16),
            *[jax.ShapeDtypeStruct((plan.half, plan.segment), whitened.dtype)] * plan.windows,
        ),
    )
    (total,) = call(
        near_kernel,
        "near",
        (*[swap_cores(array) for array in same], whitened),
        (sums,),
        (rows, pltpu.VMEM(toeplitz, jnp.bfloat16), pltpu.VMEM((LANES, width), jnp.bfloat16)),
    )
    across, total = lax.optimization_barrier((across, total))
    across_other = swap_cores(across)
    lagged, left, right = call(
        across_kernel,
        "across",
        (across, total),
        (
            jax.ShapeDtypeStruct(toeplitz, jnp.bfloat16),
            jax.ShapeDtypeStruct((plan.targets * plan.rows, plan.half_lanes), jnp.float32),
            jax.ShapeDtypeStruct((height, plan.half_lanes), jnp.float32),
        ),
        (rows, pltpu.VMEM(columns, jnp.bfloat16)),
    )
    sent = call(
        finish_kernel,
        "finish",
        (across_other, lagged, left, right),
        (jax.ShapeDtypeStruct((plan.rows, LANES), jnp.bfloat16),) * plan.targets,
        (pltpu.VMEM(columns, jnp.bfloat16),),
    )
    arrived = [swap_blk(array, hop) for array, hop in zip(sent, HOPS)]
    out_shape = (plan.own, LAG_COUNT, plan.source_count)
    return pl.pallas_call(
        functools.partial(expand_kernel, plan),
        out_shape=jax.ShapeDtypeStruct(out_shape, jnp.float32),
        in_specs=[vmem] * (1 + len(arrived)),
        out_specs=pl.BlockSpec(memory_space=pl.ANY),
        scratch_shapes=[pltpu.VMEM(out_shape, jnp.float32), pltpu.SemaphoreType.DMA((plan.own,))],
        compiler_params=params,
        name="expand",
    )(chosen, *arrived)


def body(traces, valid_flags, source_index):
    plan = Plan(
        traces.shape[0],
        traces.shape[1],
        traces.shape[2],
        lax.axis_size("blk"),
        lax.axis_size("src"),
        source_index.shape[0],
    )
    if plan.fits():
        return few_channels(plan, traces, valid_flags, source_index)
    return many_channels(traces, valid_flags, source_index)


def solution(mesh):
    in_specs = (P(("fibre", "src"), "blk", None), P(("fibre", "src"), "blk"), P())
    out_specs = P(("fibre", "src", "blk"), None, None)
    return jax.shard_map(body, mesh=mesh, in_specs=in_specs, out_specs=out_specs, check_vma=False)
```

```python
import functools
import math

import jax
import jax.numpy as jnp
from jax import lax
from jax.experimental import pallas as pl
from jax.experimental.pallas import tpu as pltpu
from jax.sharding import PartitionSpec as P

MAXLAG = 64
LAG_COUNT = 2 * MAXLAG + 1
LANES = 256
IN_PARTS = 4
GROUP = 8
HOPS = (3, 2, 1, 0)


def broadcast(value, axis, source):
    kept = jnp.where(lax.axis_index(axis) == source, value, 0).astype(value.dtype)
    return lax.psum(kept, axis)


def toeplitz_rows(group, lag_count, segment):
    shifted = jnp.stack(
        [group[:, :, lag_step : lag_step + segment] for lag_step in range(lag_count)], axis=1
    )
    return shifted.reshape(group.shape[0] * lag_count, -1)


def many_channels(traces, valid_flags, source_index):
    segment = traces.shape[2]
    centered = traces - jnp.mean(traces, axis=2, keepdims=True)
    mean_power = jnp.mean(centered * centered, axis=2, keepdims=True)
    flag_values = valid_flags[:, :, None].astype(jnp.float32)
    whitened = (centered * lax.rsqrt(mean_power + 1e-05) * flag_values).astype(jnp.bfloat16)
    pieces = []
    for owner in range(lax.axis_size("src")):
        pieces.append(broadcast(whitened, "src", owner))
    everyone = jnp.concatenate(pieces, axis=0)
    sources = jnp.take(everyone, source_index, axis=0)
    source_count = sources.shape[0]
    norm_factor = 1.0 / math.sqrt(traces.shape[1] * lax.axis_size("blk") * segment)
    own_rows = whitened.shape[0] // lax.axis_size("blk")
    flat_sources = sources.reshape(source_count, -1)
    padded = jnp.pad(whitened, ((0, 0), (0, 0), (MAXLAG, MAXLAG)))
    block_rows = math.gcd(lax.axis_size("blk") * own_rows, 16)
    grouped = padded.reshape(
        (lax.axis_size("blk") * own_rows // block_rows, block_rows) + padded.shape[1:]
    )

    def one_block(group):
        toeplitz = toeplitz_rows(group, LAG_COUNT, segment)
        products = lax.dot_general(
            toeplitz, flat_sources, (((1,), (1,)), ((), ())), preferred_element_type=jnp.float32
        )
        return (products * norm_factor).reshape(block_rows, LAG_COUNT, source_count)

    result = lax.map(one_block, grouped)
    return lax.psum_scatter(
        result.reshape(lax.axis_size("blk") * own_rows, LAG_COUNT, source_count),
        "blk",
        scatter_dimension=0,
        tiled=True,
    )


class Plan:
    def __init__(self, half, windows, segment, blk_size, src_size, source_count):
        self.half = half
        self.windows = windows
        self.segment = segment
        self.blk_size = blk_size
        self.src_size = src_size
        self.channels = half * src_size
        self.source_count = source_count
        self.half_lanes = LANES // 2
        self.coarse = self.half_lanes // half
        if self.coarse == 0:
            return
        self.fine = -(-LAG_COUNT // self.coarse)
        self.fine_padded = -(-self.fine // (2 * GROUP)) * 2 * GROUP
        self.own = half // blk_size
        reach = segment + (self.coarse - 1) * self.fine
        self.span = -(-max(reach, segment + 2 * MAXLAG) // 128) * 128
        self.whole_groups = self.fine // GROUP * GROUP
        self.rest = self.fine - self.whole_groups
        rows = self.own * self.fine
        self.rows = -(-rows // 16) * 16
        self.height = self.own * self.fine_padded
        self.targets = blk_size // 2
        self.norm_factor = 1.0 / math.sqrt(windows * blk_size * segment)

    def fits(self):
        return (
            self.coarse >= 2
            and self.src_size == 2
            and self.half % self.blk_size == 0
            and self.half % GROUP == 0
            and self.channels % 16 == 0
            and self.windows * self.half % 16 == 0
            and self.blk_size == 8
        )


def whiten_kernel(plan, traces_hbm, flags_hbm, out_ref, traces_ref, flags_ref, sems):
    part = plan.half // IN_PARTS
    copies = [pltpu.make_async_copy(flags_hbm, flags_ref, sems.at[IN_PARTS])]
    for index in range(IN_PARTS):
        at = pl.ds(index * part, part)
        copies.append(pltpu.make_async_copy(traces_hbm.at[at], traces_ref.at[at], sems.at[index]))
    for copy in copies:
        copy.start()
    for copy in copies:
        copy.wait()
    pieces = []
    for window in range(plan.windows):
        values = traces_ref[:, window, :]
        centered = values - jnp.mean(values, axis=1, keepdims=True)
        mean_power = jnp.mean(centered * centered, axis=1, keepdims=True)
        flag_values = flags_ref[window : window + 1, :].astype(jnp.float32).reshape(plan.half, 1)
        pieces.append(centered * lax.rsqrt(mean_power + 1e-05) * flag_values)
    out_ref[...] = jnp.concatenate(pieces, axis=0).astype(jnp.bfloat16)


def lag_rows(plan, rows_ref, toeplitz_ref):
    span = plan.span
    me = lax.axis_index("blk")
    filler = jnp.zeros((1, span - plan.segment), jnp.float32)
    for window in range(plan.windows):
        at = slice(window * span, (window + 1) * span)
        for place, hop in enumerate(HOPS):
            for member in range(plan.own):
                channel = window * plan.half + (me ^ hop) * plan.own + member
                row = jnp.concatenate([rows_ref[pl.ds(channel, 1), :], filler], axis=1)
                row = jnp.broadcast_to(row, (GROUP, span))
                pieces = [
                    pltpu.roll(row, (MAXLAG - plan.fine_padded + 1 + lag) % span, 1, stride=1, stride_axis=0)
                    for lag in range(0, plan.fine_padded, GROUP)
                ]
                first = place * plan.height + member * plan.fine_padded
                toeplitz_ref[first : first + plan.fine_padded, at] = jnp.concatenate(pieces, axis=0).astype(
                    jnp.bfloat16
                )


def fill_columns(plan, values, columns_ref):
    span = plan.span
    filler = jnp.zeros((plan.half, span - plan.segment), jnp.float32)
    spare = jnp.zeros((plan.half_lanes - plan.coarse * plan.half, span), jnp.float32)
    for window in range(plan.windows):
        rows = jnp.concatenate([values[window * plan.half : (window + 1) * plan.half], filler], axis=1)
        pieces = [rows] + [pltpu.roll(rows, step * plan.fine, 1) for step in range(1, plan.coarse)]
        if spare.shape[0]:
            pieces.append(spare)
        columns_ref[:, window * span : (window + 1) * span] = jnp.concatenate(pieces, axis=0).astype(jnp.bfloat16)


def product(toeplitz_ref, columns_ref):
    return lax.dot_general(
        toeplitz_ref[...], columns_ref[...], (((1,), (1,)), ((), ())), preferred_element_type=jnp.float32
    )


def near_kernel(plan, *refs):
    mine_refs, (other_ref, sum_ref, rows_ref, toeplitz_ref, columns_ref) = refs[: plan.windows], refs[plan.windows :]
    for window, mine_ref in enumerate(mine_refs):
        rows_ref[window * plan.half : (window + 1) * plan.half, :] = mine_ref[...].astype(jnp.float32)
    lag_rows(plan, rows_ref, toeplitz_ref)
    fill_columns(plan, rows_ref[...], columns_ref.at[: plan.half_lanes])
    fill_columns(plan, other_ref[...].astype(jnp.float32), columns_ref.at[plan.half_lanes :])
    sum_ref[...] = product(toeplitz_ref, columns_ref)


def across_kernel(plan, mine_ref, prior_ref, toeplitz_ref, left_ref, right_ref, rows_ref, columns_ref):
    rows_ref[...] = mine_ref[...].astype(jnp.float32)
    lag_rows(plan, rows_ref, toeplitz_ref)
    fill_columns(plan, rows_ref[...], columns_ref)
    left = prior_ref[:, : plan.half_lanes] + product(toeplitz_ref, columns_ref)
    for place, block in enumerate(pack(plan, left)):
        left_ref[place * plan.rows : (place + 1) * plan.rows, :] = block
    right_ref[...] = prior_ref[:, plan.half_lanes :]


def pack(plan, products):
    width = products.shape[1]
    back = GROUP - 1 - lax.broadcasted_iota(jnp.int32, (GROUP, width), 0)
    packed = []
    for place in range(plan.targets):
        whole, rest = [], []
        for member in range(plan.own):
            last = place * plan.height + (member + 1) * plan.fine_padded
            tiles = [
                jnp.take_along_axis(products[last - lag - GROUP : last - lag], back, axis=0)
                for lag in range(0, plan.fine, GROUP)
            ]
            whole += tiles[: plan.whole_groups // GROUP]
            if plan.rest:
                rest.append(tiles[-1][: plan.rest])
        pieces = whole + rest
        if plan.rows > plan.own * plan.fine:
            pieces.append(jnp.zeros((plan.rows - plan.own * plan.fine, width), jnp.float32))
        packed.append(jnp.concatenate(pieces, axis=0))
    return packed


def finish_kernel(plan, other_ref, toeplitz_ref, left_ref, right_ref, *refs):
    *out_refs, columns_ref = refs
    fill_columns(plan, other_ref[...].astype(jnp.float32), columns_ref)
    right = pack(plan, right_ref[...] + product(toeplitz_ref, columns_ref))
    for place, out_ref in enumerate(out_refs):
        rows = slice(place * plan.rows, (place + 1) * plan.rows)
        out_ref[...] = jnp.concatenate([left_ref[rows, :], right[place]], axis=1).astype(jnp.bfloat16)


def spread(plan, values):
    high = values.astype(jnp.bfloat16).astype(jnp.float32)
    low = values - high
    lane = lax.broadcasted_iota(jnp.int32, values.shape, 1)
    lane = jnp.where(lane >= plan.half_lanes, lane - plan.half_lanes, lane)
    up = pltpu.roll(low, plan.half, 1)
    down = pltpu.roll(low, LANES - plan.half, 1)
    pieces = []
    for step in range(plan.coarse):
        beside, moved = (step + 1, up) if step + 1 < plan.coarse else (step - 1, down)
        kept = jnp.where((lane >= step * plan.half) & (lane < (step + 1) * plan.half), high, 0.0)
        there = (lane >= beside * plan.half) & (lane < (beside + 1) * plan.half)
        pieces.append(jnp.where(there, moved, kept).astype(jnp.bfloat16))
    return jnp.concatenate(pieces, axis=0)


def choose_kernel(plan, index_ref, whitened_ref, chosen_ref, *same_refs):
    whitened = whitened_ref[...].astype(jnp.float32)
    for window, same_ref in enumerate(same_refs):
        same_ref[...] = whitened[window * plan.half : (window + 1) * plan.half].astype(jnp.bfloat16)
    first = lax.axis_index("src") * plan.half
    index = index_ref[...] - first
    index = jnp.where(index < 0, index + plan.channels, index)
    lane = jnp.where(index >= plan.half, index - plan.half + plan.half_lanes, index)
    at_column = lax.broadcasted_iota(jnp.int32, (LANES, plan.source_count), 0)
    chosen = jnp.zeros((LANES, plan.source_count), jnp.bool_)
    for step in range(plan.coarse):
        chosen = chosen | (at_column == lane + step * plan.half)
    chosen_ref[...] = chosen.astype(jnp.float32).astype(jnp.bfloat16)


def expand_kernel(plan, chosen_ref, *refs):
    *arrived_refs, out_hbm, out_ref, sems = refs
    total = sum(ref[...].astype(jnp.float32) for ref in arrived_refs) * plan.norm_factor
    chosen = chosen_ref[...]
    filler = jnp.zeros((plan.fine_padded - plan.fine, LANES), jnp.float32)
    copies = []
    for member in range(plan.own):
        rest = plan.own * plan.whole_groups + member * plan.rest
        rows = jnp.concatenate(
            [
                total[member * plan.whole_groups : (member + 1) * plan.whole_groups],
                total[rest : rest + plan.rest],
                filler,
            ],
            axis=0,
        )
        expanded = jnp.dot(spread(plan, rows), chosen, preferred_element_type=jnp.float32)
        for step in range(plan.coarse):
            start = step * plan.fine
            count = min(plan.fine, LAG_COUNT - start)
            first = step * plan.fine_padded
            out_ref[member, start : start + count, :] = expanded[first : first + count]
        copies.append(pltpu.make_async_copy(out_ref.at[member], out_hbm.at[member], sems.at[member]))
        copies[-1].start()
    for copy in copies:
        copy.wait()


def few_channels(plan, traces, valid_flags, source_index):
    vmem = pl.BlockSpec(memory_space=pltpu.VMEM)
    params = pltpu.CompilerParams(vmem_limit_bytes=32 * 1024 * 1024)
    packed_rows = plan.windows * plan.half
    flags = valid_flags.T

    def swap_cores(array):
        return lax.ppermute(array, "src", [(0, 1), (1, 0)])

    def swap_blk(array, hop):
        pairs = [
            (place * plan.src_size + core, (place ^ hop) * plan.src_size + 1 - core)
            for place in range(plan.blk_size)
            for core in range(plan.src_size)
        ]
        return lax.ppermute(array, ("blk", "src"), pairs)

    whitened = pl.pallas_call(
        functools.partial(whiten_kernel, plan),
        out_shape=pltpu.VMEM((packed_rows, plan.segment), jnp.bfloat16),
        in_specs=[pl.BlockSpec(memory_space=pl.ANY)] * 2,
        out_specs=vmem,
        scratch_shapes=[
            pltpu.VMEM(traces.shape, jnp.float32),
            pltpu.VMEM(flags.shape, jnp.int32),
            pltpu.SemaphoreType.DMA((IN_PARTS + 1,)),
        ],
        compiler_params=pltpu.CompilerParams(vmem_limit_bytes=60 * 1024 * 1024),
        name="whiten",
    )(traces, flags)

    height = plan.targets * plan.height
    width = plan.windows * plan.span
    rows = pltpu.VMEM((packed_rows, plan.segment), jnp.float32)
    toeplitz = (height, width)
    columns = (plan.half_lanes, width)
    sums = jax.ShapeDtypeStruct((height, LANES), jnp.float32)

    def call(kernel, name, operands, outputs, scratch=()):
        return pl.pallas_call(
            functools.partial(kernel, plan),
            out_shape=outputs,
            in_specs=[vmem] * len(operands),
            out_specs=[vmem] * len(outputs),
            scratch_shapes=scratch,
            compiler_params=params,
            name=name,
        )(*operands)

    across = swap_blk(whitened, plan.targets)
    chosen, *same = call(
        choose_kernel,
        "choose",
        (source_index.reshape(1, -1), whitened),
        (
            jax.ShapeDtypeStruct((LANES, plan.source_count), jnp.bfloat16),
            *[jax.ShapeDtypeStruct((plan.half, plan.segment), whitened.dtype)] * plan.windows,
        ),
    )
    (total,) = call(
        near_kernel,
        "near",
        (*[swap_cores(array) for array in same], whitened),
        (sums,),
        (rows, pltpu.VMEM(toeplitz, jnp.bfloat16), pltpu.VMEM((LANES, width), jnp.bfloat16)),
    )
    across, total = lax.optimization_barrier((across, total))
    across_other = swap_cores(across)
    lagged, left, right = call(
        across_kernel,
        "across",
        (across, total),
        (
            jax.ShapeDtypeStruct(toeplitz, jnp.bfloat16),
            jax.ShapeDtypeStruct((plan.targets * plan.rows, plan.half_lanes), jnp.float32),
            jax.ShapeDtypeStruct((height, plan.half_lanes), jnp.float32),
        ),
        (rows, pltpu.VMEM(columns, jnp.bfloat16)),
    )
    sent = call(
        finish_kernel,
        "finish",
        (across_other, lagged, left, right),
        (jax.ShapeDtypeStruct((plan.rows, LANES), jnp.bfloat16),) * plan.targets,
        (pltpu.VMEM(columns, jnp.bfloat16),),
    )
    arrived = [swap_blk(array, hop) for array, hop in zip(sent, HOPS)]
    out_shape = (plan.own, LAG_COUNT, plan.source_count)
    return pl.pallas_call(
        functools.partial(expand_kernel, plan),
        out_shape=jax.ShapeDtypeStruct(out_shape, jnp.float32),
        in_specs=[vmem] * (1 + len(arrived)),
        out_specs=pl.BlockSpec(memory_space=pl.ANY),
        scratch_shapes=[pltpu.VMEM(out_shape, jnp.float32), pltpu.SemaphoreType.DMA((plan.own,))],
        compiler_params=params,
        name="expand",
    )(chosen, *arrived)


def body(traces, valid_flags, source_index):
    plan = Plan(
        traces.shape[0],
        traces.shape[1],
        traces.shape[2],
        lax.axis_size("blk"),
        lax.axis_size("src"),
        source_index.shape[0],
    )
    if plan.fits():
        return few_channels(plan, traces, valid_flags, source_index)
    return many_channels(traces, valid_flags, source_index)


def solution(mesh):
    in_specs = (P(("fibre", "src"), "blk", None), P(("fibre", "src"), "blk"), P())
    out_specs = P(("fibre", "src", "blk"), None, None)
    return jax.shard_map(body, mesh=mesh, in_specs=in_specs, out_specs=out_specs, check_vma=False)
```

```python
import functools
import math

import jax
import jax.numpy as jnp
from jax import lax
from jax.experimental import pallas as pl
from jax.experimental.pallas import tpu as pltpu
from jax.sharding import PartitionSpec as P

MAXLAG = 64
LAG_COUNT = 2 * MAXLAG + 1
LANES = 256
IN_PARTS = 4
GROUP = 8
HOPS = (3, 2, 1, 0)


def broadcast(value, axis, source):
    kept = jnp.where(lax.axis_index(axis) == source, value, 0).astype(value.dtype)
    return lax.psum(kept, axis)


def toeplitz_rows(group, lag_count, segment):
    shifted = jnp.stack(
        [group[:, :, lag_step : lag_step + segment] for lag_step in range(lag_count)], axis=1
    )
    return shifted.reshape(group.shape[0] * lag_count, -1)


def many_channels(traces, valid_flags, source_index):
    segment = traces.shape[2]
    centered = traces - jnp.mean(traces, axis=2, keepdims=True)
    mean_power = jnp.mean(centered * centered, axis=2, keepdims=True)
    flag_values = valid_flags[:, :, None].astype(jnp.float32)
    whitened = (centered * lax.rsqrt(mean_power + 1e-05) * flag_values).astype(jnp.bfloat16)
    pieces = []
    for owner in range(lax.axis_size("src")):
        pieces.append(broadcast(whitened, "src", owner))
    everyone = jnp.concatenate(pieces, axis=0)
    sources = jnp.take(everyone, source_index, axis=0)
    source_count = sources.shape[0]
    norm_factor = 1.0 / math.sqrt(traces.shape[1] * lax.axis_size("blk") * segment)
    own_rows = whitened.shape[0] // lax.axis_size("blk")
    flat_sources = sources.reshape(source_count, -1)
    padded = jnp.pad(whitened, ((0, 0), (0, 0), (MAXLAG, MAXLAG)))
    block_rows = math.gcd(lax.axis_size("blk") * own_rows, 16)
    grouped = padded.reshape(
        (lax.axis_size("blk") * own_rows // block_rows, block_rows) + padded.shape[1:]
    )

    def one_block(group):
        toeplitz = toeplitz_rows(group, LAG_COUNT, segment)
        products = lax.dot_general(
            toeplitz, flat_sources, (((1,), (1,)), ((), ())), preferred_element_type=jnp.float32
        )
        return (products * norm_factor).reshape(block_rows, LAG_COUNT, source_count)

    result = lax.map(one_block, grouped)
    return lax.psum_scatter(
        result.reshape(lax.axis_size("blk") * own_rows, LAG_COUNT, source_count),
        "blk",
        scatter_dimension=0,
        tiled=True,
    )


class Plan:
    def __init__(self, half, windows, segment, blk_size, src_size, source_count):
        self.half = half
        self.windows = windows
        self.segment = segment
        self.blk_size = blk_size
        self.src_size = src_size
        self.channels = half * src_size
        self.source_count = source_count
        self.half_lanes = LANES // 2
        self.coarse = self.half_lanes // half
        if self.coarse == 0:
            return
        self.fine = -(-LAG_COUNT // self.coarse)
        self.fine_padded = -(-self.fine // (2 * GROUP)) * 2 * GROUP
        self.own = half // blk_size
        reach = segment + (self.coarse - 1) * self.fine
        self.span = -(-max(reach, segment + 2 * MAXLAG) // 128) * 128
        self.whole_groups = self.fine // GROUP * GROUP
        self.rest = self.fine - self.whole_groups
        rows = self.own * self.fine
        self.rows = -(-rows // 16) * 16
        self.targets = blk_size // 2
        self.receivers = self.targets * self.own
        self.lag_rows = -(-self.receivers * self.fine // 32) * 32
        self.norm_factor = 1.0 / math.sqrt(windows * blk_size * segment)

    def fits(self):
        return (
            self.coarse >= 2
            and self.src_size == 2
            and self.half % self.blk_size == 0
            and self.half % GROUP == 0
            and self.channels % 16 == 0
            and self.windows * self.half % 16 == 0
            and self.blk_size == 8
            and self.rest > 0
            and GROUP % self.rest == 0
            and self.receivers * self.rest % GROUP == 0
            and self.receivers % 2 == 0
            and self.receivers * self.whole_groups % 16 == 0
        )


def whiten_kernel(plan, traces_hbm, flags_hbm, out_ref, traces_ref, flags_ref, sems):
    part = plan.half // IN_PARTS
    copies = [pltpu.make_async_copy(flags_hbm, flags_ref, sems.at[IN_PARTS])]
    for index in range(IN_PARTS):
        at = pl.ds(index * part, part)
        copies.append(pltpu.make_async_copy(traces_hbm.at[at], traces_ref.at[at], sems.at[index]))
    for copy in copies:
        copy.start()
    for copy in copies:
        copy.wait()
    pieces = []
    for window in range(plan.windows):
        values = traces_ref[:, window, :]
        centered = values - jnp.mean(values, axis=1, keepdims=True)
        mean_power = jnp.mean(centered * centered, axis=1, keepdims=True)
        flag_values = flags_ref[window : window + 1, :].astype(jnp.float32).reshape(plan.half, 1)
        pieces.append(centered * lax.rsqrt(mean_power + 1e-05) * flag_values)
    out_ref[...] = jnp.concatenate(pieces, axis=0).astype(jnp.bfloat16)


def lag_rows(plan, rows_ref, toeplitz_ref):
    span = plan.span
    me = lax.axis_index("blk")
    filler = jnp.zeros((1, span - plan.segment), jnp.float32)
    spare = jnp.zeros((plan.lag_rows - plan.receivers * plan.fine, span), jnp.float32)
    sublane = lax.broadcasted_iota(jnp.int32, (GROUP, span), 0)
    for window in range(plan.windows):
        at = slice(window * span, (window + 1) * span)
        spread_rows = []
        for hop in HOPS:
            for member in range(plan.own):
                channel = window * plan.half + (me ^ hop) * plan.own + member
                row = jnp.concatenate([rows_ref[pl.ds(channel, 1), :], filler], axis=1)
                spread_rows.append(jnp.broadcast_to(row, (GROUP, span)))
        for first in range(0, plan.receivers, 2):
            pieces = [
                pltpu.roll(row, (MAXLAG - plan.whole_groups + 1 + lag) % span, 1, stride=1, stride_axis=0)
                for row in spread_rows[first : first + 2]
                for lag in range(0, plan.whole_groups, GROUP)
            ]
            start = first * plan.whole_groups
            toeplitz_ref[start : start + 2 * plan.whole_groups, at] = jnp.concatenate(pieces, axis=0).astype(
                jnp.bfloat16
            )
        pieces = []
        for first in range(0, plan.receivers, GROUP // plan.rest):
            mixed = spread_rows[first]
            for index in range(1, GROUP // plan.rest):
                mixed = jnp.where(sublane >= index * plan.rest, spread_rows[first + index], mixed)
            tile = pltpu.roll(mixed, (MAXLAG - plan.whole_groups) % span, 1)
            for lag in range(1, plan.rest):
                later = pltpu.roll(mixed, (MAXLAG - plan.whole_groups - lag) % span, 1)
                tile = jnp.where(sublane % plan.rest == lag, later, tile)
            pieces.append(tile)
        start = plan.receivers * plan.whole_groups
        toeplitz_ref[start:, at] = jnp.concatenate(pieces + [spare], axis=0).astype(jnp.bfloat16)


def fill_columns(plan, values, columns_ref):
    span = plan.span
    filler = jnp.zeros((plan.half, span - plan.segment), jnp.float32)
    spare = jnp.zeros((plan.half_lanes - plan.coarse * plan.half, span), jnp.float32)
    for window in range(plan.windows):
        rows = jnp.concatenate([values[window * plan.half : (window + 1) * plan.half], filler], axis=1)
        pieces = [rows] + [pltpu.roll(rows, step * plan.fine, 1) for step in range(1, plan.coarse)]
        if spare.shape[0]:
            pieces.append(spare)
        columns_ref[:, window * span : (window + 1) * span] = jnp.concatenate(pieces, axis=0).astype(jnp.bfloat16)


def product(toeplitz_ref, columns_ref):
    return lax.dot_general(
        toeplitz_ref[...], columns_ref[...], (((1,), (1,)), ((), ())), preferred_element_type=jnp.float32
    )


def near_kernel(plan, *refs):
    mine_refs, (other_ref, sum_ref, rows_ref, toeplitz_ref, columns_ref) = refs[: plan.windows], refs[plan.windows :]
    for window, mine_ref in enumerate(mine_refs):
        rows_ref[window * plan.half : (window + 1) * plan.half, :] = mine_ref[...].astype(jnp.float32)
    lag_rows(plan, rows_ref, toeplitz_ref)
    fill_columns(plan, rows_ref[...], columns_ref.at[: plan.half_lanes])
    fill_columns(plan, other_ref[...].astype(jnp.float32), columns_ref.at[plan.half_lanes :])
    sum_ref[...] = product(toeplitz_ref, columns_ref)


def across_kernel(plan, mine_ref, prior_ref, toeplitz_ref, left_ref, right_ref, rows_ref, columns_ref):
    rows_ref[...] = mine_ref[...].astype(jnp.float32)
    lag_rows(plan, rows_ref, toeplitz_ref)
    fill_columns(plan, rows_ref[...], columns_ref)
    left = prior_ref[:, : plan.half_lanes] + product(toeplitz_ref, columns_ref)
    for place, block in enumerate(pack(plan, left)):
        left_ref[place * plan.rows : (place + 1) * plan.rows, :] = block
    right_ref[...] = prior_ref[:, plan.half_lanes :]


def pack(plan, products):
    width = products.shape[1]
    back = GROUP - 1 - lax.broadcasted_iota(jnp.int32, (GROUP, width), 0)
    packed = []
    for place in range(plan.targets):
        pieces = []
        for receiver in range(place * plan.own, (place + 1) * plan.own):
            last = (receiver + 1) * plan.whole_groups
            pieces += [
                jnp.take_along_axis(products[last - lag - GROUP : last - lag], back, axis=0)
                for lag in range(0, plan.whole_groups, GROUP)
            ]
        first = plan.receivers * plan.whole_groups + place * plan.own * plan.rest
        pieces.append(products[first : first + plan.own * plan.rest])
        if plan.rows > plan.own * plan.fine:
            pieces.append(jnp.zeros((plan.rows - plan.own * plan.fine, width), jnp.float32))
        packed.append(jnp.concatenate(pieces, axis=0))
    return packed


def finish_kernel(plan, other_ref, toeplitz_ref, left_ref, right_ref, *refs):
    *out_refs, columns_ref = refs
    fill_columns(plan, other_ref[...].astype(jnp.float32), columns_ref)
    right = pack(plan, right_ref[...] + product(toeplitz_ref, columns_ref))
    for place, out_ref in enumerate(out_refs):
        rows = slice(place * plan.rows, (place + 1) * plan.rows)
        out_ref[...] = jnp.concatenate([left_ref[rows, :], right[place]], axis=1).astype(jnp.bfloat16)


def spread(plan, values):
    high = values.astype(jnp.bfloat16).astype(jnp.float32)
    low = values - high
    lane = lax.broadcasted_iota(jnp.int32, values.shape, 1)
    lane = jnp.where(lane >= plan.half_lanes, lane - plan.half_lanes, lane)
    up = pltpu.roll(low, plan.half, 1)
    down = pltpu.roll(low, LANES - plan.half, 1)
    pieces = []
    for step in range(plan.coarse):
        beside, moved = (step + 1, up) if step + 1 < plan.coarse else (step - 1, down)
        kept = jnp.where((lane >= step * plan.half) & (lane < (step + 1) * plan.half), high, 0.0)
        there = (lane >= beside * plan.half) & (lane < (beside + 1) * plan.half)
        pieces.append(jnp.where(there, moved, kept).astype(jnp.bfloat16))
    return jnp.concatenate(pieces, axis=0)


def choose_kernel(plan, index_ref, whitened_ref, chosen_ref, *same_refs):
    whitened = whitened_ref[...].astype(jnp.float32)
    for window, same_ref in enumerate(same_refs):
        same_ref[...] = whitened[window * plan.half : (window + 1) * plan.half].astype(jnp.bfloat16)
    first = lax.axis_index("src") * plan.half
    index = index_ref[...] - first
    index = jnp.where(index < 0, index + plan.channels, index)
    lane = jnp.where(index >= plan.half, index - plan.half + plan.half_lanes, index)
    at_column = lax.broadcasted_iota(jnp.int32, (LANES, plan.source_count), 0)
    chosen = jnp.zeros((LANES, plan.source_count), jnp.bool_)
    for step in range(plan.coarse):
        chosen = chosen | (at_column == lane + step * plan.half)
    chosen_ref[...] = chosen.astype(jnp.float32).astype(jnp.bfloat16)


def expand_kernel(plan, chosen_ref, *refs):
    *arrived_refs, out_hbm, out_ref, sems = refs
    total = sum(ref[...].astype(jnp.float32) for ref in arrived_refs) * plan.norm_factor
    chosen = chosen_ref[...]
    filler = jnp.zeros((plan.fine_padded - plan.fine, LANES), jnp.float32)
    copies = []
    for member in range(plan.own):
        rest = plan.own * plan.whole_groups + member * plan.rest
        rows = jnp.concatenate(
            [
                total[member * plan.whole_groups : (member + 1) * plan.whole_groups],
                total[rest : rest + plan.rest],
                filler,
            ],
            axis=0,
        )
        expanded = jnp.dot(spread(plan, rows), chosen, preferred_element_type=jnp.float32)
        for step in range(plan.coarse):
            start = step * plan.fine
            count = min(plan.fine, LAG_COUNT - start)
            first = step * plan.fine_padded
            out_ref[member, start : start + count, :] = expanded[first : first + count]
        copies.append(pltpu.make_async_copy(out_ref.at[member], out_hbm.at[member], sems.at[member]))
        copies[-1].start()
    for copy in copies:
        copy.wait()


def few_channels(plan, traces, valid_flags, source_index):
    vmem = pl.BlockSpec(memory_space=pltpu.VMEM)
    params = pltpu.CompilerParams(vmem_limit_bytes=32 * 1024 * 1024)
    packed_rows = plan.windows * plan.half
    flags = valid_flags.T

    def swap_cores(array):
        return lax.ppermute(array, "src", [(0, 1), (1, 0)])

    def swap_blk(array, hop):
        pairs = [
            (place * plan.src_size + core, (place ^ hop) * plan.src_size + 1 - core)
            for place in range(plan.blk_size)
            for core in range(plan.src_size)
        ]
        return lax.ppermute(array, ("blk", "src"), pairs)

    whitened = pl.pallas_call(
        functools.partial(whiten_kernel, plan),
        out_shape=pltpu.VMEM((packed_rows, plan.segment), jnp.bfloat16),
        in_specs=[pl.BlockSpec(memory_space=pl.ANY)] * 2,
        out_specs=vmem,
        scratch_shapes=[
            pltpu.VMEM(traces.shape, jnp.float32),
            pltpu.VMEM(flags.shape, jnp.int32),
            pltpu.SemaphoreType.DMA((IN_PARTS + 1,)),
        ],
        compiler_params=pltpu.CompilerParams(vmem_limit_bytes=60 * 1024 * 1024),
        name="whiten",
    )(traces, flags)

    height = plan.lag_rows
    width = plan.windows * plan.span
    rows = pltpu.VMEM((packed_rows, plan.segment), jnp.float32)
    toeplitz = (height, width)
    columns = (plan.half_lanes, width)
    sums = jax.ShapeDtypeStruct((height, LANES), jnp.float32)

    def call(kernel, name, operands, outputs, scratch=()):
        return pl.pallas_call(
            functools.partial(kernel, plan),
            out_shape=outputs,
            in_specs=[vmem] * len(operands),
            out_specs=[vmem] * len(outputs),
            scratch_shapes=scratch,
            compiler_params=params,
            name=name,
        )(*operands)

    across = swap_blk(whitened, plan.targets)
    chosen, *same = call(
        choose_kernel,
        "choose",
        (source_index.reshape(1, -1), whitened),
        (
            jax.ShapeDtypeStruct((LANES, plan.source_count), jnp.bfloat16),
            *[jax.ShapeDtypeStruct((plan.half, plan.segment), whitened.dtype)] * plan.windows,
        ),
    )
    (total,) = call(
        near_kernel,
        "near",
        (*[swap_cores(array) for array in same], whitened),
        (sums,),
        (rows, pltpu.VMEM(toeplitz, jnp.bfloat16), pltpu.VMEM((LANES, width), jnp.bfloat16)),
    )
    across, total = lax.optimization_barrier((across, total))
    across_other = swap_cores(across)
    lagged, left, right = call(
        across_kernel,
        "across",
        (across, total),
        (
            jax.ShapeDtypeStruct(toeplitz, jnp.bfloat16),
            jax.ShapeDtypeStruct((plan.targets * plan.rows, plan.half_lanes), jnp.float32),
            jax.ShapeDtypeStruct((height, plan.half_lanes), jnp.float32),
        ),
        (rows, pltpu.VMEM(columns, jnp.bfloat16)),
    )
    sent = call(
        finish_kernel,
        "finish",
        (across_other, lagged, left, right),
        (jax.ShapeDtypeStruct((plan.rows, LANES), jnp.bfloat16),) * plan.targets,
        (pltpu.VMEM(columns, jnp.bfloat16),),
    )
    arrived = [swap_blk(array, hop) for array, hop in zip(sent, HOPS)]
    out_shape = (plan.own, LAG_COUNT, plan.source_count)
    return pl.pallas_call(
        functools.partial(expand_kernel, plan),
        out_shape=jax.ShapeDtypeStruct(out_shape, jnp.float32),
        in_specs=[vmem] * (1 + len(arrived)),
        out_specs=pl.BlockSpec(memory_space=pl.ANY),
        scratch_shapes=[pltpu.VMEM(out_shape, jnp.float32), pltpu.SemaphoreType.DMA((plan.own,))],
        compiler_params=params,
        name="expand",
    )(chosen, *arrived)


def body(traces, valid_flags, source_index):
    plan = Plan(
        traces.shape[0],
        traces.shape[1],
        traces.shape[2],
        lax.axis_size("blk"),
        lax.axis_size("src"),
        source_index.shape[0],
    )
    if plan.fits():
        return few_channels(plan, traces, valid_flags, source_index)
    return many_channels(traces, valid_flags, source_index)


def solution(mesh):
    in_specs = (P(("fibre", "src"), "blk", None), P(("fibre", "src"), "blk"), P())
    out_specs = P(("fibre", "src", "blk"), None, None)
    return jax.shard_map(body, mesh=mesh, in_specs=in_specs, out_specs=out_specs, check_vma=False)
```

```python
import functools
import math

import jax
import jax.numpy as jnp
from jax import lax
from jax.experimental import pallas as pl
from jax.experimental.pallas import tpu as pltpu
from jax.sharding import PartitionSpec as P

MAXLAG = 64
LAG_COUNT = 2 * MAXLAG + 1
LANES = 256
IN_PARTS = 4
GROUP = 8
HOPS = (3, 2, 1, 0)


def broadcast(value, axis, source):
    kept = jnp.where(lax.axis_index(axis) == source, value, 0).astype(value.dtype)
    return lax.psum(kept, axis)


def toeplitz_rows(group, lag_count, segment):
    shifted = jnp.stack(
        [group[:, :, lag_step : lag_step + segment] for lag_step in range(lag_count)], axis=1
    )
    return shifted.reshape(group.shape[0] * lag_count, -1)


def many_channels(traces, valid_flags, source_index):
    segment = traces.shape[2]
    centered = traces - jnp.mean(traces, axis=2, keepdims=True)
    mean_power = jnp.mean(centered * centered, axis=2, keepdims=True)
    flag_values = valid_flags[:, :, None].astype(jnp.float32)
    whitened = (centered * lax.rsqrt(mean_power + 1e-05) * flag_values).astype(jnp.bfloat16)
    pieces = []
    for owner in range(lax.axis_size("src")):
        pieces.append(broadcast(whitened, "src", owner))
    everyone = jnp.concatenate(pieces, axis=0)
    sources = jnp.take(everyone, source_index, axis=0)
    source_count = sources.shape[0]
    norm_factor = 1.0 / math.sqrt(traces.shape[1] * lax.axis_size("blk") * segment)
    own_rows = whitened.shape[0] // lax.axis_size("blk")
    flat_sources = sources.reshape(source_count, -1)
    padded = jnp.pad(whitened, ((0, 0), (0, 0), (MAXLAG, MAXLAG)))
    block_rows = math.gcd(lax.axis_size("blk") * own_rows, 16)
    grouped = padded.reshape(
        (lax.axis_size("blk") * own_rows // block_rows, block_rows) + padded.shape[1:]
    )

    def one_block(group):
        toeplitz = toeplitz_rows(group, LAG_COUNT, segment)
        products = lax.dot_general(
            toeplitz, flat_sources, (((1,), (1,)), ((), ())), preferred_element_type=jnp.float32
        )
        return (products * norm_factor).reshape(block_rows, LAG_COUNT, source_count)

    result = lax.map(one_block, grouped)
    return lax.psum_scatter(
        result.reshape(lax.axis_size("blk") * own_rows, LAG_COUNT, source_count),
        "blk",
        scatter_dimension=0,
        tiled=True,
    )


class Plan:
    def __init__(self, half, windows, segment, blk_size, src_size, source_count):
        self.half = half
        self.windows = windows
        self.segment = segment
        self.blk_size = blk_size
        self.src_size = src_size
        self.channels = half * src_size
        self.source_count = source_count
        self.half_lanes = LANES // 2
        self.coarse = self.half_lanes // half
        if self.coarse == 0:
            return
        self.fine = -(-LAG_COUNT // self.coarse)
        self.fine_padded = -(-self.fine // (2 * GROUP)) * 2 * GROUP
        self.own = half // blk_size
        reach = segment + (self.coarse - 1) * self.fine
        self.span = -(-max(reach, segment + 2 * MAXLAG) // 128) * 128
        self.whole_groups = self.fine // GROUP * GROUP
        self.rest = self.fine - self.whole_groups
        rows = self.own * self.fine
        self.rows = -(-rows // 16) * 16
        self.targets = blk_size // 2
        self.receivers = self.targets * self.own
        self.lag_rows = -(-self.receivers * self.fine // 32) * 32
        self.norm_factor = 1.0 / math.sqrt(windows * blk_size * segment)

    def fits(self):
        return (
            self.coarse >= 2
            and self.src_size == 2
            and self.half % self.blk_size == 0
            and self.half % GROUP == 0
            and self.channels % 16 == 0
            and self.windows * self.half % 16 == 0
            and self.blk_size == 8
            and self.rest > 0
            and GROUP % self.rest == 0
            and self.receivers * self.rest % GROUP == 0
            and self.receivers % 2 == 0
            and self.receivers * self.whole_groups % 16 == 0
        )


def whiten_kernel(plan, traces_hbm, flags_hbm, out_ref, traces_ref, flags_ref, sems):
    part = plan.half // IN_PARTS
    copies = [pltpu.make_async_copy(flags_hbm, flags_ref, sems.at[IN_PARTS])]
    for index in range(IN_PARTS):
        at = pl.ds(index * part, part)
        copies.append(pltpu.make_async_copy(traces_hbm.at[at], traces_ref.at[at], sems.at[index]))
    for copy in copies:
        copy.start()
    copies[0].wait()
    flag_values = [
        flags_ref[window : window + 1, :].astype(jnp.float32).reshape(plan.half, 1) for window in range(plan.windows)
    ]
    for copy in copies[1:]:
        copy.wait()
    pieces = []
    for window in range(plan.windows):
        values = traces_ref[:, window, :]
        centered = values - jnp.mean(values, axis=1, keepdims=True)
        mean_power = jnp.mean(centered * centered, axis=1, keepdims=True)
        pieces.append(centered * lax.rsqrt(mean_power + 1e-05) * flag_values[window])
    out_ref[...] = jnp.concatenate(pieces, axis=0).astype(jnp.bfloat16)


def lag_rows(plan, rows_ref, toeplitz_ref):
    span = plan.span
    me = lax.axis_index("blk")
    filler = jnp.zeros((1, span - plan.segment), jnp.float32)
    spare = jnp.zeros((plan.lag_rows - plan.receivers * plan.fine, span), jnp.float32)
    sublane = lax.broadcasted_iota(jnp.int32, (GROUP, span), 0)
    for window in range(plan.windows):
        at = slice(window * span, (window + 1) * span)
        spread_rows = []
        for hop in HOPS:
            for member in range(plan.own):
                channel = window * plan.half + (me ^ hop) * plan.own + member
                row = jnp.concatenate([rows_ref[pl.ds(channel, 1), :], filler], axis=1)
                spread_rows.append(jnp.broadcast_to(row, (GROUP, span)))
        for first in range(0, plan.receivers, 2):
            pieces = [
                pltpu.roll(row, (MAXLAG - plan.whole_groups + 1 + lag) % span, 1, stride=1, stride_axis=0)
                for row in spread_rows[first : first + 2]
                for lag in range(0, plan.whole_groups, GROUP)
            ]
            start = first * plan.whole_groups
            toeplitz_ref[start : start + 2 * plan.whole_groups, at] = jnp.concatenate(pieces, axis=0).astype(
                jnp.bfloat16
            )
        pieces = []
        for first in range(0, plan.receivers, GROUP // plan.rest):
            mixed = spread_rows[first]
            for index in range(1, GROUP // plan.rest):
                mixed = jnp.where(sublane >= index * plan.rest, spread_rows[first + index], mixed)
            tile = pltpu.roll(mixed, (MAXLAG - plan.whole_groups) % span, 1)
            for lag in range(1, plan.rest):
                later = pltpu.roll(mixed, (MAXLAG - plan.whole_groups - lag) % span, 1)
                tile = jnp.where(sublane % plan.rest == lag, later, tile)
            pieces.append(tile)
        start = plan.receivers * plan.whole_groups
        toeplitz_ref[start:, at] = jnp.concatenate(pieces + [spare], axis=0).astype(jnp.bfloat16)


def fill_columns(plan, values, columns_ref):
    span = plan.span
    filler = jnp.zeros((plan.half, span - plan.segment), jnp.float32)
    spare = jnp.zeros((plan.half_lanes - plan.coarse * plan.half, span), jnp.float32)
    for window in range(plan.windows):
        rows = jnp.concatenate([values[window * plan.half : (window + 1) * plan.half], filler], axis=1)
        pieces = [rows] + [pltpu.roll(rows, step * plan.fine, 1) for step in range(1, plan.coarse)]
        if spare.shape[0]:
            pieces.append(spare)
        columns_ref[:, window * span : (window + 1) * span] = jnp.concatenate(pieces, axis=0).astype(jnp.bfloat16)


def product(toeplitz_ref, columns_ref):
    return lax.dot_general(
        toeplitz_ref[...], columns_ref[...], (((1,), (1,)), ((), ())), preferred_element_type=jnp.float32
    )


def near_kernel(plan, *refs):
    mine_refs, (other_ref, sum_ref, rows_ref, toeplitz_ref, columns_ref) = refs[: plan.windows], refs[plan.windows :]
    for window, mine_ref in enumerate(mine_refs):
        rows_ref[window * plan.half : (window + 1) * plan.half, :] = mine_ref[...].astype(jnp.float32)
    lag_rows(plan, rows_ref, toeplitz_ref)
    fill_columns(plan, rows_ref[...], columns_ref.at[: plan.half_lanes])
    fill_columns(plan, other_ref[...].astype(jnp.float32), columns_ref.at[plan.half_lanes :])
    sum_ref[...] = product(toeplitz_ref, columns_ref)


def across_kernel(plan, mine_ref, prior_ref, toeplitz_ref, left_ref, right_ref, rows_ref, columns_ref):
    rows_ref[...] = mine_ref[...].astype(jnp.float32)
    lag_rows(plan, rows_ref, toeplitz_ref)
    fill_columns(plan, rows_ref[...], columns_ref)
    left = prior_ref[:, : plan.half_lanes] + product(toeplitz_ref, columns_ref)
    for place, block in enumerate(pack(plan, left)):
        left_ref[place * plan.rows : (place + 1) * plan.rows, :] = block
    right_ref[...] = prior_ref[:, plan.half_lanes :]


def pack(plan, products):
    width = products.shape[1]
    back = GROUP - 1 - lax.broadcasted_iota(jnp.int32, (GROUP, width), 0)
    packed = []
    for place in range(plan.targets):
        pieces = []
        for receiver in range(place * plan.own, (place + 1) * plan.own):
            last = (receiver + 1) * plan.whole_groups
            pieces += [
                jnp.take_along_axis(products[last - lag - GROUP : last - lag], back, axis=0)
                for lag in range(0, plan.whole_groups, GROUP)
            ]
        first = plan.receivers * plan.whole_groups + place * plan.own * plan.rest
        pieces.append(products[first : first + plan.own * plan.rest])
        if plan.rows > plan.own * plan.fine:
            pieces.append(jnp.zeros((plan.rows - plan.own * plan.fine, width), jnp.float32))
        packed.append(jnp.concatenate(pieces, axis=0))
    return packed


def finish_kernel(plan, other_ref, toeplitz_ref, left_ref, right_ref, *refs):
    *out_refs, columns_ref = refs
    fill_columns(plan, other_ref[...].astype(jnp.float32), columns_ref)
    right = pack(plan, right_ref[...] + product(toeplitz_ref, columns_ref))
    for place, out_ref in enumerate(out_refs):
        rows = slice(place * plan.rows, (place + 1) * plan.rows)
        out_ref[...] = jnp.concatenate([left_ref[rows, :], right[place]], axis=1).astype(jnp.bfloat16)


def spread(plan, values):
    high = values.astype(jnp.bfloat16).astype(jnp.float32)
    low = values - high
    lane = lax.broadcasted_iota(jnp.int32, values.shape, 1)
    lane = jnp.where(lane >= plan.half_lanes, lane - plan.half_lanes, lane)
    up = pltpu.roll(low, plan.half, 1)
    down = pltpu.roll(low, LANES - plan.half, 1)
    pieces = []
    for step in range(plan.coarse):
        beside, moved = (step + 1, up) if step + 1 < plan.coarse else (step - 1, down)
        kept = jnp.where((lane >= step * plan.half) & (lane < (step + 1) * plan.half), high, 0.0)
        there = (lane >= beside * plan.half) & (lane < (beside + 1) * plan.half)
        pieces.append(jnp.where(there, moved, kept).astype(jnp.bfloat16))
    return jnp.concatenate(pieces, axis=0)


def choose_kernel(plan, index_ref, whitened_ref, chosen_ref, *same_refs):
    whitened = whitened_ref[...].astype(jnp.float32)
    for window, same_ref in enumerate(same_refs):
        same_ref[...] = whitened[window * plan.half : (window + 1) * plan.half].astype(jnp.bfloat16)
    first = lax.axis_index("src") * plan.half
    index = index_ref[...] - first
    index = jnp.where(index < 0, index + plan.channels, index)
    lane = jnp.where(index >= plan.half, index - plan.half + plan.half_lanes, index)
    at_column = lax.broadcasted_iota(jnp.int32, (LANES, plan.source_count), 0)
    chosen = jnp.zeros((LANES, plan.source_count), jnp.bool_)
    for step in range(plan.coarse):
        chosen = chosen | (at_column == lane + step * plan.half)
    chosen_ref[...] = chosen.astype(jnp.float32).astype(jnp.bfloat16)


def expand_kernel(plan, chosen_ref, *refs):
    *arrived_refs, out_hbm, out_ref, sems = refs
    total = sum(ref[...].astype(jnp.float32) for ref in arrived_refs) * plan.norm_factor
    chosen = chosen_ref[...]
    filler = jnp.zeros((plan.fine_padded - plan.fine, LANES), jnp.float32)
    copies = []
    for member in range(plan.own):
        rest = plan.own * plan.whole_groups + member * plan.rest
        rows = jnp.concatenate(
            [
                total[member * plan.whole_groups : (member + 1) * plan.whole_groups],
                total[rest : rest + plan.rest],
                filler,
            ],
            axis=0,
        )
        expanded = jnp.dot(spread(plan, rows), chosen, preferred_element_type=jnp.float32)
        for step in range(plan.coarse):
            start = step * plan.fine
            count = min(plan.fine, LAG_COUNT - start)
            first = step * plan.fine_padded
            out_ref[member, start : start + count, :] = expanded[first : first + count]
        copies.append(pltpu.make_async_copy(out_ref.at[member], out_hbm.at[member], sems.at[member]))
        copies[-1].start()
    for copy in copies:
        copy.wait()


def few_channels(plan, traces, valid_flags, source_index):
    vmem = pl.BlockSpec(memory_space=pltpu.VMEM)
    params = pltpu.CompilerParams(vmem_limit_bytes=32 * 1024 * 1024)
    packed_rows = plan.windows * plan.half
    flags = valid_flags.T

    def swap_cores(array):
        return lax.ppermute(array, "src", [(0, 1), (1, 0)])

    def swap_blk(array, hop):
        pairs = [
            (place * plan.src_size + core, (place ^ hop) * plan.src_size + 1 - core)
            for place in range(plan.blk_size)
            for core in range(plan.src_size)
        ]
        return lax.ppermute(array, ("blk", "src"), pairs)

    whitened = pl.pallas_call(
        functools.partial(whiten_kernel, plan),
        out_shape=pltpu.VMEM((packed_rows, plan.segment), jnp.bfloat16),
        in_specs=[pl.BlockSpec(memory_space=pl.ANY)] * 2,
        out_specs=vmem,
        scratch_shapes=[
            pltpu.VMEM(traces.shape, jnp.float32),
            pltpu.VMEM(flags.shape, jnp.int32),
            pltpu.SemaphoreType.DMA((IN_PARTS + 1,)),
        ],
        compiler_params=pltpu.CompilerParams(vmem_limit_bytes=60 * 1024 * 1024),
        name="whiten",
    )(traces, flags)

    height = plan.lag_rows
    width = plan.windows * plan.span
    rows = pltpu.VMEM((packed_rows, plan.segment), jnp.float32)
    toeplitz = (height, width)
    columns = (plan.half_lanes, width)
    sums = jax.ShapeDtypeStruct((height, LANES), jnp.float32)

    def call(kernel, name, operands, outputs, scratch=()):
        return pl.pallas_call(
            functools.partial(kernel, plan),
            out_shape=outputs,
            in_specs=[vmem] * len(operands),
            out_specs=[vmem] * len(outputs),
            scratch_shapes=scratch,
            compiler_params=params,
            name=name,
        )(*operands)

    across = swap_blk(whitened, plan.targets)
    chosen, *same = call(
        choose_kernel,
        "choose",
        (source_index.reshape(1, -1), whitened),
        (
            jax.ShapeDtypeStruct((LANES, plan.source_count), jnp.bfloat16),
            *[jax.ShapeDtypeStruct((plan.half, plan.segment), whitened.dtype)] * plan.windows,
        ),
    )
    (total,) = call(
        near_kernel,
        "near",
        (*[swap_cores(array) for array in same], whitened),
        (sums,),
        (rows, pltpu.VMEM(toeplitz, jnp.bfloat16), pltpu.VMEM((LANES, width), jnp.bfloat16)),
    )
    across, total = lax.optimization_barrier((across, total))
    across_other = swap_cores(across)
    lagged, left, right = call(
        across_kernel,
        "across",
        (across, total),
        (
            jax.ShapeDtypeStruct(toeplitz, jnp.bfloat16),
            jax.ShapeDtypeStruct((plan.targets * plan.rows, plan.half_lanes), jnp.float32),
            jax.ShapeDtypeStruct((height, plan.half_lanes), jnp.float32),
        ),
        (rows, pltpu.VMEM(columns, jnp.bfloat16)),
    )
    sent = call(
        finish_kernel,
        "finish",
        (across_other, lagged, left, right),
        (jax.ShapeDtypeStruct((plan.rows, LANES), jnp.bfloat16),) * plan.targets,
        (pltpu.VMEM(columns, jnp.bfloat16),),
    )
    arrived = [swap_blk(array, hop) for array, hop in zip(sent, HOPS)]
    out_shape = (plan.own, LAG_COUNT, plan.source_count)
    return pl.pallas_call(
        functools.partial(expand_kernel, plan),
        out_shape=jax.ShapeDtypeStruct(out_shape, jnp.float32),
        in_specs=[vmem] * (1 + len(arrived)),
        out_specs=pl.BlockSpec(memory_space=pl.ANY),
        scratch_shapes=[pltpu.VMEM(out_shape, jnp.float32), pltpu.SemaphoreType.DMA((plan.own,))],
        compiler_params=params,
        name="expand",
    )(chosen, *arrived)


def body(traces, valid_flags, source_index):
    plan = Plan(
        traces.shape[0],
        traces.shape[1],
        traces.shape[2],
        lax.axis_size("blk"),
        lax.axis_size("src"),
        source_index.shape[0],
    )
    if plan.fits():
        return few_channels(plan, traces, valid_flags, source_index)
    return many_channels(traces, valid_flags, source_index)


def solution(mesh):
    in_specs = (P(("fibre", "src"), "blk", None), P(("fibre", "src"), "blk"), P())
    out_specs = P(("fibre", "src", "blk"), None, None)
    return jax.shard_map(body, mesh=mesh, in_specs=in_specs, out_specs=out_specs, check_vma=False)
```

```python
import functools
import math

import jax
import jax.numpy as jnp
from jax import lax
from jax.experimental import pallas as pl
from jax.experimental.pallas import tpu as pltpu
from jax.sharding import PartitionSpec as P

MAXLAG = 64
LAG_COUNT = 2 * MAXLAG + 1
LANES = 256
IN_PARTS = 4
GROUP = 8
HOPS = (3, 2, 1, 0)


def broadcast(value, axis, source):
    kept = jnp.where(lax.axis_index(axis) == source, value, 0).astype(value.dtype)
    return lax.psum(kept, axis)


def toeplitz_rows(group, lag_count, segment):
    shifted = jnp.stack(
        [group[:, :, lag_step : lag_step + segment] for lag_step in range(lag_count)], axis=1
    )
    return shifted.reshape(group.shape[0] * lag_count, -1)


def many_channels(traces, valid_flags, source_index):
    segment = traces.shape[2]
    centered = traces - jnp.mean(traces, axis=2, keepdims=True)
    mean_power = jnp.mean(centered * centered, axis=2, keepdims=True)
    flag_values = valid_flags[:, :, None].astype(jnp.float32)
    whitened = (centered * lax.rsqrt(mean_power + 1e-05) * flag_values).astype(jnp.bfloat16)
    pieces = []
    for owner in range(lax.axis_size("src")):
        pieces.append(broadcast(whitened, "src", owner))
    everyone = jnp.concatenate(pieces, axis=0)
    sources = jnp.take(everyone, source_index, axis=0)
    source_count = sources.shape[0]
    norm_factor = 1.0 / math.sqrt(traces.shape[1] * lax.axis_size("blk") * segment)
    own_rows = whitened.shape[0] // lax.axis_size("blk")
    flat_sources = sources.reshape(source_count, -1)
    padded = jnp.pad(whitened, ((0, 0), (0, 0), (MAXLAG, MAXLAG)))
    block_rows = math.gcd(lax.axis_size("blk") * own_rows, 16)
    grouped = padded.reshape(
        (lax.axis_size("blk") * own_rows // block_rows, block_rows) + padded.shape[1:]
    )

    def one_block(group):
        toeplitz = toeplitz_rows(group, LAG_COUNT, segment)
        products = lax.dot_general(
            toeplitz, flat_sources, (((1,), (1,)), ((), ())), preferred_element_type=jnp.float32
        )
        return (products * norm_factor).reshape(block_rows, LAG_COUNT, source_count)

    result = lax.map(one_block, grouped)
    return lax.psum_scatter(
        result.reshape(lax.axis_size("blk") * own_rows, LAG_COUNT, source_count),
        "blk",
        scatter_dimension=0,
        tiled=True,
    )


class Plan:
    def __init__(self, half, windows, segment, blk_size, src_size, source_count):
        self.half = half
        self.windows = windows
        self.segment = segment
        self.blk_size = blk_size
        self.src_size = src_size
        self.channels = half * src_size
        self.source_count = source_count
        self.half_lanes = LANES // 2
        self.coarse = self.half_lanes // half
        if self.coarse == 0:
            return
        self.fine = -(-LAG_COUNT // self.coarse)
        self.fine_padded = -(-self.fine // (2 * GROUP)) * 2 * GROUP
        self.own = half // blk_size
        reach = segment + (self.coarse - 1) * self.fine
        self.span = -(-max(reach, segment + 2 * MAXLAG) // 128) * 128
        self.whole_groups = self.fine // GROUP * GROUP
        self.rest = self.fine - self.whole_groups
        rows = self.own * self.fine
        self.rows = -(-rows // 16) * 16
        self.targets = blk_size // 2
        self.receivers = self.targets * self.own
        self.lag_rows = -(-self.receivers * self.fine // 32) * 32
        self.norm_factor = 1.0 / math.sqrt(windows * blk_size * segment)

    def fits(self):
        return (
            self.coarse >= 2
            and self.src_size == 2
            and self.half % self.blk_size == 0
            and self.half % GROUP == 0
            and self.channels % 16 == 0
            and self.windows * self.half % 16 == 0
            and self.blk_size == 8
            and self.rest > 0
            and GROUP % self.rest == 0
            and self.receivers * self.rest % GROUP == 0
            and self.receivers % 2 == 0
            and self.receivers * self.whole_groups % 16 == 0
        )


def whiten_kernel(plan, traces_hbm, flags_hbm, out_ref, traces_ref, flags_ref, sems):
    part = plan.half // IN_PARTS
    copies = [pltpu.make_async_copy(flags_hbm, flags_ref, sems.at[IN_PARTS])]
    for index in range(IN_PARTS):
        at = pl.ds(index * part, part)
        copies.append(pltpu.make_async_copy(traces_hbm.at[at], traces_ref.at[at], sems.at[index]))
    for copy in copies:
        copy.start()
    copies[0].wait()
    flag_values = [
        flags_ref[window : window + 1, :].astype(jnp.float32).reshape(plan.half, 1) for window in range(plan.windows)
    ]
    for copy in copies[1:]:
        copy.wait()
    pieces = []
    for window in range(plan.windows):
        values = traces_ref[:, window, :]
        centered = values - jnp.mean(values, axis=1, keepdims=True)
        mean_power = jnp.mean(centered * centered, axis=1, keepdims=True)
        pieces.append(centered * lax.rsqrt(mean_power + 1e-05) * flag_values[window])
    out_ref[...] = jnp.concatenate(pieces, axis=0).astype(jnp.bfloat16)


def lag_rows(plan, rows_ref, toeplitz_ref):
    span = plan.span
    me = lax.axis_index("blk")
    filler = jnp.zeros((1, span - plan.segment), jnp.float32)
    spare = jnp.zeros((plan.lag_rows - plan.receivers * plan.fine, span), jnp.float32)
    sublane = lax.broadcasted_iota(jnp.int32, (GROUP, span), 0)
    for window in range(plan.windows):
        at = slice(window * span, (window + 1) * span)
        spread_rows = []
        for hop in HOPS:
            for member in range(plan.own):
                channel = window * plan.half + (me ^ hop) * plan.own + member
                row = jnp.concatenate([rows_ref[pl.ds(channel, 1), :], filler], axis=1)
                spread_rows.append(jnp.broadcast_to(row, (GROUP, span)))
        for first in range(0, plan.receivers, 2):
            pieces = [
                pltpu.roll(row, (MAXLAG - plan.whole_groups + 1 + lag) % span, 1, stride=1, stride_axis=0)
                for row in spread_rows[first : first + 2]
                for lag in range(0, plan.whole_groups, GROUP)
            ]
            start = first * plan.whole_groups
            toeplitz_ref[start : start + 2 * plan.whole_groups, at] = jnp.concatenate(pieces, axis=0).astype(
                jnp.bfloat16
            )
        pieces = []
        for first in range(0, plan.receivers, GROUP // plan.rest):
            mixed = spread_rows[first]
            for index in range(1, GROUP // plan.rest):
                mixed = jnp.where(sublane >= index * plan.rest, spread_rows[first + index], mixed)
            tile = pltpu.roll(mixed, (MAXLAG - plan.whole_groups) % span, 1)
            for lag in range(1, plan.rest):
                later = pltpu.roll(mixed, (MAXLAG - plan.whole_groups - lag) % span, 1)
                tile = jnp.where(sublane % plan.rest == lag, later, tile)
            pieces.append(tile)
        start = plan.receivers * plan.whole_groups
        toeplitz_ref[start:, at] = jnp.concatenate(pieces + [spare], axis=0).astype(jnp.bfloat16)


def fill_columns(plan, values, columns_ref):
    span = plan.span
    filler = jnp.zeros((plan.half, span - plan.segment), jnp.float32)
    spare = jnp.zeros((plan.half_lanes - plan.coarse * plan.half, span), jnp.float32)
    for window in range(plan.windows):
        rows = jnp.concatenate([values[window * plan.half : (window + 1) * plan.half], filler], axis=1)
        pieces = [rows] + [pltpu.roll(rows, step * plan.fine, 1) for step in range(1, plan.coarse)]
        if spare.shape[0]:
            pieces.append(spare)
        columns_ref[:, window * span : (window + 1) * span] = jnp.concatenate(pieces, axis=0).astype(jnp.bfloat16)


def product(toeplitz_ref, columns_ref):
    return lax.dot_general(
        toeplitz_ref[...], columns_ref[...], (((1,), (1,)), ((), ())), preferred_element_type=jnp.float32
    )


def near_kernel(plan, *refs):
    mine_refs, (other_ref, sum_ref, rows_ref, toeplitz_ref, columns_ref) = refs[: plan.windows], refs[plan.windows :]
    for window, mine_ref in enumerate(mine_refs):
        rows_ref[window * plan.half : (window + 1) * plan.half, :] = mine_ref[...].astype(jnp.float32)
    lag_rows(plan, rows_ref, toeplitz_ref)
    fill_columns(plan, rows_ref[...], columns_ref.at[: plan.half_lanes])
    fill_columns(plan, other_ref[...].astype(jnp.float32), columns_ref.at[plan.half_lanes :])
    sum_ref[...] = product(toeplitz_ref, columns_ref)


def across_kernel(plan, mine_ref, prior_ref, toeplitz_ref, left_ref, right_ref, rows_ref, columns_ref):
    rows_ref[...] = mine_ref[...].astype(jnp.float32)
    lag_rows(plan, rows_ref, toeplitz_ref)
    fill_columns(plan, rows_ref[...], columns_ref)
    left = prior_ref[:, : plan.half_lanes] + product(toeplitz_ref, columns_ref)
    for place, block in enumerate(pack(plan, left)):
        left_ref[place * plan.rows : (place + 1) * plan.rows, :] = block
    right_ref[...] = prior_ref[:, plan.half_lanes :]


def pack(plan, products):
    width = products.shape[1]
    back = GROUP - 1 - lax.broadcasted_iota(jnp.int32, (GROUP, width), 0)
    packed = []
    for place in range(plan.targets):
        pieces = []
        for receiver in range(place * plan.own, (place + 1) * plan.own):
            last = (receiver + 1) * plan.whole_groups
            pieces += [
                jnp.take_along_axis(products[last - lag - GROUP : last - lag], back, axis=0)
                for lag in range(0, plan.whole_groups, GROUP)
            ]
        first = plan.receivers * plan.whole_groups + place * plan.own * plan.rest
        pieces.append(products[first : first + plan.own * plan.rest])
        if plan.rows > plan.own * plan.fine:
            pieces.append(jnp.zeros((plan.rows - plan.own * plan.fine, width), jnp.float32))
        packed.append(jnp.concatenate(pieces, axis=0))
    return packed


def finish_kernel(plan, other_ref, toeplitz_ref, left_ref, right_ref, *refs):
    *out_refs, columns_ref = refs
    fill_columns(plan, other_ref[...].astype(jnp.float32), columns_ref)
    right = pack(plan, right_ref[...] + product(toeplitz_ref, columns_ref))
    for place, out_ref in enumerate(out_refs):
        rows = slice(place * plan.rows, (place + 1) * plan.rows)
        out_ref[...] = jnp.concatenate([left_ref[rows, :], right[place]], axis=1).astype(jnp.bfloat16)


def spread(plan, values):
    high = values.astype(jnp.bfloat16).astype(jnp.float32)
    low = values - high
    lane = lax.broadcasted_iota(jnp.int32, values.shape, 1)
    lane = jnp.where(lane >= plan.half_lanes, lane - plan.half_lanes, lane)
    up = pltpu.roll(low, plan.half, 1)
    down = pltpu.roll(low, LANES - plan.half, 1)
    pieces = []
    for step in range(plan.coarse):
        beside, moved = (step + 1, up) if step + 1 < plan.coarse else (step - 1, down)
        kept = jnp.where((lane >= step * plan.half) & (lane < (step + 1) * plan.half), high, 0.0)
        there = (lane >= beside * plan.half) & (lane < (beside + 1) * plan.half)
        pieces.append(jnp.where(there, moved, kept).astype(jnp.bfloat16))
    return jnp.concatenate(pieces, axis=0)


def choose_kernel(plan, index_ref, whitened_ref, chosen_ref, *same_refs):
    whitened = whitened_ref[...].astype(jnp.float32)
    for window, same_ref in enumerate(same_refs):
        same_ref[...] = whitened[window * plan.half : (window + 1) * plan.half].astype(jnp.bfloat16)
    first = lax.axis_index("src") * plan.half
    index = index_ref[...] - first
    index = jnp.where(index < 0, index + plan.channels, index)
    lane = jnp.where(index >= plan.half, index - plan.half + plan.half_lanes, index)
    at_column = lax.broadcasted_iota(jnp.int32, (LANES, plan.source_count), 0)
    chosen = jnp.zeros((LANES, plan.source_count), jnp.bool_)
    for step in range(plan.coarse):
        chosen = chosen | (at_column == lane + step * plan.half)
    chosen_ref[...] = chosen.astype(jnp.float32).astype(jnp.bfloat16)


def expand_kernel(plan, chosen_ref, *refs):
    *arrived_refs, out_hbm, out_ref, sems = refs
    total = sum(ref[...].astype(jnp.float32) for ref in arrived_refs) * plan.norm_factor
    chosen = chosen_ref[...]
    filler = jnp.zeros((plan.fine_padded - plan.fine, LANES), jnp.float32)
    copies = []
    for member in range(plan.own):
        rest = plan.own * plan.whole_groups + member * plan.rest
        rows = jnp.concatenate(
            [
                total[member * plan.whole_groups : (member + 1) * plan.whole_groups],
                total[rest : rest + plan.rest],
                filler,
            ],
            axis=0,
        )
        expanded = jnp.dot(spread(plan, rows), chosen, preferred_element_type=jnp.float32)
        for step in range(plan.coarse):
            start = step * plan.fine
            count = min(plan.fine, LAG_COUNT - start)
            first = step * plan.fine_padded
            out_ref[member, start : start + count, :] = expanded[first : first + count]
        copies.append(pltpu.make_async_copy(out_ref.at[member], out_hbm.at[member], sems.at[member]))
        copies[-1].start()
    for copy in copies:
        copy.wait()


def few_channels(plan, traces, valid_flags, source_index):
    vmem = pl.BlockSpec(memory_space=pltpu.VMEM)
    params = pltpu.CompilerParams(vmem_limit_bytes=32 * 1024 * 1024)
    packed_rows = plan.windows * plan.half
    flags = valid_flags.T

    def swap_cores(array):
        return lax.ppermute(array, "src", [(0, 1), (1, 0)])

    def swap_blk(array, hop):
        pairs = [
            (place * plan.src_size + core, (place ^ hop) * plan.src_size + 1 - core)
            for place in range(plan.blk_size)
            for core in range(plan.src_size)
        ]
        return lax.ppermute(array, ("blk", "src"), pairs)

    whitened = pl.pallas_call(
        functools.partial(whiten_kernel, plan),
        out_shape=pltpu.VMEM((packed_rows, plan.segment), jnp.bfloat16),
        in_specs=[pl.BlockSpec(memory_space=pl.ANY)] * 2,
        out_specs=vmem,
        scratch_shapes=[
            pltpu.VMEM(traces.shape, jnp.float32),
            pltpu.VMEM(flags.shape, jnp.int32),
            pltpu.SemaphoreType.DMA((IN_PARTS + 1,)),
        ],
        compiler_params=pltpu.CompilerParams(vmem_limit_bytes=60 * 1024 * 1024),
        name="whiten",
    )(traces, flags)

    height = plan.lag_rows
    width = plan.windows * plan.span
    rows = pltpu.VMEM((packed_rows, plan.segment), jnp.float32)
    toeplitz = (height, width)
    columns = (plan.half_lanes, width)
    sums = jax.ShapeDtypeStruct((height, LANES), jnp.float32)

    def call(kernel, name, operands, outputs, scratch=()):
        return pl.pallas_call(
            functools.partial(kernel, plan),
            out_shape=outputs,
            in_specs=[vmem] * len(operands),
            out_specs=[vmem] * len(outputs),
            scratch_shapes=scratch,
            compiler_params=params,
            name=name,
        )(*operands)

    across = swap_blk(whitened, plan.blk_size - 2)
    chosen, *same = call(
        choose_kernel,
        "choose",
        (source_index.reshape(1, -1), whitened),
        (
            jax.ShapeDtypeStruct((LANES, plan.source_count), jnp.bfloat16),
            *[jax.ShapeDtypeStruct((plan.half, plan.segment), whitened.dtype)] * plan.windows,
        ),
    )
    (total,) = call(
        near_kernel,
        "near",
        (*[swap_cores(array) for array in same], whitened),
        (sums,),
        (rows, pltpu.VMEM(toeplitz, jnp.bfloat16), pltpu.VMEM((LANES, width), jnp.bfloat16)),
    )
    across, total = lax.optimization_barrier((across, total))
    across_other = swap_cores(across)
    lagged, left, right = call(
        across_kernel,
        "across",
        (across, total),
        (
            jax.ShapeDtypeStruct(toeplitz, jnp.bfloat16),
            jax.ShapeDtypeStruct((plan.targets * plan.rows, plan.half_lanes), jnp.float32),
            jax.ShapeDtypeStruct((height, plan.half_lanes), jnp.float32),
        ),
        (rows, pltpu.VMEM(columns, jnp.bfloat16)),
    )
    sent = call(
        finish_kernel,
        "finish",
        (across_other, lagged, left, right),
        (jax.ShapeDtypeStruct((plan.rows, LANES), jnp.bfloat16),) * plan.targets,
        (pltpu.VMEM(columns, jnp.bfloat16),),
    )
    arrived = [swap_blk(array, hop) for array, hop in zip(sent, HOPS)]
    out_shape = (plan.own, LAG_COUNT, plan.source_count)
    return pl.pallas_call(
        functools.partial(expand_kernel, plan),
        out_shape=jax.ShapeDtypeStruct(out_shape, jnp.float32),
        in_specs=[vmem] * (1 + len(arrived)),
        out_specs=pl.BlockSpec(memory_space=pl.ANY),
        scratch_shapes=[pltpu.VMEM(out_shape, jnp.float32), pltpu.SemaphoreType.DMA((plan.own,))],
        compiler_params=params,
        name="expand",
    )(chosen, *arrived)


def body(traces, valid_flags, source_index):
    plan = Plan(
        traces.shape[0],
        traces.shape[1],
        traces.shape[2],
        lax.axis_size("blk"),
        lax.axis_size("src"),
        source_index.shape[0],
    )
    if plan.fits():
        return few_channels(plan, traces, valid_flags, source_index)
    return many_channels(traces, valid_flags, source_index)


def solution(mesh):
    in_specs = (P(("fibre", "src"), "blk", None), P(("fibre", "src"), "blk"), P())
    out_specs = P(("fibre", "src", "blk"), None, None)
    return jax.shard_map(body, mesh=mesh, in_specs=in_specs, out_specs=out_specs, check_vma=False)
```

```python
import functools
import math

import jax
import jax.numpy as jnp
from jax import lax
from jax.experimental import pallas as pl
from jax.experimental.pallas import tpu as pltpu
from jax.sharding import PartitionSpec as P

MAXLAG = 64
LAG_COUNT = 2 * MAXLAG + 1
LANES = 256
IN_PARTS = 4
GROUP = 8
HOPS = (3, 2, 1, 0)


def broadcast(value, axis, source):
    kept = jnp.where(lax.axis_index(axis) == source, value, 0).astype(value.dtype)
    return lax.psum(kept, axis)


def toeplitz_rows(group, lag_count, segment):
    shifted = jnp.stack(
        [group[:, :, lag_step : lag_step + segment] for lag_step in range(lag_count)], axis=1
    )
    return shifted.reshape(group.shape[0] * lag_count, -1)


def many_channels(traces, valid_flags, source_index):
    segment = traces.shape[2]
    centered = traces - jnp.mean(traces, axis=2, keepdims=True)
    mean_power = jnp.mean(centered * centered, axis=2, keepdims=True)
    flag_values = valid_flags[:, :, None].astype(jnp.float32)
    whitened = (centered * lax.rsqrt(mean_power + 1e-05) * flag_values).astype(jnp.bfloat16)
    pieces = []
    for owner in range(lax.axis_size("src")):
        pieces.append(broadcast(whitened, "src", owner))
    everyone = jnp.concatenate(pieces, axis=0)
    sources = jnp.take(everyone, source_index, axis=0)
    source_count = sources.shape[0]
    norm_factor = 1.0 / math.sqrt(traces.shape[1] * lax.axis_size("blk") * segment)
    own_rows = whitened.shape[0] // lax.axis_size("blk")
    flat_sources = sources.reshape(source_count, -1)
    padded = jnp.pad(whitened, ((0, 0), (0, 0), (MAXLAG, MAXLAG)))
    block_rows = math.gcd(lax.axis_size("blk") * own_rows, 16)
    grouped = padded.reshape(
        (lax.axis_size("blk") * own_rows // block_rows, block_rows) + padded.shape[1:]
    )

    def one_block(group):
        toeplitz = toeplitz_rows(group, LAG_COUNT, segment)
        products = lax.dot_general(
            toeplitz, flat_sources, (((1,), (1,)), ((), ())), preferred_element_type=jnp.float32
        )
        return (products * norm_factor).reshape(block_rows, LAG_COUNT, source_count)

    result = lax.map(one_block, grouped)
    return lax.psum_scatter(
        result.reshape(lax.axis_size("blk") * own_rows, LAG_COUNT, source_count),
        "blk",
        scatter_dimension=0,
        tiled=True,
    )


class Plan:
    def __init__(self, half, windows, segment, blk_size, src_size, source_count):
        self.half = half
        self.windows = windows
        self.segment = segment
        self.blk_size = blk_size
        self.src_size = src_size
        self.channels = half * src_size
        self.source_count = source_count
        self.half_lanes = LANES // 2
        self.coarse = self.half_lanes // half
        if self.coarse == 0:
            return
        self.fine = -(-LAG_COUNT // self.coarse)
        self.fine_padded = -(-self.fine // (2 * GROUP)) * 2 * GROUP
        self.own = half // blk_size
        reach = segment + (self.coarse - 1) * self.fine
        self.span = -(-max(reach, segment + 2 * MAXLAG) // 128) * 128
        self.whole_groups = self.fine // GROUP * GROUP
        self.rest = self.fine - self.whole_groups
        rows = self.own * self.fine
        self.rows = -(-rows // 16) * 16
        self.targets = blk_size // 2
        self.receivers = self.targets * self.own
        self.lag_rows = -(-self.receivers * self.fine // 32) * 32
        self.norm_factor = 1.0 / math.sqrt(windows * blk_size * segment)

    def fits(self):
        return (
            self.coarse >= 2
            and self.src_size == 2
            and self.half % self.blk_size == 0
            and self.half % GROUP == 0
            and self.channels % 16 == 0
            and self.windows * self.half % 16 == 0
            and self.blk_size == 8
            and self.rest > 0
            and GROUP % self.rest == 0
            and self.receivers * self.rest % GROUP == 0
            and self.receivers % 2 == 0
            and self.receivers * self.whole_groups % 16 == 0
        )


def whiten_kernel(plan, traces_hbm, flags_hbm, out_ref, traces_ref, flags_ref, sems):
    part = plan.half // IN_PARTS
    copies = [pltpu.make_async_copy(flags_hbm, flags_ref, sems.at[IN_PARTS])]
    for index in range(IN_PARTS):
        at = pl.ds(index * part, part)
        copies.append(pltpu.make_async_copy(traces_hbm.at[at], traces_ref.at[at], sems.at[index]))
    for copy in copies:
        copy.start()
    copies[0].wait()
    flag_values = [
        flags_ref[window : window + 1, :].astype(jnp.float32).reshape(plan.half, 1) for window in range(plan.windows)
    ]
    for copy in copies[1:]:
        copy.wait()
    pieces = []
    for window in range(plan.windows):
        values = traces_ref[:, window, :]
        centered = values - jnp.mean(values, axis=1, keepdims=True)
        mean_power = jnp.mean(centered * centered, axis=1, keepdims=True)
        pieces.append(centered * lax.rsqrt(mean_power + 1e-05) * flag_values[window])
    out_ref[...] = jnp.concatenate(pieces, axis=0).astype(jnp.bfloat16)


def lag_rows(plan, rows_ref, toeplitz_ref):
    span = plan.span
    me = lax.axis_index("blk")
    filler = jnp.zeros((1, span - plan.segment), jnp.float32)
    spare = jnp.zeros((plan.lag_rows - plan.receivers * plan.fine, span), jnp.float32)
    sublane = lax.broadcasted_iota(jnp.int32, (GROUP, span), 0)
    for window in range(plan.windows):
        at = slice(window * span, (window + 1) * span)
        spread_rows = []
        for hop in HOPS:
            for member in range(plan.own):
                channel = window * plan.half + (me ^ hop) * plan.own + member
                row = jnp.concatenate([rows_ref[pl.ds(channel, 1), :], filler], axis=1)
                spread_rows.append(jnp.broadcast_to(row, (GROUP, span)))
        for first in range(0, plan.receivers, 2):
            pieces = [
                pltpu.roll(row, (MAXLAG - plan.whole_groups + 1 + lag) % span, 1, stride=1, stride_axis=0)
                for row in spread_rows[first : first + 2]
                for lag in range(0, plan.whole_groups, GROUP)
            ]
            start = first * plan.whole_groups
            toeplitz_ref[start : start + 2 * plan.whole_groups, at] = jnp.concatenate(pieces, axis=0).astype(
                jnp.bfloat16
            )
        pieces = []
        for first in range(0, plan.receivers, GROUP // plan.rest):
            mixed = spread_rows[first]
            for index in range(1, GROUP // plan.rest):
                mixed = jnp.where(sublane >= index * plan.rest, spread_rows[first + index], mixed)
            tile = pltpu.roll(mixed, (MAXLAG - plan.whole_groups) % span, 1)
            for lag in range(1, plan.rest):
                later = pltpu.roll(mixed, (MAXLAG - plan.whole_groups - lag) % span, 1)
                tile = jnp.where(sublane % plan.rest == lag, later, tile)
            pieces.append(tile)
        start = plan.receivers * plan.whole_groups
        toeplitz_ref[start:, at] = jnp.concatenate(pieces + [spare], axis=0).astype(jnp.bfloat16)


def fill_columns(plan, values, columns_ref):
    span = plan.span
    filler = jnp.zeros((plan.half, span - plan.segment), jnp.float32)
    spare = jnp.zeros((plan.half_lanes - plan.coarse * plan.half, span), jnp.float32)
    for window in range(plan.windows):
        rows = jnp.concatenate([values[window * plan.half : (window + 1) * plan.half], filler], axis=1)
        pieces = [rows] + [pltpu.roll(rows, step * plan.fine, 1) for step in range(1, plan.coarse)]
        if spare.shape[0]:
            pieces.append(spare)
        columns_ref[:, window * span : (window + 1) * span] = jnp.concatenate(pieces, axis=0).astype(jnp.bfloat16)


def product(toeplitz_ref, columns_ref):
    return lax.dot_general(
        toeplitz_ref[...], columns_ref[...], (((1,), (1,)), ((), ())), preferred_element_type=jnp.float32
    )


def near_kernel(plan, *refs):
    mine_refs, (other_ref, sum_ref, rows_ref, toeplitz_ref, columns_ref) = refs[: plan.windows], refs[plan.windows :]
    for window, mine_ref in enumerate(mine_refs):
        rows_ref[window * plan.half : (window + 1) * plan.half, :] = mine_ref[...].astype(jnp.float32)
    lag_rows(plan, rows_ref, toeplitz_ref)
    fill_columns(plan, rows_ref[...], columns_ref.at[: plan.half_lanes])
    fill_columns(plan, other_ref[...].astype(jnp.float32), columns_ref.at[plan.half_lanes :])
    sum_ref[...] = product(toeplitz_ref, columns_ref)


def across_kernel(plan, mine_ref, prior_ref, toeplitz_ref, left_ref, right_ref, rows_ref, columns_ref):
    rows_ref[...] = mine_ref[...].astype(jnp.float32)
    lag_rows(plan, rows_ref, toeplitz_ref)
    fill_columns(plan, rows_ref[...], columns_ref)
    left = prior_ref[:, : plan.half_lanes] + product(toeplitz_ref, columns_ref)
    for place, block in enumerate(pack(plan, left)):
        left_ref[place * plan.rows : (place + 1) * plan.rows, :] = block
    right_ref[...] = prior_ref[:, plan.half_lanes :]


def pack(plan, products):
    width = products.shape[1]
    back = GROUP - 1 - lax.broadcasted_iota(jnp.int32, (GROUP, width), 0)
    packed = []
    for place in range(plan.targets):
        pieces = []
        for receiver in range(place * plan.own, (place + 1) * plan.own):
            last = (receiver + 1) * plan.whole_groups
            pieces += [
                jnp.take_along_axis(products[last - lag - GROUP : last - lag], back, axis=0)
                for lag in range(0, plan.whole_groups, GROUP)
            ]
        first = plan.receivers * plan.whole_groups + place * plan.own * plan.rest
        pieces.append(products[first : first + plan.own * plan.rest])
        if plan.rows > plan.own * plan.fine:
            pieces.append(jnp.zeros((plan.rows - plan.own * plan.fine, width), jnp.float32))
        packed.append(jnp.concatenate(pieces, axis=0))
    return packed


def finish_kernel(plan, other_ref, toeplitz_ref, left_ref, right_ref, *refs):
    *out_refs, columns_ref = refs
    fill_columns(plan, other_ref[...].astype(jnp.float32), columns_ref)
    right = pack(plan, right_ref[...] + product(toeplitz_ref, columns_ref))
    for place, out_ref in enumerate(out_refs):
        rows = slice(place * plan.rows, (place + 1) * plan.rows)
        out_ref[...] = jnp.concatenate([left_ref[rows, :], right[place]], axis=1).astype(jnp.bfloat16)


def spread(plan, values):
    high = values.astype(jnp.bfloat16).astype(jnp.float32)
    low = values - high
    lane = lax.broadcasted_iota(jnp.int32, values.shape, 1)
    lane = jnp.where(lane >= plan.half_lanes, lane - plan.half_lanes, lane)
    up = pltpu.roll(low, plan.half, 1)
    down = pltpu.roll(low, LANES - plan.half, 1)
    pieces = []
    for step in range(plan.coarse):
        beside, moved = (step + 1, up) if step + 1 < plan.coarse else (step - 1, down)
        kept = jnp.where((lane >= step * plan.half) & (lane < (step + 1) * plan.half), high, 0.0)
        there = (lane >= beside * plan.half) & (lane < (beside + 1) * plan.half)
        pieces.append(jnp.where(there, moved, kept).astype(jnp.bfloat16))
    return jnp.concatenate(pieces, axis=0)


def choose_kernel(plan, index_ref, whitened_ref, chosen_ref, *same_refs):
    whitened = whitened_ref[...].astype(jnp.float32)
    for window, same_ref in enumerate(same_refs):
        same_ref[...] = whitened[window * plan.half : (window + 1) * plan.half].astype(jnp.bfloat16)
    first = lax.axis_index("src") * plan.half
    index = index_ref[...] - first
    index = jnp.where(index < 0, index + plan.channels, index)
    lane = jnp.where(index >= plan.half, index - plan.half + plan.half_lanes, index)
    at_column = lax.broadcasted_iota(jnp.int32, (LANES, plan.source_count), 0)
    chosen = jnp.zeros((LANES, plan.source_count), jnp.bool_)
    for step in range(plan.coarse):
        chosen = chosen | (at_column == lane + step * plan.half)
    chosen_ref[...] = chosen.astype(jnp.float32).astype(jnp.bfloat16)


def expand_kernel(plan, chosen_ref, *refs):
    *arrived_refs, out_hbm, out_ref, sems = refs
    total = sum(ref[...].astype(jnp.float32) for ref in arrived_refs) * plan.norm_factor
    chosen = chosen_ref[...]
    filler = jnp.zeros((plan.fine_padded - plan.fine, LANES), jnp.float32)
    copies = []
    for member in range(plan.own):
        rest = plan.own * plan.whole_groups + member * plan.rest
        rows = jnp.concatenate(
            [
                total[member * plan.whole_groups : (member + 1) * plan.whole_groups],
                total[rest : rest + plan.rest],
                filler,
            ],
            axis=0,
        )
        expanded = jnp.dot(spread(plan, rows), chosen, preferred_element_type=jnp.float32)
        for step in range(plan.coarse):
            start = step * plan.fine
            count = min(plan.fine, LAG_COUNT - start)
            first = step * plan.fine_padded
            out_ref[member, start : start + count, :] = expanded[first : first + count]
        whole = LAG_COUNT // GROUP * GROUP
        for part, rows in enumerate((pl.ds(0, whole), pl.ds(whole, LAG_COUNT - whole))):
            at = (member, rows)
            copies.append(pltpu.make_async_copy(out_ref.at[at], out_hbm.at[at], sems.at[member, part]))
            copies[-1].start()
    for copy in copies:
        copy.wait()


def few_channels(plan, traces, valid_flags, source_index):
    vmem = pl.BlockSpec(memory_space=pltpu.VMEM)
    params = pltpu.CompilerParams(vmem_limit_bytes=32 * 1024 * 1024)
    packed_rows = plan.windows * plan.half
    flags = valid_flags.T

    def swap_cores(array):
        return lax.ppermute(array, "src", [(0, 1), (1, 0)])

    def swap_blk(array, hop):
        pairs = [
            (place * plan.src_size + core, (place ^ hop) * plan.src_size + 1 - core)
            for place in range(plan.blk_size)
            for core in range(plan.src_size)
        ]
        return lax.ppermute(array, ("blk", "src"), pairs)

    whitened = pl.pallas_call(
        functools.partial(whiten_kernel, plan),
        out_shape=pltpu.VMEM((packed_rows, plan.segment), jnp.bfloat16),
        in_specs=[pl.BlockSpec(memory_space=pl.ANY)] * 2,
        out_specs=vmem,
        scratch_shapes=[
            pltpu.VMEM(traces.shape, jnp.float32),
            pltpu.VMEM(flags.shape, jnp.int32),
            pltpu.SemaphoreType.DMA((IN_PARTS + 1,)),
        ],
        compiler_params=pltpu.CompilerParams(vmem_limit_bytes=60 * 1024 * 1024),
        name="whiten",
    )(traces, flags)

    height = plan.lag_rows
    width = plan.windows * plan.span
    rows = pltpu.VMEM((packed_rows, plan.segment), jnp.float32)
    toeplitz = (height, width)
    columns = (plan.half_lanes, width)
    sums = jax.ShapeDtypeStruct((height, LANES), jnp.float32)

    def call(kernel, name, operands, outputs, scratch=()):
        return pl.pallas_call(
            functools.partial(kernel, plan),
            out_shape=outputs,
            in_specs=[vmem] * len(operands),
            out_specs=[vmem] * len(outputs),
            scratch_shapes=scratch,
            compiler_params=params,
            name=name,
        )(*operands)

    across = swap_blk(whitened, plan.targets)
    chosen, *same = call(
        choose_kernel,
        "choose",
        (source_index.reshape(1, -1), whitened),
        (
            jax.ShapeDtypeStruct((LANES, plan.source_count), jnp.bfloat16),
            *[jax.ShapeDtypeStruct((plan.half, plan.segment), whitened.dtype)] * plan.windows,
        ),
    )
    (total,) = call(
        near_kernel,
        "near",
        (*[swap_cores(array) for array in same], whitened),
        (sums,),
        (rows, pltpu.VMEM(toeplitz, jnp.bfloat16), pltpu.VMEM((LANES, width), jnp.bfloat16)),
    )
    across, total = lax.optimization_barrier((across, total))
    across_other = swap_cores(across)
    lagged, left, right = call(
        across_kernel,
        "across",
        (across, total),
        (
            jax.ShapeDtypeStruct(toeplitz, jnp.bfloat16),
            jax.ShapeDtypeStruct((plan.targets * plan.rows, plan.half_lanes), jnp.float32),
            jax.ShapeDtypeStruct((height, plan.half_lanes), jnp.float32),
        ),
        (rows, pltpu.VMEM(columns, jnp.bfloat16)),
    )
    sent = call(
        finish_kernel,
        "finish",
        (across_other, lagged, left, right),
        (jax.ShapeDtypeStruct((plan.rows, LANES), jnp.bfloat16),) * plan.targets,
        (pltpu.VMEM(columns, jnp.bfloat16),),
    )
    arrived = [swap_blk(array, hop) for array, hop in zip(sent, HOPS)]
    out_shape = (plan.own, LAG_COUNT, plan.source_count)
    return pl.pallas_call(
        functools.partial(expand_kernel, plan),
        out_shape=jax.ShapeDtypeStruct(out_shape, jnp.float32),
        in_specs=[vmem] * (1 + len(arrived)),
        out_specs=pl.BlockSpec(memory_space=pl.ANY),
        scratch_shapes=[pltpu.VMEM(out_shape, jnp.float32), pltpu.SemaphoreType.DMA((plan.own, 2))],
        compiler_params=params,
        name="expand",
    )(chosen, *arrived)


def body(traces, valid_flags, source_index):
    plan = Plan(
        traces.shape[0],
        traces.shape[1],
        traces.shape[2],
        lax.axis_size("blk"),
        lax.axis_size("src"),
        source_index.shape[0],
    )
    if plan.fits():
        return few_channels(plan, traces, valid_flags, source_index)
    return many_channels(traces, valid_flags, source_index)


def solution(mesh):
    in_specs = (P(("fibre", "src"), "blk", None), P(("fibre", "src"), "blk"), P())
    out_specs = P(("fibre", "src", "blk"), None, None)
    return jax.shard_map(body, mesh=mesh, in_specs=in_specs, out_specs=out_specs, check_vma=False)
```

```python
import functools
import math

import jax
import jax.numpy as jnp
from jax import lax
from jax.experimental import pallas as pl
from jax.experimental.pallas import tpu as pltpu
from jax.sharding import PartitionSpec as P

MAXLAG = 64
LAG_COUNT = 2 * MAXLAG + 1
LANES = 256
IN_PARTS = 4
GROUP = 8
HOPS = (3, 2, 1, 0)


def broadcast(value, axis, source):
    kept = jnp.where(lax.axis_index(axis) == source, value, 0).astype(value.dtype)
    return lax.psum(kept, axis)


def toeplitz_rows(group, lag_count, segment):
    shifted = jnp.stack(
        [group[:, :, lag_step : lag_step + segment] for lag_step in range(lag_count)], axis=1
    )
    return shifted.reshape(group.shape[0] * lag_count, -1)


def many_channels(traces, valid_flags, source_index):
    segment = traces.shape[2]
    centered = traces - jnp.mean(traces, axis=2, keepdims=True)
    mean_power = jnp.mean(centered * centered, axis=2, keepdims=True)
    flag_values = valid_flags[:, :, None].astype(jnp.float32)
    whitened = (centered * lax.rsqrt(mean_power + 1e-05) * flag_values).astype(jnp.bfloat16)
    pieces = []
    for owner in range(lax.axis_size("src")):
        pieces.append(broadcast(whitened, "src", owner))
    everyone = jnp.concatenate(pieces, axis=0)
    sources = jnp.take(everyone, source_index, axis=0)
    source_count = sources.shape[0]
    norm_factor = 1.0 / math.sqrt(traces.shape[1] * lax.axis_size("blk") * segment)
    own_rows = whitened.shape[0] // lax.axis_size("blk")
    flat_sources = sources.reshape(source_count, -1)
    padded = jnp.pad(whitened, ((0, 0), (0, 0), (MAXLAG, MAXLAG)))
    block_rows = math.gcd(lax.axis_size("blk") * own_rows, 16)
    grouped = padded.reshape(
        (lax.axis_size("blk") * own_rows // block_rows, block_rows) + padded.shape[1:]
    )

    def one_block(group):
        toeplitz = toeplitz_rows(group, LAG_COUNT, segment)
        products = lax.dot_general(
            toeplitz, flat_sources, (((1,), (1,)), ((), ())), preferred_element_type=jnp.float32
        )
        return (products * norm_factor).reshape(block_rows, LAG_COUNT, source_count)

    result = lax.map(one_block, grouped)
    return lax.psum_scatter(
        result.reshape(lax.axis_size("blk") * own_rows, LAG_COUNT, source_count),
        "blk",
        scatter_dimension=0,
        tiled=True,
    )


class Plan:
    def __init__(self, half, windows, segment, blk_size, src_size, source_count):
        self.half = half
        self.windows = windows
        self.segment = segment
        self.blk_size = blk_size
        self.src_size = src_size
        self.channels = half * src_size
        self.source_count = source_count
        self.half_lanes = LANES // 2
        self.coarse = self.half_lanes // half
        if self.coarse == 0:
            return
        self.fine = -(-LAG_COUNT // self.coarse)
        self.fine_padded = -(-self.fine // (2 * GROUP)) * 2 * GROUP
        self.own = half // blk_size
        reach = segment + (self.coarse - 1) * self.fine
        self.span = -(-max(reach, segment + 2 * MAXLAG) // 128) * 128
        self.whole_groups = self.fine // GROUP * GROUP
        self.rest = self.fine - self.whole_groups
        rows = self.own * self.fine
        self.rows = -(-rows // 16) * 16
        self.targets = blk_size // 2
        self.receivers = self.targets * self.own
        self.lag_rows = -(-self.receivers * self.fine // 32) * 32
        self.norm_factor = 1.0 / math.sqrt(windows * blk_size * segment)

    def fits(self):
        return (
            self.coarse >= 2
            and self.src_size == 2
            and self.half % self.blk_size == 0
            and self.half % GROUP == 0
            and self.channels % 16 == 0
            and self.windows * self.half % 16 == 0
            and self.blk_size == 8
            and self.rest > 0
            and GROUP % self.rest == 0
            and self.receivers * self.rest % GROUP == 0
            and self.receivers % 2 == 0
            and self.receivers * self.whole_groups % 16 == 0
        )


def whiten_kernel(plan, traces_hbm, flags_hbm, out_ref, traces_ref, flags_ref, sems):
    part = plan.half // IN_PARTS
    copies = [pltpu.make_async_copy(flags_hbm, flags_ref, sems.at[IN_PARTS])]
    for index in range(IN_PARTS):
        at = pl.ds(index * part, part)
        copies.append(pltpu.make_async_copy(traces_hbm.at[at], traces_ref.at[at], sems.at[index]))
    for copy in copies:
        copy.start()
    copies[0].wait()
    flag_values = [
        flags_ref[window : window + 1, :].astype(jnp.float32).reshape(plan.half, 1) for window in range(plan.windows)
    ]
    for copy in copies[1:]:
        copy.wait()
    pieces = []
    for window in range(plan.windows):
        values = traces_ref[:, window, :]
        centered = values - jnp.mean(values, axis=1, keepdims=True)
        mean_power = jnp.mean(centered * centered, axis=1, keepdims=True)
        pieces.append(centered * lax.rsqrt(mean_power + 1e-05) * flag_values[window])
    out_ref[...] = jnp.concatenate(pieces, axis=0).astype(jnp.bfloat16)


def lag_rows(plan, rows_ref, toeplitz_ref):
    span = plan.span
    me = lax.axis_index("blk")
    filler = jnp.zeros((1, span - plan.segment), jnp.float32)
    spare = jnp.zeros((plan.lag_rows - plan.receivers * plan.fine, span), jnp.float32)
    sublane = lax.broadcasted_iota(jnp.int32, (GROUP, span), 0)
    for window in range(plan.windows):
        at = slice(window * span, (window + 1) * span)
        spread_rows = []
        for hop in HOPS:
            for member in range(plan.own):
                channel = window * plan.half + (me ^ hop) * plan.own + member
                row = jnp.concatenate([rows_ref[pl.ds(channel, 1), :], filler], axis=1)
                spread_rows.append(jnp.broadcast_to(row, (GROUP, span)))
        for first in range(0, plan.receivers, 2):
            pieces = [
                pltpu.roll(row, (MAXLAG - plan.whole_groups + 1 + lag) % span, 1, stride=1, stride_axis=0)
                for row in spread_rows[first : first + 2]
                for lag in range(0, plan.whole_groups, GROUP)
            ]
            start = first * plan.whole_groups
            toeplitz_ref[start : start + 2 * plan.whole_groups, at] = jnp.concatenate(pieces, axis=0).astype(
                jnp.bfloat16
            )
        pieces = []
        for first in range(0, plan.receivers, GROUP // plan.rest):
            mixed = spread_rows[first]
            for index in range(1, GROUP // plan.rest):
                mixed = jnp.where(sublane >= index * plan.rest, spread_rows[first + index], mixed)
            tile = pltpu.roll(mixed, (MAXLAG - plan.whole_groups) % span, 1)
            for lag in range(1, plan.rest):
                later = pltpu.roll(mixed, (MAXLAG - plan.whole_groups - lag) % span, 1)
                tile = jnp.where(sublane % plan.rest == lag, later, tile)
            pieces.append(tile)
        start = plan.receivers * plan.whole_groups
        toeplitz_ref[start:, at] = jnp.concatenate(pieces + [spare], axis=0).astype(jnp.bfloat16)


def fill_columns(plan, values, columns_ref):
    span = plan.span
    filler = jnp.zeros((plan.half, span - plan.segment), jnp.float32)
    spare = jnp.zeros((plan.half_lanes - plan.coarse * plan.half, span), jnp.float32)
    for window in range(plan.windows):
        rows = jnp.concatenate([values[window * plan.half : (window + 1) * plan.half], filler], axis=1)
        pieces = [rows] + [pltpu.roll(rows, step * plan.fine, 1) for step in range(1, plan.coarse)]
        if spare.shape[0]:
            pieces.append(spare)
        columns_ref[:, window * span : (window + 1) * span] = jnp.concatenate(pieces, axis=0).astype(jnp.bfloat16)


def product(toeplitz_ref, columns_ref):
    return lax.dot_general(
        toeplitz_ref[...], columns_ref[...], (((1,), (1,)), ((), ())), preferred_element_type=jnp.float32
    )


def near_kernel(plan, *refs):
    mine_refs, (other_ref, sum_ref, rows_ref, toeplitz_ref, columns_ref) = refs[: plan.windows], refs[plan.windows :]
    for window, mine_ref in enumerate(mine_refs):
        rows_ref[window * plan.half : (window + 1) * plan.half, :] = mine_ref[...].astype(jnp.float32)
    lag_rows(plan, rows_ref, toeplitz_ref)
    fill_columns(plan, rows_ref[...], columns_ref.at[: plan.half_lanes])
    fill_columns(plan, other_ref[...].astype(jnp.float32), columns_ref.at[plan.half_lanes :])
    sum_ref[...] = product(toeplitz_ref, columns_ref)


def across_kernel(plan, mine_ref, prior_ref, toeplitz_ref, left_ref, right_ref, rows_ref, columns_ref):
    rows_ref[...] = mine_ref[...].astype(jnp.float32)
    lag_rows(plan, rows_ref, toeplitz_ref)
    fill_columns(plan, rows_ref[...], columns_ref)
    left = prior_ref[:, : plan.half_lanes] + product(toeplitz_ref, columns_ref)
    for place, block in enumerate(pack(plan, left)):
        left_ref[place * plan.rows : (place + 1) * plan.rows, :] = block
    right_ref[...] = prior_ref[:, plan.half_lanes :]


def pack(plan, products):
    width = products.shape[1]
    back = GROUP - 1 - lax.broadcasted_iota(jnp.int32, (GROUP, width), 0)
    packed = []
    for place in range(plan.targets):
        pieces = []
        for receiver in range(place * plan.own, (place + 1) * plan.own):
            last = (receiver + 1) * plan.whole_groups
            pieces += [
                jnp.take_along_axis(products[last - lag - GROUP : last - lag], back, axis=0)
                for lag in range(0, plan.whole_groups, GROUP)
            ]
        first = plan.receivers * plan.whole_groups + place * plan.own * plan.rest
        pieces.append(products[first : first + plan.own * plan.rest])
        if plan.rows > plan.own * plan.fine:
            pieces.append(jnp.zeros((plan.rows - plan.own * plan.fine, width), jnp.float32))
        packed.append(jnp.concatenate(pieces, axis=0))
    return packed


def finish_kernel(plan, other_ref, toeplitz_ref, left_ref, right_ref, *refs):
    *out_refs, columns_ref = refs
    fill_columns(plan, other_ref[...].astype(jnp.float32), columns_ref)
    right = pack(plan, right_ref[...] + product(toeplitz_ref, columns_ref))
    for place, out_ref in enumerate(out_refs):
        rows = slice(place * plan.rows, (place + 1) * plan.rows)
        out_ref[...] = jnp.concatenate([left_ref[rows, :], right[place]], axis=1).astype(jnp.bfloat16)


def spread(plan, values):
    high = values.astype(jnp.bfloat16).astype(jnp.float32)
    low = values - high
    lane = lax.broadcasted_iota(jnp.int32, values.shape, 1)
    lane = jnp.where(lane >= plan.half_lanes, lane - plan.half_lanes, lane)
    up = pltpu.roll(low, plan.half, 1)
    down = pltpu.roll(low, LANES - plan.half, 1)
    pieces = []
    for step in range(plan.coarse):
        beside, moved = (step + 1, up) if step + 1 < plan.coarse else (step - 1, down)
        kept = jnp.where((lane >= step * plan.half) & (lane < (step + 1) * plan.half), high, 0.0)
        there = (lane >= beside * plan.half) & (lane < (beside + 1) * plan.half)
        pieces.append(jnp.where(there, moved, kept).astype(jnp.bfloat16))
    return jnp.concatenate(pieces, axis=0)


def choose_kernel(plan, index_ref, whitened_ref, chosen_ref, *same_refs):
    whitened = whitened_ref[...].astype(jnp.float32)
    for window, same_ref in enumerate(same_refs):
        same_ref[...] = whitened[window * plan.half : (window + 1) * plan.half].astype(jnp.bfloat16)
    first = lax.axis_index("src") * plan.half
    index = index_ref[...] - first
    index = jnp.where(index < 0, index + plan.channels, index)
    lane = jnp.where(index >= plan.half, index - plan.half + plan.half_lanes, index)
    at_column = lax.broadcasted_iota(jnp.int32, (LANES, plan.source_count), 0)
    chosen = jnp.zeros((LANES, plan.source_count), jnp.bool_)
    for step in range(plan.coarse):
        chosen = chosen | (at_column == lane + step * plan.half)
    chosen_ref[...] = chosen.astype(jnp.float32).astype(jnp.bfloat16)


def expand_kernel(plan, chosen_ref, *refs):
    *arrived_refs, out_hbm, out_ref, sem = refs
    total = sum(ref[...].astype(jnp.float32) for ref in arrived_refs) * plan.norm_factor
    chosen = chosen_ref[...]
    filler = jnp.zeros((plan.fine_padded - plan.fine, LANES), jnp.float32)
    for member in range(plan.own):
        rest = plan.own * plan.whole_groups + member * plan.rest
        rows = jnp.concatenate(
            [
                total[member * plan.whole_groups : (member + 1) * plan.whole_groups],
                total[rest : rest + plan.rest],
                filler,
            ],
            axis=0,
        )
        expanded = jnp.dot(spread(plan, rows), chosen, preferred_element_type=jnp.float32)
        for step in range(plan.coarse):
            start = step * plan.fine
            count = min(plan.fine, LAG_COUNT - start)
            first = step * plan.fine_padded
            out_ref[member, start : start + count, :] = expanded[first : first + count]
    copy = pltpu.make_async_copy(out_ref, out_hbm, sem)
    copy.start()
    copy.wait()


def few_channels(plan, traces, valid_flags, source_index):
    vmem = pl.BlockSpec(memory_space=pltpu.VMEM)
    params = pltpu.CompilerParams(vmem_limit_bytes=32 * 1024 * 1024)
    packed_rows = plan.windows * plan.half
    flags = valid_flags.T

    def swap_cores(array):
        return lax.ppermute(array, "src", [(0, 1), (1, 0)])

    def swap_blk(array, hop):
        pairs = [
            (place * plan.src_size + core, (place ^ hop) * plan.src_size + 1 - core)
            for place in range(plan.blk_size)
            for core in range(plan.src_size)
        ]
        return lax.ppermute(array, ("blk", "src"), pairs)

    whitened = pl.pallas_call(
        functools.partial(whiten_kernel, plan),
        out_shape=pltpu.VMEM((packed_rows, plan.segment), jnp.bfloat16),
        in_specs=[pl.BlockSpec(memory_space=pl.ANY)] * 2,
        out_specs=vmem,
        scratch_shapes=[
            pltpu.VMEM(traces.shape, jnp.float32),
            pltpu.VMEM(flags.shape, jnp.int32),
            pltpu.SemaphoreType.DMA((IN_PARTS + 1,)),
        ],
        compiler_params=pltpu.CompilerParams(vmem_limit_bytes=60 * 1024 * 1024),
        name="whiten",
    )(traces, flags)

    height = plan.lag_rows
    width = plan.windows * plan.span
    rows = pltpu.VMEM((packed_rows, plan.segment), jnp.float32)
    toeplitz = (height, width)
    columns = (plan.half_lanes, width)
    sums = jax.ShapeDtypeStruct((height, LANES), jnp.float32)

    def call(kernel, name, operands, outputs, scratch=()):
        return pl.pallas_call(
            functools.partial(kernel, plan),
            out_shape=outputs,
            in_specs=[vmem] * len(operands),
            out_specs=[vmem] * len(outputs),
            scratch_shapes=scratch,
            compiler_params=params,
            name=name,
        )(*operands)

    across = swap_blk(whitened, plan.targets)
    chosen, *same = call(
        choose_kernel,
        "choose",
        (source_index.reshape(1, -1), whitened),
        (
            jax.ShapeDtypeStruct((LANES, plan.source_count), jnp.bfloat16),
            *[jax.ShapeDtypeStruct((plan.half, plan.segment), whitened.dtype)] * plan.windows,
        ),
    )
    (total,) = call(
        near_kernel,
        "near",
        (*[swap_cores(array) for array in same], whitened),
        (sums,),
        (rows, pltpu.VMEM(toeplitz, jnp.bfloat16), pltpu.VMEM((LANES, width), jnp.bfloat16)),
    )
    across, total = lax.optimization_barrier((across, total))
    across_other = swap_cores(across)
    lagged, left, right = call(
        across_kernel,
        "across",
        (across, total),
        (
            jax.ShapeDtypeStruct(toeplitz, jnp.bfloat16),
            jax.ShapeDtypeStruct((plan.targets * plan.rows, plan.half_lanes), jnp.float32),
            jax.ShapeDtypeStruct((height, plan.half_lanes), jnp.float32),
        ),
        (rows, pltpu.VMEM(columns, jnp.bfloat16)),
    )
    sent = call(
        finish_kernel,
        "finish",
        (across_other, lagged, left, right),
        (jax.ShapeDtypeStruct((plan.rows, LANES), jnp.bfloat16),) * plan.targets,
        (pltpu.VMEM(columns, jnp.bfloat16),),
    )
    arrived = [swap_blk(array, hop) for array, hop in zip(sent, HOPS)]
    out_shape = (plan.own, LAG_COUNT, plan.source_count)
    return pl.pallas_call(
        functools.partial(expand_kernel, plan),
        out_shape=jax.ShapeDtypeStruct(out_shape, jnp.float32),
        in_specs=[vmem] * (1 + len(arrived)),
        out_specs=pl.BlockSpec(memory_space=pl.ANY),
        scratch_shapes=[pltpu.VMEM(out_shape, jnp.float32), pltpu.SemaphoreType.DMA],
        compiler_params=params,
        name="expand",
    )(chosen, *arrived)


def body(traces, valid_flags, source_index):
    plan = Plan(
        traces.shape[0],
        traces.shape[1],
        traces.shape[2],
        lax.axis_size("blk"),
        lax.axis_size("src"),
        source_index.shape[0],
    )
    if plan.fits():
        return few_channels(plan, traces, valid_flags, source_index)
    return many_channels(traces, valid_flags, source_index)


def solution(mesh):
    in_specs = (P(("fibre", "src"), "blk", None), P(("fibre", "src"), "blk"), P())
    out_specs = P(("fibre", "src", "blk"), None, None)
    return jax.shard_map(body, mesh=mesh, in_specs=in_specs, out_specs=out_specs, check_vma=False)
```

```python
import functools
import math

import jax
import jax.numpy as jnp
from jax import lax
from jax.experimental import pallas as pl
from jax.experimental.pallas import tpu as pltpu
from jax.sharding import PartitionSpec as P

MAXLAG = 64
LAG_COUNT = 2 * MAXLAG + 1
LANES = 256
IN_PARTS = 8
GROUP = 8
HOPS = (3, 2, 1, 0)


def broadcast(value, axis, source):
    kept = jnp.where(lax.axis_index(axis) == source, value, 0).astype(value.dtype)
    return lax.psum(kept, axis)


def toeplitz_rows(group, lag_count, segment):
    shifted = jnp.stack(
        [group[:, :, lag_step : lag_step + segment] for lag_step in range(lag_count)], axis=1
    )
    return shifted.reshape(group.shape[0] * lag_count, -1)


def many_channels(traces, valid_flags, source_index):
    segment = traces.shape[2]
    centered = traces - jnp.mean(traces, axis=2, keepdims=True)
    mean_power = jnp.mean(centered * centered, axis=2, keepdims=True)
    flag_values = valid_flags[:, :, None].astype(jnp.float32)
    whitened = (centered * lax.rsqrt(mean_power + 1e-05) * flag_values).astype(jnp.bfloat16)
    pieces = []
    for owner in range(lax.axis_size("src")):
        pieces.append(broadcast(whitened, "src", owner))
    everyone = jnp.concatenate(pieces, axis=0)
    sources = jnp.take(everyone, source_index, axis=0)
    source_count = sources.shape[0]
    norm_factor = 1.0 / math.sqrt(traces.shape[1] * lax.axis_size("blk") * segment)
    own_rows = whitened.shape[0] // lax.axis_size("blk")
    flat_sources = sources.reshape(source_count, -1)
    padded = jnp.pad(whitened, ((0, 0), (0, 0), (MAXLAG, MAXLAG)))
    block_rows = math.gcd(lax.axis_size("blk") * own_rows, 16)
    grouped = padded.reshape(
        (lax.axis_size("blk") * own_rows // block_rows, block_rows) + padded.shape[1:]
    )

    def one_block(group):
        toeplitz = toeplitz_rows(group, LAG_COUNT, segment)
        products = lax.dot_general(
            toeplitz, flat_sources, (((1,), (1,)), ((), ())), preferred_element_type=jnp.float32
        )
        return (products * norm_factor).reshape(block_rows, LAG_COUNT, source_count)

    result = lax.map(one_block, grouped)
    return lax.psum_scatter(
        result.reshape(lax.axis_size("blk") * own_rows, LAG_COUNT, source_count),
        "blk",
        scatter_dimension=0,
        tiled=True,
    )


class Plan:
    def __init__(self, half, windows, segment, blk_size, src_size, source_count):
        self.half = half
        self.windows = windows
        self.segment = segment
        self.blk_size = blk_size
        self.src_size = src_size
        self.channels = half * src_size
        self.source_count = source_count
        self.half_lanes = LANES // 2
        self.coarse = self.half_lanes // half
        if self.coarse == 0:
            return
        self.fine = -(-LAG_COUNT // self.coarse)
        self.fine_padded = -(-self.fine // (2 * GROUP)) * 2 * GROUP
        self.own = half // blk_size
        reach = segment + (self.coarse - 1) * self.fine
        self.span = -(-max(reach, segment + 2 * MAXLAG) // 128) * 128
        self.whole_groups = self.fine // GROUP * GROUP
        self.rest = self.fine - self.whole_groups
        rows = self.own * self.fine
        self.rows = -(-rows // 16) * 16
        self.targets = blk_size // 2
        self.receivers = self.targets * self.own
        self.lag_rows = -(-self.receivers * self.fine // 32) * 32
        self.norm_factor = 1.0 / math.sqrt(windows * blk_size * segment)

    def fits(self):
        return (
            self.coarse >= 2
            and self.src_size == 2
            and self.half % self.blk_size == 0
            and self.half % GROUP == 0
            and self.channels % 16 == 0
            and self.windows * self.half % 16 == 0
            and self.blk_size == 8
            and self.rest > 0
            and GROUP % self.rest == 0
            and self.receivers * self.rest % GROUP == 0
            and self.receivers % 2 == 0
            and self.receivers * self.whole_groups % 16 == 0
        )


def whiten_kernel(plan, traces_hbm, flags_hbm, out_ref, traces_ref, flags_ref, sems):
    part = plan.half // IN_PARTS
    copies = [pltpu.make_async_copy(flags_hbm, flags_ref, sems.at[IN_PARTS])]
    for index in range(IN_PARTS):
        at = pl.ds(index * part, part)
        copies.append(pltpu.make_async_copy(traces_hbm.at[at], traces_ref.at[at], sems.at[index]))
    for copy in copies:
        copy.start()
    copies[0].wait()
    flag_values = [
        flags_ref[window : window + 1, :].astype(jnp.float32).reshape(plan.half, 1) for window in range(plan.windows)
    ]
    for copy in copies[1:]:
        copy.wait()
    pieces = []
    for window in range(plan.windows):
        values = traces_ref[:, window, :]
        centered = values - jnp.mean(values, axis=1, keepdims=True)
        mean_power = jnp.mean(centered * centered, axis=1, keepdims=True)
        pieces.append(centered * lax.rsqrt(mean_power + 1e-05) * flag_values[window])
    out_ref[...] = jnp.concatenate(pieces, axis=0).astype(jnp.bfloat16)


def lag_rows(plan, rows_ref, toeplitz_ref):
    span = plan.span
    me = lax.axis_index("blk")
    filler = jnp.zeros((1, span - plan.segment), jnp.float32)
    spare = jnp.zeros((plan.lag_rows - plan.receivers * plan.fine, span), jnp.float32)
    sublane = lax.broadcasted_iota(jnp.int32, (GROUP, span), 0)
    for window in range(plan.windows):
        at = slice(window * span, (window + 1) * span)
        spread_rows = []
        for hop in HOPS:
            for member in range(plan.own):
                channel = window * plan.half + (me ^ hop) * plan.own + member
                row = jnp.concatenate([rows_ref[pl.ds(channel, 1), :], filler], axis=1)
                spread_rows.append(jnp.broadcast_to(row, (GROUP, span)))
        for first in range(0, plan.receivers, 2):
            pieces = [
                pltpu.roll(row, (MAXLAG - plan.whole_groups + 1 + lag) % span, 1, stride=1, stride_axis=0)
                for row in spread_rows[first : first + 2]
                for lag in range(0, plan.whole_groups, GROUP)
            ]
            start = first * plan.whole_groups
            toeplitz_ref[start : start + 2 * plan.whole_groups, at] = jnp.concatenate(pieces, axis=0).astype(
                jnp.bfloat16
            )
        pieces = []
        for first in range(0, plan.receivers, GROUP // plan.rest):
            mixed = spread_rows[first]
            for index in range(1, GROUP // plan.rest):
                mixed = jnp.where(sublane >= index * plan.rest, spread_rows[first + index], mixed)
            tile = pltpu.roll(mixed, (MAXLAG - plan.whole_groups) % span, 1)
            for lag in range(1, plan.rest):
                later = pltpu.roll(mixed, (MAXLAG - plan.whole_groups - lag) % span, 1)
                tile = jnp.where(sublane % plan.rest == lag, later, tile)
            pieces.append(tile)
        start = plan.receivers * plan.whole_groups
        toeplitz_ref[start:, at] = jnp.concatenate(pieces + [spare], axis=0).astype(jnp.bfloat16)


def fill_columns(plan, values, columns_ref):
    span = plan.span
    filler = jnp.zeros((plan.half, span - plan.segment), jnp.float32)
    spare = jnp.zeros((plan.half_lanes - plan.coarse * plan.half, span), jnp.float32)
    for window in range(plan.windows):
        rows = jnp.concatenate([values[window * plan.half : (window + 1) * plan.half], filler], axis=1)
        pieces = [rows] + [pltpu.roll(rows, step * plan.fine, 1) for step in range(1, plan.coarse)]
        if spare.shape[0]:
            pieces.append(spare)
        columns_ref[:, window * span : (window + 1) * span] = jnp.concatenate(pieces, axis=0).astype(jnp.bfloat16)


def product(toeplitz_ref, columns_ref):
    return lax.dot_general(
        toeplitz_ref[...], columns_ref[...], (((1,), (1,)), ((), ())), preferred_element_type=jnp.float32
    )


def near_kernel(plan, *refs):
    mine_refs, (other_ref, sum_ref, rows_ref, toeplitz_ref, columns_ref) = refs[: plan.windows], refs[plan.windows :]
    for window, mine_ref in enumerate(mine_refs):
        rows_ref[window * plan.half : (window + 1) * plan.half, :] = mine_ref[...].astype(jnp.float32)
    lag_rows(plan, rows_ref, toeplitz_ref)
    fill_columns(plan, rows_ref[...], columns_ref.at[: plan.half_lanes])
    fill_columns(plan, other_ref[...].astype(jnp.float32), columns_ref.at[plan.half_lanes :])
    sum_ref[...] = product(toeplitz_ref, columns_ref)


def across_kernel(plan, mine_ref, prior_ref, toeplitz_ref, left_ref, right_ref, rows_ref, columns_ref):
    rows_ref[...] = mine_ref[...].astype(jnp.float32)
    lag_rows(plan, rows_ref, toeplitz_ref)
    fill_columns(plan, rows_ref[...], columns_ref)
    left = prior_ref[:, : plan.half_lanes] + product(toeplitz_ref, columns_ref)
    for place, block in enumerate(pack(plan, left)):
        left_ref[place * plan.rows : (place + 1) * plan.rows, :] = block
    right_ref[...] = prior_ref[:, plan.half_lanes :]


def pack(plan, products):
    width = products.shape[1]
    back = GROUP - 1 - lax.broadcasted_iota(jnp.int32, (GROUP, width), 0)
    packed = []
    for place in range(plan.targets):
        pieces = []
        for receiver in range(place * plan.own, (place + 1) * plan.own):
            last = (receiver + 1) * plan.whole_groups
            pieces += [
                jnp.take_along_axis(products[last - lag - GROUP : last - lag], back, axis=0)
                for lag in range(0, plan.whole_groups, GROUP)
            ]
        first = plan.receivers * plan.whole_groups + place * plan.own * plan.rest
        pieces.append(products[first : first + plan.own * plan.rest])
        if plan.rows > plan.own * plan.fine:
            pieces.append(jnp.zeros((plan.rows - plan.own * plan.fine, width), jnp.float32))
        packed.append(jnp.concatenate(pieces, axis=0))
    return packed


def finish_kernel(plan, other_ref, toeplitz_ref, left_ref, right_ref, *refs):
    *out_refs, columns_ref = refs
    fill_columns(plan, other_ref[...].astype(jnp.float32), columns_ref)
    right = pack(plan, right_ref[...] + product(toeplitz_ref, columns_ref))
    for place, out_ref in enumerate(out_refs):
        rows = slice(place * plan.rows, (place + 1) * plan.rows)
        out_ref[...] = jnp.concatenate([left_ref[rows, :], right[place]], axis=1).astype(jnp.bfloat16)


def spread(plan, values):
    high = values.astype(jnp.bfloat16).astype(jnp.float32)
    low = values - high
    lane = lax.broadcasted_iota(jnp.int32, values.shape, 1)
    lane = jnp.where(lane >= plan.half_lanes, lane - plan.half_lanes, lane)
    up = pltpu.roll(low, plan.half, 1)
    down = pltpu.roll(low, LANES - plan.half, 1)
    pieces = []
    for step in range(plan.coarse):
        beside, moved = (step + 1, up) if step + 1 < plan.coarse else (step - 1, down)
        kept = jnp.where((lane >= step * plan.half) & (lane < (step + 1) * plan.half), high, 0.0)
        there = (lane >= beside * plan.half) & (lane < (beside + 1) * plan.half)
        pieces.append(jnp.where(there, moved, kept).astype(jnp.bfloat16))
    return jnp.concatenate(pieces, axis=0)


def choose_kernel(plan, index_ref, whitened_ref, chosen_ref, *same_refs):
    whitened = whitened_ref[...].astype(jnp.float32)
    for window, same_ref in enumerate(same_refs):
        same_ref[...] = whitened[window * plan.half : (window + 1) * plan.half].astype(jnp.bfloat16)
    first = lax.axis_index("src") * plan.half
    index = index_ref[...] - first
    index = jnp.where(index < 0, index + plan.channels, index)
    lane = jnp.where(index >= plan.half, index - plan.half + plan.half_lanes, index)
    at_column = lax.broadcasted_iota(jnp.int32, (LANES, plan.source_count), 0)
    chosen = jnp.zeros((LANES, plan.source_count), jnp.bool_)
    for step in range(plan.coarse):
        chosen = chosen | (at_column == lane + step * plan.half)
    chosen_ref[...] = chosen.astype(jnp.float32).astype(jnp.bfloat16)


def expand_kernel(plan, chosen_ref, *refs):
    *arrived_refs, out_hbm, out_ref, sems = refs
    total = sum(ref[...].astype(jnp.float32) for ref in arrived_refs) * plan.norm_factor
    chosen = chosen_ref[...]
    filler = jnp.zeros((plan.fine_padded - plan.fine, LANES), jnp.float32)
    copies = []
    for member in range(plan.own):
        rest = plan.own * plan.whole_groups + member * plan.rest
        rows = jnp.concatenate(
            [
                total[member * plan.whole_groups : (member + 1) * plan.whole_groups],
                total[rest : rest + plan.rest],
                filler,
            ],
            axis=0,
        )
        expanded = jnp.dot(spread(plan, rows), chosen, preferred_element_type=jnp.float32)
        for step in range(plan.coarse):
            start = step * plan.fine
            count = min(plan.fine, LAG_COUNT - start)
            first = step * plan.fine_padded
            out_ref[member, start : start + count, :] = expanded[first : first + count]
        copies.append(pltpu.make_async_copy(out_ref.at[member], out_hbm.at[member], sems.at[member]))
        copies[-1].start()
    for copy in copies:
        copy.wait()


def few_channels(plan, traces, valid_flags, source_index):
    vmem = pl.BlockSpec(memory_space=pltpu.VMEM)
    params = pltpu.CompilerParams(vmem_limit_bytes=32 * 1024 * 1024)
    packed_rows = plan.windows * plan.half
    flags = valid_flags.T

    def swap_cores(array):
        return lax.ppermute(array, "src", [(0, 1), (1, 0)])

    def swap_blk(array, hop):
        pairs = [
            (place * plan.src_size + core, (place ^ hop) * plan.src_size + 1 - core)
            for place in range(plan.blk_size)
            for core in range(plan.src_size)
        ]
        return lax.ppermute(array, ("blk", "src"), pairs)

    whitened = pl.pallas_call(
        functools.partial(whiten_kernel, plan),
        out_shape=pltpu.VMEM((packed_rows, plan.segment), jnp.bfloat16),
        in_specs=[pl.BlockSpec(memory_space=pl.ANY)] * 2,
        out_specs=vmem,
        scratch_shapes=[
            pltpu.VMEM(traces.shape, jnp.float32),
            pltpu.VMEM(flags.shape, jnp.int32),
            pltpu.SemaphoreType.DMA((IN_PARTS + 1,)),
        ],
        compiler_params=pltpu.CompilerParams(vmem_limit_bytes=60 * 1024 * 1024),
        name="whiten",
    )(traces, flags)

    height = plan.lag_rows
    width = plan.windows * plan.span
    rows = pltpu.VMEM((packed_rows, plan.segment), jnp.float32)
    toeplitz = (height, width)
    columns = (plan.half_lanes, width)
    sums = jax.ShapeDtypeStruct((height, LANES), jnp.float32)

    def call(kernel, name, operands, outputs, scratch=()):
        return pl.pallas_call(
            functools.partial(kernel, plan),
            out_shape=outputs,
            in_specs=[vmem] * len(operands),
            out_specs=[vmem] * len(outputs),
            scratch_shapes=scratch,
            compiler_params=params,
            name=name,
        )(*operands)

    across = swap_blk(whitened, plan.targets)
    chosen, *same = call(
        choose_kernel,
        "choose",
        (source_index.reshape(1, -1), whitened),
        (
            jax.ShapeDtypeStruct((LANES, plan.source_count), jnp.bfloat16),
            *[jax.ShapeDtypeStruct((plan.half, plan.segment), whitened.dtype)] * plan.windows,
        ),
    )
    (total,) = call(
        near_kernel,
        "near",
        (*[swap_cores(array) for array in same], whitened),
        (sums,),
        (rows, pltpu.VMEM(toeplitz, jnp.bfloat16), pltpu.VMEM((LANES, width), jnp.bfloat16)),
    )
    across, total = lax.optimization_barrier((across, total))
    across_other = swap_cores(across)
    lagged, left, right = call(
        across_kernel,
        "across",
        (across, total),
        (
            jax.ShapeDtypeStruct(toeplitz, jnp.bfloat16),
            jax.ShapeDtypeStruct((plan.targets * plan.rows, plan.half_lanes), jnp.float32),
            jax.ShapeDtypeStruct((height, plan.half_lanes), jnp.float32),
        ),
        (rows, pltpu.VMEM(columns, jnp.bfloat16)),
    )
    sent = call(
        finish_kernel,
        "finish",
        (across_other, lagged, left, right),
        (jax.ShapeDtypeStruct((plan.rows, LANES), jnp.bfloat16),) * plan.targets,
        (pltpu.VMEM(columns, jnp.bfloat16),),
    )
    arrived = [swap_blk(array, hop) for array, hop in zip(sent, HOPS)]
    out_shape = (plan.own, LAG_COUNT, plan.source_count)
    return pl.pallas_call(
        functools.partial(expand_kernel, plan),
        out_shape=jax.ShapeDtypeStruct(out_shape, jnp.float32),
        in_specs=[vmem] * (1 + len(arrived)),
        out_specs=pl.BlockSpec(memory_space=pl.ANY),
        scratch_shapes=[pltpu.VMEM(out_shape, jnp.float32), pltpu.SemaphoreType.DMA((plan.own,))],
        compiler_params=params,
        name="expand",
    )(chosen, *arrived)


def body(traces, valid_flags, source_index):
    plan = Plan(
        traces.shape[0],
        traces.shape[1],
        traces.shape[2],
        lax.axis_size("blk"),
        lax.axis_size("src"),
        source_index.shape[0],
    )
    if plan.fits():
        return few_channels(plan, traces, valid_flags, source_index)
    return many_channels(traces, valid_flags, source_index)


def solution(mesh):
    in_specs = (P(("fibre", "src"), "blk", None), P(("fibre", "src"), "blk"), P())
    out_specs = P(("fibre", "src", "blk"), None, None)
    return jax.shard_map(body, mesh=mesh, in_specs=in_specs, out_specs=out_specs, check_vma=False)
```

```python
import functools
import math

import jax
import jax.numpy as jnp
from jax import lax
from jax.experimental import pallas as pl
from jax.experimental.pallas import tpu as pltpu
from jax.sharding import PartitionSpec as P

MAXLAG = 64
LAG_COUNT = 2 * MAXLAG + 1
LANES = 256
IN_PARTS = 3
GROUP = 8
HOPS = (3, 2, 1, 0)


def broadcast(value, axis, source):
    kept = jnp.where(lax.axis_index(axis) == source, value, 0).astype(value.dtype)
    return lax.psum(kept, axis)


def toeplitz_rows(group, lag_count, segment):
    shifted = jnp.stack(
        [group[:, :, lag_step : lag_step + segment] for lag_step in range(lag_count)], axis=1
    )
    return shifted.reshape(group.shape[0] * lag_count, -1)


def many_channels(traces, valid_flags, source_index):
    segment = traces.shape[2]
    centered = traces - jnp.mean(traces, axis=2, keepdims=True)
    mean_power = jnp.mean(centered * centered, axis=2, keepdims=True)
    flag_values = valid_flags[:, :, None].astype(jnp.float32)
    whitened = (centered * lax.rsqrt(mean_power + 1e-05) * flag_values).astype(jnp.bfloat16)
    pieces = []
    for owner in range(lax.axis_size("src")):
        pieces.append(broadcast(whitened, "src", owner))
    everyone = jnp.concatenate(pieces, axis=0)
    sources = jnp.take(everyone, source_index, axis=0)
    source_count = sources.shape[0]
    norm_factor = 1.0 / math.sqrt(traces.shape[1] * lax.axis_size("blk") * segment)
    own_rows = whitened.shape[0] // lax.axis_size("blk")
    flat_sources = sources.reshape(source_count, -1)
    padded = jnp.pad(whitened, ((0, 0), (0, 0), (MAXLAG, MAXLAG)))
    block_rows = math.gcd(lax.axis_size("blk") * own_rows, 16)
    grouped = padded.reshape(
        (lax.axis_size("blk") * own_rows // block_rows, block_rows) + padded.shape[1:]
    )

    def one_block(group):
        toeplitz = toeplitz_rows(group, LAG_COUNT, segment)
        products = lax.dot_general(
            toeplitz, flat_sources, (((1,), (1,)), ((), ())), preferred_element_type=jnp.float32
        )
        return (products * norm_factor).reshape(block_rows, LAG_COUNT, source_count)

    result = lax.map(one_block, grouped)
    return lax.psum_scatter(
        result.reshape(lax.axis_size("blk") * own_rows, LAG_COUNT, source_count),
        "blk",
        scatter_dimension=0,
        tiled=True,
    )


class Plan:
    def __init__(self, half, windows, segment, blk_size, src_size, source_count):
        self.half = half
        self.windows = windows
        self.segment = segment
        self.blk_size = blk_size
        self.src_size = src_size
        self.channels = half * src_size
        self.source_count = source_count
        self.half_lanes = LANES // 2
        self.coarse = self.half_lanes // half
        if self.coarse == 0:
            return
        self.fine = -(-LAG_COUNT // self.coarse)
        self.fine_padded = -(-self.fine // (2 * GROUP)) * 2 * GROUP
        self.own = half // blk_size
        reach = segment + (self.coarse - 1) * self.fine
        self.span = -(-max(reach, segment + 2 * MAXLAG) // 128) * 128
        self.whole_groups = self.fine // GROUP * GROUP
        self.rest = self.fine - self.whole_groups
        rows = self.own * self.fine
        self.rows = -(-rows // 16) * 16
        self.targets = blk_size // 2
        self.receivers = self.targets * self.own
        self.lag_rows = -(-self.receivers * self.fine // 32) * 32
        self.norm_factor = 1.0 / math.sqrt(windows * blk_size * segment)

    def fits(self):
        return (
            self.coarse >= 2
            and self.src_size == 2
            and self.half % self.blk_size == 0
            and self.half % GROUP == 0
            and self.half % IN_PARTS == 0
            and self.channels % 16 == 0
            and self.windows * self.half % 16 == 0
            and self.blk_size == 8
            and self.rest > 0
            and GROUP % self.rest == 0
            and self.receivers * self.rest % GROUP == 0
            and self.receivers % 2 == 0
            and self.receivers * self.whole_groups % 16 == 0
        )


def whiten_kernel(plan, traces_hbm, flags_hbm, out_ref, traces_ref, flags_ref, sems):
    part = plan.half // IN_PARTS
    copies = [pltpu.make_async_copy(flags_hbm, flags_ref, sems.at[IN_PARTS])]
    for index in range(IN_PARTS):
        at = pl.ds(index * part, part)
        copies.append(pltpu.make_async_copy(traces_hbm.at[at], traces_ref.at[at], sems.at[index]))
    for copy in copies:
        copy.start()
    copies[0].wait()
    flag_values = [
        flags_ref[window : window + 1, :].astype(jnp.float32).reshape(plan.half, 1) for window in range(plan.windows)
    ]
    for copy in copies[1:]:
        copy.wait()
    pieces = []
    for window in range(plan.windows):
        values = traces_ref[:, window, :]
        centered = values - jnp.mean(values, axis=1, keepdims=True)
        mean_power = jnp.mean(centered * centered, axis=1, keepdims=True)
        pieces.append(centered * lax.rsqrt(mean_power + 1e-05) * flag_values[window])
    out_ref[...] = jnp.concatenate(pieces, axis=0).astype(jnp.bfloat16)


def lag_rows(plan, rows_ref, toeplitz_ref):
    span = plan.span
    me = lax.axis_index("blk")
    filler = jnp.zeros((1, span - plan.segment), jnp.float32)
    spare = jnp.zeros((plan.lag_rows - plan.receivers * plan.fine, span), jnp.float32)
    sublane = lax.broadcasted_iota(jnp.int32, (GROUP, span), 0)
    for window in range(plan.windows):
        at = slice(window * span, (window + 1) * span)
        spread_rows = []
        for hop in HOPS:
            for member in range(plan.own):
                channel = window * plan.half + (me ^ hop) * plan.own + member
                row = jnp.concatenate([rows_ref[pl.ds(channel, 1), :], filler], axis=1)
                spread_rows.append(jnp.broadcast_to(row, (GROUP, span)))
        for first in range(0, plan.receivers, 2):
            pieces = [
                pltpu.roll(row, (MAXLAG - plan.whole_groups + 1 + lag) % span, 1, stride=1, stride_axis=0)
                for row in spread_rows[first : first + 2]
                for lag in range(0, plan.whole_groups, GROUP)
            ]
            start = first * plan.whole_groups
            toeplitz_ref[start : start + 2 * plan.whole_groups, at] = jnp.concatenate(pieces, axis=0).astype(
                jnp.bfloat16
            )
        pieces = []
        for first in range(0, plan.receivers, GROUP // plan.rest):
            mixed = spread_rows[first]
            for index in range(1, GROUP // plan.rest):
                mixed = jnp.where(sublane >= index * plan.rest, spread_rows[first + index], mixed)
            tile = pltpu.roll(mixed, (MAXLAG - plan.whole_groups) % span, 1)
            for lag in range(1, plan.rest):
                later = pltpu.roll(mixed, (MAXLAG - plan.whole_groups - lag) % span, 1)
                tile = jnp.where(sublane % plan.rest == lag, later, tile)
            pieces.append(tile)
        start = plan.receivers * plan.whole_groups
        toeplitz_ref[start:, at] = jnp.concatenate(pieces + [spare], axis=0).astype(jnp.bfloat16)


def fill_columns(plan, values, columns_ref):
    span = plan.span
    filler = jnp.zeros((plan.half, span - plan.segment), jnp.float32)
    spare = jnp.zeros((plan.half_lanes - plan.coarse * plan.half, span), jnp.float32)
    for window in range(plan.windows):
        rows = jnp.concatenate([values[window * plan.half : (window + 1) * plan.half], filler], axis=1)
        pieces = [rows] + [pltpu.roll(rows, step * plan.fine, 1) for step in range(1, plan.coarse)]
        if spare.shape[0]:
            pieces.append(spare)
        columns_ref[:, window * span : (window + 1) * span] = jnp.concatenate(pieces, axis=0).astype(jnp.bfloat16)


def product(toeplitz_ref, columns_ref):
    return lax.dot_general(
        toeplitz_ref[...], columns_ref[...], (((1,), (1,)), ((), ())), preferred_element_type=jnp.float32
    )


def near_kernel(plan, *refs):
    mine_refs, (other_ref, sum_ref, rows_ref, toeplitz_ref, columns_ref) = refs[: plan.windows], refs[plan.windows :]
    for window, mine_ref in enumerate(mine_refs):
        rows_ref[window * plan.half : (window + 1) * plan.half, :] = mine_ref[...].astype(jnp.float32)
    lag_rows(plan, rows_ref, toeplitz_ref)
    fill_columns(plan, rows_ref[...], columns_ref.at[: plan.half_lanes])
    fill_columns(plan, other_ref[...].astype(jnp.float32), columns_ref.at[plan.half_lanes :])
    sum_ref[...] = product(toeplitz_ref, columns_ref)


def across_kernel(plan, mine_ref, prior_ref, toeplitz_ref, left_ref, right_ref, rows_ref, columns_ref):
    rows_ref[...] = mine_ref[...].astype(jnp.float32)
    lag_rows(plan, rows_ref, toeplitz_ref)
    fill_columns(plan, rows_ref[...], columns_ref)
    left = prior_ref[:, : plan.half_lanes] + product(toeplitz_ref, columns_ref)
    for place, block in enumerate(pack(plan, left)):
        left_ref[place * plan.rows : (place + 1) * plan.rows, :] = block
    right_ref[...] = prior_ref[:, plan.half_lanes :]


def pack(plan, products):
    width = products.shape[1]
    back = GROUP - 1 - lax.broadcasted_iota(jnp.int32, (GROUP, width), 0)
    packed = []
    for place in range(plan.targets):
        pieces = []
        for receiver in range(place * plan.own, (place + 1) * plan.own):
            last = (receiver + 1) * plan.whole_groups
            pieces += [
                jnp.take_along_axis(products[last - lag - GROUP : last - lag], back, axis=0)
                for lag in range(0, plan.whole_groups, GROUP)
            ]
        first = plan.receivers * plan.whole_groups + place * plan.own * plan.rest
        pieces.append(products[first : first + plan.own * plan.rest])
        if plan.rows > plan.own * plan.fine:
            pieces.append(jnp.zeros((plan.rows - plan.own * plan.fine, width), jnp.float32))
        packed.append(jnp.concatenate(pieces, axis=0))
    return packed


def finish_kernel(plan, other_ref, toeplitz_ref, left_ref, right_ref, *refs):
    *out_refs, columns_ref = refs
    fill_columns(plan, other_ref[...].astype(jnp.float32), columns_ref)
    right = pack(plan, right_ref[...] + product(toeplitz_ref, columns_ref))
    for place, out_ref in enumerate(out_refs):
        rows = slice(place * plan.rows, (place + 1) * plan.rows)
        out_ref[...] = jnp.concatenate([left_ref[rows, :], right[place]], axis=1).astype(jnp.bfloat16)


def spread(plan, values):
    high = values.astype(jnp.bfloat16).astype(jnp.float32)
    low = values - high
    lane = lax.broadcasted_iota(jnp.int32, values.shape, 1)
    lane = jnp.where(lane >= plan.half_lanes, lane - plan.half_lanes, lane)
    up = pltpu.roll(low, plan.half, 1)
    down = pltpu.roll(low, LANES - plan.half, 1)
    pieces = []
    for step in range(plan.coarse):
        beside, moved = (step + 1, up) if step + 1 < plan.coarse else (step - 1, down)
        kept = jnp.where((lane >= step * plan.half) & (lane < (step + 1) * plan.half), high, 0.0)
        there = (lane >= beside * plan.half) & (lane < (beside + 1) * plan.half)
        pieces.append(jnp.where(there, moved, kept).astype(jnp.bfloat16))
    return jnp.concatenate(pieces, axis=0)


def choose_kernel(plan, index_ref, whitened_ref, chosen_ref, *same_refs):
    whitened = whitened_ref[...].astype(jnp.float32)
    for window, same_ref in enumerate(same_refs):
        same_ref[...] = whitened[window * plan.half : (window + 1) * plan.half].astype(jnp.bfloat16)
    first = lax.axis_index("src") * plan.half
    index = index_ref[...] - first
    index = jnp.where(index < 0, index + plan.channels, index)
    lane = jnp.where(index >= plan.half, index - plan.half + plan.half_lanes, index)
    at_column = lax.broadcasted_iota(jnp.int32, (LANES, plan.source_count), 0)
    chosen = jnp.zeros((LANES, plan.source_count), jnp.bool_)
    for step in range(plan.coarse):
        chosen = chosen | (at_column == lane + step * plan.half)
    chosen_ref[...] = chosen.astype(jnp.float32).astype(jnp.bfloat16)


def expand_kernel(plan, chosen_ref, *refs):
    *arrived_refs, out_hbm, out_ref, sems = refs
    total = sum(ref[...].astype(jnp.float32) for ref in arrived_refs) * plan.norm_factor
    chosen = chosen_ref[...]
    filler = jnp.zeros((plan.fine_padded - plan.fine, LANES), jnp.float32)
    copies = []
    for member in range(plan.own):
        rest = plan.own * plan.whole_groups + member * plan.rest
        rows = jnp.concatenate(
            [
                total[member * plan.whole_groups : (member + 1) * plan.whole_groups],
                total[rest : rest + plan.rest],
                filler,
            ],
            axis=0,
        )
        expanded = jnp.dot(spread(plan, rows), chosen, preferred_element_type=jnp.float32)
        for step in range(plan.coarse):
            start = step * plan.fine
            count = min(plan.fine, LAG_COUNT - start)
            first = step * plan.fine_padded
            out_ref[member, start : start + count, :] = expanded[first : first + count]
        copies.append(pltpu.make_async_copy(out_ref.at[member], out_hbm.at[member], sems.at[member]))
        copies[-1].start()
    for copy in copies:
        copy.wait()


def few_channels(plan, traces, valid_flags, source_index):
    vmem = pl.BlockSpec(memory_space=pltpu.VMEM)
    params = pltpu.CompilerParams(vmem_limit_bytes=32 * 1024 * 1024)
    packed_rows = plan.windows * plan.half
    flags = valid_flags.T

    def swap_cores(array):
        return lax.ppermute(array, "src", [(0, 1), (1, 0)])

    def swap_blk(array, hop):
        pairs = [
            (place * plan.src_size + core, (place ^ hop) * plan.src_size + 1 - core)
            for place in range(plan.blk_size)
            for core in range(plan.src_size)
        ]
        return lax.ppermute(array, ("blk", "src"), pairs)

    whitened = pl.pallas_call(
        functools.partial(whiten_kernel, plan),
        out_shape=pltpu.VMEM((packed_rows, plan.segment), jnp.bfloat16),
        in_specs=[pl.BlockSpec(memory_space=pl.ANY)] * 2,
        out_specs=vmem,
        scratch_shapes=[
            pltpu.VMEM(traces.shape, jnp.float32),
            pltpu.VMEM(flags.shape, jnp.int32),
            pltpu.SemaphoreType.DMA((IN_PARTS + 1,)),
        ],
        compiler_params=pltpu.CompilerParams(vmem_limit_bytes=60 * 1024 * 1024),
        name="whiten",
    )(traces, flags)

    height = plan.lag_rows
    width = plan.windows * plan.span
    rows = pltpu.VMEM((packed_rows, plan.segment), jnp.float32)
    toeplitz = (height, width)
    columns = (plan.half_lanes, width)
    sums = jax.ShapeDtypeStruct((height, LANES), jnp.float32)

    def call(kernel, name, operands, outputs, scratch=()):
        return pl.pallas_call(
            functools.partial(kernel, plan),
            out_shape=outputs,
            in_specs=[vmem] * len(operands),
            out_specs=[vmem] * len(outputs),
            scratch_shapes=scratch,
            compiler_params=params,
            name=name,
        )(*operands)

    across = swap_blk(whitened, plan.targets)
    chosen, *same = call(
        choose_kernel,
        "choose",
        (source_index.reshape(1, -1), whitened),
        (
            jax.ShapeDtypeStruct((LANES, plan.source_count), jnp.bfloat16),
            *[jax.ShapeDtypeStruct((plan.half, plan.segment), whitened.dtype)] * plan.windows,
        ),
    )
    (total,) = call(
        near_kernel,
        "near",
        (*[swap_cores(array) for array in same], whitened),
        (sums,),
        (rows, pltpu.VMEM(toeplitz, jnp.bfloat16), pltpu.VMEM((LANES, width), jnp.bfloat16)),
    )
    across, total = lax.optimization_barrier((across, total))
    across_other = swap_cores(across)
    lagged, left, right = call(
        across_kernel,
        "across",
        (across, total),
        (
            jax.ShapeDtypeStruct(toeplitz, jnp.bfloat16),
            jax.ShapeDtypeStruct((plan.targets * plan.rows, plan.half_lanes), jnp.float32),
            jax.ShapeDtypeStruct((height, plan.half_lanes), jnp.float32),
        ),
        (rows, pltpu.VMEM(columns, jnp.bfloat16)),
    )
    sent = call(
        finish_kernel,
        "finish",
        (across_other, lagged, left, right),
        (jax.ShapeDtypeStruct((plan.rows, LANES), jnp.bfloat16),) * plan.targets,
        (pltpu.VMEM(columns, jnp.bfloat16),),
    )
    arrived = [swap_blk(array, hop) for array, hop in zip(sent, HOPS)]
    out_shape = (plan.own, LAG_COUNT, plan.source_count)
    return pl.pallas_call(
        functools.partial(expand_kernel, plan),
        out_shape=jax.ShapeDtypeStruct(out_shape, jnp.float32),
        in_specs=[vmem] * (1 + len(arrived)),
        out_specs=pl.BlockSpec(memory_space=pl.ANY),
        scratch_shapes=[pltpu.VMEM(out_shape, jnp.float32), pltpu.SemaphoreType.DMA((plan.own,))],
        compiler_params=params,
        name="expand",
    )(chosen, *arrived)


def body(traces, valid_flags, source_index):
    plan = Plan(
        traces.shape[0],
        traces.shape[1],
        traces.shape[2],
        lax.axis_size("blk"),
        lax.axis_size("src"),
        source_index.shape[0],
    )
    if plan.fits():
        return few_channels(plan, traces, valid_flags, source_index)
    return many_channels(traces, valid_flags, source_index)


def solution(mesh):
    in_specs = (P(("fibre", "src"), "blk", None), P(("fibre", "src"), "blk"), P())
    out_specs = P(("fibre", "src", "blk"), None, None)
    return jax.shard_map(body, mesh=mesh, in_specs=in_specs, out_specs=out_specs, check_vma=False)
```

```python
import functools
import math

import jax
import jax.numpy as jnp
from jax import lax
from jax.experimental import pallas as pl
from jax.experimental.pallas import tpu as pltpu
from jax.sharding import PartitionSpec as P

MAXLAG = 64
LAG_COUNT = 2 * MAXLAG + 1
LANES = 256
IN_PARTS = 3
GROUP = 8
HOPS = (3, 1, 2, 0)


def broadcast(value, axis, source):
    kept = jnp.where(lax.axis_index(axis) == source, value, 0).astype(value.dtype)
    return lax.psum(kept, axis)


def toeplitz_rows(group, lag_count, segment):
    shifted = jnp.stack(
        [group[:, :, lag_step : lag_step + segment] for lag_step in range(lag_count)], axis=1
    )
    return shifted.reshape(group.shape[0] * lag_count, -1)


def many_channels(traces, valid_flags, source_index):
    segment = traces.shape[2]
    centered = traces - jnp.mean(traces, axis=2, keepdims=True)
    mean_power = jnp.mean(centered * centered, axis=2, keepdims=True)
    flag_values = valid_flags[:, :, None].astype(jnp.float32)
    whitened = (centered * lax.rsqrt(mean_power + 1e-05) * flag_values).astype(jnp.bfloat16)
    pieces = []
    for owner in range(lax.axis_size("src")):
        pieces.append(broadcast(whitened, "src", owner))
    everyone = jnp.concatenate(pieces, axis=0)
    sources = jnp.take(everyone, source_index, axis=0)
    source_count = sources.shape[0]
    norm_factor = 1.0 / math.sqrt(traces.shape[1] * lax.axis_size("blk") * segment)
    own_rows = whitened.shape[0] // lax.axis_size("blk")
    flat_sources = sources.reshape(source_count, -1)
    padded = jnp.pad(whitened, ((0, 0), (0, 0), (MAXLAG, MAXLAG)))
    block_rows = math.gcd(lax.axis_size("blk") * own_rows, 16)
    grouped = padded.reshape(
        (lax.axis_size("blk") * own_rows // block_rows, block_rows) + padded.shape[1:]
    )

    def one_block(group):
        toeplitz = toeplitz_rows(group, LAG_COUNT, segment)
        products = lax.dot_general(
            toeplitz, flat_sources, (((1,), (1,)), ((), ())), preferred_element_type=jnp.float32
        )
        return (products * norm_factor).reshape(block_rows, LAG_COUNT, source_count)

    result = lax.map(one_block, grouped)
    return lax.psum_scatter(
        result.reshape(lax.axis_size("blk") * own_rows, LAG_COUNT, source_count),
        "blk",
        scatter_dimension=0,
        tiled=True,
    )


class Plan:
    def __init__(self, half, windows, segment, blk_size, src_size, source_count):
        self.half = half
        self.windows = windows
        self.segment = segment
        self.blk_size = blk_size
        self.src_size = src_size
        self.channels = half * src_size
        self.source_count = source_count
        self.half_lanes = LANES // 2
        self.coarse = self.half_lanes // half
        if self.coarse == 0:
            return
        self.fine = -(-LAG_COUNT // self.coarse)
        self.fine_padded = -(-self.fine // (2 * GROUP)) * 2 * GROUP
        self.own = half // blk_size
        reach = segment + (self.coarse - 1) * self.fine
        self.span = -(-max(reach, segment + 2 * MAXLAG) // 128) * 128
        self.whole_groups = self.fine // GROUP * GROUP
        self.rest = self.fine - self.whole_groups
        rows = self.own * self.fine
        self.rows = -(-rows // 16) * 16
        self.targets = blk_size // 2
        self.receivers = self.targets * self.own
        self.lag_rows = -(-self.receivers * self.fine // 32) * 32
        self.norm_factor = 1.0 / math.sqrt(windows * blk_size * segment)

    def fits(self):
        return (
            self.coarse >= 2
            and self.src_size == 2
            and self.half % self.blk_size == 0
            and self.half % GROUP == 0
            and self.half % IN_PARTS == 0
            and self.channels % 16 == 0
            and self.windows * self.half % 16 == 0
            and self.blk_size == 8
            and self.rest > 0
            and GROUP % self.rest == 0
            and self.receivers * self.rest % GROUP == 0
            and self.receivers % 2 == 0
            and self.receivers * self.whole_groups % 16 == 0
        )


def whiten_kernel(plan, traces_hbm, flags_hbm, out_ref, traces_ref, flags_ref, sems):
    part = plan.half // IN_PARTS
    copies = [pltpu.make_async_copy(flags_hbm, flags_ref, sems.at[IN_PARTS])]
    for index in range(IN_PARTS):
        at = pl.ds(index * part, part)
        copies.append(pltpu.make_async_copy(traces_hbm.at[at], traces_ref.at[at], sems.at[index]))
    for copy in copies:
        copy.start()
    copies[0].wait()
    flag_values = [
        flags_ref[window : window + 1, :].astype(jnp.float32).reshape(plan.half, 1) for window in range(plan.windows)
    ]
    for copy in copies[1:]:
        copy.wait()
    pieces = []
    for window in range(plan.windows):
        values = traces_ref[:, window, :]
        centered = values - jnp.mean(values, axis=1, keepdims=True)
        mean_power = jnp.mean(centered * centered, axis=1, keepdims=True)
        pieces.append(centered * lax.rsqrt(mean_power + 1e-05) * flag_values[window])
    out_ref[...] = jnp.concatenate(pieces, axis=0).astype(jnp.bfloat16)


def lag_rows(plan, rows_ref, toeplitz_ref):
    span = plan.span
    me = lax.axis_index("blk")
    filler = jnp.zeros((1, span - plan.segment), jnp.float32)
    spare = jnp.zeros((plan.lag_rows - plan.receivers * plan.fine, span), jnp.float32)
    sublane = lax.broadcasted_iota(jnp.int32, (GROUP, span), 0)
    for window in range(plan.windows):
        at = slice(window * span, (window + 1) * span)
        spread_rows = []
        for hop in HOPS:
            for member in range(plan.own):
                channel = window * plan.half + (me ^ hop) * plan.own + member
                row = jnp.concatenate([rows_ref[pl.ds(channel, 1), :], filler], axis=1)
                spread_rows.append(jnp.broadcast_to(row, (GROUP, span)))
        for first in range(0, plan.receivers, 2):
            pieces = [
                pltpu.roll(row, (MAXLAG - plan.whole_groups + 1 + lag) % span, 1, stride=1, stride_axis=0)
                for row in spread_rows[first : first + 2]
                for lag in range(0, plan.whole_groups, GROUP)
            ]
            start = first * plan.whole_groups
            toeplitz_ref[start : start + 2 * plan.whole_groups, at] = jnp.concatenate(pieces, axis=0).astype(
                jnp.bfloat16
            )
        pieces = []
        for first in range(0, plan.receivers, GROUP // plan.rest):
            mixed = spread_rows[first]
            for index in range(1, GROUP // plan.rest):
                mixed = jnp.where(sublane >= index * plan.rest, spread_rows[first + index], mixed)
            tile = pltpu.roll(mixed, (MAXLAG - plan.whole_groups) % span, 1)
            for lag in range(1, plan.rest):
                later = pltpu.roll(mixed, (MAXLAG - plan.whole_groups - lag) % span, 1)
                tile = jnp.where(sublane % plan.rest == lag, later, tile)
            pieces.append(tile)
        start = plan.receivers * plan.whole_groups
        toeplitz_ref[start:, at] = jnp.concatenate(pieces + [spare], axis=0).astype(jnp.bfloat16)


def fill_columns(plan, values, columns_ref):
    span = plan.span
    filler = jnp.zeros((plan.half, span - plan.segment), jnp.float32)
    spare = jnp.zeros((plan.half_lanes - plan.coarse * plan.half, span), jnp.float32)
    for window in range(plan.windows):
        rows = jnp.concatenate([values[window * plan.half : (window + 1) * plan.half], filler], axis=1)
        pieces = [rows] + [pltpu.roll(rows, step * plan.fine, 1) for step in range(1, plan.coarse)]
        if spare.shape[0]:
            pieces.append(spare)
        columns_ref[:, window * span : (window + 1) * span] = jnp.concatenate(pieces, axis=0).astype(jnp.bfloat16)


def product(toeplitz_ref, columns_ref):
    return lax.dot_general(
        toeplitz_ref[...], columns_ref[...], (((1,), (1,)), ((), ())), preferred_element_type=jnp.float32
    )


def near_kernel(plan, *refs):
    mine_refs, (other_ref, sum_ref, rows_ref, toeplitz_ref, columns_ref) = refs[: plan.windows], refs[plan.windows :]
    for window, mine_ref in enumerate(mine_refs):
        rows_ref[window * plan.half : (window + 1) * plan.half, :] = mine_ref[...].astype(jnp.float32)
    lag_rows(plan, rows_ref, toeplitz_ref)
    fill_columns(plan, rows_ref[...], columns_ref.at[: plan.half_lanes])
    fill_columns(plan, other_ref[...].astype(jnp.float32), columns_ref.at[plan.half_lanes :])
    sum_ref[...] = product(toeplitz_ref, columns_ref)


def across_kernel(plan, mine_ref, prior_ref, toeplitz_ref, left_ref, right_ref, rows_ref, columns_ref):
    rows_ref[...] = mine_ref[...].astype(jnp.float32)
    lag_rows(plan, rows_ref, toeplitz_ref)
    fill_columns(plan, rows_ref[...], columns_ref)
    left = prior_ref[:, : plan.half_lanes] + product(toeplitz_ref, columns_ref)
    for place, block in enumerate(pack(plan, left)):
        left_ref[place * plan.rows : (place + 1) * plan.rows, :] = block
    right_ref[...] = prior_ref[:, plan.half_lanes :]


def pack(plan, products):
    width = products.shape[1]
    back = GROUP - 1 - lax.broadcasted_iota(jnp.int32, (GROUP, width), 0)
    packed = []
    for place in range(plan.targets):
        pieces = []
        for receiver in range(place * plan.own, (place + 1) * plan.own):
            last = (receiver + 1) * plan.whole_groups
            pieces += [
                jnp.take_along_axis(products[last - lag - GROUP : last - lag], back, axis=0)
                for lag in range(0, plan.whole_groups, GROUP)
            ]
        first = plan.receivers * plan.whole_groups + place * plan.own * plan.rest
        pieces.append(products[first : first + plan.own * plan.rest])
        if plan.rows > plan.own * plan.fine:
            pieces.append(jnp.zeros((plan.rows - plan.own * plan.fine, width), jnp.float32))
        packed.append(jnp.concatenate(pieces, axis=0))
    return packed


def finish_kernel(plan, other_ref, toeplitz_ref, left_ref, right_ref, *refs):
    *out_refs, columns_ref = refs
    fill_columns(plan, other_ref[...].astype(jnp.float32), columns_ref)
    right = pack(plan, right_ref[...] + product(toeplitz_ref, columns_ref))
    for place, out_ref in enumerate(out_refs):
        rows = slice(place * plan.rows, (place + 1) * plan.rows)
        out_ref[...] = jnp.concatenate([left_ref[rows, :], right[place]], axis=1).astype(jnp.bfloat16)


def spread(plan, values):
    high = values.astype(jnp.bfloat16).astype(jnp.float32)
    low = values - high
    lane = lax.broadcasted_iota(jnp.int32, values.shape, 1)
    lane = jnp.where(lane >= plan.half_lanes, lane - plan.half_lanes, lane)
    up = pltpu.roll(low, plan.half, 1)
    down = pltpu.roll(low, LANES - plan.half, 1)
    pieces = []
    for step in range(plan.coarse):
        beside, moved = (step + 1, up) if step + 1 < plan.coarse else (step - 1, down)
        kept = jnp.where((lane >= step * plan.half) & (lane < (step + 1) * plan.half), high, 0.0)
        there = (lane >= beside * plan.half) & (lane < (beside + 1) * plan.half)
        pieces.append(jnp.where(there, moved, kept).astype(jnp.bfloat16))
    return jnp.concatenate(pieces, axis=0)


def choose_kernel(plan, index_ref, whitened_ref, chosen_ref, *same_refs):
    whitened = whitened_ref[...].astype(jnp.float32)
    for window, same_ref in enumerate(same_refs):
        same_ref[...] = whitened[window * plan.half : (window + 1) * plan.half].astype(jnp.bfloat16)
    first = lax.axis_index("src") * plan.half
    index = index_ref[...] - first
    index = jnp.where(index < 0, index + plan.channels, index)
    lane = jnp.where(index >= plan.half, index - plan.half + plan.half_lanes, index)
    at_column = lax.broadcasted_iota(jnp.int32, (LANES, plan.source_count), 0)
    chosen = jnp.zeros((LANES, plan.source_count), jnp.bool_)
    for step in range(plan.coarse):
        chosen = chosen | (at_column == lane + step * plan.half)
    chosen_ref[...] = chosen.astype(jnp.float32).astype(jnp.bfloat16)


def expand_kernel(plan, chosen_ref, *refs):
    *arrived_refs, out_hbm, out_ref, sems = refs
    total = sum(ref[...].astype(jnp.float32) for ref in arrived_refs) * plan.norm_factor
    chosen = chosen_ref[...]
    filler = jnp.zeros((plan.fine_padded - plan.fine, LANES), jnp.float32)
    copies = []
    for member in range(plan.own):
        rest = plan.own * plan.whole_groups + member * plan.rest
        rows = jnp.concatenate(
            [
                total[member * plan.whole_groups : (member + 1) * plan.whole_groups],
                total[rest : rest + plan.rest],
                filler,
            ],
            axis=0,
        )
        expanded = jnp.dot(spread(plan, rows), chosen, preferred_element_type=jnp.float32)
        for step in range(plan.coarse):
            start = step * plan.fine
            count = min(plan.fine, LAG_COUNT - start)
            first = step * plan.fine_padded
            out_ref[member, start : start + count, :] = expanded[first : first + count]
        copies.append(pltpu.make_async_copy(out_ref.at[member], out_hbm.at[member], sems.at[member]))
        copies[-1].start()
    for copy in copies:
        copy.wait()


def few_channels(plan, traces, valid_flags, source_index):
    vmem = pl.BlockSpec(memory_space=pltpu.VMEM)
    params = pltpu.CompilerParams(vmem_limit_bytes=32 * 1024 * 1024)
    packed_rows = plan.windows * plan.half
    flags = valid_flags.T

    def swap_cores(array):
        return lax.ppermute(array, "src", [(0, 1), (1, 0)])

    def swap_blk(array, hop):
        pairs = [
            (place * plan.src_size + core, (place ^ hop) * plan.src_size + 1 - core)
            for place in range(plan.blk_size)
            for core in range(plan.src_size)
        ]
        return lax.ppermute(array, ("blk", "src"), pairs)

    whitened = pl.pallas_call(
        functools.partial(whiten_kernel, plan),
        out_shape=pltpu.VMEM((packed_rows, plan.segment), jnp.bfloat16),
        in_specs=[pl.BlockSpec(memory_space=pl.ANY)] * 2,
        out_specs=vmem,
        scratch_shapes=[
            pltpu.VMEM(traces.shape, jnp.float32),
            pltpu.VMEM(flags.shape, jnp.int32),
            pltpu.SemaphoreType.DMA((IN_PARTS + 1,)),
        ],
        compiler_params=pltpu.CompilerParams(vmem_limit_bytes=60 * 1024 * 1024),
        name="whiten",
    )(traces, flags)

    height = plan.lag_rows
    width = plan.windows * plan.span
    rows = pltpu.VMEM((packed_rows, plan.segment), jnp.float32)
    toeplitz = (height, width)
    columns = (plan.half_lanes, width)
    sums = jax.ShapeDtypeStruct((height, LANES), jnp.float32)

    def call(kernel, name, operands, outputs, scratch=()):
        return pl.pallas_call(
            functools.partial(kernel, plan),
            out_shape=outputs,
            in_specs=[vmem] * len(operands),
            out_specs=[vmem] * len(outputs),
            scratch_shapes=scratch,
            compiler_params=params,
            name=name,
        )(*operands)

    across = swap_blk(whitened, plan.targets)
    chosen, *same = call(
        choose_kernel,
        "choose",
        (source_index.reshape(1, -1), whitened),
        (
            jax.ShapeDtypeStruct((LANES, plan.source_count), jnp.bfloat16),
            *[jax.ShapeDtypeStruct((plan.half, plan.segment), whitened.dtype)] * plan.windows,
        ),
    )
    (total,) = call(
        near_kernel,
        "near",
        (*[swap_cores(array) for array in same], whitened),
        (sums,),
        (rows, pltpu.VMEM(toeplitz, jnp.bfloat16), pltpu.VMEM((LANES, width), jnp.bfloat16)),
    )
    across, total = lax.optimization_barrier((across, total))
    across_other = swap_cores(across)
    lagged, left, right = call(
        across_kernel,
        "across",
        (across, total),
        (
            jax.ShapeDtypeStruct(toeplitz, jnp.bfloat16),
            jax.ShapeDtypeStruct((plan.targets * plan.rows, plan.half_lanes), jnp.float32),
            jax.ShapeDtypeStruct((height, plan.half_lanes), jnp.float32),
        ),
        (rows, pltpu.VMEM(columns, jnp.bfloat16)),
    )
    sent = call(
        finish_kernel,
        "finish",
        (across_other, lagged, left, right),
        (jax.ShapeDtypeStruct((plan.rows, LANES), jnp.bfloat16),) * plan.targets,
        (pltpu.VMEM(columns, jnp.bfloat16),),
    )
    arrived = [swap_blk(array, hop) for array, hop in zip(sent, HOPS)]
    out_shape = (plan.own, LAG_COUNT, plan.source_count)
    return pl.pallas_call(
        functools.partial(expand_kernel, plan),
        out_shape=jax.ShapeDtypeStruct(out_shape, jnp.float32),
        in_specs=[vmem] * (1 + len(arrived)),
        out_specs=pl.BlockSpec(memory_space=pl.ANY),
        scratch_shapes=[pltpu.VMEM(out_shape, jnp.float32), pltpu.SemaphoreType.DMA((plan.own,))],
        compiler_params=params,
        name="expand",
    )(chosen, *arrived)


def body(traces, valid_flags, source_index):
    plan = Plan(
        traces.shape[0],
        traces.shape[1],
        traces.shape[2],
        lax.axis_size("blk"),
        lax.axis_size("src"),
        source_index.shape[0],
    )
    if plan.fits():
        return few_channels(plan, traces, valid_flags, source_index)
    return many_channels(traces, valid_flags, source_index)


def solution(mesh):
    in_specs = (P(("fibre", "src"), "blk", None), P(("fibre", "src"), "blk"), P())
    out_specs = P(("fibre", "src", "blk"), None, None)
    return jax.shard_map(body, mesh=mesh, in_specs=in_specs, out_specs=out_specs, check_vma=False)
```
